32 devices in a mesh: seq: 4 (over z), stream: 8 (over y, x, core).
Axes of the slice: x: 2, y: 2, z: 4, core: 2. Of those that a mesh axis runs over, the one named last changes fastest.
Arguments:
- frames: bfloat16 [16, 2048, 80], P('stream', 'seq'), may hold values from -6 to 6
- targets: int32 [16, 2048], P('stream', 'seq'), may hold values from 0 to 1023
- frame_count: int32 [16], P('stream'), may hold values from 512 to 2048, as said below
- memory: bfloat16 [2, 16, 512, 512], P(None, 'stream'), may hold values from -6 to 6
- memory_len: int32 [16], P('stream'), may hold values from 0 to 512, as said below
- input_weight: float32 [80, 512], P(None, 'stream'), may hold values from -0.625 to 0.625
- project_weight: float32 [2, 512, 1536], P(None, 'stream'), may hold values from -0.25 to 0.25
- output_weight: float32 [2, 512, 512], P(None, 'stream'), may hold values from -1 to 1
- up_weight: float32 [2, 512, 2048], P(None, 'stream'), may hold values from -0.25 to 0.25
- down_weight: float32 [2, 2048, 512], P(None, 'stream'), may hold values from -0.125 to 0.125
- head_weight: float32 [512, 1024], P('stream'), may hold values from -0.25 to 0.25
- vectors: float32 [11, 512], P(None, 'stream'), may hold values from -1.6 to 2
- slopes: float32 [2, 8], replicated, may hold values from 0.00048828125 to 0.00390625
- first_input: float32 [80, 512], P(None, 'stream'), may hold values from -4.7683716e-07 to 4.7683716e-07
- first_project: float32 [2, 512, 1536], P(None, 'stream'), may hold values from -4.7683716e-07 to 4.7683716e-07
- first_output: float32 [2, 512, 512], P(None, 'stream'), may hold values from -4.7683716e-07 to 4.7683716e-07
- first_up: float32 [2, 512, 2048], P(None, 'stream'), may hold values from -4.7683716e-07 to 4.7683716e-07
- first_down: float32 [2, 2048, 512], P(None, 'stream'), may hold values from -4.7683716e-07 to 4.7683716e-07
- first_head: float32 [512, 1024], P('stream'), may hold values from -4.7683716e-07 to 4.7683716e-07
- first_vectors: float32 [11, 512], P(None, 'stream'), may hold values from -4.7683716e-07 to 4.7683716e-07
- first_slopes: float32 [2, 8], replicated, may hold values from -4.7683716e-07 to 4.7683716e-07
- second_input: float32 [80, 512], P(None, 'stream'), may hold values from 5.8289055e-17 to 2.3315622e-16
- second_project: float32 [2, 512, 1536], P(None, 'stream'), may hold values from 5.8289054e-16 to 2.3315622e-15
- second_output: float32 [2, 512, 512], P(None, 'stream'), may hold values from 5.8289054e-16 to 2.3315622e-15
- second_up: float32 [2, 512, 2048], P(None, 'stream'), may hold values from 5.8289054e-16 to 2.3315622e-15
- second_down: float32 [2, 2048, 512], P(None, 'stream'), may hold values from 5.8289054e-16 to 2.3315622e-15
- second_head: float32 [512, 1024], P('stream'), may hold values from 5.8289054e-16 to 2.3315622e-15
- second_vectors: float32 [11, 512], P(None, 'stream'), may hold values from 5.8289054e-16 to 2.3315622e-15
- second_slopes: float32 [2, 8], replicated, may hold values from 5.8289054e-16 to 2.3315622e-15
Outputs:
- loss: float32 [], replicated
- layer_inputs: bfloat16 [2, 16, 2048, 512], P(None, 'stream', 'seq')
- clip_norm: float32 [], replicated
- norms: float32 [22, 2], replicated
- updated_input: float32 [80, 512], P(None, 'stream')
- updated_project: float32 [2, 512, 1536], P(None, 'stream')
- updated_output: float32 [2, 512, 512], P(None, 'stream')
- updated_up: float32 [2, 512, 2048], P(None, 'stream')
- updated_down: float32 [2, 2048, 512], P(None, 'stream')
- updated_head: float32 [512, 1024], P('stream')
- updated_vectors: float32 [11, 512], P(None, 'stream')
- updated_slopes: float32 [2, 8], replicated
- new_first_input: float32 [80, 512], P(None, 'stream')
- new_first_project: float32 [2, 512, 1536], P(None, 'stream')
- new_first_output: float32 [2, 512, 512], P(None, 'stream')
- new_first_up: float32 [2, 512, 2048], P(None, 'stream')
- new_first_down: float32 [2, 2048, 512], P(None, 'stream')
- new_first_head: float32 [512, 1024], P('stream')
- new_first_vectors: float32 [11, 512], P(None, 'stream')
- new_first_slopes: float32 [2, 8], replicated
- new_second_input: float32 [80, 512], P(None, 'stream')
- new_second_project: float32 [2, 512, 1536], P(None, 'stream')
- new_second_output: float32 [2, 512, 512], P(None, 'stream')
- new_second_up: float32 [2, 512, 2048], P(None, 'stream')
- new_second_down: float32 [2, 2048, 512], P(None, 'stream')
- new_second_head: float32 [512, 1024], P('stream')
- new_second_vectors: float32 [11, 512], P(None, 'stream')
- new_second_slopes: float32 [2, 8], replicated
The draws below stay inside these ranges and needn't reach their ends.
Inputs may be any that keep to these rules, and one draw needn't show every extreme that they name: Each stream counts its first frame_count frames; some stream counts all 2048. The last memory_len rows of a stream's memory are valid; some stream has all 512, another none.
All inputs are finite; a program needn't handle non-finite values.
Results may differ from the reference program's by a relative error of at most 0.019.
Values may be sent and summed in bfloat16 or wider, within the bound.
A program may use at most 384 MiB of HBM per device.

```python
import math
import jax
import jax.numpy as jnp
from jax import lax

D = 512
H = 8
FF = 2048
V = 1024
IN = 80
LAYERS = 2
SPAN = 512
STEP = 10
STREAMS = 16
SEQ = 2048
NVEC = 11
NPARAM = 6862352


def draw_frame_count(key, part):
    key = jax.random.fold_in(key, 11)
    count_key, pick_key = jax.random.split(key)
    counts = jax.random.randint(count_key, (STREAMS,), SEQ // 4, SEQ + 1)
    chosen = jax.random.randint(pick_key, (), 0, STREAMS)
    return jnp.where(jnp.arange(STREAMS) == chosen, SEQ, counts).astype(jnp.int32)


def draw_memory_len(key, part):
    key = jax.random.fold_in(key, 12)
    keys = jax.random.split(key, 3)
    lengths = jax.random.randint(keys[0], (STREAMS,), 0, SPAN + 1)
    full = jax.random.randint(keys[1], (), 0, STREAMS)
    empty = (full + 1 + jax.random.randint(keys[2], (), 0, STREAMS - 1)) % STREAMS
    index = jnp.arange(STREAMS)
    lengths = jnp.where(index == full, SPAN, lengths)
    return jnp.where(index == empty, 0, lengths).astype(jnp.int32)


def draw_vectors(key, part):
    key = jax.random.fold_in(key, 13)
    noise_key, bias_key = jax.random.split(key)
    row_index = jnp.arange(NVEC)[:, None]
    column = jnp.arange(D)[None, :].astype(jnp.float32) / D
    is_gain = jnp.logical_or(row_index == 1, jnp.logical_and(row_index >= 3, (row_index - 3) % 2 == 0))
    gains = (0.5 + column) * jax.random.uniform(noise_key, (NVEC, D), minval=0.8, maxval=1.2)
    biases = jax.random.uniform(bias_key, (NVEC, D), minval=-0.5, maxval=0.5)
    biases = jnp.where(row_index == 0, 2.0 * biases, biases)
    return jnp.where(is_gain, gains, biases).astype(jnp.float32)


def plant(entries, key, smallest, top_value):
    shape = entries.shape
    place = [jax.random.randint(jax.random.fold_in(key, axis), (), 0, shape[axis]) for axis in range(len(shape))]
    entries = entries.at[tuple(place)].set(smallest)
    longest = shape.index(max(shape))
    place[longest] = (place[longest] + 1) % shape[longest]
    return entries.at[tuple(place)].set(top_value)


def steps_of(stream_key, extent, cuts, low, largest):
    def one(dim, shards_of):
        steps = jax.random.uniform(jax.random.fold_in(jax.random.fold_in(stream_key, 6), dim), (shards_of,), jnp.float32, low / len(cuts), largest / len(cuts))
        return jnp.repeat(jnp.exp(steps), extent[dim] // shards_of).reshape((-1,) + (1,) * (len(extent) - dim - 1))

    loudness = one(*cuts[0])
    for cut in cuts[1:]:
        loudness = loudness * one(*cut)
    return loudness


def normal_values(own_key, dims, spread, bound, cuts=(), held_as=jnp.bfloat16):
    entries = spread * jax.random.normal(own_key, dims, jnp.float32)
    if cuts:
        entries = entries * steps_of(own_key, dims, cuts, -0.22, 0.18)
    return jnp.clip(entries, -bound, bound).astype(held_as)


def setup_inputs(seed: int = 0) -> dict:
    streams_of = jax.random.split(jax.random.key(seed), 30)
    return {
        "frames": normal_values(streams_of[0], (STREAMS, SEQ, IN), 1.0, 6.0, ((0, 8), (1, 4))),
        "targets": plant(jax.random.randint(streams_of[1], (STREAMS, SEQ), 0, V), jax.random.fold_in(streams_of[1], 1), 0, V - 1).astype(jnp.int32),
        "frame_count": draw_frame_count(jax.random.fold_in(streams_of[29], 71), 0),
        "memory": normal_values(streams_of[3], (LAYERS, STREAMS, SPAN, D), 1.0, 6.0, ((1, 8),)),
        "memory_len": draw_memory_len(jax.random.fold_in(streams_of[29], 71), 0),
        "input_weight": normal_values(streams_of[5], (IN, D), IN ** -0.5, 0.625, ((1, 8),), jnp.float32),
        "project_weight": normal_values(streams_of[6], (LAYERS, D, 3 * D), D ** -0.5, 0.25, ((1, 8),), jnp.float32),
        "output_weight": normal_values(streams_of[7], (LAYERS, D, D), (D // 16) ** -0.5, 1.0, ((1, 8),), jnp.float32),
        "up_weight": normal_values(streams_of[8], (LAYERS, D, FF), D ** -0.5, 0.25, ((1, 8),), jnp.float32),
        "down_weight": normal_values(streams_of[9], (LAYERS, FF, D), FF ** -0.5, 0.125, ((1, 8),), jnp.float32),
        "head_weight": normal_values(streams_of[10], (D, V), D ** -0.5, 0.25, ((0, 8),), jnp.float32),
        "vectors": draw_vectors(jax.random.fold_in(streams_of[29], 71), 0),
        "slopes": jnp.clip(jnp.exp(jax.random.uniform(streams_of[12], (LAYERS, H), jnp.float32, math.log(0.00048828125), math.log(0.00390625))), 0.00048828125, 0.00390625),
        "first_input": normal_values(streams_of[13], (IN, D), (0.00022 * NPARAM ** -0.5), 4.76837158203125e-07, ((1, 8),), jnp.float32),
        "first_project": normal_values(streams_of[14], (LAYERS, D, 3 * D), (0.00022 * NPARAM ** -0.5), 4.76837158203125e-07, ((1, 8),), jnp.float32),
        "first_output": normal_values(streams_of[15], (LAYERS, D, D), (0.00022 * NPARAM ** -0.5), 4.76837158203125e-07, ((1, 8),), jnp.float32),
        "first_up": normal_values(streams_of[16], (LAYERS, D, FF), (0.00022 * NPARAM ** -0.5), 4.76837158203125e-07, ((1, 8),), jnp.float32),
        "first_down": normal_values(streams_of[17], (LAYERS, FF, D), (0.00022 * NPARAM ** -0.5), 4.76837158203125e-07, ((1, 8),), jnp.float32),
        "first_head": normal_values(streams_of[18], (D, V), (0.00022 * NPARAM ** -0.5), 4.76837158203125e-07, ((0, 8),), jnp.float32),
        "first_vectors": normal_values(streams_of[19], (NVEC, D), (0.00022 * NPARAM ** -0.5), 4.76837158203125e-07, ((1, 8),), jnp.float32),
        "first_slopes": normal_values(streams_of[20], (LAYERS, H), (0.00022 * NPARAM ** -0.5), 4.76837158203125e-07, (), jnp.float32),
        "second_input": jnp.clip(jnp.exp(math.log(2.3315622135512964e-16) - 1.3862944 * jax.random.uniform(streams_of[21], (IN, D), jnp.float32) ** steps_of(streams_of[21], (IN, D), ((1, 8),), -0.2, 0.2)), 5.828905533878241e-17, 2.3315622135512964e-16),
        "second_project": jnp.clip(jnp.exp(math.log(2.331562160611737e-15) - 1.3862944 * jax.random.uniform(streams_of[22], (LAYERS, D, 3 * D), jnp.float32) ** steps_of(streams_of[22], (LAYERS, D, 3 * D), ((1, 8),), -0.2, 0.2)), 5.828905401529343e-16, 2.331562160611737e-15),
        "second_output": jnp.clip(jnp.exp(math.log(2.331562160611737e-15) - 1.3862944 * jax.random.uniform(streams_of[23], (LAYERS, D, D), jnp.float32) ** steps_of(streams_of[23], (LAYERS, D, D), ((1, 8),), -0.2, 0.2)), 5.828905401529343e-16, 2.331562160611737e-15),
        "second_up": jnp.clip(jnp.exp(math.log(2.331562160611737e-15) - 1.3862944 * jax.random.uniform(streams_of[24], (LAYERS, D, FF), jnp.float32) ** steps_of(streams_of[24], (LAYERS, D, FF), ((1, 8),), -0.2, 0.2)), 5.828905401529343e-16, 2.331562160611737e-15),
        "second_down": jnp.clip(jnp.exp(math.log(2.331562160611737e-15) - 1.3862944 * jax.random.uniform(streams_of[25], (LAYERS, FF, D), jnp.float32) ** steps_of(streams_of[25], (LAYERS, FF, D), ((1, 8),), -0.2, 0.2)), 5.828905401529343e-16, 2.331562160611737e-15),
        "second_head": jnp.clip(jnp.exp(math.log(2.331562160611737e-15) - 1.3862944 * jax.random.uniform(streams_of[26], (D, V), jnp.float32) ** steps_of(streams_of[26], (D, V), ((0, 8),), -0.2, 0.2)), 5.828905401529343e-16, 2.331562160611737e-15),
        "second_vectors": jnp.clip(jnp.exp(math.log(2.331562160611737e-15) - 1.3862944 * jax.random.uniform(streams_of[27], (NVEC, D), jnp.float32) ** steps_of(streams_of[27], (NVEC, D), ((1, 8),), -0.2, 0.2)), 5.828905401529343e-16, 2.331562160611737e-15),
        "second_slopes": jnp.clip(jnp.exp(jax.random.uniform(streams_of[28], (LAYERS, H), jnp.float32, math.log(5.828905401529343e-16), math.log(2.331562160611737e-15))), 5.828905401529343e-16, 2.331562160611737e-15),
    }


ln_eps = 1e-05
clip_limit = 0.002
beta_one = 0.9
beta_two = 0.999
lamb_rate = 0.3
slope_rate = 0.001
decay_rate = 0.01
adam_eps = 1e-11
masked_score = -1e+30
highest = lax.Precision.HIGHEST

@jax.custom_vjp
def low(v):
    return lax.optimization_barrier(v.astype(jnp.bfloat16)).astype(jnp.float32)

@jax.custom_vjp
def low_back(v):
    return v

def low_keep(v):
    return (low(v), None)

def low_pass(kept, grad):
    return (grad,)

def back_keep(v):
    return (v, None)

def back_low(kept, grad):
    return (low(grad),)
low.defvjp(low_keep, low_pass)
low_back.defvjp(back_keep, back_low)

def matmul(left, right):
    return jnp.dot(left, right, precision=highest, preferred_element_type=jnp.float32)

def layer_norm(values, gain, bias):
    centred = values - lax.optimization_barrier(jnp.mean(values, axis=-1, keepdims=True))
    variance = lax.optimization_barrier(jnp.mean(centred * centred, axis=-1, keepdims=True))
    return centred * lax.rsqrt(variance + ln_eps) * gain + bias

def span_attention(query, keys, values, allowed, distance, slope):
    scale = query.shape[-1] ** (-0.5)
    raw = jnp.einsum('qhd,khd->hqk', query, keys, precision=highest) * scale
    raw = low_back(raw - slope[:, None, None] * distance[None])
    score = jnp.where(allowed[None], raw, masked_score)
    peak = lax.optimization_barrier(jnp.max(score, axis=-1, keepdims=True))
    exponent = jnp.exp(score - peak)
    attention = low(exponent / lax.optimization_barrier(jnp.sum(exponent, axis=-1, keepdims=True)))
    return jnp.einsum('hqk,khd->qhd', attention, values, precision=highest)

def transformer_layer(residual, weights, rows, slope, memory_rows, memory_len):
    project, output, upward, downward = weights
    gain_one, bias_one, gain_two, bias_two = rows
    width = residual.shape[-1]
    span = memory_rows.shape[0]
    heads = slope.shape[0]
    blocks = residual.shape[0] // span
    normed = low(layer_norm(residual, gain_one, bias_one))
    projected = low_back(low(matmul(normed, project)))
    memory_normed = low(layer_norm(memory_rows, gain_one, bias_one))
    memory_kv = low_back(low(matmul(memory_normed, project[:, width:])))
    key_value = projected[:, width:]
    prior = jnp.concatenate([memory_kv, key_value[:-span]], axis=0)
    shape_four = (blocks, span, heads, width // heads)
    queries = projected[:, :width].reshape(shape_four)
    keys_all = jnp.concatenate([prior[:, :width].reshape(shape_four), key_value[:, :width].reshape(shape_four)], axis=1)
    values_all = jnp.concatenate([prior[:, width:].reshape(shape_four), key_value[:, width:].reshape(shape_four)], axis=1)
    query_pos = jnp.arange(span)
    key_pos = jnp.arange(2 * span)
    distance = (query_pos[:, None] + span - key_pos[None]).astype(jnp.float32)

    def block_attention(item):
        query, keys, values, block = item
        prior_ok = jnp.logical_or(block > 0, key_pos >= span - memory_len)
        local_ok = key_pos[None] - span <= query_pos[:, None]
        allowed = jnp.where(key_pos[None] < span, prior_ok[None], local_ok)
        return span_attention(query, keys, values, allowed, distance, slope)
    attended = lax.map(jax.checkpoint(block_attention), (queries, keys_all, values_all, jnp.arange(blocks)))
    mixed = low_back(low(attended.reshape((blocks * span, width))))
    after = residual + low_back(matmul(mixed, output))
    normed_two = low(layer_norm(after, gain_two, bias_two))
    hidden = low_back(matmul(normed_two, upward))
    active = low(jax.nn.gelu(hidden, approximate=False))
    return after + low_back(matmul(active, downward))

def stream_loss(params, frames, targets, count, memory, memory_len):
    input_low = low(params[0])
    project_low = low(params[1])
    output_low = low(params[2])
    up_low = low(params[3])
    down_low = low(params[4])
    head_low = low(params[5])
    rows_all = low(params[6])
    slopes = params[7]
    residual = low_back(matmul(frames, input_low)) + rows_all[0]
    inputs = []
    for layer in range(LAYERS):
        inputs.append(residual)
        rows = rows_all[3 + 4 * layer:7 + 4 * layer]
        weights = (project_low[layer], output_low[layer], up_low[layer], down_low[layer])
        residual = transformer_layer(residual, weights, rows, slopes[layer], memory[layer], memory_len)
    normed = low(layer_norm(residual, rows_all[1], rows_all[2]))
    logits = low_back(matmul(normed, head_low))
    log_total = jax.nn.logsumexp(logits, axis=-1)
    onehot = jnp.arange(logits.shape[-1])[None] == targets[:, None]
    picked = lax.optimization_barrier(jnp.sum(jnp.where(onehot, logits, 0.0), axis=-1))
    share = jnp.where(jnp.arange(SEQ) < count, 1.0 / (count.astype(jnp.float32) * STREAMS), 0.0)
    return (jnp.sum(share * (log_total - picked)), jnp.stack(inputs))

def adam_direction(weight, grad, first, second, decay):
    new_first = beta_one * first + (1.0 - beta_one) * grad
    new_second = beta_two * second + (1.0 - beta_two) * grad * grad
    first_hat = new_first / (1.0 - beta_one ** STEP)
    second_hat = new_second / (1.0 - beta_two ** STEP)
    return (new_first, new_second, first_hat / (jnp.sqrt(second_hat) + adam_eps) + decay * weight)

def lamb_group(weight, grad, first, second, axes):
    new_first, new_second, update = adam_direction(weight, grad, first, second, decay_rate)
    weight_norm = jnp.sqrt(lax.optimization_barrier(jnp.sum(weight * weight, axis=axes, keepdims=True)))
    update_norm = jnp.sqrt(lax.optimization_barrier(jnp.sum(update * update, axis=axes, keepdims=True)))
    fresh = weight - lamb_rate * (weight_norm / update_norm) * update
    return (fresh, new_first, new_second, weight_norm.reshape(-1), update_norm.reshape(-1))

def reference(frames, targets, frame_count, memory, memory_len, input_weight, project_weight, output_weight, up_weight, down_weight, head_weight, vectors, slopes, first_input, first_project, first_output, first_up, first_down, first_head, first_vectors, first_slopes, second_input, second_project, second_output, second_up, second_down, second_head, second_vectors, second_slopes):
    params = tuple((item.astype(jnp.float32) for item in (input_weight, project_weight, output_weight, up_weight, down_weight, head_weight, vectors, slopes)))

    def one_stream(totals, item):
        frames_one, targets_one, count_one, memory_one, length_one = item

        def objective(weights):
            return stream_loss(weights, frames_one.astype(jnp.float32), targets_one, count_one, memory_one.astype(jnp.float32), length_one)
        loss_one, backward, inputs_one = jax.vjp(objective, params, has_aux=True)
        grads = backward(jnp.ones_like(loss_one))[0]
        summed = tuple((left + right for left, right in zip(totals[1], grads)))
        return ((totals[0] + loss_one, summed), inputs_one.astype(jnp.bfloat16))
    start = (jnp.zeros((), jnp.float32), tuple((jnp.zeros_like(item) for item in params)))
    (loss, grads), inputs = lax.scan(one_stream, start, (frames, targets, frame_count, jnp.swapaxes(memory, 0, 1), memory_len))
    layer_inputs = jnp.swapaxes(inputs, 0, 1)
    squares = jnp.zeros((), jnp.float32)
    for item in grads:
        squares = squares + jnp.sum(item * item)
    clip_norm = jnp.sqrt(squares)
    factor = jnp.minimum(1.0, clip_limit / clip_norm)
    firsts = (first_input, first_project, first_output, first_up, first_down, first_head, first_vectors)
    seconds = (second_input, second_project, second_output, second_up, second_down, second_head, second_vectors)
    axes_list = ((0, 1), (1, 2), (1, 2), (1, 2), (1, 2), (0, 1), (1,))
    fresh_list, first_list, second_list, weight_norms, update_norms = ([], [], [], [], [])
    for index in range(7):
        fresh, new_first, new_second, weight_norm, update_norm = lamb_group(params[index], grads[index] * factor, firsts[index], seconds[index], axes_list[index])
        fresh_list.append(fresh)
        first_list.append(new_first)
        second_list.append(new_second)
        weight_norms.append(weight_norm)
        update_norms.append(update_norm)
    slope_first, slope_second, slope_update = adam_direction(params[7], grads[7] * factor, first_slopes, second_slopes, 0.0)
    fresh_list.append(params[7] - slope_rate * slope_update)
    first_list.append(slope_first)
    second_list.append(slope_second)
    weight_norms.append(jnp.sqrt(jnp.sum(params[7] * params[7])).reshape(1))
    update_norms.append(jnp.sqrt(jnp.sum(slope_update * slope_update)).reshape(1))
    norms = jnp.stack([jnp.concatenate(weight_norms), jnp.concatenate(update_norms)], axis=1)
    return (loss, layer_inputs, clip_norm, norms, fresh_list[0], fresh_list[1], fresh_list[2], fresh_list[3], fresh_list[4], fresh_list[5], fresh_list[6], fresh_list[7], first_list[0], first_list[1], first_list[2], first_list[3], first_list[4], first_list[5], first_list[6], first_list[7], second_list[0], second_list[1], second_list[2], second_list[3], second_list[4], second_list[5], second_list[6], second_list[7])
```

```python
import functools

import jax
import jax.numpy as jnp
from jax import lax
from jax.experimental import pallas as pl
from jax.experimental.pallas import tpu as pltpu
from jax.sharding import PartitionSpec as P

STEP = 10


ln_eps = 1e-05
clip_limit = 0.002
beta_one = 0.9
beta_two = 0.999
lamb_rate = 0.3
slope_rate = 0.001
decay_rate = 0.01
adam_eps = 1e-11
masked_score = -1e30

tail_terms = (
    0.16918934881687164,
    0.1706908941268921,
    0.1485215127468109,
    0.21418032050132751,
    -0.09282323718070984,
    0.5449625253677368,
    -0.5097681879997253,
    0.48429951071739197,
    -0.12925273180007935,
)

NN = (((1,), (0,)), ((), ()))
NT = (((1,), (1,)), ((), ()))
TN = (((0,), (0,)), ((), ()))
VMEM_LIMIT = 63 * 1024 * 1024
f32 = jnp.float32
bf16 = jnp.bfloat16


def mm(left, right, dims=NN):
    return lax.dot_general(left, right, dims, preferred_element_type=f32)


def from_behind(block, axis, distance):
    devices = range(lax.axis_size(axis))
    route = [(i - distance, i) for i in devices if i - distance in devices]
    return lax.ppermute(block, axis, route)


def normalize(values):
    centred = values - jnp.mean(values, axis=-1, keepdims=True)
    scale = lax.rsqrt(jnp.mean(centred * centred, axis=-1, keepdims=True) + ln_eps)
    return (centred * scale, scale)


def norm_back(grad_out, standard, scale, gain):
    scaled = grad_out * gain
    return scale * (
        scaled
        - jnp.mean(scaled, axis=-1, keepdims=True)
        - standard * jnp.mean(scaled * standard, axis=-1, keepdims=True)
    )


def gelu_pair(x):
    size = jnp.abs(x)
    t = 1.0 / (1.0 + 0.21213203435596423 * size)
    poly = jnp.full_like(t, tail_terms[-1])
    for term in tail_terms[-2::-1]:
        poly = poly * t + term
    bell = jnp.exp(-0.5 * x * x)
    tail = 0.5 * t * poly * bell
    cumulative = jnp.where(x >= 0.0, 1.0 - tail, tail)
    return (x * cumulative, cumulative + x * (bell * 0.3989422804014327))


def tile(index, size):
    return pl.ds(pl.multiple_of(index * size, size), size)


def half_masks():
    lane = lax.broadcasted_iota(jnp.int32, (1, 128), 1)
    left = jnp.where(lane < 64, 1.0, 0.0).astype(bf16)
    right = jnp.where(lane < 64, 0.0, 1.0).astype(bf16)
    return (left, right)


def attend(streams, span, heads, q_ref, k_ref, v_ref, kf_ref, qf_ref, o_ref, lse_ref):
    pairs = heads // 2
    step = span // 2
    masks = half_masks()
    key_at = lax.broadcasted_iota(jnp.int32, (step, step), 0)
    query_at = lax.broadcasted_iota(jnp.int32, (step, step), 1)

    def one(stream, pair):
        cols = tile(pair, 128)
        k_pair = k_ref[tile(stream, 2 * span), cols]
        v_pair = v_ref[tile(stream, 2 * span), cols]
        outs = []
        for part in range(2):
            done = []
            for half in range(2):
                seen = span + part * step
                q_pair = q_ref[pl.ds(pl.multiple_of(stream * span + part * step, step), step), cols]
                head = 2 * pair + half
                q_aug = q_pair * masks[half] + qf_ref[pl.ds(head, 1), :].astype(bf16)
                k_aug = k_pair[: seen + step] * masks[half] + kf_ref[stream, half, : seen + step]
                v_aug = v_pair[: seen + step] * masks[half] + masks[1 - half]
                wide = mm(k_aug[:seen], q_aug, NT)
                near = mm(k_aug[seen:], q_aug, NT)
                near = jnp.where(key_at <= query_at, near, masked_score)
                peak = jnp.maximum(
                    jnp.max(wide, axis=0, keepdims=True), jnp.max(near, axis=0, keepdims=True)
                )
                wide = jnp.exp(wide - peak).astype(bf16)
                near = jnp.exp(near - peak).astype(bf16)
                mixed = mm(v_aug[:seen], wide, TN) + mm(v_aug[seen:], near, TN)
                own = mixed[half * 64 : half * 64 + 64]
                total = mixed[64 - half * 64 : 128 - half * 64]
                done.append(own / total)
                lse_ref[pl.ds(stream * heads + head, 1), part * step : (part + 1) * step] = (
                    peak + jnp.log(total[:1])
                )
            outs.append(jnp.concatenate(done, axis=0).T)
        for part in range(2):
            o_ref[pl.ds(pl.multiple_of(stream * span + part * step, step), step), cols] = outs[
                part
            ].astype(bf16)

    def over(stream, carry):
        def inner(pair, carry):
            one(stream, pair)
            return carry

        return lax.fori_loop(0, pairs, inner, carry)

    lax.fori_loop(0, streams, over, 0)


def forward_kernel(layer, streams, span, heads, *refs):
    n_in = 12
    if layer == 0:
        (first_ref, rows_ref, frames_ref, halo_ref, small_ref, mem_ref, kf_ref, qf_ref, wp, wo, wu, wd) = refs[:n_in]
        (r_ref, low_ref, pr_ref, a_ref, ap_ref, q_ref, k_ref, v_ref, o_ref, lse_ref, r1_ref, a2_ref, u_ref, gp_ref, out_ref, next_ref) = refs[n_in:]
    else:
        (first_ref, rows_ref, r_ref, a_ref, halo_ref, mem_ref, kf_ref, qf_ref, wp, wo, wu, wd) = refs[:n_in]
        (low_ref, ap_ref, q_ref, k_ref, v_ref, o_ref, lse_ref, r1_ref, a2_ref, u_ref, gp_ref, out_ref) = refs[n_in:]
    width = wp.shape[0]
    first = first_ref[0] > 0
    row = 3 + 4 * layer
    g1, b1, g2, b2 = (rows_ref[row + i : row + i + 1, :] for i in range(4))
    step = span // 2
    for_streams = functools.partial(lax.fori_loop, 0, streams)

    def project(stream, carry):
        for part in range(2):
            at = pl.ds(pl.multiple_of(stream * span + part * step, step), step)
            behind = pl.ds(pl.multiple_of(stream * 2 * span + part * step, step), step)
            here = pl.ds(pl.multiple_of(stream * 2 * span + span + part * step, step), step)
            if layer == 0:
                r = mm(frames_ref[at, :], small_ref[...], NT)
                r_ref[at, :] = r
                low_ref[at, :] = r.astype(bf16)
                a = (normalize(r)[0] * g1 + b1).astype(bf16)
                a_ref[at, :] = a
                before = mm(halo_ref[at, :], small_ref[...], NT)
                before = jnp.where(first, mem_ref[at, :].astype(f32), before)
                pr_ref[at, :] = before
                ap = (normalize(before)[0] * g1 + b1).astype(bf16)
            else:
                low_ref[at, :] = r_ref[at, :].astype(bf16)
                a = a_ref[at, :]
                ap = (normalize(mem_ref[at, :].astype(f32))[0] * g1 + b1).astype(bf16)
                ap = jnp.where(first, ap.astype(f32), halo_ref[at, :].astype(f32)).astype(bf16)
            ap_ref[at, :] = ap
            q_ref[at, :] = (mm(a, wp[:, :width]) * 0.125).astype(bf16)
            k_ref[here, :] = mm(a, wp[:, width : 2 * width]).astype(bf16)
            v_ref[here, :] = mm(a, wp[:, 2 * width :]).astype(bf16)
            k_ref[behind, :] = mm(ap, wp[:, width : 2 * width]).astype(bf16)
            v_ref[behind, :] = mm(ap, wp[:, 2 * width :]).astype(bf16)
        return carry

    for_streams(project, 0)
    attend(streams, span, heads, q_ref, k_ref, v_ref, kf_ref, qf_ref, o_ref, lse_ref)

    def feed(stream, carry):
        at = tile(stream, span)
        after = r_ref[at, :] + mm(o_ref[at, :], wo[...])
        r1_ref[at, :] = after
        a2 = (normalize(after)[0] * g2 + b2).astype(bf16)
        a2_ref[at, :] = a2
        total = after
        for part in range(wu.shape[1] // 512):
            cols = slice(part * 512, (part + 1) * 512)
            active, slope = gelu_pair(mm(a2, wu[:, cols]))
            active = active.astype(bf16)
            u_ref[at, cols] = active
            gp_ref[at, cols] = slope.astype(bf16)
            total = total + mm(active, wd[cols, :])
        out_ref[at, :] = total
        if layer == 0:
            g, b = rows_ref[row + 4 : row + 5, :], rows_ref[row + 5 : row + 6, :]
            next_ref[at, :] = (normalize(total)[0] * g + b).astype(bf16)
        return carry

    for_streams(feed, 0)


def head_kernel(rows_ref, r_ref, wh, target_ref, share_ref, dwh_ref, dr_ref, gr_ref, loss_ref, acc):
    gain, bias = rows_ref[1:2, :], rows_ref[2:3, :]
    step = 256
    acc[...] = jnp.zeros_like(acc)
    gr_ref[...] = jnp.zeros_like(gr_ref)
    loss_ref[...] = jnp.zeros_like(loss_ref)

    def one(index, carry):
        at = tile(index, step)
        standard, scale = normalize(r_ref[at, :])
        f = (standard * gain + bias).astype(bf16)
        z = mm(f, wh[...])
        share = share_ref[at, :]
        peak = jnp.max(z, axis=-1, keepdims=True)
        raised = jnp.exp(z - peak)
        total = jnp.sum(raised, axis=-1, keepdims=True)
        code = lax.broadcasted_iota(jnp.int32, z.shape, 1)
        hit = code == target_ref[at, :]
        picked = jnp.sum(jnp.where(hit, z, 0.0), axis=-1, keepdims=True)
        loss_ref[...] += jnp.sum(share * (peak + jnp.log(total) - picked))
        soft = raised * (1.0 / total)
        dz = (share * jnp.where(hit, soft - 1.0, soft)).astype(bf16)
        acc[...] += mm(f, dz, TN)
        df = mm(dz, wh[...], NT)
        gr_ref[0:1, :] += jnp.sum(df * standard, axis=0, keepdims=True)
        gr_ref[1:2, :] += jnp.sum(df, axis=0, keepdims=True)
        dr_ref[at, :] = norm_back(df, standard, scale, gain)
        return carry

    lax.fori_loop(0, r_ref.shape[0] // step, one, 0)
    dwh_ref[...] = acc[...].astype(bf16)


def attend_back(streams, span, heads, refs):
    (q_ref, k_ref, v_ref, o_ref, lse_ref, kf_ref, qf_ref, do_ref, dq_ref, dk_ref, dv_ref, gs_ref, dk_acc, dv_acc) = refs
    pairs = heads // 2
    step = span // 2
    masks = half_masks()
    key_at = lax.broadcasted_iota(jnp.int32, (step, step), 0)
    query_at = lax.broadcasted_iota(jnp.int32, (step, step), 1)
    head_row = lax.broadcasted_iota(jnp.int32, (8, 128), 0)
    place = lax.broadcasted_iota(jnp.int32, (1, step), 1)
    gs_ref[...] = jnp.zeros_like(gs_ref)

    def one(stream, pair):
        cols = tile(pair, 128)
        k_pair = k_ref[tile(stream, 2 * span), cols]
        v_pair = v_ref[tile(stream, 2 * span), cols]
        dk_acc[...] = jnp.zeros_like(dk_acc)
        dv_acc[...] = jnp.zeros_like(dv_acc)
        for part in range(2):
            seen = span + part * step
            rows = pl.ds(pl.multiple_of(stream * span + part * step, step), step)
            q_pair = q_ref[rows, cols]
            do_pair = do_ref[rows, cols]
            both = (do_pair.astype(f32) * o_ref[rows, cols].astype(f32)).T
            done = []
            for half in range(2):
                head = 2 * pair + half
                mask = masks[half]
                q_own = q_pair * mask
                q_aug = q_own + qf_ref[pl.ds(head, 1), :].astype(bf16)
                k_aug = k_pair[: seen + step] * mask + kf_ref[stream, half, : seen + step]
                do_own = do_pair * mask
                delta = jnp.sum(both[half * 64 : half * 64 + 64], axis=0, keepdims=True)
                log_total = lse_ref[pl.ds(stream * heads + head, 1), part * step : (part + 1) * step]
                turned = jnp.zeros((128, step), f32)
                for low, high in ((0, seen), (seen, seen + step)):
                    score = mm(k_aug[low:high], q_aug, NT)
                    if low:
                        score = jnp.where(key_at <= query_at, score, masked_score)
                    chance = jnp.exp(score - log_total)
                    dp = mm(v_pair[low:high], do_own, NT)
                    dv_acc[low:high, :] += mm(chance.astype(bf16), do_own)
                    ds = (chance * (dp - delta)).astype(bf16)
                    dk_acc[low:high, :] += mm(ds, q_own)
                    turned = turned + mm(k_aug[low:high], ds, TN)
                done.append(turned[half * 64 : half * 64 + 64] * 0.125)
                base = 64 - half * 64
                lean = (
                    turned[base : base + 1]
                    + turned[base + 3 : base + 4]
                    - (place + (part * step + span)).astype(f32) * turned[base + 7 : base + 8]
                )
                gs_ref[...] += jnp.where(head_row == head, jnp.sum(lean), 0.0)
            dq_ref[rows, cols] = jnp.concatenate(done, axis=0).T.astype(bf16)
        dk_ref[tile(stream, 2 * span), cols] = dk_acc[...].astype(bf16)
        dv_ref[tile(stream, 2 * span), cols] = dv_acc[...].astype(bf16)

    def over(stream, carry):
        def inner(pair, carry):
            one(stream, pair)
            return carry

        return lax.fori_loop(0, pairs, inner, carry)

    lax.fori_loop(0, streams, over, 0)


def backward_kernel(layer, streams, span, heads, *refs):
    refs = list(refs)
    (first_ref, rows_ref, a_ref, ap_ref, q_ref, k_ref, v_ref, o_ref, lse_ref, r1_ref, a2_ref, u_ref, gp_ref, kf_ref, qf_ref, wp, wo, wu, wd) = refs[:19]
    rest = refs[19:]
    if layer == 0:
        (frames_ref, halo_ref, r_ref, pr_ref, dr1_in, da_in, back_ref, r_next) = rest[:8]
        (dwp, dwo, dwu, dwd, gr_ref, gs_ref, dsmall_ref) = rest[8:15]
        scratch = rest[15:]
    else:
        (dr_in, mem_ref) = rest[:2]
        (dwp, dwo, dwu, dwd, gr_ref, gs_ref, dr1_out, da_out, dap_out) = rest[2:11]
        scratch = rest[11:]
    (dr_ref, da_ref, do_ref, dq_ref, dk_ref, dv_ref, dk_acc, dv_acc, tr_ref) = scratch
    width = wp.shape[0]
    count = streams * span
    first = first_ref[0] > 0
    row = 3 + 4 * layer
    g1, b1, g2, b2 = (rows_ref[row + i : row + i + 1, :] for i in range(4))
    step = 256
    tiles = count // step
    gr_ref[...] = jnp.zeros_like(gr_ref)

    if layer == 0:
        g = rows_ref[row + 4 : row + 5, :]

        def join(index, carry):
            at = tile(index, step)
            standard, scale = normalize(r_next[at, :])
            da = da_in[at, :] + back_ref[at, :].astype(f32)
            gr_ref[4:5, :] += jnp.sum(da * standard, axis=0, keepdims=True)
            gr_ref[5:6, :] += jnp.sum(da, axis=0, keepdims=True)
            dr_ref[at, :] = dr1_in[at, :] + norm_back(da, standard, scale, g)
            return carry

        lax.fori_loop(0, tiles, join, 0)
    else:

        def take(index, carry):
            at = tile(index, step)
            dr_ref[at, :] = dr_in[at, :]
            return carry

        lax.fori_loop(0, tiles, take, 0)

    da_ref[...] = jnp.zeros_like(da_ref)
    tr_ref[...] = a2_ref[...].T

    def feed(part, carry):
        cols = tile(part, 512)
        dy = dr_ref[...].astype(bf16)
        dh = (mm(dy, wd[cols, :], NT) * gp_ref[:, cols].astype(f32)).astype(bf16)
        dwd[cols, :] = mm(u_ref[:, cols], dy, TN).astype(bf16)
        dwu[:, cols] = mm(tr_ref[...], dh).astype(bf16)
        da_ref[...] += mm(dh, wu[:, cols], NT)
        return carry

    lax.fori_loop(0, wu.shape[1] // 512, feed, 0)

    def middle(index, carry):
        at = tile(index, step)
        standard, scale = normalize(r1_ref[at, :])
        da = da_ref[at, :]
        gr_ref[2:3, :] += jnp.sum(da * standard, axis=0, keepdims=True)
        gr_ref[3:4, :] += jnp.sum(da, axis=0, keepdims=True)
        dr = dr_ref[at, :] + norm_back(da, standard, scale, g2)
        dr_ref[at, :] = dr
        do_ref[at, :] = mm(dr.astype(bf16), wo[...], NT).astype(bf16)
        return carry

    lax.fori_loop(0, tiles, middle, 0)
    dwo[...] = mm(o_ref[...], dr_ref[...].astype(bf16), TN).astype(bf16)

    attend_back(
        streams,
        span,
        heads,
        (q_ref, k_ref, v_ref, o_ref, lse_ref, kf_ref, qf_ref, do_ref, dq_ref, dk_ref, dv_ref, gs_ref, dk_acc, dv_acc),
    )

    tr_ref[...] = a_ref[...].T
    dwp[:, :width] = mm(tr_ref[...], dq_ref[...]).astype(bf16)
    for spot, ref in ((1, dk_ref), (2, dv_ref)):
        total = jnp.zeros((width, width), f32)
        for stream in range(streams):
            behind = slice(stream * 2 * span, stream * 2 * span + span)
            here = slice(stream * 2 * span + span, (stream + 1) * 2 * span)
            own = slice(stream * span, (stream + 1) * span)
            total = total + mm(tr_ref[:, own], ref[here, :])
            total = total + mm(ap_ref[own, :], ref[behind, :], TN)
        dwp[:, spot * width : (spot + 1) * width] = total.astype(bf16)

    if layer == 0:
        dsmall_ref[...] = jnp.zeros_like(dsmall_ref)

    def finish(stream, carry):
        for part in range(span // step):
            at = pl.ds(pl.multiple_of(stream * span + part * step, step), step)
            behind = pl.ds(pl.multiple_of(stream * 2 * span + part * step, step), step)
            here = pl.ds(pl.multiple_of(stream * 2 * span + span + part * step, step), step)
            wq, wk, wv = (wp[:, i * width : (i + 1) * width] for i in range(3))
            da = mm(dq_ref[at, :], wq, NT) + mm(dk_ref[here, :], wk, NT) + mm(dv_ref[here, :], wv, NT)
            dap = mm(dk_ref[behind, :], wk, NT) + mm(dv_ref[behind, :], wv, NT)
            if layer == 0:
                standard, scale = normalize(r_ref[at, :])
                before, before_scale = normalize(pr_ref[at, :])
                gr_ref[0:1, :] += jnp.sum(da * standard + dap * before, axis=0, keepdims=True)
                gr_ref[1:2, :] += jnp.sum(da + dap, axis=0, keepdims=True)
                dr = dr_ref[at, :] + norm_back(da, standard, scale, g1)
                drp = norm_back(dap, before, before_scale, g1)
                drp = jnp.where(first, 0.0, drp)
                gr_ref[6:7, :] += jnp.sum(dr + drp, axis=0, keepdims=True)
                dsmall_ref[...] += mm(dr.astype(bf16), frames_ref[at, :], TN)
                dsmall_ref[...] += mm(drp.astype(bf16), halo_ref[at, :], TN)
            else:
                da_out[at, :] = da
                dr1_out[at, :] = dr_ref[at, :]
                dap_out[at, :] = dap.astype(bf16)
                before, before_scale = normalize(mem_ref[at, :].astype(f32))
                dap = jnp.where(first, dap, 0.0)
                gr_ref[0:1, :] += jnp.sum(dap * before, axis=0, keepdims=True)
                gr_ref[1:2, :] += jnp.sum(dap, axis=0, keepdims=True)
        return carry

    lax.fori_loop(0, streams, finish, 0)


def whole(space=pltpu.VMEM):
    return pl.BlockSpec(memory_space=space)


def call(kernel, name, args, outs, scratch=(), smem=1, flops=0):
    specs = [whole(pltpu.SMEM)] * smem + [whole()] * (len(args) - smem)
    return pl.pallas_call(
        kernel,
        name=name,
        out_shape=[jax.ShapeDtypeStruct(*out) for out in outs],
        in_specs=specs,
        out_specs=[whole()] * len(outs),
        scratch_shapes=[pltpu.VMEM(*item) for item in scratch],
        compiler_params=pltpu.CompilerParams(vmem_limit_bytes=VMEM_LIMIT),
        cost_estimate=pl.CostEstimate(flops=flops, bytes_accessed=20000000, transcendentals=0),
    )(*args)


def split_three(value):
    one = value.astype(bf16)
    rest = value - one.astype(f32)
    two = rest.astype(bf16)
    rest = rest - two.astype(f32)
    return (one, two, rest.astype(bf16))


def per_matrix(arrays):
    parts = [jnp.sum(arrays[0] * arrays[0]).reshape(1)]
    for stacked in arrays[1:5]:
        parts.append(jnp.sum(stacked * stacked, axis=(1, 2)))
    parts.append(jnp.sum(arrays[5] * arrays[5]).reshape(1))
    parts.append(jnp.sum(arrays[6] * arrays[6], axis=1))
    return jnp.concatenate(parts)


def adam_direction(weight, grad, first, second, decay):
    new_first = beta_one * first + (1.0 - beta_one) * grad
    new_second = beta_two * second + (1.0 - beta_two) * grad * grad
    first_hat = new_first / (1.0 - beta_one**STEP)
    second_hat = new_second / (1.0 - beta_two**STEP)
    return (new_first, new_second, first_hat / (jnp.sqrt(second_hat) + adam_eps) + decay * weight)


def shards(
    frames,
    targets,
    frame_count,
    memory,
    memory_len,
    input_weight,
    project_weight,
    output_weight,
    up_weight,
    down_weight,
    head_weight,
    vectors,
    slopes,
    first_input,
    first_project,
    first_output,
    first_up,
    first_down,
    first_head,
    first_vectors,
    first_slopes,
    second_input,
    second_project,
    second_output,
    second_up,
    second_down,
    second_head,
    second_vectors,
    second_slopes,
):
    streams, span, features = frames.shape
    layers, heads = slopes.shape
    nvec = vectors.shape[0]
    width = project_weight.shape[2] // 3
    hidden = up_weight.shape[2]
    codes = head_weight.shape[1]
    count = streams * span
    seq_index = lax.axis_index("seq")
    first = seq_index == 0
    first_flag = jnp.where(first, 1, 0).astype(jnp.int32).reshape(1)
    streams_all = streams * lax.axis_size("stream")

    small_own = jnp.concatenate(
        [input_weight.T, vectors.T, jnp.zeros((input_weight.shape[1], 128 - features - nvec), f32)], axis=1
    ).astype(bf16)
    gather = functools.partial(lax.all_gather, axis_name="stream", tiled=True)
    small = gather(small_own, axis=0)
    weights_low = []
    for layer in range(layers):
        weights_low.append(
            (
                gather(project_weight[layer].astype(bf16), axis=0),
                gather(output_weight[layer].astype(bf16), axis=0),
                gather(up_weight[layer].astype(bf16), axis=0),
                gather(down_weight[layer].astype(bf16), axis=0),
            )
        )
    head_low = gather(head_weight.astype(bf16), axis=0)
    rows = jnp.pad(small[:, features : features + nvec].astype(f32).T, ((0, 16 - nvec), (0, 0)))

    frames_flat = frames.reshape((count, features))
    frames_flat = jnp.concatenate(
        [frames_flat, jnp.ones((count, 1), bf16), jnp.zeros((count, 127 - features), bf16)], axis=1
    )
    frames_behind = from_behind(frames_flat, "seq", 1)
    memory_flat = memory.reshape((layers, count, width))

    key_pos = jnp.arange(2 * span)
    hidden_key = jnp.logical_and(first, key_pos[None] < span - memory_len[:, None])
    coarse = (key_pos // 256 * 256).astype(bf16)
    fine = (key_pos % 256).astype(bf16)
    one = jnp.ones_like(coarse)
    shape = (streams, 2 * span)
    columns = [jnp.broadcast_to(item, shape) for item in (coarse, coarse, coarse, fine, fine, fine)]
    columns += [hidden_key.astype(bf16), jnp.broadcast_to(one, shape)]
    key_marks = jnp.pad(jnp.stack(columns, axis=-1), ((0, 0), (0, 0), (0, 56)))
    blank = jnp.zeros_like(key_marks)
    key_marks = jnp.stack(
        [jnp.concatenate([blank, key_marks], axis=-1), jnp.concatenate([key_marks, blank], axis=-1)], axis=1
    )
    parts = split_three(slopes)
    marks = jnp.stack(parts + parts + (jnp.full_like(parts[0], masked_score), jnp.zeros_like(parts[0])), axis=-1)
    marks = jnp.pad(marks, ((0, 0), (0, 0), (0, 56))).astype(f32)
    even = (jnp.arange(heads) % 2 == 0)[None, :, None]
    query_marks = jnp.concatenate([jnp.where(even, 0.0, marks), jnp.where(even, marks, 0.0)], axis=-1)

    full = ((count, width), f32)
    low = ((count, width), bf16)
    joined = ((2 * count, width), bf16)
    wide = ((count, hidden), bf16)
    lse = ((streams * heads, span), f32)
    saved_outs = [low, low, joined, joined, low, lse, full, low, wide, wide, full]
    cost = 2 * count * (5 * width * width + width * width + 2 * width * hidden) + 4 * count * 2 * span * width

    made = call(
        functools.partial(forward_kernel, 0, streams, span, heads),
        "forward_zero",
        (first_flag, rows, frames_flat, frames_behind, small, memory_flat[0], key_marks, query_marks[0]) + weights_low[0],
        [full, low, full, low] + saved_outs + [low],
        flops=cost,
    )
    r_zero, low_zero, pr_zero, a_zero = made[:4]
    saved_zero = made[4:14]
    r_one, a_one = made[14:16]
    a_behind = from_behind(a_one, "seq", 1)
    made = call(
        functools.partial(forward_kernel, 1, streams, span, heads),
        "forward_one",
        (first_flag, rows, r_one, a_one, a_behind, memory_flat[1], key_marks, query_marks[1]) + weights_low[1],
        [low] + saved_outs,
        flops=cost,
    )
    low_one = made[0]
    saved_one = made[1:11]
    r_two = made[11]

    position = seq_index * span + jnp.arange(span)
    share = jnp.where(
        position[None] < frame_count[:, None],
        1.0 / (frame_count[:, None].astype(f32) * streams_all),
        0.0,
    )
    grad_head, dr_two, last_rows, loss_tile = call(
        head_kernel,
        "head_loss",
        (rows, r_two, head_low, targets.reshape((count, 1)), share.reshape((count, 1))),
        [((width, codes), bf16), full, ((8, width), f32), ((8, 128), f32)],
        [((width, codes), f32)],
        smem=0,
        flops=6 * count * width * codes,
    )
    loss_term = loss_tile[0, 0]

    weight_outs = [
        ((width, 3 * width), bf16),
        ((width, width), bf16),
        ((width, hidden), bf16),
        ((hidden, width), bf16),
        ((8, width), f32),
        ((8, 128), f32),
    ]
    scratch = [full, full, low, low, joined, joined, ((2 * span, 128), f32), ((2 * span, 128), f32), ((width, count), bf16)]
    made = call(
        functools.partial(backward_kernel, 1, streams, span, heads),
        "backward_one",
        (first_flag, rows, a_one, *saved_one[:9], saved_one[9], key_marks, query_marks[1], *weights_low[1], dr_two, memory_flat[1]),
        weight_outs + [full, full, low],
        scratch,
        flops=2 * cost,
    )
    matrices_one, rows_one, slope_one = made[:4], made[4], made[5]
    dr1_one, da_one, dap_one = made[6:]
    back_one = from_behind(dap_one, "seq", -1)
    made = call(
        functools.partial(backward_kernel, 0, streams, span, heads),
        "backward_zero",
        (first_flag, rows, a_zero, *saved_zero[:9], saved_zero[9], key_marks, query_marks[0], *weights_low[0], frames_flat, frames_behind, r_zero, pr_zero, dr1_one, da_one, back_one, r_one),
        weight_outs + [((width, 128), f32)],
        scratch,
        flops=2 * cost,
    )
    matrices_zero, rows_zero, slope_zero, grad_small = made[:4], made[4], made[5], made[6]

    grad_rows = jnp.concatenate(
        [rows_zero[6:7], last_rows[0:2], rows_zero[0:4], rows_one[0:2] + rows_zero[4:6], rows_one[2:4]], axis=0
    )
    grad_slopes = jnp.stack([slope_zero[:, 0], slope_one[:, 0]])
    grad_small = jnp.concatenate(
        [grad_small[:, :features], grad_rows.T, jnp.zeros((width, 128 - features - nvec), f32)], axis=1
    ).astype(bf16)

    def scatter(grad):
        return lax.psum_scatter(grad, "stream", scatter_dimension=0, tiled=True)

    head_share = scatter(grad_head)
    one_share = [scatter(item) for item in matrices_one]
    zero_share = [scatter(item) for item in matrices_zero]
    small_share = scatter(grad_small)
    head_share, one_share, zero_share, small_share = lax.psum(
        (head_share, one_share, zero_share, small_share), "seq"
    )
    pairs_of = [jnp.stack([zero, one]).astype(f32) for zero, one in zip(zero_share, one_share)]
    small_share = small_share.astype(f32)
    grads = (
        small_share[:, :features].T,
        pairs_of[0],
        pairs_of[1],
        pairs_of[2],
        pairs_of[3],
        head_share.astype(f32),
        small_share[:, features : features + nvec].T,
    )
    loss, grad_slopes = lax.psum((loss_term, grad_slopes), ("seq", "stream"))
    grad_squares = lax.psum(per_matrix(grads), "stream")
    clip_norm = jnp.sqrt(jnp.sum(grad_squares) + jnp.sum(grad_slopes * grad_slopes))
    factor = jnp.minimum(1.0, clip_limit / clip_norm)
    weights = (
        input_weight,
        project_weight,
        output_weight,
        up_weight,
        down_weight,
        head_weight,
        vectors,
    )
    firsts = (
        first_input,
        first_project,
        first_output,
        first_up,
        first_down,
        first_head,
        first_vectors,
    )
    seconds = (
        second_input,
        second_project,
        second_output,
        second_up,
        second_down,
        second_head,
        second_vectors,
    )
    moved = [
        adam_direction(
            weights[index], grads[index] * factor, firsts[index], seconds[index], decay_rate
        )
        for index in range(7)
    ]
    updates = [item[2] for item in moved]
    weight_squares, update_squares = lax.psum((per_matrix(weights), per_matrix(updates)), "stream")
    weight_norm = jnp.sqrt(weight_squares)
    update_norm = jnp.sqrt(update_squares)
    ratio = weight_norm / update_norm
    layer_end = 1 + 4 * layers
    shaped = [
        ratio[0],
        ratio[1 : 1 + layers][:, None, None],
        ratio[1 + layers : 1 + 2 * layers][:, None, None],
        ratio[1 + 2 * layers : 1 + 3 * layers][:, None, None],
        ratio[1 + 3 * layers : layer_end][:, None, None],
        ratio[layer_end],
        ratio[layer_end + 1 :][:, None],
    ]
    fresh = [weights[index] - lamb_rate * shaped[index] * updates[index] for index in range(7)]
    slope_first, slope_second, slope_update = adam_direction(
        slopes, grad_slopes * factor, first_slopes, second_slopes, 0.0
    )
    fresh_slopes = slopes - slope_rate * slope_update
    slope_row = jnp.stack(
        [jnp.sqrt(jnp.sum(slopes * slopes)), jnp.sqrt(jnp.sum(slope_update * slope_update))]
    ).reshape((1, 2))
    norms = jnp.concatenate([jnp.stack([weight_norm, update_norm], axis=1), slope_row], axis=0)
    layer_inputs = jnp.stack([low_zero, low_one]).reshape((layers, streams, span, width))
    return (
        loss,
        layer_inputs,
        clip_norm,
        norms,
        *fresh,
        fresh_slopes,
        *[item[0] for item in moved],
        slope_first,
        *[item[1] for item in moved],
        slope_second,
    )


def solution(mesh):
    rows3 = P(None, "stream", None)
    state = (P(None, "stream"), rows3, rows3, rows3, rows3, P("stream", None), P(None, "stream"), P())
    in_specs = (
        P("stream", "seq", None),
        P("stream", "seq"),
        P("stream"),
        P(None, "stream", None, None),
        P("stream"),
    ) + state * 3
    out_specs = (P(), P(None, "stream", "seq", None), P(), P()) + state * 3
    return jax.shard_map(shards, mesh=mesh, in_specs=in_specs, out_specs=out_specs, check_vma=False)
```

```python
import functools

import jax
import jax.numpy as jnp
from jax import lax
from jax.experimental import pallas as pl
from jax.experimental.pallas import tpu as pltpu
from jax.sharding import PartitionSpec as P

STEP = 10


ln_eps = 1e-05
clip_limit = 0.002
beta_one = 0.9
beta_two = 0.999
lamb_rate = 0.3
slope_rate = 0.001
decay_rate = 0.01
adam_eps = 1e-11
masked_score = -1e30

tail_terms = (
    0.16918934881687164,
    0.1706908941268921,
    0.1485215127468109,
    0.21418032050132751,
    -0.09282323718070984,
    0.5449625253677368,
    -0.5097681879997253,
    0.48429951071739197,
    -0.12925273180007935,
)

NN = (((1,), (0,)), ((), ()))
NT = (((1,), (1,)), ((), ()))
TN = (((0,), (0,)), ((), ()))
VMEM_LIMIT = 63 * 1024 * 1024
f32 = jnp.float32
bf16 = jnp.bfloat16


def mm(left, right, dims=NN):
    return lax.dot_general(left, right, dims, preferred_element_type=f32)


MESH = pl.DeviceIdType.MESH


class Place:
    def __init__(self, streams, blocks):
        self.chips = streams // 2
        self.blocks = blocks
        index = lax.axis_index("stream")
        self.chip = index // 2
        self.core = index % 2
        self.block = lax.axis_index("seq")
        self.sibling = {"stream": 2 * self.chip + 1 - self.core}

    def other(self, distance):
        return (self.chip + distance) % self.chips

    def mate(self, distance):
        return {"stream": 2 * self.other(distance) + self.core}

    def greet(self, line=False):
        barrier = pltpu.get_barrier_semaphore()

        def hello(device):
            pl.semaphore_signal(barrier, inc=1, device_id=device, device_id_type=MESH)

        hello(self.sibling)
        for distance in range(1, self.chips):
            hello(self.mate(distance))
        if line:

            @pl.when(self.block > 0)
            def _():
                hello({"seq": self.block - 1})

            pl.semaphore_wait(barrier, self.chips + jnp.where(self.block < self.blocks - 1, 1, 0))
        else:
            pl.semaphore_wait(barrier, self.chips)


class Gather:
    def __init__(self, place, refs, sems, first):
        self.place, self.refs, self.sems, self.first = place, refs, sems, first

    def far(self, index, distance):
        place, ref = self.place, self.refs[index]
        out_sem, in_sem = self.sems[0], self.sems[1]
        return pltpu.make_async_remote_copy(
            src_ref=ref.at[place.chip, place.core],
            dst_ref=ref.at[place.chip, place.core],
            send_sem=out_sem.at[self.first + index, distance],
            recv_sem=in_sem.at[self.first + index, distance],
            device_id=place.mate(distance),
            device_id_type=MESH,
        )

    def near(self, index, core):
        place, ref = self.place, self.refs[index]
        out_sem, in_sem = self.sems[0], self.sems[1]
        return pltpu.make_async_remote_copy(
            src_ref=ref.at[:, core],
            dst_ref=ref.at[:, core],
            send_sem=out_sem.at[self.first + index, 0],
            recv_sem=in_sem.at[self.first + index, 0],
            device_id=place.sibling,
            device_id_type=MESH,
        )

    def push(self):
        for index in range(len(self.refs)):
            for distance in range(1, self.place.chips):
                self.far(index, distance).start()

    def relay(self):
        place = self.place
        for index in range(len(self.refs)):
            ref = self.refs[index]
            for distance in range(1, place.chips):
                source = place.other(place.chips - distance)
                pltpu.make_async_remote_copy(
                    src_ref=ref.at[source, place.core],
                    dst_ref=ref.at[source, place.core],
                    send_sem=self.sems[0].at[self.first + index, distance],
                    recv_sem=self.sems[1].at[self.first + index, distance],
                    device_id=place.mate(distance),
                    device_id_type=MESH,
                ).wait_recv()
            self.near(index, place.core).start()

    def finish(self):
        place = self.place
        for index in range(len(self.refs)):
            self.near(index, 1 - place.core).wait_recv()
            self.near(index, place.core).wait_send()
            for distance in range(1, place.chips):
                self.far(index, distance).wait_send()


class Ahead:
    def __init__(self, place, step, src, dst, sems):
        self.place, self.step, self.src, self.dst, self.sems = place, step, src, dst, sems
        self.sends = place.block < place.blocks - 1 if step > 0 else place.block > 0
        self.receives = place.block > 0 if step > 0 else place.block < place.blocks - 1

    def copy(self, slot, rows):
        return pltpu.make_async_remote_copy(
            src_ref=self.src.at[rows],
            dst_ref=self.dst.at[rows],
            send_sem=self.sems[0].at[slot],
            recv_sem=self.sems[1].at[slot],
            device_id={"seq": self.place.block + self.step},
            device_id_type=MESH,
        )

    def start(self, slot, rows):
        @pl.when(self.sends)
        def _():
            self.copy(slot, rows).start()

    def arrived(self, slot, rows):
        @pl.when(self.receives)
        def _():
            self.copy(slot, rows).wait_recv()

    def sent(self, slot, rows):
        @pl.when(self.sends)
        def _():
            self.copy(slot, rows).wait_send()


def flat(ref, cols=slice(None)):
    value = ref[:, :, :, cols]
    return value.reshape((-1, value.shape[-1]))


def flat_rows(ref, part, parts):
    chips = ref.shape[0] // parts
    value = ref[pl.ds(part * chips, chips)]
    return value.reshape((-1, value.shape[-1]))


def from_behind(block, axis, distance):
    devices = range(lax.axis_size(axis))
    route = [(i - distance, i) for i in devices if i - distance in devices]
    return lax.ppermute(block, axis, route)


def normalize(values):
    centred = values - jnp.mean(values, axis=-1, keepdims=True)
    scale = lax.rsqrt(jnp.mean(centred * centred, axis=-1, keepdims=True) + ln_eps)
    return (centred * scale, scale)


def norm_back(grad_out, standard, scale, gain):
    scaled = grad_out * gain
    return scale * (
        scaled
        - jnp.mean(scaled, axis=-1, keepdims=True)
        - standard * jnp.mean(scaled * standard, axis=-1, keepdims=True)
    )


def gelu_pair(x):
    size = jnp.abs(x)
    t = 1.0 / (1.0 + 0.21213203435596423 * size)
    poly = jnp.full_like(t, tail_terms[-1])
    for term in tail_terms[-2::-1]:
        poly = poly * t + term
    bell = jnp.exp(-0.5 * x * x)
    tail = 0.5 * t * poly * bell
    cumulative = jnp.where(x >= 0.0, 1.0 - tail, tail)
    return (x * cumulative, cumulative + x * (bell * 0.3989422804014327))


def tile(index, size):
    return pl.ds(pl.multiple_of(index * size, size), size)


def half_masks():
    lane = lax.broadcasted_iota(jnp.int32, (1, 128), 1)
    left = jnp.where(lane < 64, 1.0, 0.0).astype(bf16)
    right = jnp.where(lane < 64, 0.0, 1.0).astype(bf16)
    return (left, right)


def attend(streams, span, heads, q_ref, k_ref, v_ref, kf_ref, qf_ref, o_ref, lse_ref, between):
    pairs = heads // 2
    step = span // 2
    masks = half_masks()
    key_at = lax.broadcasted_iota(jnp.int32, (step, step), 0)
    query_at = lax.broadcasted_iota(jnp.int32, (step, step), 1)

    def one(stream, pair):
        cols = tile(pair, 128)
        k_pair = k_ref[tile(stream, 2 * span), cols]
        v_pair = v_ref[tile(stream, 2 * span), cols]
        outs = []
        for part in range(2):
            done = []
            for half in range(2):
                seen = span + part * step
                q_pair = q_ref[pl.ds(pl.multiple_of(stream * span + part * step, step), step), cols]
                head = 2 * pair + half
                q_aug = q_pair * masks[half] + qf_ref[pl.ds(head, 1), :].astype(bf16)
                k_aug = k_pair[: seen + step] * masks[half] + kf_ref[stream, half, : seen + step]
                v_aug = v_pair[: seen + step] * masks[half] + masks[1 - half]
                wide = mm(k_aug[:seen], q_aug, NT)
                near = mm(k_aug[seen:], q_aug, NT)
                near = jnp.where(key_at <= query_at, near, masked_score)
                peak = jnp.maximum(
                    jnp.max(wide, axis=0, keepdims=True), jnp.max(near, axis=0, keepdims=True)
                )
                wide = jnp.exp(wide - peak).astype(bf16)
                near = jnp.exp(near - peak).astype(bf16)
                mixed = mm(v_aug[:seen], wide, TN) + mm(v_aug[seen:], near, TN)
                own = mixed[half * 64 : half * 64 + 64]
                total = mixed[64 - half * 64 : 128 - half * 64]
                done.append(own / total)
                lse_ref[pl.ds(stream * heads + head, 1), part * step : (part + 1) * step] = (
                    peak + jnp.log(total[:1])
                )
            outs.append(jnp.concatenate(done, axis=0).T)
        for part in range(2):
            o_ref[pl.ds(pl.multiple_of(stream * span + part * step, step), step), cols] = outs[
                part
            ].astype(bf16)

    def over(stream, carry):
        def inner(pair, carry):
            one(stream, pair)
            return carry

        carry = lax.fori_loop(0, pairs, inner, carry)
        between(stream)
        return carry

    lax.fori_loop(0, streams, over, 0)


def forward_kernel(layer, sizes, *refs):
    (stream_devices, block_devices, streams, span, heads, features, nvec) = sizes
    place = Place(stream_devices, block_devices)
    chip, core = place.chip, place.core
    if layer == 0:
        (first_ref, small_own, frames_ref, mem_ref, kf_ref, qf_ref, pw, ow, uw, dw) = refs[:10]
        (rows_ref, r_ref, low_ref, pr_ref, a_ref, ap_ref, q_ref, k_ref, v_ref, o_ref, lse_ref, r1_ref, a2_ref, u_ref, gp_ref, out_ref) = refs[10:26]
        (next_ref, behind_ref, halo_ref, small, wp, wo, wu, wd, wp_next, wo_next) = refs[26:36]
        (out_sem, in_sem, frame_sem, next_out, next_in) = refs[36:]
        sems = (out_sem, in_sem)
        early = Gather(place, [small, wp], sems, 0)
        middle = Gather(place, [wo, wu, wd], sems, 2)
        late = Gather(place, [wp_next, wo_next], sems, 5)
        frames_ahead = Ahead(place, 1, frames_ref, halo_ref, (frame_sem.at[0], frame_sem.at[1]))
        next_ahead = Ahead(place, 1, next_ref, behind_ref, (next_out, next_in))
        every = pl.ds(0, streams * span)

        @pl.when(place.block == 0)
        def _():
            halo_ref[...] = jnp.zeros_like(halo_ref)
            behind_ref[...] = jnp.zeros_like(behind_ref)

        small[chip, core] = small_own[...]
        wp[chip, core] = pw[0].astype(bf16)
        place.greet(line=True)
        early.push()
        frames_ahead.start(0, every)
        wo[chip, core] = ow[0].astype(bf16)
        wu[chip, core] = uw[0].astype(bf16)
        wd[chip, core] = dw[0].astype(bf16)
        wp_next[chip, core] = pw[1].astype(bf16)
        wo_next[chip, core] = ow[1].astype(bf16)
        early.relay()
        middle.push()
        early.finish()
        turned = flat(small).astype(f32).T
        rows_ref[...] = jnp.zeros_like(rows_ref)
        rows_ref[:nvec, :] = turned[features : features + nvec]
        frames_ahead.arrived(0, every)
        halfway = middle
    else:
        (first_ref, rows_ref, r_ref, a_ref, halo_ref, mem_ref, kf_ref, qf_ref, wp, wo, uw, dw, hw) = refs[:13]
        (low_ref, ap_ref, q_ref, k_ref, v_ref, o_ref, lse_ref, r1_ref, a2_ref, u_ref, gp_ref, out_ref) = refs[13:25]
        (wu, wd, wh) = refs[25:28]
        (out_sem, in_sem) = refs[28:]
        halfway = Gather(place, [wu, wd, wh], (out_sem, in_sem), 0)
        wu[chip, core] = uw[1].astype(bf16)
        wd[chip, core] = dw[1].astype(bf16)
        wh[chip, core] = hw[...].astype(bf16)
        place.greet()
        halfway.push()
    width = a_ref.shape[1]
    first = first_ref[0] > 0
    row = 3 + 4 * layer
    g1, b1, g2, b2 = (rows_ref[row + i : row + i + 1, :] for i in range(4))
    step = span // 2
    for_streams = functools.partial(lax.fori_loop, 0, streams)

    def project(stream, carry):
        for part in range(2):
            at = pl.ds(pl.multiple_of(stream * span + part * step, step), step)
            behind = pl.ds(pl.multiple_of(stream * 2 * span + part * step, step), step)
            here = pl.ds(pl.multiple_of(stream * 2 * span + span + part * step, step), step)
            if layer == 0:
                r = mm(frames_ref[at, :], flat(small), NT)
                r_ref[at, :] = r
                low_ref[at, :] = r.astype(bf16)
                a = (normalize(r)[0] * g1 + b1).astype(bf16)
                a_ref[at, :] = a
                before = mm(halo_ref[at, :], flat(small), NT)
                before = jnp.where(first, mem_ref[at, :].astype(f32), before)
                pr_ref[at, :] = before
                ap = (normalize(before)[0] * g1 + b1).astype(bf16)
            else:
                low_ref[at, :] = r_ref[at, :].astype(bf16)
                a = a_ref[at, :]
                ap = (normalize(mem_ref[at, :].astype(f32))[0] * g1 + b1).astype(bf16)
                ap = jnp.where(first, ap.astype(f32), halo_ref[at, :].astype(f32)).astype(bf16)
            ap_ref[at, :] = ap
            wq, wk, wv = (flat(wp, slice(i * width, (i + 1) * width)) for i in range(3))
            q_ref[at, :] = (mm(a, wq) * 0.125).astype(bf16)
            k_ref[here, :] = mm(a, wk).astype(bf16)
            v_ref[here, :] = mm(a, wv).astype(bf16)
            k_ref[behind, :] = mm(ap, wk).astype(bf16)
            v_ref[behind, :] = mm(ap, wv).astype(bf16)
        return carry

    for_streams(project, 0)

    def between(stream):
        @pl.when(stream == 0)
        def _():
            halfway.relay()
            if layer == 0:
                late.push()

    attend(streams, span, heads, q_ref, k_ref, v_ref, kf_ref, qf_ref, o_ref, lse_ref, between)
    halfway.finish()

    def feed(stream, carry):
        at = tile(stream, span)
        after = r_ref[at, :] + mm(o_ref[at, :], flat(wo))
        r1_ref[at, :] = after
        a2 = (normalize(after)[0] * g2 + b2).astype(bf16)
        a2_ref[at, :] = a2
        total = after
        parts = wu.shape[3] // 512
        for part in range(parts):
            cols = slice(part * 512, (part + 1) * 512)
            active, slope = gelu_pair(mm(a2, flat(wu, cols)))
            active = active.astype(bf16)
            u_ref[at, cols] = active
            gp_ref[at, cols] = slope.astype(bf16)
            total = total + mm(active, flat_rows(wd, part, parts))
        out_ref[at, :] = total
        if layer == 0:
            g, b = rows_ref[row + 4 : row + 5, :], rows_ref[row + 5 : row + 6, :]
            next_ref[at, :] = (normalize(total)[0] * g + b).astype(bf16)
            next_ahead.start(stream, at)

            @pl.when(stream == 0)
            def _():
                late.relay()

        return carry

    for_streams(feed, 0)
    if layer == 0:
        late.finish()
        frames_ahead.sent(0, every)
        for stream in range(streams):
            at = tile(stream, span)
            next_ahead.sent(stream, at)
            next_ahead.arrived(stream, at)


def head_kernel(rows_ref, r_ref, wh, target_ref, share_ref, dwh_ref, dr_ref, gr_ref, loss_ref, acc):
    gain, bias = rows_ref[1:2, :], rows_ref[2:3, :]
    step = 256
    acc[...] = jnp.zeros_like(acc)
    gr_ref[...] = jnp.zeros_like(gr_ref)
    loss_ref[...] = jnp.zeros_like(loss_ref)

    def one(index, carry):
        at = tile(index, step)
        standard, scale = normalize(r_ref[at, :])
        f = (standard * gain + bias).astype(bf16)
        z = mm(f, flat(wh))
        share = share_ref[at, :]
        peak = jnp.max(z, axis=-1, keepdims=True)
        raised = jnp.exp(z - peak)
        total = jnp.sum(raised, axis=-1, keepdims=True)
        code = lax.broadcasted_iota(jnp.int32, z.shape, 1)
        hit = code == target_ref[at, :]
        picked = jnp.sum(jnp.where(hit, z, 0.0), axis=-1, keepdims=True)
        loss_ref[...] += jnp.sum(share * (peak + jnp.log(total) - picked))
        soft = raised * (1.0 / total)
        dz = (share * jnp.where(hit, soft - 1.0, soft)).astype(bf16)
        acc[...] += mm(f, dz, TN)
        df = mm(dz, flat(wh), NT)
        gr_ref[0:1, :] += jnp.sum(df * standard, axis=0, keepdims=True)
        gr_ref[1:2, :] += jnp.sum(df, axis=0, keepdims=True)
        dr_ref[at, :] = norm_back(df, standard, scale, gain)
        return carry

    lax.fori_loop(0, r_ref.shape[0] // step, one, 0)
    dwh_ref[...] = acc[...].astype(bf16)


def attend_back(streams, span, heads, refs):
    (q_ref, k_ref, v_ref, o_ref, lse_ref, kf_ref, qf_ref, do_ref, dq_ref, dk_ref, dv_ref, gs_ref, dk_acc, dv_acc) = refs
    pairs = heads // 2
    step = span // 2
    masks = half_masks()
    key_at = lax.broadcasted_iota(jnp.int32, (step, step), 0)
    query_at = lax.broadcasted_iota(jnp.int32, (step, step), 1)
    head_row = lax.broadcasted_iota(jnp.int32, (8, 128), 0)
    place = lax.broadcasted_iota(jnp.int32, (1, step), 1)
    gs_ref[...] = jnp.zeros_like(gs_ref)

    def one(stream, pair):
        cols = tile(pair, 128)
        k_pair = k_ref[tile(stream, 2 * span), cols]
        v_pair = v_ref[tile(stream, 2 * span), cols]
        dk_acc[...] = jnp.zeros_like(dk_acc)
        dv_acc[...] = jnp.zeros_like(dv_acc)
        for part in range(2):
            seen = span + part * step
            rows = pl.ds(pl.multiple_of(stream * span + part * step, step), step)
            q_pair = q_ref[rows, cols]
            do_pair = do_ref[rows, cols]
            both = (do_pair.astype(f32) * o_ref[rows, cols].astype(f32)).T
            done = []
            for half in range(2):
                head = 2 * pair + half
                mask = masks[half]
                q_own = q_pair * mask
                q_aug = q_own + qf_ref[pl.ds(head, 1), :].astype(bf16)
                k_aug = k_pair[: seen + step] * mask + kf_ref[stream, half, : seen + step]
                do_own = do_pair * mask
                delta = jnp.sum(both[half * 64 : half * 64 + 64], axis=0, keepdims=True)
                log_total = lse_ref[pl.ds(stream * heads + head, 1), part * step : (part + 1) * step]
                turned = jnp.zeros((128, step), f32)
                for low, high in ((0, seen), (seen, seen + step)):
                    score = mm(k_aug[low:high], q_aug, NT)
                    if low:
                        score = jnp.where(key_at <= query_at, score, masked_score)
                    chance = jnp.exp(score - log_total)
                    dp = mm(v_pair[low:high], do_own, NT)
                    dv_acc[low:high, :] += mm(chance.astype(bf16), do_own)
                    ds = (chance * (dp - delta)).astype(bf16)
                    dk_acc[low:high, :] += mm(ds, q_own)
                    turned = turned + mm(k_aug[low:high], ds, TN)
                done.append(turned[half * 64 : half * 64 + 64] * 0.125)
                base = 64 - half * 64
                lean = (
                    turned[base : base + 1]
                    + turned[base + 3 : base + 4]
                    - (place + (part * step + span)).astype(f32) * turned[base + 7 : base + 8]
                )
                gs_ref[...] += jnp.where(head_row == head, jnp.sum(lean), 0.0)
            dq_ref[rows, cols] = jnp.concatenate(done, axis=0).T.astype(bf16)
        dk_ref[tile(stream, 2 * span), cols] = dk_acc[...].astype(bf16)
        dv_ref[tile(stream, 2 * span), cols] = dv_acc[...].astype(bf16)

    def over(stream, carry):
        def inner(pair, carry):
            one(stream, pair)
            return carry

        return lax.fori_loop(0, pairs, inner, carry)

    lax.fori_loop(0, streams, over, 0)


def backward_kernel(layer, streams, span, heads, *refs):
    refs = list(refs)
    (first_ref, rows_ref, a_ref, ap_ref, q_ref, k_ref, v_ref, o_ref, lse_ref, r1_ref, a2_ref, u_ref, gp_ref, kf_ref, qf_ref, wp, wo, wu, wd) = refs[:19]
    rest = refs[19:]
    if layer == 0:
        (frames_ref, halo_ref, r_ref, pr_ref, dr1_in, da_in, back_ref, r_next) = rest[:8]
        (dwp, dwo, dwu, dwd, gr_ref, gs_ref, dsmall_ref) = rest[8:15]
        scratch = rest[15:]
    else:
        (dr_in, mem_ref) = rest[:2]
        (dwp, dwo, dwu, dwd, gr_ref, gs_ref, dr1_out, da_out, dap_out) = rest[2:11]
        scratch = rest[11:]
    (dr_ref, da_ref, do_ref, dq_ref, dk_ref, dv_ref, dk_acc, dv_acc, tr_ref) = scratch
    width = a_ref.shape[1]
    count = streams * span
    first = first_ref[0] > 0
    row = 3 + 4 * layer
    g1, b1, g2, b2 = (rows_ref[row + i : row + i + 1, :] for i in range(4))
    step = 256
    tiles = count // step
    gr_ref[...] = jnp.zeros_like(gr_ref)

    if layer == 0:
        g = rows_ref[row + 4 : row + 5, :]

        def join(index, carry):
            at = tile(index, step)
            standard, scale = normalize(r_next[at, :])
            da = da_in[at, :] + back_ref[at, :].astype(f32)
            gr_ref[4:5, :] += jnp.sum(da * standard, axis=0, keepdims=True)
            gr_ref[5:6, :] += jnp.sum(da, axis=0, keepdims=True)
            dr_ref[at, :] = dr1_in[at, :] + norm_back(da, standard, scale, g)
            return carry

        lax.fori_loop(0, tiles, join, 0)
    else:

        def take(index, carry):
            at = tile(index, step)
            dr_ref[at, :] = dr_in[at, :]
            return carry

        lax.fori_loop(0, tiles, take, 0)

    da_ref[...] = jnp.zeros_like(da_ref)
    tr_ref[...] = a2_ref[...].T

    parts = wu.shape[3] // 512

    def feed(part, carry):
        cols = tile(part, 512)
        dy = dr_ref[...].astype(bf16)
        dh = (mm(dy, flat_rows(wd, part, parts), NT) * gp_ref[:, cols].astype(f32)).astype(bf16)
        dwd[cols, :] = mm(u_ref[:, cols], dy, TN).astype(bf16)
        dwu[:, cols] = mm(tr_ref[...], dh).astype(bf16)
        da_ref[...] += mm(dh, flat(wu, cols), NT)
        return carry

    lax.fori_loop(0, parts, feed, 0)

    def middle(index, carry):
        at = tile(index, step)
        standard, scale = normalize(r1_ref[at, :])
        da = da_ref[at, :]
        gr_ref[2:3, :] += jnp.sum(da * standard, axis=0, keepdims=True)
        gr_ref[3:4, :] += jnp.sum(da, axis=0, keepdims=True)
        dr = dr_ref[at, :] + norm_back(da, standard, scale, g2)
        dr_ref[at, :] = dr
        do_ref[at, :] = mm(dr.astype(bf16), flat(wo), NT).astype(bf16)
        return carry

    lax.fori_loop(0, tiles, middle, 0)
    dwo[...] = mm(o_ref[...], dr_ref[...].astype(bf16), TN).astype(bf16)

    attend_back(
        streams,
        span,
        heads,
        (q_ref, k_ref, v_ref, o_ref, lse_ref, kf_ref, qf_ref, do_ref, dq_ref, dk_ref, dv_ref, gs_ref, dk_acc, dv_acc),
    )

    tr_ref[...] = a_ref[...].T
    dwp[:, :width] = mm(tr_ref[...], dq_ref[...]).astype(bf16)
    for spot, ref in ((1, dk_ref), (2, dv_ref)):
        total = jnp.zeros((width, width), f32)
        for stream in range(streams):
            behind = slice(stream * 2 * span, stream * 2 * span + span)
            here = slice(stream * 2 * span + span, (stream + 1) * 2 * span)
            own = slice(stream * span, (stream + 1) * span)
            total = total + mm(tr_ref[:, own], ref[here, :])
            total = total + mm(ap_ref[own, :], ref[behind, :], TN)
        dwp[:, spot * width : (spot + 1) * width] = total.astype(bf16)

    if layer == 0:
        dsmall_ref[...] = jnp.zeros_like(dsmall_ref)

    def finish(stream, carry):
        for part in range(span // step):
            at = pl.ds(pl.multiple_of(stream * span + part * step, step), step)
            behind = pl.ds(pl.multiple_of(stream * 2 * span + part * step, step), step)
            here = pl.ds(pl.multiple_of(stream * 2 * span + span + part * step, step), step)
            wq, wk, wv = (flat(wp, slice(i * width, (i + 1) * width)) for i in range(3))
            da = mm(dq_ref[at, :], wq, NT) + mm(dk_ref[here, :], wk, NT) + mm(dv_ref[here, :], wv, NT)
            dap = mm(dk_ref[behind, :], wk, NT) + mm(dv_ref[behind, :], wv, NT)
            if layer == 0:
                standard, scale = normalize(r_ref[at, :])
                before, before_scale = normalize(pr_ref[at, :])
                gr_ref[0:1, :] += jnp.sum(da * standard + dap * before, axis=0, keepdims=True)
                gr_ref[1:2, :] += jnp.sum(da + dap, axis=0, keepdims=True)
                dr = dr_ref[at, :] + norm_back(da, standard, scale, g1)
                drp = norm_back(dap, before, before_scale, g1)
                drp = jnp.where(first, 0.0, drp)
                gr_ref[6:7, :] += jnp.sum(dr + drp, axis=0, keepdims=True)
                dsmall_ref[...] += mm(dr.astype(bf16), frames_ref[at, :], TN)
                dsmall_ref[...] += mm(drp.astype(bf16), halo_ref[at, :], TN)
            else:
                da_out[at, :] = da
                dr1_out[at, :] = dr_ref[at, :]
                dap_out[at, :] = dap.astype(bf16)
                before, before_scale = normalize(mem_ref[at, :].astype(f32))
                dap = jnp.where(first, dap, 0.0)
                gr_ref[0:1, :] += jnp.sum(dap * before, axis=0, keepdims=True)
                gr_ref[1:2, :] += jnp.sum(dap, axis=0, keepdims=True)
        return carry

    lax.fori_loop(0, streams, finish, 0)


def whole(space=pltpu.VMEM):
    return pl.BlockSpec(memory_space=space)


def call(kernel, name, args, outs, scratch=(), smem=1, flops=0, sems=(), collective=None):
    specs = [whole(pltpu.SMEM)] * smem + [whole()] * (len(args) - smem)
    return pl.pallas_call(
        kernel,
        name=name,
        out_shape=[jax.ShapeDtypeStruct(*out) for out in outs],
        in_specs=specs,
        out_specs=[whole()] * len(outs),
        scratch_shapes=[pltpu.VMEM(*item) for item in scratch] + list(sems),
        compiler_params=pltpu.CompilerParams(
            vmem_limit_bytes=VMEM_LIMIT, collective_id=collective, has_side_effects=collective is not None
        ),
        cost_estimate=pl.CostEstimate(flops=flops, bytes_accessed=20000000, transcendentals=0),
    )(*args)


def split_three(value):
    one = value.astype(bf16)
    rest = value - one.astype(f32)
    two = rest.astype(bf16)
    rest = rest - two.astype(f32)
    return (one, two, rest.astype(bf16))


def per_matrix(arrays):
    parts = [jnp.sum(arrays[0] * arrays[0]).reshape(1)]
    for stacked in arrays[1:5]:
        parts.append(jnp.sum(stacked * stacked, axis=(1, 2)))
    parts.append(jnp.sum(arrays[5] * arrays[5]).reshape(1))
    parts.append(jnp.sum(arrays[6] * arrays[6], axis=1))
    return jnp.concatenate(parts)


def adam_direction(weight, grad, first, second, decay):
    new_first = beta_one * first + (1.0 - beta_one) * grad
    new_second = beta_two * second + (1.0 - beta_two) * grad * grad
    first_hat = new_first / (1.0 - beta_one**STEP)
    second_hat = new_second / (1.0 - beta_two**STEP)
    return (new_first, new_second, first_hat / (jnp.sqrt(second_hat) + adam_eps) + decay * weight)


def shards(
    frames,
    targets,
    frame_count,
    memory,
    memory_len,
    input_weight,
    project_weight,
    output_weight,
    up_weight,
    down_weight,
    head_weight,
    vectors,
    slopes,
    first_input,
    first_project,
    first_output,
    first_up,
    first_down,
    first_head,
    first_vectors,
    first_slopes,
    second_input,
    second_project,
    second_output,
    second_up,
    second_down,
    second_head,
    second_vectors,
    second_slopes,
):
    streams, span, features = frames.shape
    layers, heads = slopes.shape
    nvec = vectors.shape[0]
    width = project_weight.shape[2] // 3
    hidden = up_weight.shape[2]
    codes = head_weight.shape[1]
    count = streams * span
    seq_index = lax.axis_index("seq")
    first = seq_index == 0
    first_flag = jnp.where(first, 1, 0).astype(jnp.int32).reshape(1)
    streams_all = streams * lax.axis_size("stream")

    small_own = jnp.concatenate(
        [input_weight.T, vectors.T, jnp.zeros((input_weight.shape[1], 128 - features - nvec), f32)], axis=1
    ).astype(bf16)
    frames_flat = frames.reshape((count, features))
    frames_flat = jnp.concatenate(
        [frames_flat, jnp.ones((count, 1), bf16), jnp.zeros((count, 127 - features), bf16)], axis=1
    )
    memory_flat = memory.reshape((layers, count, width))

    key_pos = jnp.arange(2 * span)
    hidden_key = jnp.logical_and(first, key_pos[None] < span - memory_len[:, None])
    coarse = (key_pos // 256 * 256).astype(bf16)
    fine = (key_pos % 256).astype(bf16)
    one = jnp.ones_like(coarse)
    shape = (streams, 2 * span)
    columns = [jnp.broadcast_to(item, shape) for item in (coarse, coarse, coarse, fine, fine, fine)]
    columns += [hidden_key.astype(bf16), jnp.broadcast_to(one, shape)]
    key_marks = jnp.pad(jnp.stack(columns, axis=-1), ((0, 0), (0, 0), (0, 56)))
    blank = jnp.zeros_like(key_marks)
    key_marks = jnp.stack(
        [jnp.concatenate([blank, key_marks], axis=-1), jnp.concatenate([key_marks, blank], axis=-1)], axis=1
    )
    parts = split_three(slopes)
    marks = jnp.stack(parts + parts + (jnp.full_like(parts[0], masked_score), jnp.zeros_like(parts[0])), axis=-1)
    marks = jnp.pad(marks, ((0, 0), (0, 0), (0, 56))).astype(f32)
    even = (jnp.arange(heads) % 2 == 0)[None, :, None]
    query_marks = jnp.concatenate([jnp.where(even, 0.0, marks), jnp.where(even, marks, 0.0)], axis=-1)

    full = ((count, width), f32)
    low = ((count, width), bf16)
    joined = ((2 * count, width), bf16)
    wide = ((count, hidden), bf16)
    lse = ((streams * heads, span), f32)
    saved_outs = [low, low, joined, joined, low, lse, full, low, wide, wide, full]
    cost = 2 * count * (5 * width * width + width * width + 2 * width * hidden) + 4 * count * 2 * span * width

    devices = lax.axis_size("stream")
    chips = devices // 2
    sizes = (devices, lax.axis_size("seq"), streams, span, heads, features, nvec)

    def gathered(rows_all, cols):
        return ((chips, 2, rows_all // devices, cols), bf16)

    project_shape = gathered(width, 3 * width)
    output_shape = gathered(width, width)
    up_shape = gathered(width, hidden)
    down_shape = gathered(hidden, width)
    dma = pltpu.SemaphoreType.DMA
    made = call(
        functools.partial(forward_kernel, 0, sizes),
        "forward_zero",
        (first_flag, small_own, frames_flat, memory_flat[0], key_marks, query_marks[0], project_weight, output_weight, up_weight, down_weight),
        [((16, width), f32), full, low, full, low]
        + saved_outs
        + [low, low, ((count, 128), bf16), gathered(width, 128), project_shape, output_shape, up_shape, down_shape, project_shape, output_shape],
        sems=(dma((7, chips)), dma((7, chips)), dma((2, 1)), dma((streams,)), dma((streams,))),
        flops=cost,
        collective=0,
    )
    rows, r_zero, low_zero, pr_zero, a_zero = made[:5]
    saved_zero = made[5:15]
    r_one, a_one, a_behind, frames_behind = made[15:19]
    weights_zero = made[20:24]
    project_one, output_one = made[24:]
    made = call(
        functools.partial(forward_kernel, 1, sizes),
        "forward_one",
        (first_flag, rows, r_one, a_one, a_behind, memory_flat[1], key_marks, query_marks[1], project_one, output_one, up_weight, down_weight, head_weight),
        [low] + saved_outs + [up_shape, down_shape, gathered(width, codes)],
        sems=(dma((3, chips)), dma((3, chips))),
        flops=cost,
        collective=1,
    )
    low_one = made[0]
    saved_one = made[1:11]
    r_two = made[11]
    up_one, down_one, head_low = made[12:]
    weights_low = (weights_zero, (project_one, output_one, up_one, down_one))

    position = seq_index * span + jnp.arange(span)
    share = jnp.where(
        position[None] < frame_count[:, None],
        1.0 / (frame_count[:, None].astype(f32) * streams_all),
        0.0,
    )
    grad_head, dr_two, last_rows, loss_tile = call(
        head_kernel,
        "head_loss",
        (rows, r_two, head_low, targets.reshape((count, 1)), share.reshape((count, 1))),
        [((width, codes), bf16), full, ((8, width), f32), ((8, 128), f32)],
        [((width, codes), f32)],
        smem=0,
        flops=6 * count * width * codes,
    )
    loss_term = loss_tile[0, 0]

    weight_outs = [
        ((width, 3 * width), bf16),
        ((width, width), bf16),
        ((width, hidden), bf16),
        ((hidden, width), bf16),
        ((8, width), f32),
        ((8, 128), f32),
    ]
    scratch = [full, full, low, low, joined, joined, ((2 * span, 128), f32), ((2 * span, 128), f32), ((width, count), bf16)]
    made = call(
        functools.partial(backward_kernel, 1, streams, span, heads),
        "backward_one",
        (first_flag, rows, a_one, *saved_one[:9], saved_one[9], key_marks, query_marks[1], *weights_low[1], dr_two, memory_flat[1]),
        weight_outs + [full, full, low],
        scratch,
        flops=2 * cost,
    )
    matrices_one, rows_one, slope_one = made[:4], made[4], made[5]
    dr1_one, da_one, dap_one = made[6:]
    back_one = from_behind(dap_one, "seq", -1)
    made = call(
        functools.partial(backward_kernel, 0, streams, span, heads),
        "backward_zero",
        (first_flag, rows, a_zero, *saved_zero[:9], saved_zero[9], key_marks, query_marks[0], *weights_low[0], frames_flat, frames_behind, r_zero, pr_zero, dr1_one, da_one, back_one, r_one),
        weight_outs + [((width, 128), f32)],
        scratch,
        flops=2 * cost,
    )
    matrices_zero, rows_zero, slope_zero, grad_small = made[:4], made[4], made[5], made[6]

    grad_rows = jnp.concatenate(
        [rows_zero[6:7], last_rows[0:2], rows_zero[0:4], rows_one[0:2] + rows_zero[4:6], rows_one[2:4]], axis=0
    )
    grad_slopes = jnp.stack([slope_zero[:, 0], slope_one[:, 0]])
    grad_small = jnp.concatenate(
        [grad_small[:, :features], grad_rows.T, jnp.zeros((width, 128 - features - nvec), f32)], axis=1
    ).astype(bf16)

    def scatter(grad):
        return lax.psum_scatter(grad, "stream", scatter_dimension=0, tiled=True)

    head_share = scatter(grad_head)
    one_share = [scatter(item) for item in matrices_one]
    zero_share = [scatter(item) for item in matrices_zero]
    small_share = scatter(grad_small)
    head_share, one_share, zero_share, small_share = lax.psum(
        (head_share, one_share, zero_share, small_share), "seq"
    )
    pairs_of = [jnp.stack([zero, one]).astype(f32) for zero, one in zip(zero_share, one_share)]
    small_share = small_share.astype(f32)
    grads = (
        small_share[:, :features].T,
        pairs_of[0],
        pairs_of[1],
        pairs_of[2],
        pairs_of[3],
        head_share.astype(f32),
        small_share[:, features : features + nvec].T,
    )
    loss, grad_slopes = lax.psum((loss_term, grad_slopes), ("seq", "stream"))
    grad_squares = lax.psum(per_matrix(grads), "stream")
    clip_norm = jnp.sqrt(jnp.sum(grad_squares) + jnp.sum(grad_slopes * grad_slopes))
    factor = jnp.minimum(1.0, clip_limit / clip_norm)
    weights = (
        input_weight,
        project_weight,
        output_weight,
        up_weight,
        down_weight,
        head_weight,
        vectors,
    )
    firsts = (
        first_input,
        first_project,
        first_output,
        first_up,
        first_down,
        first_head,
        first_vectors,
    )
    seconds = (
        second_input,
        second_project,
        second_output,
        second_up,
        second_down,
        second_head,
        second_vectors,
    )
    moved = [
        adam_direction(
            weights[index], grads[index] * factor, firsts[index], seconds[index], decay_rate
        )
        for index in range(7)
    ]
    updates = [item[2] for item in moved]
    weight_squares, update_squares = lax.psum((per_matrix(weights), per_matrix(updates)), "stream")
    weight_norm = jnp.sqrt(weight_squares)
    update_norm = jnp.sqrt(update_squares)
    ratio = weight_norm / update_norm
    layer_end = 1 + 4 * layers
    shaped = [
        ratio[0],
        ratio[1 : 1 + layers][:, None, None],
        ratio[1 + layers : 1 + 2 * layers][:, None, None],
        ratio[1 + 2 * layers : 1 + 3 * layers][:, None, None],
        ratio[1 + 3 * layers : layer_end][:, None, None],
        ratio[layer_end],
        ratio[layer_end + 1 :][:, None],
    ]
    fresh = [weights[index] - lamb_rate * shaped[index] * updates[index] for index in range(7)]
    slope_first, slope_second, slope_update = adam_direction(
        slopes, grad_slopes * factor, first_slopes, second_slopes, 0.0
    )
    fresh_slopes = slopes - slope_rate * slope_update
    slope_row = jnp.stack(
        [jnp.sqrt(jnp.sum(slopes * slopes)), jnp.sqrt(jnp.sum(slope_update * slope_update))]
    ).reshape((1, 2))
    norms = jnp.concatenate([jnp.stack([weight_norm, update_norm], axis=1), slope_row], axis=0)
    layer_inputs = jnp.stack([low_zero, low_one]).reshape((layers, streams, span, width))
    return (
        loss,
        layer_inputs,
        clip_norm,
        norms,
        *fresh,
        fresh_slopes,
        *[item[0] for item in moved],
        slope_first,
        *[item[1] for item in moved],
        slope_second,
    )


def solution(mesh):
    rows3 = P(None, "stream", None)
    state = (P(None, "stream"), rows3, rows3, rows3, rows3, P("stream", None), P(None, "stream"), P())
    in_specs = (
        P("stream", "seq", None),
        P("stream", "seq"),
        P("stream"),
        P(None, "stream", None, None),
        P("stream"),
    ) + state * 3
    out_specs = (P(), P(None, "stream", "seq", None), P(), P()) + state * 3
    return jax.shard_map(shards, mesh=mesh, in_specs=in_specs, out_specs=out_specs, check_vma=False)
```

```python
import functools

import jax
import jax.numpy as jnp
from jax import lax
from jax.experimental import pallas as pl
from jax.experimental.pallas import tpu as pltpu
from jax.sharding import PartitionSpec as P

STEP = 10


ln_eps = 1e-05
clip_limit = 0.002
beta_one = 0.9
beta_two = 0.999
lamb_rate = 0.3
slope_rate = 0.001
decay_rate = 0.01
adam_eps = 1e-11
masked_score = -1e30

tail_terms = (
    0.16918934881687164,
    0.1706908941268921,
    0.1485215127468109,
    0.21418032050132751,
    -0.09282323718070984,
    0.5449625253677368,
    -0.5097681879997253,
    0.48429951071739197,
    -0.12925273180007935,
)

NN = (((1,), (0,)), ((), ()))
NT = (((1,), (1,)), ((), ()))
TN = (((0,), (0,)), ((), ()))
VMEM_LIMIT = 63 * 1024 * 1024
f32 = jnp.float32
bf16 = jnp.bfloat16


def mm(left, right, dims=NN):
    return lax.dot_general(left, right, dims, preferred_element_type=f32)


MESH = pl.DeviceIdType.MESH


class Place:
    def __init__(self, streams, blocks):
        self.chips = streams // 2
        self.blocks = blocks
        index = lax.axis_index("stream")
        self.chip = index // 2
        self.core = index % 2
        self.block = lax.axis_index("seq")
        self.sibling = {"stream": 2 * self.chip + 1 - self.core}

    def other(self, distance):
        return (self.chip + distance) % self.chips

    def mate(self, distance):
        return {"stream": 2 * self.other(distance) + self.core}

    def peer(self, distance):
        return (self.block + distance) % self.blocks

    def greet(self, line=False, column=False):
        barrier = pltpu.get_barrier_semaphore()

        def hello(device):
            pl.semaphore_signal(barrier, inc=1, device_id=device, device_id_type=MESH)

        hello(self.sibling)
        for distance in range(1, self.chips):
            hello(self.mate(distance))
        if line:

            @pl.when(self.block > 0)
            def _():
                hello({"seq": self.block - 1})

            pl.semaphore_wait(barrier, self.chips + jnp.where(self.block < self.blocks - 1, 1, 0))
        elif column:
            for distance in range(1, self.blocks):
                hello({"seq": self.peer(distance)})
            pl.semaphore_wait(barrier, self.chips + self.blocks - 1)
        else:
            pl.semaphore_wait(barrier, self.chips)


class Gather:
    def __init__(self, place, refs, sems, first):
        self.place, self.refs, self.sems, self.first = place, refs, sems, first

    def far(self, index, distance):
        place, ref = self.place, self.refs[index]
        out_sem, in_sem = self.sems[0], self.sems[1]
        return pltpu.make_async_remote_copy(
            src_ref=ref.at[place.chip, place.core],
            dst_ref=ref.at[place.chip, place.core],
            send_sem=out_sem.at[self.first + index, distance],
            recv_sem=in_sem.at[self.first + index, distance],
            device_id=place.mate(distance),
            device_id_type=MESH,
        )

    def near(self, index, core):
        place, ref = self.place, self.refs[index]
        out_sem, in_sem = self.sems[0], self.sems[1]
        return pltpu.make_async_remote_copy(
            src_ref=ref.at[:, core],
            dst_ref=ref.at[:, core],
            send_sem=out_sem.at[self.first + index, 0],
            recv_sem=in_sem.at[self.first + index, 0],
            device_id=place.sibling,
            device_id_type=MESH,
        )

    def push(self):
        for index in range(len(self.refs)):
            for distance in range(1, self.place.chips):
                self.far(index, distance).start()

    def relay(self):
        place = self.place
        for index in range(len(self.refs)):
            ref = self.refs[index]
            for distance in range(1, place.chips):
                source = place.other(place.chips - distance)
                pltpu.make_async_remote_copy(
                    src_ref=ref.at[source, place.core],
                    dst_ref=ref.at[source, place.core],
                    send_sem=self.sems[0].at[self.first + index, distance],
                    recv_sem=self.sems[1].at[self.first + index, distance],
                    device_id=place.mate(distance),
                    device_id_type=MESH,
                ).wait_recv()
            self.near(index, place.core).start()

    def finish(self):
        place = self.place
        for index in range(len(self.refs)):
            self.near(index, 1 - place.core).wait_recv()
            self.near(index, place.core).wait_send()
            for distance in range(1, place.chips):
                self.far(index, distance).wait_send()


class Reduce:
    def __init__(self, place, sems, row, grad=None, pair=None, mates=None, own=None, line=None, total=None):
        self.place, self.sems, self.row = place, sems, row
        self.grad, self.pair, self.mates = grad, pair, mates
        self.own, self.line, self.total = own, line, total

    def copy(self, phase, slot, src, dst, device):
        return pltpu.make_async_remote_copy(
            src_ref=src,
            dst_ref=dst,
            send_sem=self.sems[0].at[self.row + phase, slot],
            recv_sem=self.sems[1].at[self.row + phase, slot],
            device_id=device,
            device_id_type=MESH,
        )

    def copy_a(self):
        place = self.place
        return self.copy(0, 0, self.grad.at[:, 1 - place.core], self.pair, place.sibling)

    def copy_b(self, distance, source=None):
        place = self.place
        slot = place.chip if source is None else source
        return self.copy(
            1, distance, self.pair.at[place.other(distance)], self.mates.at[slot], place.mate(distance)
        )

    def piece(self, block):
        size = self.own.shape[0] // self.place.blocks
        return pl.ds(block * size, size)

    def copy_c(self, distance, source=None):
        place = self.place
        slot = place.block if source is None else source
        there = place.peer(distance)
        return self.copy(2, distance, self.own.at[self.piece(there)], self.line.at[slot], {"seq": there})

    def copy_d(self, distance, source=None):
        place = self.place
        slot = self.piece(place.block if source is None else source)
        return self.copy(3, distance, self.total.at[slot], self.total.at[slot], {"seq": place.peer(distance)})

    def start_a(self):
        self.copy_a().start()

    def end_a(self):
        place = self.place
        self.copy_a().wait_recv()

        def add(chip, carry):
            self.pair[chip] = (self.pair[chip].astype(f32) + self.grad[chip, place.core].astype(f32)).astype(bf16)
            return carry

        lax.fori_loop(0, place.chips, add, 0)
        self.copy_a().wait_send()

    def start_b(self):
        for distance in range(1, self.place.chips):
            self.copy_b(distance).start()

    def end_b(self):
        place = self.place
        total = self.pair[place.chip].astype(f32)
        for distance in range(1, place.chips):
            source = place.other(place.chips - distance)
            self.copy_b(distance, source).wait_recv()
            total = total + self.mates[source].astype(f32)
        self.own[...] = total.astype(bf16)
        for distance in range(1, place.chips):
            self.copy_b(distance).wait_send()

    def start_c(self):
        for distance in range(1, self.place.blocks):
            self.copy_c(distance).start()

    def end_c(self):
        place = self.place
        mine = self.piece(place.block)
        total = self.own[mine].astype(f32)
        for distance in range(1, place.blocks):
            source = place.peer(place.blocks - distance)
            self.copy_c(distance, source).wait_recv()
            total = total + self.line[source].astype(f32)
        self.total[mine] = total.astype(bf16)
        for distance in range(1, place.blocks):
            self.copy_c(distance).wait_send()

    def start_d(self):
        for distance in range(1, self.place.blocks):
            self.copy_d(distance).start()

    def end_d(self):
        place = self.place
        for distance in range(1, place.blocks):
            self.copy_d(distance, place.peer(place.blocks - distance)).wait_recv()
        for distance in range(1, place.blocks):
            self.copy_d(distance).wait_send()


def put_blocks(grad, base, value):
    chips, cores, unused_blocks, rows, lanes = grad.shape
    for spot in range(value.shape[1] // lanes):
        part = value[:, spot * lanes : (spot + 1) * lanes].astype(bf16)
        grad[:, :, base + spot] = part.reshape((chips, cores, rows, lanes))


def put_down(grad, base, value, part, parts):
    chips, cores, unused_blocks, rows, lanes = grad.shape
    few = chips // parts
    high = value.shape[0] // (few * cores * rows)
    wide = value.shape[1] // lanes
    value = value.astype(bf16).reshape((few, cores, high, rows, value.shape[1]))
    for up in range(high):
        for spot in range(wide):
            grad[pl.ds(part * few, few), :, base + up * wide + spot] = value[
                :, :, up, :, spot * lanes : (spot + 1) * lanes
            ]


class Refs:
    def __init__(self, names, refs, lazy, flush):
        for name, ref in zip(names, refs, strict=True):
            setattr(self, name, ref)
        self.lazy, self.flush_names = list(lazy), list(flush)

    def load(self, name):
        return pltpu.make_async_copy(
            getattr(self, "far_" + name), getattr(self, name), self.load_sem.at[self.lazy.index(name)]
        )

    def fetch(self, *names):
        for name in names:
            self.load(name).start()

    def ready(self, *names):
        for name in names:
            self.load(name).wait()

    def store(self, name):
        return pltpu.make_async_copy(
            getattr(self, name), getattr(self, "far_" + name), self.store_sem.at[self.flush_names.index(name)]
        )

    def flush(self, *names):
        for name in names:
            self.store(name).start()

    def flushed(self, *names):
        for name in names or self.flush_names:
            self.store(name).wait()


class Ahead:
    def __init__(self, place, step, src, dst, sems):
        self.place, self.step, self.src, self.dst, self.sems = place, step, src, dst, sems
        self.sends = place.block < place.blocks - 1 if step > 0 else place.block > 0
        self.receives = place.block > 0 if step > 0 else place.block < place.blocks - 1

    def copy(self, slot, rows):
        return pltpu.make_async_remote_copy(
            src_ref=self.src.at[rows],
            dst_ref=self.dst.at[rows],
            send_sem=self.sems[0].at[slot],
            recv_sem=self.sems[1].at[slot],
            device_id={"seq": self.place.block + self.step},
            device_id_type=MESH,
        )

    def start(self, slot, rows):
        @pl.when(self.sends)
        def _():
            self.copy(slot, rows).start()

    def arrived(self, slot, rows):
        @pl.when(self.receives)
        def _():
            self.copy(slot, rows).wait_recv()

    def sent(self, slot, rows):
        @pl.when(self.sends)
        def _():
            self.copy(slot, rows).wait_send()


def flat(ref, cols=slice(None)):
    value = ref[:, :, :, cols]
    return value.reshape((-1, value.shape[-1]))


def flat_rows(ref, part, parts):
    chips = ref.shape[0] // parts
    value = ref[pl.ds(part * chips, chips)]
    return value.reshape((-1, value.shape[-1]))


def normalize(values):
    centred = values - jnp.mean(values, axis=-1, keepdims=True)
    scale = lax.rsqrt(jnp.mean(centred * centred, axis=-1, keepdims=True) + ln_eps)
    return (centred * scale, scale)


def norm_back(grad_out, standard, scale, gain):
    scaled = grad_out * gain
    return scale * (
        scaled
        - jnp.mean(scaled, axis=-1, keepdims=True)
        - standard * jnp.mean(scaled * standard, axis=-1, keepdims=True)
    )


def gelu_pair(x):
    size = jnp.abs(x)
    t = 1.0 / (1.0 + 0.21213203435596423 * size)
    poly = jnp.full_like(t, tail_terms[-1])
    for term in tail_terms[-2::-1]:
        poly = poly * t + term
    bell = jnp.exp(-0.5 * x * x)
    tail = 0.5 * t * poly * bell
    cumulative = jnp.where(x >= 0.0, 1.0 - tail, tail)
    return (x * cumulative, cumulative + x * (bell * 0.3989422804014327))


def tile(index, size):
    return pl.ds(pl.multiple_of(index * size, size), size)


def half_masks():
    lane = lax.broadcasted_iota(jnp.int32, (1, 128), 1)
    left = jnp.where(lane < 64, 1.0, 0.0).astype(bf16)
    right = jnp.where(lane < 64, 0.0, 1.0).astype(bf16)
    return (left, right)


def attend(streams, span, heads, q_ref, k_ref, v_ref, kf_ref, qf_ref, o_ref, lse_ref, between):
    pairs = heads // 2
    step = span // 2
    masks = half_masks()
    key_at = lax.broadcasted_iota(jnp.int32, (step, step), 0)
    query_at = lax.broadcasted_iota(jnp.int32, (step, step), 1)

    def one(stream, pair):
        cols = tile(pair, 128)
        k_pair = k_ref[tile(stream, 2 * span), cols]
        v_pair = v_ref[tile(stream, 2 * span), cols]
        outs = []
        for part in range(2):
            done = []
            for half in range(2):
                seen = span + part * step
                q_pair = q_ref[pl.ds(pl.multiple_of(stream * span + part * step, step), step), cols]
                head = 2 * pair + half
                q_aug = q_pair * masks[half] + qf_ref[pl.ds(head, 1), :].astype(bf16)
                k_aug = k_pair[: seen + step] * masks[half] + kf_ref[stream, half, : seen + step]
                v_aug = v_pair[: seen + step] * masks[half] + masks[1 - half]
                wide = mm(k_aug[:seen], q_aug, NT)
                near = mm(k_aug[seen:], q_aug, NT)
                near = jnp.where(key_at <= query_at, near, masked_score)
                peak = jnp.maximum(
                    jnp.max(wide, axis=0, keepdims=True), jnp.max(near, axis=0, keepdims=True)
                )
                wide = jnp.exp(wide - peak).astype(bf16)
                near = jnp.exp(near - peak).astype(bf16)
                mixed = mm(v_aug[:seen], wide, TN) + mm(v_aug[seen:], near, TN)
                own = mixed[half * 64 : half * 64 + 64]
                total = mixed[64 - half * 64 : 128 - half * 64]
                done.append(own / total)
                lse_ref[pl.ds(stream * heads + head, 1), part * step : (part + 1) * step] = (
                    peak + jnp.log(total[:1])
                )
            outs.append(jnp.concatenate(done, axis=0).T)
        for part in range(2):
            o_ref[pl.ds(pl.multiple_of(stream * span + part * step, step), step), cols] = outs[
                part
            ].astype(bf16)

    def over(stream, carry):
        def inner(pair, carry):
            one(stream, pair)
            return carry

        carry = lax.fori_loop(0, pairs, inner, carry)
        between(stream)
        return carry

    lax.fori_loop(0, streams, over, 0)


def forward_kernel(layer, sizes, *refs):
    (stream_devices, block_devices, streams, span, heads, features, nvec) = sizes
    place = Place(stream_devices, block_devices)
    chip, core = place.chip, place.core
    if layer == 0:
        (first_ref, small_own, frames_ref, mem_ref, kf_ref, qf_ref, pw, ow, uw, dw) = refs[:10]
        (rows_ref, r_ref, low_ref, pr_ref, a_ref, ap_ref, q_ref, k_ref, v_ref, o_ref, lse_ref, r1_ref, a2_ref, u_ref, gp_ref, out_ref) = refs[10:26]
        (next_ref, behind_ref, halo_ref, small, wp, wo, wu, wd, wp_next, wo_next) = refs[26:36]
        (out_sem, in_sem, frame_sem, next_out, next_in) = refs[36:]
        sems = (out_sem, in_sem)
        early = Gather(place, [small, wp], sems, 0)
        middle = Gather(place, [wo, wu, wd], sems, 2)
        late = Gather(place, [wp_next, wo_next], sems, 5)
        frames_ahead = Ahead(place, 1, frames_ref, halo_ref, (frame_sem.at[0], frame_sem.at[1]))
        next_ahead = Ahead(place, 1, next_ref, behind_ref, (next_out, next_in))
        every = pl.ds(0, streams * span)

        @pl.when(place.block == 0)
        def _():
            halo_ref[...] = jnp.zeros_like(halo_ref)
            behind_ref[...] = jnp.zeros_like(behind_ref)

        small[chip, core] = small_own[...]
        wp[chip, core] = pw[0].astype(bf16)
        place.greet(line=True)
        early.push()
        frames_ahead.start(0, every)
        wo[chip, core] = ow[0].astype(bf16)
        wu[chip, core] = uw[0].astype(bf16)
        wd[chip, core] = dw[0].astype(bf16)
        wp_next[chip, core] = pw[1].astype(bf16)
        wo_next[chip, core] = ow[1].astype(bf16)
        early.relay()
        middle.push()
        early.finish()
        turned = flat(small).astype(f32).T
        rows_ref[...] = jnp.zeros_like(rows_ref)
        rows_ref[:nvec, :] = turned[features : features + nvec]
        frames_ahead.arrived(0, every)
        halfway = middle
    else:
        (first_ref, rows_ref, r_ref, a_ref, halo_ref, mem_ref, kf_ref, qf_ref, wp, wo, uw, dw, hw) = refs[:13]
        (low_ref, ap_ref, q_ref, k_ref, v_ref, o_ref, lse_ref, r1_ref, a2_ref, u_ref, gp_ref, out_ref) = refs[13:25]
        (wu, wd, wh) = refs[25:28]
        (out_sem, in_sem) = refs[28:]
        halfway = Gather(place, [wu, wd, wh], (out_sem, in_sem), 0)
        wu[chip, core] = uw[1].astype(bf16)
        wd[chip, core] = dw[1].astype(bf16)
        wh[chip, core] = hw[...].astype(bf16)
        place.greet()
        halfway.push()
    width = a_ref.shape[1]
    first = first_ref[0] > 0
    row = 3 + 4 * layer
    g1, b1, g2, b2 = (rows_ref[row + i : row + i + 1, :] for i in range(4))
    step = span // 2
    for_streams = functools.partial(lax.fori_loop, 0, streams)

    def project(stream, carry):
        for part in range(2):
            at = pl.ds(pl.multiple_of(stream * span + part * step, step), step)
            behind = pl.ds(pl.multiple_of(stream * 2 * span + part * step, step), step)
            here = pl.ds(pl.multiple_of(stream * 2 * span + span + part * step, step), step)
            if layer == 0:
                r = mm(frames_ref[at, :], flat(small), NT)
                r_ref[at, :] = r
                low_ref[at, :] = r.astype(bf16)
                a = (normalize(r)[0] * g1 + b1).astype(bf16)
                a_ref[at, :] = a
                before = mm(halo_ref[at, :], flat(small), NT)
                before = jnp.where(first, mem_ref[at, :].astype(f32), before)
                pr_ref[at, :] = before
                ap = (normalize(before)[0] * g1 + b1).astype(bf16)
            else:
                low_ref[at, :] = r_ref[at, :].astype(bf16)
                a = a_ref[at, :]
                ap = (normalize(mem_ref[at, :].astype(f32))[0] * g1 + b1).astype(bf16)
                ap = jnp.where(first, ap.astype(f32), halo_ref[at, :].astype(f32)).astype(bf16)
            ap_ref[at, :] = ap
            wq, wk, wv = (flat(wp, slice(i * width, (i + 1) * width)) for i in range(3))
            q_ref[at, :] = (mm(a, wq) * 0.125).astype(bf16)
            k_ref[here, :] = mm(a, wk).astype(bf16)
            v_ref[here, :] = mm(a, wv).astype(bf16)
            k_ref[behind, :] = mm(ap, wk).astype(bf16)
            v_ref[behind, :] = mm(ap, wv).astype(bf16)
        return carry

    for_streams(project, 0)

    def between(stream):
        @pl.when(stream == 0)
        def _():
            halfway.relay()
            if layer == 0:
                late.push()

    attend(streams, span, heads, q_ref, k_ref, v_ref, kf_ref, qf_ref, o_ref, lse_ref, between)
    halfway.finish()

    def feed(stream, carry):
        at = tile(stream, span)
        after = r_ref[at, :] + mm(o_ref[at, :], flat(wo))
        r1_ref[at, :] = after
        a2 = (normalize(after)[0] * g2 + b2).astype(bf16)
        a2_ref[at, :] = a2
        total = after
        parts = wu.shape[3] // 512
        for part in range(parts):
            cols = slice(part * 512, (part + 1) * 512)
            active, slope = gelu_pair(mm(a2, flat(wu, cols)))
            active = active.astype(bf16)
            u_ref[at, cols] = active
            gp_ref[at, cols] = slope.astype(bf16)
            total = total + mm(active, flat_rows(wd, part, parts))
        out_ref[at, :] = total
        if layer == 0:
            g, b = rows_ref[row + 4 : row + 5, :], rows_ref[row + 5 : row + 6, :]
            next_ref[at, :] = (normalize(total)[0] * g + b).astype(bf16)
            next_ahead.start(stream, at)

            @pl.when(stream == 0)
            def _():
                late.relay()

        return carry

    for_streams(feed, 0)
    if layer == 0:
        late.finish()
        frames_ahead.sent(0, every)
        for stream in range(streams):
            at = tile(stream, span)
            next_ahead.sent(stream, at)
            next_ahead.arrived(stream, at)


def head_kernel(rows_ref, r_ref, wh, target_ref, share_ref, dwh_ref, dr_ref, gr_ref, loss_ref, acc):
    gain, bias = rows_ref[1:2, :], rows_ref[2:3, :]
    step = 256
    acc[...] = jnp.zeros_like(acc)
    gr_ref[...] = jnp.zeros_like(gr_ref)
    loss_ref[...] = jnp.zeros_like(loss_ref)

    def one(index, carry):
        at = tile(index, step)
        standard, scale = normalize(r_ref[at, :])
        f = (standard * gain + bias).astype(bf16)
        z = mm(f, flat(wh))
        share = share_ref[at, :]
        peak = jnp.max(z, axis=-1, keepdims=True)
        raised = jnp.exp(z - peak)
        total = jnp.sum(raised, axis=-1, keepdims=True)
        code = lax.broadcasted_iota(jnp.int32, z.shape, 1)
        hit = code == target_ref[at, :]
        picked = jnp.sum(jnp.where(hit, z, 0.0), axis=-1, keepdims=True)
        loss_ref[...] += jnp.sum(share * (peak + jnp.log(total) - picked))
        soft = raised * (1.0 / total)
        dz = (share * jnp.where(hit, soft - 1.0, soft)).astype(bf16)
        acc[...] += mm(f, dz, TN)
        df = mm(dz, flat(wh), NT)
        gr_ref[0:1, :] += jnp.sum(df * standard, axis=0, keepdims=True)
        gr_ref[1:2, :] += jnp.sum(df, axis=0, keepdims=True)
        dr_ref[at, :] = norm_back(df, standard, scale, gain)
        return carry

    lax.fori_loop(0, r_ref.shape[0] // step, one, 0)
    put_blocks(dwh_ref, 0, acc[...])


def attend_back(streams, span, heads, refs, early, between):
    (q_ref, k_ref, v_ref, o_ref, lse_ref, kf_ref, qf_ref, do_ref, dq_ref, dk_ref, dv_ref, gs_ref, dk_acc, dv_acc) = refs
    pairs = heads // 2
    step = span // 2
    masks = half_masks()
    key_at = lax.broadcasted_iota(jnp.int32, (step, step), 0)
    query_at = lax.broadcasted_iota(jnp.int32, (step, step), 1)
    head_row = lax.broadcasted_iota(jnp.int32, (8, 128), 0)
    place = lax.broadcasted_iota(jnp.int32, (1, step), 1)
    gs_ref[...] = jnp.zeros_like(gs_ref)

    def one(stream, pair):
        cols = tile(pair, 128)
        k_pair = k_ref[tile(stream, 2 * span), cols]
        v_pair = v_ref[tile(stream, 2 * span), cols]
        dk_acc[...] = jnp.zeros_like(dk_acc)
        dv_acc[...] = jnp.zeros_like(dv_acc)
        for part in range(2):
            seen = span + part * step
            rows = pl.ds(pl.multiple_of(stream * span + part * step, step), step)
            q_pair = q_ref[rows, cols]
            do_pair = do_ref[rows, cols]
            both = (do_pair.astype(f32) * o_ref[rows, cols].astype(f32)).T
            done = []
            for half in range(2):
                head = 2 * pair + half
                mask = masks[half]
                q_own = q_pair * mask
                q_aug = q_own + qf_ref[pl.ds(head, 1), :].astype(bf16)
                k_aug = k_pair[: seen + step] * mask + kf_ref[stream, half, : seen + step]
                do_own = do_pair * mask
                delta = jnp.sum(both[half * 64 : half * 64 + 64], axis=0, keepdims=True)
                log_total = lse_ref[pl.ds(stream * heads + head, 1), part * step : (part + 1) * step]
                turned = jnp.zeros((128, step), f32)
                for low, high in ((0, seen), (seen, seen + step)):
                    score = mm(k_aug[low:high], q_aug, NT)
                    if low:
                        score = jnp.where(key_at <= query_at, score, masked_score)
                    chance = jnp.exp(score - log_total)
                    dp = mm(v_pair[low:high], do_own, NT)
                    dv_acc[low:high, :] += mm(chance.astype(bf16), do_own)
                    ds = (chance * (dp - delta)).astype(bf16)
                    dk_acc[low:high, :] += mm(ds, q_own)
                    turned = turned + mm(k_aug[low:high], ds, TN)
                done.append(turned[half * 64 : half * 64 + 64] * 0.125)
                base = 64 - half * 64
                lean = (
                    turned[base : base + 1]
                    + turned[base + 3 : base + 4]
                    - (place + (part * step + span)).astype(f32) * turned[base + 7 : base + 8]
                )
                gs_ref[...] += jnp.where(head_row == head, jnp.sum(lean), 0.0)
            dq_ref[rows, cols] = jnp.concatenate(done, axis=0).T.astype(bf16)
        dk_ref[tile(stream, 2 * span), cols] = dk_acc[...].astype(bf16)
        dv_ref[tile(stream, 2 * span), cols] = dv_acc[...].astype(bf16)

    def over(stream, carry):
        def inner(pair, carry):
            one(stream, pair)
            early(stream * pairs + pair)
            return carry

        carry = lax.fori_loop(0, pairs, inner, carry)
        between(stream)
        return carry

    lax.fori_loop(0, streams, over, 0)


def backward_kernel(layer, sizes, r):
    (stream_devices, block_devices, streams, span, heads, features, nvec) = sizes
    place = Place(stream_devices, block_devices)
    width = r.a.shape[1]
    count = streams * span
    first = r.first[0] > 0
    row = 3 + 4 * layer
    g1, g2 = r.rows[row : row + 1, :], r.rows[row + 2 : row + 3, :]
    step = 256
    tiles = count // step
    sems = (r.out_sem, r.in_sem)
    broad = Reduce(place, sems, 0, grad=r.grad_a, pair=r.pair_a, mates=r.mates_a, own=r.own_a)
    if layer == 0:
        done_a = Reduce(place, sems, 4, own=r.own_a_one, line=r.line_a_one, total=r.total_a_one)
        done_b = Reduce(
            place, sems, 8, pair=r.pair_b_one, mates=r.mates_b_one, own=r.own_b_one, line=r.line_b_one, total=r.total_b_one
        )
    else:
        narrow = Reduce(place, sems, 4, grad=r.grad_b, pair=r.pair_b)
        head = Reduce(
            place, sems, 8, grad=r.grad_head, pair=r.pair_head, mates=r.mates_head, own=r.own_head, line=r.line_head, total=r.total_head
        )
        back = Ahead(place, -1, r.dap, r.back, (r.back_out, r.back_in))

        @pl.when(place.block == place.blocks - 1)
        def _():
            r.back[...] = jnp.zeros_like(r.back)

    for grad, used in ((r.grad_a, 36), (r.grad_b, 13 if layer == 0 else 12)):
        for block in range(used, grad.shape[2]):
            grad[:, :, block] = jnp.zeros(grad.shape[:2] + grad.shape[3:], bf16)
    r.gr[...] = jnp.zeros_like(r.gr)
    hidden_parts = r.wu.shape[3] // 512

    def stream_in(part, slot):
        cols = tile(part, 512)
        return (
            pltpu.make_async_copy(r.u.at[:, cols], r.u_two.at[slot], r.u_sem.at[0, slot]),
            pltpu.make_async_copy(r.gp.at[:, cols], r.gp_two.at[slot], r.u_sem.at[1, slot]),
        )

    first_loads = []
    if layer == 0:
        first_loads = [
            pltpu.make_async_copy(r.dr1_in, r.dr, r.first_sem.at[0]),
            pltpu.make_async_copy(r.r_next, r.da, r.first_sem.at[1]),
            pltpu.make_async_copy(r.da_in, r.wide_one, r.first_sem.at[2]),
        ]
        late_loads = [
            pltpu.make_async_copy(r.r, r.wide_one, r.first_sem.at[3]),
            pltpu.make_async_copy(r.pr, r.wide_two, r.first_sem.at[4]),
        ]
        late_loads[1].start()
    else:
        first_loads = [pltpu.make_async_copy(r.dr_in, r.dr, r.first_sem.at[0])]
    for load in first_loads:
        load.start()
    for load in stream_in(0, 0):
        load.start()
    r.fetch("wd", "a2", "wu", "r1", "wo", "o", "q", "k", "v", "kf", "wp", "a", "ap")
    place.greet(column=True)
    if layer == 0:
        done_a.start_c()
        done_b.start_b()

        g = r.rows[row + 4 : row + 5, :]

        def join(index, carry):
            at = tile(index, step)
            standard, scale = normalize(r.da[at, :])
            da = r.wide_one[at, :] + r.back[at, :].astype(f32)
            r.gr[4:5, :] += jnp.sum(da * standard, axis=0, keepdims=True)
            r.gr[5:6, :] += jnp.sum(da, axis=0, keepdims=True)
            r.dr[at, :] = r.dr[at, :] + norm_back(da, standard, scale, g)
            return carry

        for load in first_loads:
            load.wait()
        lax.fori_loop(0, tiles, join, 0)
        late_loads[0].start()
    else:
        head.start_a()
        first_loads[0].wait()

    r.da[...] = jnp.zeros_like(r.da)
    r.ready("wd", "a2", "wu")
    r.turned[...] = r.a2[...].T
    parts = hidden_parts

    def feed(part, carry):
        cols = tile(part, 512)
        slot = part % 2

        @pl.when(part + 1 < parts)
        def _():
            for load in stream_in(part + 1, 1 - slot):
                load.start()

        for load in stream_in(part, slot):
            load.wait()
        dy = r.dr[...].astype(bf16)
        dh = (mm(dy, flat_rows(r.wd, part, parts), NT) * r.gp_two[slot].astype(f32)).astype(bf16)
        put_down(r.grad_a, 0, mm(r.u_two[slot], dy, TN), part, parts)
        put_blocks(r.grad_a, 16 + 4 * part, mm(r.turned[...], dh))
        r.da[...] += mm(dh, flat(r.wu, cols), NT)
        if layer == 1:

            @pl.when(part == 0)
            def _():
                head.end_a()
                head.start_b()

        return carry

    lax.fori_loop(0, parts, feed, 0)
    r.ready("r1", "wo", "o")

    def middle(index, carry):
        at = tile(index, step)
        standard, scale = normalize(r.r1[at, :])
        da = r.da[at, :]
        r.gr[2:3, :] += jnp.sum(da * standard, axis=0, keepdims=True)
        r.gr[3:4, :] += jnp.sum(da, axis=0, keepdims=True)
        dr = r.dr[at, :] + norm_back(da, standard, scale, g2)
        r.dr[at, :] = dr
        r.do[at, :] = mm(dr.astype(bf16), flat(r.wo), NT).astype(bf16)
        return carry

    lax.fori_loop(0, tiles, middle, 0)
    put_blocks(r.grad_a, 32, mm(r.o[...], r.dr[...].astype(bf16), TN))
    broad.start_a()
    if layer == 0:
        done_a.end_c()
        done_a.start_d()
        done_b.end_b()
        done_b.start_c()
    else:
        head.end_b()
        head.start_c()
    wk, wv = (slice(i * width, (i + 1) * width) for i in (1, 2))

    def behind_gradient(at, behind):
        return mm(r.dk[behind, :], flat(r.wp, wk), NT) + mm(r.dv[behind, :], flat(r.wp, wv), NT)

    def early(index):
        @pl.when(index == 1)
        def _():
            broad.end_a()
            broad.start_b()

    def between(stream):
        if layer == 0:

            @pl.when(stream == 0)
            def _():
                done_b.end_c()
                done_b.start_d()

        else:
            for part in range(span // step):
                at = pl.ds(pl.multiple_of(stream * span + part * step, step), step)
                behind = pl.ds(pl.multiple_of(stream * 2 * span + part * step, step), step)
                r.dap[at, :] = behind_gradient(at, behind).astype(bf16)
            back.start(stream, tile(stream, span))

            @pl.when(stream == 0)
            def _():
                head.end_c()
                head.start_d()

    r.ready("q", "k", "v", "kf", "wp")
    attend_back(
        streams,
        span,
        heads,
        (r.q, r.k, r.v, r.o, r.lse, r.kf, r.qf, r.do, r.dq, r.dk, r.dv, r.gs, r.dk_acc, r.dv_acc),
        early,
        between,
    )

    r.ready("a", "ap")
    r.turned[...] = r.a[...].T
    put_blocks(r.grad_b, 0, mm(r.turned[...], r.dq[...]))
    for spot, ref in ((1, r.dk), (2, r.dv)):
        total = jnp.zeros((width, width), f32)
        for stream in range(streams):
            behind = slice(stream * 2 * span, stream * 2 * span + span)
            here = slice(stream * 2 * span + span, (stream + 1) * 2 * span)
            own = slice(stream * span, (stream + 1) * span)
            total = total + mm(r.turned[:, own], ref[here, :])
            total = total + mm(r.ap[own, :], ref[behind, :], TN)
        put_blocks(r.grad_b, 4 * spot, total)

    if layer == 0:
        r.small_acc[...] = jnp.zeros_like(r.small_acc)
        for load in late_loads:
            load.wait()
    else:
        narrow.start_a()

    def finish(stream, carry):
        for part in range(span // step):
            at = pl.ds(pl.multiple_of(stream * span + part * step, step), step)
            behind = pl.ds(pl.multiple_of(stream * 2 * span + part * step, step), step)
            here = pl.ds(pl.multiple_of(stream * 2 * span + span + part * step, step), step)
            da = (
                mm(r.dq[at, :], flat(r.wp, slice(0, width)), NT)
                + mm(r.dk[here, :], flat(r.wp, wk), NT)
                + mm(r.dv[here, :], flat(r.wp, wv), NT)
            )
            if layer == 0:
                dap = behind_gradient(at, behind)
                standard, scale = normalize(r.wide_one[at, :])
                before, before_scale = normalize(r.wide_two[at, :])
                r.gr[0:1, :] += jnp.sum(da * standard + dap * before, axis=0, keepdims=True)
                r.gr[1:2, :] += jnp.sum(da + dap, axis=0, keepdims=True)
                dr = r.dr[at, :] + norm_back(da, standard, scale, g1)
                drp = norm_back(dap, before, before_scale, g1)
                drp = jnp.where(first, 0.0, drp)
                r.gr[6:7, :] += jnp.sum(dr + drp, axis=0, keepdims=True)
                r.small_acc[...] += mm(dr.astype(bf16), r.frames[at, :], TN)
                r.small_acc[...] += mm(drp.astype(bf16), r.halo[at, :], TN)
            else:
                r.da[at, :] = da
                before, before_scale = normalize(r.mem[at, :].astype(f32))
                dap = jnp.where(first, r.dap[at, :].astype(f32), 0.0)
                r.gr[0:1, :] += jnp.sum(dap * before, axis=0, keepdims=True)
                r.gr[1:2, :] += jnp.sum(dap, axis=0, keepdims=True)
        return carry

    lax.fori_loop(0, streams, finish, 0)
    if layer == 0:
        listed = [r.gr[6:7, :], r.gr_last[0:2, :], r.gr[0:4, :], r.gr_one[0:2, :] + r.gr[4:6, :], r.gr_one[2:4, :]]
        listed = [jnp.zeros((features, width), f32)] + listed + [jnp.zeros((128 - features - nvec, width), f32)]
        lane = lax.broadcasted_iota(jnp.int32, (1, 128), 1)
        merged = jnp.where(lane < features, r.small_acc[...], jnp.concatenate(listed, axis=0).T)
        put_blocks(r.grad_b, 12, merged)
        done_b.end_d()
        done_a.end_d()
        broad.end_b()
    else:
        head.end_d()
        narrow.end_a()
        broad.end_b()
        for stream in range(streams):
            at = tile(stream, span)
            back.sent(stream, at)
            back.arrived(stream, at)


def send_tile(src, dst, sems, slot_out, slot_in, device):
    return pltpu.make_async_remote_copy(
        src_ref=src, dst_ref=dst, send_sem=sems[0].at[slot_out], recv_sem=sems[1].at[slot_in], device_id=device, device_id_type=MESH
    )


def row_sum(values, axis=None):
    return jnp.sum(values) if axis is None else jnp.sum(values, axis=axis, keepdims=True)


def state_blocks(layers, rows, totals):
    for layer in range(layers):
        wide, narrow = totals[2 * layer], totals[2 * layer + 1]
        for spot in range(12):
            yield (1, layer, slice(0, rows), spot, (narrow, spot), 1 + layer)
        for spot in range(4):
            yield (2, layer, slice(0, rows), spot, (wide, 32 + spot), 1 + layers + layer)
        for spot in range(16):
            yield (3, layer, slice(0, rows), spot, (wide, 16 + spot), 1 + 2 * layers + layer)
        for up in range(4):
            for spot in range(4):
                yield (4, layer, slice(up * rows, (up + 1) * rows), spot, (wide, 4 * up + spot), 1 + 3 * layers + layer)
    for spot in range(8):
        yield (5, None, slice(0, rows), spot, (totals[2 * layers], spot), 1 + 4 * layers)


def take_block(ref, layer, rows, spot):
    cols = slice(spot * 128, (spot + 1) * 128)
    return ref[rows, cols] if layer is None else ref[layer, rows, cols]


def tail_kernel(sizes, layers, r):
    (stream_devices, block_devices, streams, span, heads, features, nvec) = sizes
    place = Place(stream_devices, block_devices)
    index = lax.axis_index("stream")
    sems = (r.out_sem, r.in_sem)
    broad = Reduce(place, sems, 0, own=r.own_a, line=r.line_a, total=r.total_a)
    narrow = Reduce(place, sems, 4, grad=r.grad_b, pair=r.pair_b, mates=r.mates_b, own=r.own_b, line=r.line_b, total=r.total_b)
    states = [
        ("input", "project", "output", "up", "down", "head", "vectors"),
    ][0]
    copies = []
    for kind in ("weight", "first", "second"):
        for name in states:
            number = len(copies)
            copies.append(
                pltpu.make_async_copy(
                    getattr(r, kind + "_" + name), getattr(r, "held_" + kind + "_" + name), r.load_sem.at[number]
                )
            )
    for copy in copies:
        copy.start()
    barrier = pltpu.get_barrier_semaphore()
    for distance in range(1, stream_devices):
        pl.semaphore_signal(
            barrier, inc=1, device_id={"stream": (index + distance) % stream_devices}, device_id_type=MESH
        )
    for distance in range(1, block_devices):
        pl.semaphore_signal(barrier, inc=1, device_id={"seq": place.peer(distance)}, device_id_type=MESH)
    pl.semaphore_wait(barrier, stream_devices - 1 + block_devices - 1)
    narrow.start_a()
    r.plain[0:8, :] = r.gs_zero[...]
    r.plain[8:16, :] = r.gs_one[...]
    r.plain[16:24, :] = r.loss[...]
    sum_sems = (r.sum_out, r.sum_in)
    near = send_tile(r.plain, r.plain_near, sum_sems, 0, 0, place.sibling)
    near.start()
    broad.start_c()
    narrow.end_a()
    narrow.start_b()
    near.wait_recv()
    near.wait_send()
    r.plain_chips[place.chip] = r.plain[...] + r.plain_near[...]

    def chip_copy(distance, source):
        return send_tile(
            r.plain_chips.at[source], r.plain_chips.at[source], sum_sems, distance, distance, place.mate(distance)
        )

    for distance in range(1, place.chips):
        chip_copy(distance, place.chip).start()
    broad.end_c()
    broad.start_d()
    for distance in range(1, place.chips):
        chip_copy(distance, place.other(place.chips - distance)).wait_recv()
    for distance in range(1, place.chips):
        chip_copy(distance, place.chip).wait_send()
    r.plain_blocks[place.block] = jnp.sum(r.plain_chips[...], axis=0)

    def block_copy(distance, source):
        slot = place.chips + distance
        return send_tile(
            r.plain_blocks.at[source], r.plain_blocks.at[source], sum_sems, slot, slot, {"seq": place.peer(distance)}
        )

    for distance in range(1, place.blocks):
        block_copy(distance, place.block).start()
    narrow.end_b()
    narrow.start_c()
    for copy in copies:
        copy.wait()
    weights = [getattr(r, "held_weight_" + name) for name in states]
    firsts = [getattr(r, "held_first_" + name) for name in states]
    seconds = [getattr(r, "held_second_" + name) for name in states]
    rows = r.own_a.shape[1]
    last = 2 + 4 * layers
    r.squares[index] = jnp.zeros(r.squares.shape[1:], f32)
    r.squares_two[index] = jnp.zeros(r.squares.shape[1:], f32)

    def put(ref, slot, at, value):
        ref[slot, at : at + 1, :] = jnp.full((1, 128), value)

    mine = index
    put(r.squares, mine, 0, jnp.sum(weights[0][...] * weights[0][...]))
    for array in range(1, 5):
        for layer in range(layers):
            put(r.squares, mine, 1 + (array - 1) * layers + layer, jnp.sum(weights[array][layer] * weights[array][layer]))
    put(r.squares, mine, 1 + 4 * layers, jnp.sum(weights[5][...] * weights[5][...]))
    r.squares[mine, last : last + nvec, :] = jnp.broadcast_to(
        jnp.sum(weights[6][...] * weights[6][...], axis=1, keepdims=True), (nvec, 128)
    )
    totals = [r.total_a, r.total_b, r.total_a_one, r.total_b_one, r.total_head]
    square = jnp.zeros((rows, 128), f32)
    for ref in totals:
        if ref is not r.total_b:
            value = ref[...].astype(f32) if ref is not r.total_a else None
            if value is not None:
                square = square + jnp.sum(value * value, axis=0)
    narrow.end_c()
    narrow.start_d()
    broad.end_d()
    value = r.total_a[...].astype(f32)
    square = square + jnp.sum(value * value, axis=0)
    for distance in range(1, place.blocks):
        block_copy(distance, place.peer(place.blocks - distance)).wait_recv()
    for distance in range(1, place.blocks):
        block_copy(distance, place.block).wait_send()
    summed = jnp.sum(r.plain_blocks[...], axis=0)
    r.sums[0:24, :] = summed
    narrow.end_d()
    value = r.total_b[...].astype(f32)
    square = square + jnp.sum(value * value, axis=0)
    put(r.squares, mine, 31, jnp.sum(square))

    def exchange(ref, first):
        def copy(distance, source):
            return send_tile(
                ref.at[source], ref.at[source], (r.all_out, r.all_in), first + distance, first + distance, {"stream": (index + distance) % stream_devices}
            )

        for distance in range(1, stream_devices):
            copy(distance, mine).start()
        for distance in range(1, stream_devices):
            copy(distance, (index + stream_devices - distance) % stream_devices).wait_recv()
        for distance in range(1, stream_devices):
            copy(distance, mine).wait_send()
        return jnp.sum(ref[...], axis=0)

    gathered = exchange(r.squares, 0)
    grad_slopes = summed[0:16, :]
    clip = jnp.sqrt(gathered[31:32, :] + jnp.sum(grad_slopes * grad_slopes, axis=0, keepdims=True))
    factor = jnp.minimum(1.0, clip_limit / clip)
    r.sums[24:25, :] = clip
    r.sums[25:26, :] = factor
    totals_two = {}
    for array, layer, at, spot, (ref, block), matrix in state_blocks(layers, rows, totals):
        direction = adam_direction(
            take_block(weights[array], layer, at, spot),
            ref[block].astype(f32) * factor,
            take_block(firsts[array], layer, at, spot),
            take_block(seconds[array], layer, at, spot),
            decay_rate,
        )[2]
        old = totals_two.get(matrix)
        totals_two[matrix] = direction * direction if old is None else old + direction * direction
    for matrix, value in totals_two.items():
        put(r.squares_two, mine, matrix, jnp.sum(value))
    small = r.total_b[12].astype(f32).T
    scale = factor[:, 0:1]
    direction = adam_direction(weights[0][...], small[:features] * scale, firsts[0][...], seconds[0][...], decay_rate)[2]
    put(r.squares_two, mine, 0, jnp.sum(direction * direction))
    direction = adam_direction(
        weights[6][...], small[features : features + nvec] * scale, firsts[6][...], seconds[6][...], decay_rate
    )[2]
    r.squares_two[mine, last : last + nvec, :] = jnp.broadcast_to(
        jnp.sum(direction * direction, axis=1, keepdims=True), (nvec, 128)
    )
    gathered_two = exchange(r.squares_two, stream_devices)
    r.norms[0:32, :] = jnp.sqrt(gathered)
    r.norms[32:64, :] = jnp.sqrt(gathered_two)


def update_kernel(sizes, layers, r):
    (stream_devices, block_devices, streams, span, heads, features, nvec) = sizes
    states = ("input", "project", "output", "up", "down", "head", "vectors")
    weights = [getattr(r, "weight_" + name) for name in states]
    firsts = [getattr(r, "first_" + name) for name in states]
    seconds = [getattr(r, "second_" + name) for name in states]
    fresh = [getattr(r, "fresh_" + name) for name in states]
    new_firsts = [getattr(r, "new_first_" + name) for name in states]
    new_seconds = [getattr(r, "new_second_" + name) for name in states]
    rows = r.total_a.shape[1]
    last = 2 + 4 * layers
    factor = r.sums[25:26, :]
    ratio = r.norms[0:32, :] / r.norms[32:64, :]
    totals = [r.total_a, r.total_b, r.total_a_one, r.total_b_one, r.total_head]
    for array, layer, at, spot, (ref, block), matrix in state_blocks(layers, rows, totals):
        weight = take_block(weights[array], layer, at, spot)
        first, second, direction = adam_direction(
            weight,
            ref[block].astype(f32) * factor,
            take_block(firsts[array], layer, at, spot),
            take_block(seconds[array], layer, at, spot),
            decay_rate,
        )
        cols = slice(spot * 128, (spot + 1) * 128)
        where = (at, cols) if layer is None else (layer, at, cols)
        new_firsts[array][where] = first
        new_seconds[array][where] = second
        fresh[array][where] = weight - lamb_rate * ratio[matrix : matrix + 1, :] * direction
    small = r.total_b[12].astype(f32).T
    scale = factor[:, 0:1]
    for array, grad, share in (
        (0, small[:features], ratio[0:1, 0:1]),
        (6, small[features : features + nvec], ratio[last : last + nvec, 0:1]),
    ):
        weight = weights[array][...]
        first, second, direction = adam_direction(
            weight, grad * scale, firsts[array][...], seconds[array][...], decay_rate
        )
        new_firsts[array][...] = first
        new_seconds[array][...] = second
        fresh[array][...] = weight - lamb_rate * share * direction
    spread = jnp.where(
        lax.broadcasted_iota(jnp.int32, (heads, 128), 0) == lax.broadcasted_iota(jnp.int32, (heads, 128), 1), 1.0, 0.0
    )
    turned = [
        jnp.sum(r.sums[layer * heads : (layer + 1) * heads, :] * spread, axis=0, keepdims=True)[:, :heads]
        for layer in range(layers)
    ]
    slopes = r.slopes[...]
    first, second, direction = adam_direction(
        slopes, jnp.concatenate(turned, axis=0) * scale, r.first_slopes[...], r.second_slopes[...], 0.0
    )
    r.new_first_slopes[...] = first
    r.new_second_slopes[...] = second
    r.fresh_slopes[...] = slopes - slope_rate * direction
    lane = lax.broadcasted_iota(jnp.int32, (last + nvec, 128), 1)
    r.norm_table[0 : last + nvec, :] = jnp.where(
        lane == 0, r.norms[0 : last + nvec, :], r.norms[32 : 32 + last + nvec, :]
    )
    lane = lax.broadcasted_iota(jnp.int32, (1, 128), 1)
    r.norm_table[last + nvec : last + nvec + 1, :] = jnp.where(
        lane == 0, jnp.sqrt(jnp.sum(slopes * slopes)), jnp.sqrt(jnp.sum(direction * direction))
    )


def whole(space=pltpu.VMEM):
    return pl.BlockSpec(memory_space=space)


def call(kernel, name, args, outs, scratch=(), smem=1, flops=0, sems=(), collective=None):
    specs = [whole(pltpu.SMEM)] * smem + [whole()] * (len(args) - smem)
    return pl.pallas_call(
        kernel,
        name=name,
        out_shape=[jax.ShapeDtypeStruct(*out) for out in outs],
        in_specs=specs,
        out_specs=[whole()] * len(outs),
        scratch_shapes=[pltpu.VMEM(*item) for item in scratch] + list(sems),
        compiler_params=pltpu.CompilerParams(
            vmem_limit_bytes=VMEM_LIMIT, collective_id=collective, has_side_effects=collective is not None
        ),
        cost_estimate=pl.CostEstimate(flops=flops, bytes_accessed=20000000, transcendentals=0),
    )(*args)


def call_named(
    kernel, name, ins, outs, scratch=None, sems=None, any_ins=(), lazy=(), flush=(), smem=(), flops=0, collective=None
):
    scratch, sems = dict(scratch or {}), dict(sems or {})
    dma = pltpu.SemaphoreType.DMA
    for key in lazy:
        scratch[key] = (ins[key].shape, ins[key].dtype)
    for key in flush:
        scratch[key] = outs[key]
    if lazy:
        sems["load_sem"] = dma((len(lazy),))
    if flush:
        sems["store_sem"] = dma((len(flush),))
    moved = tuple(lazy) + tuple(flush)
    names = ["far_" + key if key in moved else key for key in list(ins) + list(outs)] + list(scratch) + list(sems)

    def space(key):
        return pltpu.SMEM if key in smem else pl.ANY if key in any_ins or key in moved else pltpu.VMEM

    made = pl.pallas_call(
        lambda *refs: kernel(Refs(names, refs, lazy, flush)),
        name=name,
        out_shape=[jax.ShapeDtypeStruct(*out) for out in outs.values()],
        in_specs=[whole(space(key)) for key in ins],
        out_specs=[whole(space(key)) for key in outs],
        scratch_shapes=[pltpu.VMEM(*item) for item in scratch.values()] + list(sems.values()),
        compiler_params=pltpu.CompilerParams(
            vmem_limit_bytes=VMEM_LIMIT, collective_id=collective, has_side_effects=collective is not None
        ),
        cost_estimate=pl.CostEstimate(flops=flops, bytes_accessed=20000000, transcendentals=0),
    )(*ins.values())
    return dict(zip(outs, made))


def split_three(value):
    one = value.astype(bf16)
    rest = value - one.astype(f32)
    two = rest.astype(bf16)
    rest = rest - two.astype(f32)
    return (one, two, rest.astype(bf16))


def adam_direction(weight, grad, first, second, decay):
    new_first = beta_one * first + (1.0 - beta_one) * grad
    new_second = beta_two * second + (1.0 - beta_two) * grad * grad
    first_hat = new_first / (1.0 - beta_one**STEP)
    second_hat = new_second / (1.0 - beta_two**STEP)
    return (new_first, new_second, first_hat / (jnp.sqrt(second_hat) + adam_eps) + decay * weight)


def shards(
    frames,
    targets,
    frame_count,
    memory,
    memory_len,
    input_weight,
    project_weight,
    output_weight,
    up_weight,
    down_weight,
    head_weight,
    vectors,
    slopes,
    first_input,
    first_project,
    first_output,
    first_up,
    first_down,
    first_head,
    first_vectors,
    first_slopes,
    second_input,
    second_project,
    second_output,
    second_up,
    second_down,
    second_head,
    second_vectors,
    second_slopes,
):
    streams, span, features = frames.shape
    layers, heads = slopes.shape
    nvec = vectors.shape[0]
    width = project_weight.shape[2] // 3
    hidden = up_weight.shape[2]
    codes = head_weight.shape[1]
    count = streams * span
    seq_index = lax.axis_index("seq")
    first = seq_index == 0
    first_flag = jnp.where(first, 1, 0).astype(jnp.int32).reshape(1)
    streams_all = streams * lax.axis_size("stream")

    small_own = jnp.concatenate(
        [input_weight.T, vectors.T, jnp.zeros((input_weight.shape[1], 128 - features - nvec), f32)], axis=1
    ).astype(bf16)
    frames_flat = frames.reshape((count, features))
    frames_flat = jnp.concatenate(
        [frames_flat, jnp.ones((count, 1), bf16), jnp.zeros((count, 127 - features), bf16)], axis=1
    )
    memory_flat = memory.reshape((layers, count, width))

    key_pos = jnp.arange(2 * span)
    hidden_key = jnp.logical_and(first, key_pos[None] < span - memory_len[:, None])
    coarse = (key_pos // 256 * 256).astype(bf16)
    fine = (key_pos % 256).astype(bf16)
    one = jnp.ones_like(coarse)
    shape = (streams, 2 * span)
    columns = [jnp.broadcast_to(item, shape) for item in (coarse, coarse, coarse, fine, fine, fine)]
    columns += [hidden_key.astype(bf16), jnp.broadcast_to(one, shape)]
    key_marks = jnp.pad(jnp.stack(columns, axis=-1), ((0, 0), (0, 0), (0, 56)))
    blank = jnp.zeros_like(key_marks)
    key_marks = jnp.stack(
        [jnp.concatenate([blank, key_marks], axis=-1), jnp.concatenate([key_marks, blank], axis=-1)], axis=1
    )
    parts = split_three(slopes)
    marks = jnp.stack(parts + parts + (jnp.full_like(parts[0], masked_score), jnp.zeros_like(parts[0])), axis=-1)
    marks = jnp.pad(marks, ((0, 0), (0, 0), (0, 56))).astype(f32)
    even = (jnp.arange(heads) % 2 == 0)[None, :, None]
    query_marks = jnp.concatenate([jnp.where(even, 0.0, marks), jnp.where(even, marks, 0.0)], axis=-1)

    full = ((count, width), f32)
    low = ((count, width), bf16)
    joined = ((2 * count, width), bf16)
    wide = ((count, hidden), bf16)
    lse = ((streams * heads, span), f32)
    saved_outs = [low, low, joined, joined, low, lse, full, low, wide, wide, full]
    cost = 2 * count * (5 * width * width + width * width + 2 * width * hidden) + 4 * count * 2 * span * width

    devices = lax.axis_size("stream")
    chips = devices // 2
    sizes = (devices, lax.axis_size("seq"), streams, span, heads, features, nvec)

    def gathered(rows_all, cols):
        return ((chips, 2, rows_all // devices, cols), bf16)

    project_shape = gathered(width, 3 * width)
    output_shape = gathered(width, width)
    up_shape = gathered(width, hidden)
    down_shape = gathered(hidden, width)
    dma = pltpu.SemaphoreType.DMA
    made = call(
        functools.partial(forward_kernel, 0, sizes),
        "forward_zero",
        (first_flag, small_own, frames_flat, memory_flat[0], key_marks, query_marks[0], project_weight, output_weight, up_weight, down_weight),
        [((16, width), f32), full, low, full, low]
        + saved_outs
        + [low, low, ((count, 128), bf16), gathered(width, 128), project_shape, output_shape, up_shape, down_shape, project_shape, output_shape],
        sems=(dma((7, chips)), dma((7, chips)), dma((2, 1)), dma((streams,)), dma((streams,))),
        flops=cost,
        collective=0,
    )
    rows, r_zero, low_zero, pr_zero, a_zero = made[:5]
    saved_zero = made[5:15]
    r_one, a_one, a_behind, frames_behind = made[15:19]
    weights_zero = made[20:24]
    project_one, output_one = made[24:]
    made = call(
        functools.partial(forward_kernel, 1, sizes),
        "forward_one",
        (first_flag, rows, r_one, a_one, a_behind, memory_flat[1], key_marks, query_marks[1], project_one, output_one, up_weight, down_weight, head_weight),
        [low] + saved_outs + [up_shape, down_shape, gathered(width, codes)],
        sems=(dma((3, chips)), dma((3, chips))),
        flops=cost,
        collective=1,
    )
    low_one = made[0]
    saved_one = made[1:11]
    r_two = made[11]
    up_one, down_one, head_low = made[12:]
    weights_low = (weights_zero, (project_one, output_one, up_one, down_one))

    position = seq_index * span + jnp.arange(span)
    share = jnp.where(
        position[None] < frame_count[:, None],
        1.0 / (frame_count[:, None].astype(f32) * streams_all),
        0.0,
    )
    blocks = lax.axis_size("seq")
    rows_each = width // devices

    def grads_of(number):
        number = -(-number // blocks) * blocks
        return {
            "grad": ((chips, 2, number, rows_each, 128), bf16),
            "pair": ((chips, number, rows_each, 128), bf16),
            "mates": ((chips, number, rows_each, 128), bf16),
            "own": ((number, rows_each, 128), bf16),
            "line": ((blocks, number // blocks, rows_each, 128), bf16),
            "total": ((number, rows_each, 128), bf16),
        }

    group_a, group_b, group_last, group_head = grads_of(36), grads_of(12), grads_of(13), grads_of(8)
    grad_head, dr_two, last_rows, loss_tile = call(
        head_kernel,
        "head_loss",
        (rows, r_two, head_low, targets.reshape((count, 1)), share.reshape((count, 1))),
        [group_head["grad"], full, ((8, width), f32), ((8, 128), f32)],
        [((width, codes), f32)],
        smem=0,
        flops=6 * count * width * codes,
    )
    slots = max(chips, blocks)
    saved_names = ("ap", "q", "k", "v", "o", "lse", "r1", "a2", "u", "gp")
    weight_names = ("wp", "wo", "wu", "wd")
    work = {
        "do": low,
        "dq": low,
        "dk": joined,
        "dv": joined,
        "dk_acc": ((2 * span, 128), f32),
        "dv_acc": ((2 * span, 128), f32),
        "turned": ((width, count), bf16),
        "pair_a": group_a["pair"],
        "mates_a": group_a["mates"],
        "grad_a": group_a["grad"],
        "u_two": ((2, count, 512), bf16),
        "gp_two": ((2, count, 512), bf16),
    }
    lazy = ("wd", "a2", "wu", "r1", "wo", "o", "q", "k", "v", "kf", "wp", "a", "ap")
    work_sems = dict(
        out_sem=dma((12, slots)), in_sem=dma((12, slots)), u_sem=dma((2, 2)), first_sem=dma((5,))
    )
    one = call_named(
        functools.partial(backward_kernel, 1, sizes),
        "backward_one",
        dict(
            first=first_flag,
            rows=rows,
            a=a_one,
            **dict(zip(saved_names, saved_one)),
            kf=key_marks,
            qf=query_marks[1],
            **dict(zip(weight_names, weights_low[1])),
            dr_in=dr_two,
            mem=memory_flat[1],
            grad_head=grad_head,
        ),
        dict(
            gr=((8, width), f32),
            gs=((8, 128), f32),
            dr=full,
            da=full,
            back=low,
            own_a=group_a["own"],
            pair_b=group_b["pair"],
            total_head=group_head["total"],
        ),
        dict(
            work,
            dap=low,
            grad_b=group_b["grad"],
            **{key + "_head": group_head[key] for key in ("pair", "mates", "own", "line")},
        ),
        dict(work_sems, back_out=dma((streams,)), back_in=dma((streams,))),
        any_ins=("u", "gp", "dr_in"),
        lazy=lazy,
        smem=("first",),
        flops=2 * cost,
        collective=2,
    )
    zero = call_named(
        functools.partial(backward_kernel, 0, sizes),
        "backward_zero",
        dict(
            first=first_flag,
            rows=rows,
            a=a_zero,
            **dict(zip(saved_names, saved_zero)),
            kf=key_marks,
            qf=query_marks[0],
            **dict(zip(weight_names, weights_low[0])),
            frames=frames_flat,
            halo=frames_behind,
            r=r_zero,
            pr=pr_zero,
            dr1_in=one["dr"],
            da_in=one["da"],
            back=one["back"],
            r_next=r_one,
            gr_last=last_rows,
            gr_one=one["gr"],
            own_a_one=one["own_a"],
            pair_b_one=one["pair_b"],
        ),
        dict(
            gs=((8, 128), f32),
            own_a=group_a["own"],
            grad_b=group_last["grad"],
            total_a_one=group_a["total"],
            total_b_one=group_b["total"],
        ),
        dict(
            work,
            gr=((8, width), f32),
            dr=full,
            da=full,
            small_acc=((width, 128), f32),
            wide_one=full,
            wide_two=full,
            line_a_one=group_a["line"],
            **{key + "_b_one": group_b[key] for key in ("mates", "own", "line")},
        ),
        work_sems,
        any_ins=("u", "gp", "dr1_in", "da_in", "r_next", "r", "pr"),
        lazy=lazy,
        smem=("first",),
        flops=2 * cost,
        collective=3,
    )
    state_names = ("input", "project", "output", "up", "down", "head", "vectors")
    state = {}
    for kind, arrays in (
        (
            "weight",
            (input_weight, project_weight, output_weight, up_weight, down_weight, head_weight, vectors),
        ),
        ("first", (first_input, first_project, first_output, first_up, first_down, first_head, first_vectors)),
        (
            "second",
            (second_input, second_project, second_output, second_up, second_down, second_head, second_vectors),
        ),
    ):
        state.update({kind + "_" + name: array for name, array in zip(state_names, arrays)})
    sums_shape = ((32, 128), f32)
    tail = call_named(
        functools.partial(tail_kernel, sizes, layers),
        "tail",
        dict(
            state,
            own_a=zero["own_a"],
            grad_b=zero["grad_b"],
            total_a_one=zero["total_a_one"],
            total_b_one=zero["total_b_one"],
            total_head=one["total_head"],
            gs_zero=zero["gs"],
            gs_one=one["gs"],
            loss=loss_tile,
        ),
        dict(total_a=group_a["total"], total_b=group_last["total"], sums=sums_shape, norms=((64, 128), f32)),
        dict(
            {"held_" + key: (array.shape, f32) for key, array in state.items()},
            line_a=group_a["line"],
            **{key + "_b": group_last[key] for key in ("pair", "mates", "own", "line")},
            plain=((24, 128), f32),
            plain_near=((24, 128), f32),
            plain_chips=((chips, 24, 128), f32),
            plain_blocks=((blocks, 24, 128), f32),
            squares=((devices, 32, 128), f32),
            squares_two=((devices, 32, 128), f32),
        ),
        dict(
            out_sem=dma((8, slots)),
            in_sem=dma((8, slots)),
            load_sem=dma((len(state),)),
            sum_out=dma((chips + blocks,)),
            sum_in=dma((chips + blocks,)),
            all_out=dma((2 * devices,)),
            all_in=dma((2 * devices,)),
        ),
        any_ins=tuple(state),
        collective=4,
    )
    outs = {}
    for kind in ("fresh", "new_first", "new_second"):
        for name in state_names:
            outs[kind + "_" + name] = (state["weight_" + name].shape, f32)
        outs[kind + "_slopes"] = (slopes.shape, f32)
    table_rows = 2 + 4 * layers + nvec + 1
    fresh = call_named(
        functools.partial(update_kernel, sizes, layers),
        "update",
        dict(
            state,
            slopes=slopes,
            first_slopes=first_slopes,
            second_slopes=second_slopes,
            total_a=tail["total_a"],
            total_b=tail["total_b"],
            total_a_one=zero["total_a_one"],
            total_b_one=zero["total_b_one"],
            total_head=one["total_head"],
            sums=tail["sums"],
            norms=tail["norms"],
        ),
        dict(outs, norm_table=((table_rows, 128), f32)),
    )
    layer_inputs = jnp.stack([low_zero, low_one]).reshape((layers, streams, span, width))
    return (
        tail["sums"][16, 0],
        layer_inputs,
        tail["sums"][24, 0],
        fresh["norm_table"][:, :2],
        *[fresh[key] for key in outs],
    )


def solution(mesh):
    rows3 = P(None, "stream", None)
    state = (P(None, "stream"), rows3, rows3, rows3, rows3, P("stream", None), P(None, "stream"), P())
    in_specs = (
        P("stream", "seq", None),
        P("stream", "seq"),
        P("stream"),
        P(None, "stream", None, None),
        P("stream"),
    ) + state * 3
    out_specs = (P(), P(None, "stream", "seq", None), P(), P()) + state * 3
    return jax.shard_map(shards, mesh=mesh, in_specs=in_specs, out_specs=out_specs, check_vma=False)
```

```python
import functools

import jax
import jax.numpy as jnp
from jax import lax
from jax.experimental import pallas as pl
from jax.experimental.pallas import tpu as pltpu
from jax.sharding import PartitionSpec as P

STEP = 10


ln_eps = 1e-05
clip_limit = 0.002
beta_one = 0.9
beta_two = 0.999
lamb_rate = 0.3
slope_rate = 0.001
decay_rate = 0.01
adam_eps = 1e-11
masked_score = -1e30

STREAM, SEQ, FAR = "stream", "seq", "far_"
KINDS = ("weight", "first", "second")
NN = (((1,), (0,)), ((), ()))
NT = (((1,), (1,)), ((), ()))
TN = (((0,), (0,)), ((), ()))
VMEM_LIMIT = 63 * 1024 * 1024
f32 = jnp.float32
bf16 = jnp.bfloat16


def mm(left, right, dims=NN):
    return lax.dot_general(left, right, dims, preferred_element_type=f32)


MESH = pl.DeviceIdType.MESH


class Place:
    def __init__(self, streams, blocks):
        self.chips = streams // 2
        self.blocks = blocks
        index = lax.axis_index(STREAM)
        self.chip = index // 2
        self.core = index % 2
        self.block = lax.axis_index(SEQ)
        self.sibling = {STREAM: 2 * self.chip + 1 - self.core}

    def other(self, distance):
        return (self.chip + distance) % self.chips

    def mate(self, distance):
        return {STREAM: 2 * self.other(distance) + self.core}

    def peer(self, distance):
        return (self.block + distance) % self.blocks

    def greet(self, line=False, column=False):
        barrier = pltpu.get_barrier_semaphore()

        def hello(device):
            pl.semaphore_signal(barrier, inc=1, device_id=device, device_id_type=MESH)

        hello(self.sibling)
        for distance in range(1, self.chips):
            hello(self.mate(distance))
        if line:

            @pl.when(self.block > 0)
            def _():
                hello({SEQ: self.block - 1})

            pl.semaphore_wait(barrier, self.chips + jnp.where(self.block < self.blocks - 1, 1, 0))
        elif column:
            for distance in range(1, self.blocks):
                hello({SEQ: self.peer(distance)})
            pl.semaphore_wait(barrier, self.chips + self.blocks - 1)
        else:
            pl.semaphore_wait(barrier, self.chips)


class Gather:
    def __init__(self, place, refs, sems, first):
        self.place, self.refs, self.sems, self.first = place, refs, sems, first

    def far(self, index, distance):
        place, ref = self.place, self.refs[index]
        out_sem, in_sem = self.sems[0], self.sems[1]
        return pltpu.make_async_remote_copy(
            src_ref=ref.at[place.chip, place.core],
            dst_ref=ref.at[place.chip, place.core],
            send_sem=out_sem.at[self.first + index, distance],
            recv_sem=in_sem.at[self.first + index, distance],
            device_id=place.mate(distance),
            device_id_type=MESH,
        )

    def near(self, index, core):
        place, ref = self.place, self.refs[index]
        out_sem, in_sem = self.sems[0], self.sems[1]
        return pltpu.make_async_remote_copy(
            src_ref=ref.at[:, core],
            dst_ref=ref.at[:, core],
            send_sem=out_sem.at[self.first + index, 0],
            recv_sem=in_sem.at[self.first + index, 0],
            device_id=place.sibling,
            device_id_type=MESH,
        )

    def push(self):
        for index in range(len(self.refs)):
            for distance in range(1, self.place.chips):
                self.far(index, distance).start()

    def relay(self):
        place = self.place
        for index in range(len(self.refs)):
            ref = self.refs[index]
            for distance in range(1, place.chips):
                source = place.other(place.chips - distance)
                pltpu.make_async_remote_copy(
                    src_ref=ref.at[source, place.core],
                    dst_ref=ref.at[source, place.core],
                    send_sem=self.sems[0].at[self.first + index, distance],
                    recv_sem=self.sems[1].at[self.first + index, distance],
                    device_id=place.mate(distance),
                    device_id_type=MESH,
                ).wait_recv()
            self.near(index, place.core).start()

    def finish(self):
        place = self.place
        for index in range(len(self.refs)):
            self.near(index, 1 - place.core).wait_recv()
            self.near(index, place.core).wait_send()
            for distance in range(1, place.chips):
                self.far(index, distance).wait_send()


class Reduce:
    def __init__(self, place, sems, row, grad=None, pair=None, mates=None, own=None, line=None, total=None, part=None):
        self.part = part
        self.place, self.sems, self.row = place, sems, row
        self.grad, self.pair, self.mates = grad, pair, mates
        self.own, self.line, self.total = own, line, total

    def copy(self, phase, slot, src, dst, device):
        return pltpu.make_async_remote_copy(
            src_ref=src,
            dst_ref=dst,
            send_sem=self.sems[0].at[self.row + phase, slot],
            recv_sem=self.sems[1].at[self.row + phase, slot],
            device_id=device,
            device_id_type=MESH,
        )

    def copy_a(self):
        place = self.place
        return self.copy(0, 0, self.grad.at[:, 1 - place.core], self.pair, place.sibling)

    def copy_b(self, distance, source=None):
        place = self.place
        slot = place.chip if source is None else source
        return self.copy(
            1, distance, self.pair.at[place.other(distance)], self.mates.at[slot], place.mate(distance)
        )

    def piece(self, block):
        size = (self.total if self.own is None else self.own).shape[0] // self.place.blocks
        return pl.ds(block * size, size)

    def copy_c(self, distance, source=None):
        place = self.place
        slot = place.block if source is None else source
        there = place.peer(distance)
        return self.copy(2, distance, self.own.at[self.piece(there)], self.line.at[slot], {SEQ: there})

    def copy_d(self, distance, source=None):
        place = self.place
        slot = self.piece(place.block if source is None else source)
        return self.copy(3, distance, self.total.at[slot], self.total.at[slot], {SEQ: place.peer(distance)})

    def start_a(self):
        self.copy_a().start()

    def end_a(self):
        place = self.place
        self.copy_a().wait_recv()

        def add(chip, carry):
            self.pair[chip] = (self.pair[chip].astype(f32) + self.grad[chip, place.core].astype(f32)).astype(bf16)
            return carry

        lax.fori_loop(0, place.chips, add, 0)
        self.copy_a().wait_send()

    def start_b(self):
        for distance in range(1, self.place.chips):
            self.copy_b(distance).start()

    def end_b(self):
        place = self.place
        total = self.pair[place.chip].astype(f32)
        for distance in range(1, place.chips):
            source = place.other(place.chips - distance)
            self.copy_b(distance, source).wait_recv()
            total = total + self.mates[source].astype(f32)
        self.own[...] = total.astype(bf16)
        for distance in range(1, place.chips):
            self.copy_b(distance).wait_send()

    def start_c(self):
        for distance in range(1, self.place.blocks):
            self.copy_c(distance).start()

    def end_c(self):
        place = self.place
        mine = self.piece(place.block)
        total = self.own[mine].astype(f32)
        for distance in range(1, place.blocks):
            source = place.peer(place.blocks - distance)
            self.copy_c(distance, source).wait_recv()
            total = total + self.line[source].astype(f32)
        if self.part is None:
            self.total[mine] = total.astype(bf16)
        else:
            self.part[...] = total.astype(bf16)
        for distance in range(1, place.blocks):
            self.copy_c(distance).wait_send()

    def start_d(self):
        for distance in range(1, self.place.blocks):
            self.copy_d(distance).start()

    def end_d(self):
        place = self.place
        for distance in range(1, place.blocks):
            self.copy_d(distance, place.peer(place.blocks - distance)).wait_recv()
        for distance in range(1, place.blocks):
            self.copy_d(distance).wait_send()


def put_blocks(grad, layout, array, first, value):
    chips, cores, unused_blocks, rows, lanes = grad.shape
    for spot in range(value.shape[1] // lanes):
        part = value[:, spot * lanes : (spot + 1) * lanes].astype(bf16)
        grad[:, :, layout.spot(array, first + spot)] = part.reshape((chips, cores, rows, lanes))


def put_down(grad, layout, array, value, part, parts):
    chips, cores, unused_blocks, rows, lanes = grad.shape
    few = chips // parts
    high = value.shape[0] // (few * cores * rows)
    wide = value.shape[1] // lanes
    value = value.astype(bf16).reshape((few, cores, high, rows, value.shape[1]))
    for up in range(high):
        for spot in range(wide):
            grad[pl.ds(part * few, few), :, layout.spot(array, up * wide + spot)] = value[
                :, :, up, :, spot * lanes : (spot + 1) * lanes
            ]


class Refs:
    def __init__(self, names, refs, lazy, flush, layer, layered):
        for name, ref in zip(names, refs, strict=True):
            setattr(self, name, ref)
        self.loads, self.stores = {}, {}
        for number, name in enumerate(lazy):
            far = getattr(self, FAR + name)
            if name in layered:
                far = far.at[layer]
            near = getattr(self, name)
            self.loads[id(near)] = pltpu.make_async_copy(far, near, self.load_sem.at[number])
        for number, name in enumerate(flush):
            near = getattr(self, name)
            self.stores[id(near)] = pltpu.make_async_copy(near, getattr(self, FAR + name), self.store_sem.at[number])

    def fetch(self):
        for load in self.loads.values():
            load.start()

    def ready(self, *refs):
        for ref in refs:
            self.loads[id(ref)].wait()

    def flush(self, *refs):
        for ref in refs:
            self.stores[id(ref)].start()

    def flushed(self):
        for store in self.stores.values():
            store.wait()


class Layout:
    def __init__(self, devices, counts):
        self.parts, self.size = [], 0
        for count in counts:
            per = -(-count // devices)
            self.parts.append((self.size, per, count))
            self.size += per
        self.total = self.size * devices

    def spot(self, array, block):
        base, per, unused_count = self.parts[array]
        return block // per * self.size + base + block % per

    def unused(self):
        taken = {self.spot(array, block) for array, part in enumerate(self.parts) for block in range(part[2])}
        return [block for block in range(self.total) if block not in taken]


def layouts(blocks):
    return tuple(Layout(blocks, counts) for counts in ((16, 16, 4), (12,), (12, 1), (8,)))


class Ahead:
    def __init__(self, place, step, src, dst, sems):
        self.place, self.step, self.src, self.dst, self.sems = place, step, src, dst, sems
        self.sends = place.block < place.blocks - 1 if step > 0 else place.block > 0
        self.receives = place.block > 0 if step > 0 else place.block < place.blocks - 1

    def copy(self, slot, rows):
        return pltpu.make_async_remote_copy(
            src_ref=self.src.at[rows],
            dst_ref=self.dst.at[rows],
            send_sem=self.sems[0].at[slot],
            recv_sem=self.sems[1].at[slot],
            device_id={SEQ: self.place.block + self.step},
            device_id_type=MESH,
        )

    def start(self, slot, rows):
        @pl.when(self.sends)
        def _():
            self.copy(slot, rows).start()

    def arrived(self, slot, rows):
        @pl.when(self.receives)
        def _():
            self.copy(slot, rows).wait_recv()

    def sent(self, slot, rows):
        @pl.when(self.sends)
        def _():
            self.copy(slot, rows).wait_send()


def flat(ref, cols=slice(None)):
    value = ref[:, :, :, cols]
    return value.reshape((-1, value.shape[-1]))


def flat_rows(ref, part, parts):
    chips = ref.shape[0] // parts
    value = ref[pl.ds(part * chips, chips)]
    return value.reshape((-1, value.shape[-1]))


def normalize(values):
    centred = values - jnp.mean(values, axis=-1, keepdims=True)
    scale = lax.rsqrt(jnp.mean(centred * centred, axis=-1, keepdims=True) + ln_eps)
    return (centred * scale, scale)


def norm_back(grad_out, standard, scale, gain):
    scaled = grad_out * gain
    return scale * (
        scaled
        - jnp.mean(scaled, axis=-1, keepdims=True)
        - standard * jnp.mean(scaled * standard, axis=-1, keepdims=True)
    )


def gelu_pair(x):
    cumulative = 0.5 * (1.0 + lax.erf(x * 0.7071067811865476))
    bell = jnp.exp(-0.5 * x * x)
    return (x * cumulative, cumulative + x * (bell * 0.3989422804014327))


def tile(index, size):
    return pl.ds(pl.multiple_of(index * size, size), size)


def half_masks():
    lane = lax.broadcasted_iota(jnp.int32, (1, 128), 1)
    left = jnp.where(lane < 64, 1.0, 0.0).astype(bf16)
    right = jnp.where(lane < 64, 0.0, 1.0).astype(bf16)
    return (left, right)


def build_marks(kf_ref, lens_ref, first):
    streams, unused_halves, keys, lanes = kf_ref.shape
    key = lax.broadcasted_iota(jnp.int32, (keys, lanes), 0)
    lane = lax.broadcasted_iota(jnp.int32, (keys, lanes), 1)
    coarse = (key // 256 * 256).astype(f32)
    fine = (key % 256).astype(f32)
    for stream in range(streams):
        veiled = jnp.where(jnp.logical_and(first, key < keys // 2 - lens_ref[stream]), 1.0, 0.0)
        for half in range(2):
            spot = lane - 64 * (1 - half)
            value = jnp.where(spot == 6, veiled, jnp.where(spot == 7, 1.0, 0.0))
            value = jnp.where(jnp.logical_and(spot >= 3, spot < 6), fine, value)
            value = jnp.where(jnp.logical_and(spot >= 0, spot < 3), coarse, value)
            kf_ref[stream, half] = value.astype(bf16)


def query_marks(slope, half):
    spot = lax.broadcasted_iota(jnp.int32, (1, 128), 1) - 64 * (1 - half)
    whole_slope = jnp.full((1, 128), slope)
    one = whole_slope.astype(bf16).astype(f32)
    two = (whole_slope - one).astype(bf16).astype(f32)
    three = whole_slope - one - two
    value = jnp.where(spot == 6, masked_score, 0.0)
    for number, part in enumerate((one, two, three)):
        value = jnp.where(jnp.logical_or(spot == number, spot == number + 3), part, value)
    return value.astype(bf16)


def attend(span, heads, q_ref, k_ref, v_ref, kf_ref, slope_of, o_ref, lse_ref, score_refs, chance_refs, stream, early):
    pairs = heads // 2
    step = span // 2
    masks = half_masks()
    key_at = lax.broadcasted_iota(jnp.int32, (step, step), 0)
    query_at = lax.broadcasted_iota(jnp.int32, (step, step), 1)
    down = lax.broadcasted_iota(jnp.int32, (128, 1), 0)
    row_masks = (jnp.where(down < 64, 1.0, 0.0).astype(bf16), jnp.where(down < 64, 0.0, 1.0).astype(bf16))

    def group(first_pair, count):
        work = []
        for pair in [first_pair + i for i in range(count)]:
            cols = tile(pair, 128)
            k_pair = k_ref[tile(stream, 2 * span), cols]
            v_turned = v_ref[tile(stream, 2 * span), cols].T
            for part in range(2):
                for half in range(2):
                    work.append((pair, cols, k_pair, v_turned, part, half))
        peaks, mixed_rows = {}, {}

        def scores(item):
            pair, cols, k_pair, unused_v, part, half = work[item]
            seen = span + part * step
            q_pair = q_ref[pl.ds(pl.multiple_of(stream * span + part * step, step), step), cols]
            q_aug = q_pair * masks[half] + query_marks(slope_of(2 * pair + half), half)
            k_aug = k_pair[: seen + step] * masks[half] + kf_ref[stream, half, : seen + step]
            score = mm(k_aug, q_aug, NT)
            near = jnp.where(key_at <= query_at, score[seen:], masked_score)
            peaks[item] = jnp.maximum(
                jnp.max(score[:seen], axis=0, keepdims=True), jnp.max(near, axis=0, keepdims=True)
            )
            out = score_refs[item % 2]
            out[:seen, :] = score[:seen]
            out[seen : seen + step, :] = near

        def soften(item):
            seen = span + (work[item][4] + 1) * step
            chance_refs[item % 2][:seen, :] = jnp.exp(score_refs[item % 2][:seen, :] - peaks[item]).astype(bf16)

        def mix(item):
            pair, cols, unused_k, v_turned, part, half = work[item]
            seen = span + (part + 1) * step
            v_aug = v_turned[:, :seen] * row_masks[half] + row_masks[1 - half]
            mixed = mm(v_aug, chance_refs[item % 2][:seen, :])
            own = mixed[half * 64 : half * 64 + 64]
            total = mixed[64 - half * 64 : 128 - half * 64]
            mixed_rows[half] = own / total
            lse_ref[pl.ds(stream * heads + 2 * pair + half, 1), part * step : (part + 1) * step] = peaks[
                item
            ] + jnp.log(total[:1])
            if half == 1:
                rows = pl.ds(pl.multiple_of(stream * span + part * step, step), step)
                o_ref[rows, cols] = jnp.concatenate([mixed_rows[0], mixed_rows[1]], axis=0).T.astype(bf16)

        scores(0)
        for item in range(len(work)):
            if item + 1 < len(work):
                scores(item + 1)
            soften(item)
            if item > 0:
                mix(item - 1)
        mix(len(work) - 1)

    def inner(index, carry):
        group(2 * index, 2)
        early(index)
        return carry

    lax.fori_loop(0, pairs // 2, inner, 0)


def forward_kernel(sizes, r):
    (stream_devices, block_devices, streams, span, heads, features, nvec) = sizes
    place = Place(stream_devices, block_devices)
    chip, core = place.chip, place.core
    first = place.block == 0
    layers = r.mem.shape[0]
    width = r.a.shape[1]
    count = streams * span
    step = span // 2
    sems = (r.out_sem, r.in_sem)
    weight_names = ("wp", "wo", "wu", "wd")
    weights = [[getattr(r, f"{name}_{layer}") for name in weight_names] for layer in range(layers)]
    gather_small, gather_head = (Gather(place, [ref], sems, number) for number, ref in enumerate((r.small, r.wh)))
    gathers = [
        [Gather(place, [ref], sems, 2 + 4 * layer + number) for number, ref in enumerate(weights[layer])]
        for layer in range(layers)
    ]
    early_names, look_names, feed_names = ("ap", "q", "k", "v", "low"), ("o", "lse"), ("r1", "a2", "u", "gp")
    saved_names = early_names + look_names + feed_names + ("a", "res")

    def save(layer, name, stream, source=None):
        source = getattr(r, name) if source is None else source
        size = source.shape[0] // streams
        at = tile(stream, size)
        far = getattr(r, FAR + name)
        return pltpu.make_async_copy(
            source.at[at], far.at[layer, at], r.save_sem.at[layer, saved_names.index(name), stream]
        )

    def save_weight(layer, number):
        return pltpu.make_async_copy(
            weights[layer][number],
            getattr(r, f"{FAR}{weight_names[number]}_{layer}"),
            r.weight_sem.at[layer, number],
        )

    r.fetch()
    frames_ahead = Ahead(place, 1, r.frames_wide, r.halo, (r.frame_sem.at[0], r.frame_sem.at[1]))
    next_ahead = Ahead(place, 1, r.nxt, r.behind, (r.next_out, r.next_in))
    every = pl.ds(0, count)

    @pl.when(first)
    def _():
        r.halo[...] = jnp.zeros_like(r.halo)
        r.behind[...] = jnp.zeros_like(r.behind)

    r.small_rows[...] = jnp.zeros_like(r.small_rows)
    r.small_rows[0:nvec, :] = r.vectors[...]
    own_rows = jnp.concatenate([r.input_turned[...], r.small_rows[...].T], axis=1)
    r.small[chip, core] = own_rows.astype(bf16)
    r.frames_tall[...] = jnp.zeros_like(r.frames_tall)
    r.frames_tall[features : features + 16, :] = jnp.where(
        lax.broadcasted_iota(jnp.int32, (16, span), 0) == 0, 1.0, 0.0
    ).astype(bf16)
    for stream in range(streams):
        r.frames_tall[0:features, :] = r.frames[stream]
        r.frames_wide[stream * span : (stream + 1) * span, :] = r.frames_tall[...].T
    r.ready(r.pw)
    r.wp_0[chip, core] = r.pw[0].astype(bf16)
    place.greet(line=True)
    gather_small.push()
    gathers[0][0].push()
    frames_ahead.start(0, every)
    r.ready(r.ow, r.uw, r.dw, r.hw)
    r.wo_0[chip, core] = r.ow[0].astype(bf16)
    r.wu_0[chip, core] = r.uw[0].astype(bf16)
    r.wd_0[chip, core] = r.dw[0].astype(bf16)
    r.wp_1[chip, core] = r.pw[1].astype(bf16)
    r.wo_1[chip, core] = r.ow[1].astype(bf16)
    r.wu_1[chip, core] = r.uw[1].astype(bf16)
    r.wd_1[chip, core] = r.dw[1].astype(bf16)
    r.wh[chip, core] = r.hw[...].astype(bf16)
    build_marks(r.kf, r.memory_len, first)
    r.rows[...] = jnp.zeros_like(r.rows)
    r.ready(r.mem)
    gather_small.relay()
    gathers[0][0].relay()
    for gather in gathers[0][1:]:
        gather.push()
    gather_small.finish()
    r.rows[:nvec, :] = flat(r.small).astype(f32).T[features : features + nvec]
    gathers[0][0].finish()
    frames_ahead.arrived(0, every)
    residuals = (r.res, r.res_two)

    for layer in range(layers):
        residual, outcome = residuals[layer % 2], residuals[(layer + 1) % 2]
        row = 3 + 4 * layer
        g1, b1, g2, b2 = (r.rows[row + i : row + i + 1, :] for i in range(4))
        wp, wo, wu, wd = weights[layer]
        own_a = r.a if layer == 0 else r.nxt

        def wait_old(names, stream):
            if layer > 0:
                for name in names:
                    save(layer - 1, name, stream).wait()

        def project(stream):
            wait_old(early_names, stream)
            for part in range(2):
                at = pl.ds(pl.multiple_of(stream * span + part * step, step), step)
                behind = pl.ds(pl.multiple_of(stream * 2 * span + part * step, step), step)
                here = pl.ds(pl.multiple_of(stream * 2 * span + span + part * step, step), step)
                if layer == 0:
                    value = mm(r.frames_wide[at, :], flat(r.small), NT)
                    residual[at, :] = value
                    own_a[at, :] = (normalize(value)[0] * g1 + b1).astype(bf16)
                    before = mm(r.halo[at, :], flat(r.small), NT)
                    before = jnp.where(first, r.mem[layer, at, :].astype(f32), before)
                    r.pr[at, :] = before
                    ap = (normalize(before)[0] * g1 + b1).astype(bf16)
                else:
                    value = residual[at, :]
                    ap = (normalize(r.mem[layer, at, :].astype(f32))[0] * g1 + b1).astype(bf16)
                    ap = jnp.where(first, ap.astype(f32), r.behind[at, :].astype(f32)).astype(bf16)
                r.low[at, :] = value.astype(bf16)
                a = own_a[at, :]
                r.ap[at, :] = ap
                wq, wk, wv = (flat(wp, slice(i * width, (i + 1) * width)) for i in range(3))
                r.q[at, :] = (mm(a, wq) * 0.125).astype(bf16)
                r.k[here, :] = mm(a, wk).astype(bf16)
                r.v[here, :] = mm(a, wv).astype(bf16)
                r.k[behind, :] = mm(ap, wk).astype(bf16)
                r.v[behind, :] = mm(ap, wv).astype(bf16)
            for name in early_names:
                save(layer, name, stream).start()
            save(layer, saved_names[-1], stream, residual).start()
            save(layer, saved_names[-2], stream, own_a).start()
            if layer == 0:
                at = tile(stream, span)
                pltpu.make_async_copy(r.pr.at[at], r.far_pr.at[at], r.pr_sem.at[stream]).start()

        def look(stream):
            wait_old(look_names, stream)

            def early(pair):
                if layer == 0:

                    @pl.when(jnp.logical_and(stream == 1, pair == 0))
                    def _():
                        gathers[0][1].relay()
                        gathers[0][2].relay()

                else:

                    @pl.when(jnp.logical_and(stream == 1, pair == 0))
                    def _():
                        gathers[1][2].relay()

            attend(
                span,
                heads,
                r.q,
                r.k,
                r.v,
                r.kf,
                lambda head: r.slopes[layer, head],
                r.o,
                r.lse,
                (r.score_one, r.score_two),
                (r.chance_one, r.chance_two),
                stream,
                early,
            )
            for name in look_names:
                save(layer, name, stream).start()

        def feed(stream, carry):
            if layer > 0:
                save(layer - 1, saved_names[-1], stream, outcome).wait()
            wait_old(feed_names, stream)
            at = tile(stream, span)
            after = residual[at, :] + mm(r.o[at, :], flat(wo))
            r.r1[at, :] = after
            a2 = (normalize(after)[0] * g2 + b2).astype(bf16)
            r.a2[at, :] = a2
            for name in feed_names[:2]:
                save(layer, name, stream).start()
            total = after
            parts = wu.shape[3] // 512
            later = mm(a2, flat(wu, slice(0, 512)))
            for part in range(parts):
                cols = slice(part * 512, (part + 1) * 512)
                value = later
                if part + 1 < parts:
                    later = mm(a2, flat(wu, slice((part + 1) * 512, (part + 2) * 512)))
                active, slope = gelu_pair(value)
                active = active.astype(bf16)
                r.u[at, cols] = active
                r.gp[at, cols] = slope.astype(bf16)
                total = total + mm(active, flat_rows(wd, part, parts))
            outcome[at, :] = total
            for name in feed_names[2:]:
                save(layer, name, stream).start()
            if layer == 0:
                g, b = r.rows[row + 4 : row + 5, :], r.rows[row + 5 : row + 6, :]
                r.nxt[at, :] = (normalize(total)[0] * g + b).astype(bf16)
                next_ahead.start(stream, at)

                @pl.when(stream == 0)
                def _():
                    gathers[1][0].relay()
                    gathers[1][1].relay()
                    for gather in gathers[1][2:] + [gather_head]:
                        gather.push()

            return carry

        if layer == 0:

            def all_project(stream, carry):
                project(stream)
                return carry

            def all_look(stream, carry):
                look(stream)
                return carry

            lax.fori_loop(0, streams, all_project, 0)
            lax.fori_loop(0, streams, all_look, 0)
            gathers[0][3].relay()
            gathers[1][0].push()
            gathers[1][1].push()
            for gather in gathers[0][1:]:
                gather.finish()
        else:
            gathers[1][0].finish()
            gathers[1][1].finish()

            def both(stream, carry):
                next_ahead.arrived(stream, tile(stream, span))
                project(stream)
                look(stream)
                return carry

            lax.fori_loop(0, streams, both, 0)
            gathers[1][3].relay()
            gather_head.relay()
            gathers[1][2].finish()
            gathers[1][3].finish()
        for number in range(4):
            save_weight(layer, number).start()
        lax.fori_loop(0, streams, feed, 0)
    gather_head.finish()
    head_stage(place, streams, span, stream_devices, residuals[layers % 2], r)
    for layer in range(layers):
        for number in range(4):
            save_weight(layer, number).wait()
    for stream in range(streams):
        at = tile(stream, span)
        for name in early_names + look_names + feed_names:
            save(layers - 1, name, stream).wait()
        for layer in range(layers):
            save(layer, saved_names[-2], stream, r.a if layer == 0 else r.nxt).wait()
        save(layers - 1, saved_names[-1], stream, residuals[(layers - 1) % 2]).wait()
        pltpu.make_async_copy(r.pr.at[at], r.far_pr.at[at], r.pr_sem.at[stream]).wait()
        next_ahead.sent(stream, at)
    frames_ahead.sent(0, every)


def head_stage(place, streams, span, stream_devices, residual, r):
    gain, bias = r.rows[1:2, :], r.rows[2:3, :]
    step = span // 2
    r.acc[...] = jnp.zeros_like(r.acc)
    r.gr_last[...] = jnp.zeros_like(r.gr_last)
    r.loss[...] = jnp.zeros_like(r.loss)
    target_columns = r.targets[...].T
    lane = lax.broadcasted_iota(jnp.int32, target_columns.shape, 1)

    def column(index):
        return jnp.sum(jnp.where(lane == index, target_columns, 0.0), axis=1, keepdims=True)

    def one(index, carry):
        at = tile(index, step)
        stream, part = index // 2, index % 2
        standard, scale = normalize(residual[at, :])
        f = (standard * gain + bias).astype(bf16)
        z = mm(f, flat(r.wh))
        per = step // 128
        target = jnp.concatenate([column(index * per + i) for i in range(per)], axis=0)
        frames = jnp.full((step, 1), r.frame_count[stream])
        position = lax.broadcasted_iota(jnp.int32, (step, 1), 0) + (place.block * span + part * step)
        share = jnp.where(position < frames, 1.0 / (frames.astype(f32) * (streams * stream_devices)), 0.0)
        peak = jnp.max(z, axis=-1, keepdims=True)
        raised = jnp.exp(z - peak)
        total = jnp.sum(raised, axis=-1, keepdims=True)
        code = lax.broadcasted_iota(jnp.int32, z.shape, 1)
        hit = code == target.astype(jnp.int32)
        picked = jnp.sum(jnp.where(hit, z, 0.0), axis=-1, keepdims=True)
        r.loss[...] += jnp.sum(share * (peak + jnp.log(total) - picked))
        soft = raised * (1.0 / total)
        dz = (share * jnp.where(hit, soft - 1.0, soft)).astype(bf16)
        r.acc[...] += mm(f, dz, TN)
        df = mm(dz, flat(r.wh), NT)
        r.gr_last[0:1, :] += jnp.sum(df * standard, axis=0, keepdims=True)
        r.gr_last[1:2, :] += jnp.sum(df, axis=0, keepdims=True)
        r.dr[at, :] = norm_back(df, standard, scale, gain)
        return carry

    lax.fori_loop(0, streams * 2, one, 0)
    put_blocks(r.grad_head, layouts(place.blocks)[3], 0, 0, r.acc[...])


def attend_back(streams, span, heads, refs, early, between):
    (q_ref, k_ref, v_ref, o_ref, lse_ref, kf_ref, slope_of, do_ref, dq_ref, dk_ref, dv_ref, gs_ref, p_ref, ds_ref) = refs
    pairs = heads // 2
    step = span // 2
    masks = half_masks()
    key_at = lax.broadcasted_iota(jnp.int32, (step, step), 0)
    query_at = lax.broadcasted_iota(jnp.int32, (step, step), 1)
    head_row = lax.broadcasted_iota(jnp.int32, (8, 128), 0)
    place = lax.broadcasted_iota(jnp.int32, (1, step), 1)
    gs_ref[...] = jnp.zeros_like(gs_ref)

    def one(stream, pair):
        cols = tile(pair, 128)
        k_pair = k_ref[tile(stream, 2 * span), cols]
        v_pair = v_ref[tile(stream, 2 * span), cols]
        k_augs = [k_pair * masks[half] + kf_ref[stream, half] for half in range(2)]
        queries, outs = [], []
        for part in range(2):
            seen = span + part * step
            rows = pl.ds(pl.multiple_of(stream * span + part * step, step), step)
            q_pair, do_pair = q_ref[rows, cols], do_ref[rows, cols]
            both = (do_pair.astype(f32) * o_ref[rows, cols].astype(f32)).T
            for half in range(2):
                head = 2 * pair + half
                q_own, do_own = q_pair * masks[half], do_pair * masks[half]
                queries.append(q_own)
                outs.append(do_own)
                delta = jnp.sum(both[half * 64 : half * 64 + 64], axis=0, keepdims=True)
                log_total = lse_ref[pl.ds(stream * heads + head, 1), part * step : (part + 1) * step]
                scores = mm(k_augs[half][: seen + step], q_own + query_marks(slope_of(head), half), NT)
                dp = mm(v_pair[: seen + step], do_own, NT)
                at = slice(half * step, (half + 1) * step)
                for low, high in ((0, seen), (seen, seen + step)):
                    score = scores[low:high]
                    if low:
                        score = jnp.where(key_at <= query_at, score, masked_score)
                    chance = jnp.exp(score - log_total)
                    p_ref[part, low:high, at] = chance.astype(bf16)
                    ds_ref[part, low:high, at] = (chance * (dp[low:high] - delta)).astype(bf16)
        common = span + step
        q_parts = [jnp.concatenate(queries[2 * part : 2 * part + 2], axis=0) for part in range(2)]
        do_parts = [jnp.concatenate(outs[2 * part : 2 * part + 2], axis=0) for part in range(2)]
        base = stream * 2 * span
        for source, out_ref, parts in ((p_ref, dv_ref, do_parts), (ds_ref, dk_ref, q_parts)):
            out_ref[pl.ds(pl.multiple_of(base, step), common), cols] = (
                mm(source[0, :common, :], parts[0]) + mm(source[1, :common, :], parts[1])
            ).astype(bf16)
            out_ref[pl.ds(pl.multiple_of(base + common, step), step), cols] = mm(
                source[1, common:, :], parts[1]
            ).astype(bf16)
        k_turned = [k_aug.T for k_aug in k_augs]
        for part in range(2):
            seen = span + (part + 1) * step
            done = []
            for half in range(2):
                head = 2 * pair + half
                turned = mm(k_turned[half][:, :seen], ds_ref[part, :seen, half * step : (half + 1) * step])
                done.append(turned[half * 64 : half * 64 + 64] * 0.125)
                base_row = 64 - half * 64
                lean = (
                    turned[base_row : base_row + 1]
                    + turned[base_row + 3 : base_row + 4]
                    - (place + (part * step + span)).astype(f32) * turned[base_row + 7 : base_row + 8]
                )
                gs_ref[...] += jnp.where(head_row == head, jnp.sum(lean), 0.0)
            rows = pl.ds(pl.multiple_of(stream * span + part * step, step), step)
            dq_ref[rows, cols] = jnp.concatenate(done, axis=0).T.astype(bf16)

    def over(stream, carry):
        def inner(pair, carry):
            one(stream, pair)
            early(stream * pairs + pair)
            return carry

        carry = lax.fori_loop(0, pairs, inner, carry)
        between(stream)
        return carry

    lax.fori_loop(0, streams, over, 0)


def backward_kernel(layer, sizes, r):
    (stream_devices, block_devices, streams, span, heads, features, nvec) = sizes
    place = Place(stream_devices, block_devices)
    width = r.a.shape[1]
    count = streams * span
    first = place.block == 0
    row = 3 + 4 * layer
    g1, g2 = r.rows[row : row + 1, :], r.rows[row + 2 : row + 3, :]
    step = 256
    tiles = count // step
    sems = (r.out_sem, r.in_sem)
    layout_a, layout_b = layouts(place.blocks)[0], layouts(place.blocks)[2 if layer == 0 else 1]
    broad = Reduce(place, sems, 0, grad=r.grad_a, pair=r.pair_a, mates=r.mates_a, own=r.own_a)
    if layer == 0:
        broad.line, broad.part = r.line_a, r.part_a
    if layer == 0:
        done_a = Reduce(place, sems, 4, own=r.own_a_one, line=r.line_a_one, total=r.total_a_one)
        done_b = Reduce(
            place, sems, 8, pair=r.pair_b_one, mates=r.mates_b_one, own=r.own_b_one, line=r.line_b_one, total=r.total_b_one
        )
    else:
        narrow = Reduce(place, sems, 4, grad=r.grad_b, pair=r.pair_b)
        head = Reduce(
            place, sems, 8, grad=r.grad_head, pair=r.pair_head, mates=r.mates_head, own=r.own_head, line=r.line_head, total=r.total_head
        )
        back = Ahead(place, -1, r.dap, r.back, (r.back_out, r.back_in))

        @pl.when(place.block == place.blocks - 1)
        def _():
            r.back[...] = jnp.zeros_like(r.back)

    for grad, layout in ((r.grad_a, layout_a), (r.grad_b, layout_b)):
        for block in layout.unused():
            grad[:, :, block] = jnp.zeros(grad.shape[:2] + grad.shape[3:], bf16)
    r.gr[...] = jnp.zeros_like(r.gr)
    hidden_parts = r.wu.shape[3] // 512

    def stream_in(part, slot):
        cols = tile(part, 512)
        return (
            pltpu.make_async_copy(r.u.at[layer, :, cols], r.u_two.at[slot], r.u_sem.at[0, slot]),
            pltpu.make_async_copy(r.gp.at[layer, :, cols], r.gp_two.at[slot], r.u_sem.at[1, slot]),
        )

    first_loads = []
    if layer == 0:
        first_loads = [
            pltpu.make_async_copy(r.dr1_in, r.dr, r.first_sem.at[0]),
            pltpu.make_async_copy(r.r.at[1], r.da, r.first_sem.at[1]),
            pltpu.make_async_copy(r.da_in, r.wide_one, r.first_sem.at[2]),
        ]
        late_loads = [
            pltpu.make_async_copy(r.r.at[0], r.wide_one, r.first_sem.at[3]),
            pltpu.make_async_copy(r.pr, r.wide_two, r.first_sem.at[4]),
        ]
        late_loads[1].start()
    else:
        first_loads = [pltpu.make_async_copy(r.dr_in, r.dr, r.first_sem.at[0])]
    for load in first_loads:
        load.start()
    for load in stream_in(0, 0):
        load.start()
    r.fetch()
    place.greet(column=True)
    if layer == 0:
        done_a.start_c()
        done_b.start_b()

        g = r.rows[row + 4 : row + 5, :]

        def join(index, carry):
            at = tile(index, step)
            standard, scale = normalize(r.da[at, :])
            da = r.wide_one[at, :] + r.back[at, :].astype(f32)
            r.gr[4:5, :] += jnp.sum(da * standard, axis=0, keepdims=True)
            r.gr[5:6, :] += jnp.sum(da, axis=0, keepdims=True)
            r.dr[at, :] = r.dr[at, :] + norm_back(da, standard, scale, g)
            return carry

        build_marks(r.kf, r.memory_len, first)
        for load in first_loads:
            load.wait()
        lax.fori_loop(0, tiles, join, 0)
        late_loads[0].start()
    else:
        head.start_a()
        build_marks(r.kf, r.memory_len, first)
        first_loads[0].wait()

    r.da[...] = jnp.zeros_like(r.da)
    r.ready(r.wd, r.a2, r.wu)
    r.turned[...] = r.a2[...].T
    parts = hidden_parts

    def feed(part, carry):
        cols = tile(part, 512)
        slot = part % 2

        @pl.when(part + 1 < parts)
        def _():
            for load in stream_in(part + 1, 1 - slot):
                load.start()

        for load in stream_in(part, slot):
            load.wait()
        dy = r.dr[...].astype(bf16)
        dh = (mm(dy, flat_rows(r.wd, part, parts), NT) * r.gp_two[slot].astype(f32)).astype(bf16)
        put_down(r.grad_a, layout_a, 0, mm(r.u_two[slot], dy, TN), part, parts)
        put_blocks(r.grad_a, layout_a, 1, 4 * part, mm(r.turned[...], dh))
        r.da[...] += mm(dh, flat(r.wu, cols), NT)
        if layer == 1:

            @pl.when(part == 0)
            def _():
                head.end_a()
                head.start_b()

        return carry

    lax.fori_loop(0, parts, feed, 0)
    r.ready(r.r1, r.wo, r.o, r.lse)

    def middle(index, carry):
        at = tile(index, step)
        standard, scale = normalize(r.r1[at, :])
        da = r.da[at, :]
        r.gr[2:3, :] += jnp.sum(da * standard, axis=0, keepdims=True)
        r.gr[3:4, :] += jnp.sum(da, axis=0, keepdims=True)
        dr = r.dr[at, :] + norm_back(da, standard, scale, g2)
        r.dr[at, :] = dr
        r.do[at, :] = mm(dr.astype(bf16), flat(r.wo), NT).astype(bf16)
        return carry

    lax.fori_loop(0, tiles, middle, 0)
    put_blocks(r.grad_a, layout_a, 2, 0, mm(r.o[...], r.dr[...].astype(bf16), TN))
    broad.start_a()
    if layer == 0:
        done_a.end_c()
        done_a.start_d()
        done_b.end_b()
        done_b.start_c()
    else:
        head.end_b()
        head.start_c()
    wk, wv = (slice(i * width, (i + 1) * width) for i in (1, 2))

    def behind_gradient(at, behind):
        return mm(r.dk[behind, :], flat(r.wp, wk), NT) + mm(r.dv[behind, :], flat(r.wp, wv), NT)

    def early(index):
        @pl.when(index == 1)
        def _():
            broad.end_a()
            broad.start_b()

    def between(stream):
        if layer == 0:

            @pl.when(stream == 0)
            def _():
                done_b.end_c()
                done_b.start_d()

        else:
            for part in range(span // step):
                at = pl.ds(pl.multiple_of(stream * span + part * step, step), step)
                behind = pl.ds(pl.multiple_of(stream * 2 * span + part * step, step), step)
                r.dap[at, :] = behind_gradient(at, behind).astype(bf16)
            back.start(stream, tile(stream, span))

            @pl.when(stream == 0)
            def _():
                head.end_c()
                head.start_d()

    r.ready(r.q, r.k, r.v, r.wp)
    attend_back(
        streams,
        span,
        heads,
        (r.q, r.k, r.v, r.o, r.lse, r.kf, lambda head: r.slopes[layer, head], r.do, r.dq, r.dk, r.dv, r.gs, r.u_two, r.gp_two),
        early,
        between,
    )

    r.ready(r.a, r.ap)
    r.turned[...] = r.a[...].T
    put_blocks(r.grad_b, layout_b, 0, 0, mm(r.turned[...], r.dq[...]))
    for spot, ref in ((1, r.dk), (2, r.dv)):
        total = jnp.zeros((width, width), f32)
        for stream in range(streams):
            behind = slice(stream * 2 * span, stream * 2 * span + span)
            here = slice(stream * 2 * span + span, (stream + 1) * 2 * span)
            own = slice(stream * span, (stream + 1) * span)
            total = total + mm(r.turned[:, own], ref[here, :])
            total = total + mm(r.ap[own, :], ref[behind, :], TN)
        put_blocks(r.grad_b, layout_b, 0, 4 * spot, total)

    if layer == 0:
        r.small_acc[...] = jnp.zeros_like(r.small_acc)
        for load in late_loads:
            load.wait()
        broad.end_b()
        broad.start_c()
    else:
        narrow.start_a()
        r.ready(r.mem)

    def finish(stream, carry):
        for part in range(span // step):
            at = pl.ds(pl.multiple_of(stream * span + part * step, step), step)
            behind = pl.ds(pl.multiple_of(stream * 2 * span + part * step, step), step)
            here = pl.ds(pl.multiple_of(stream * 2 * span + span + part * step, step), step)
            da = (
                mm(r.dq[at, :], flat(r.wp, slice(0, width)), NT)
                + mm(r.dk[here, :], flat(r.wp, wk), NT)
                + mm(r.dv[here, :], flat(r.wp, wv), NT)
            )
            if layer == 0:
                dap = behind_gradient(at, behind)
                standard, scale = normalize(r.wide_one[at, :])
                before, before_scale = normalize(r.wide_two[at, :])
                r.gr[0:1, :] += jnp.sum(da * standard + dap * before, axis=0, keepdims=True)
                r.gr[1:2, :] += jnp.sum(da + dap, axis=0, keepdims=True)
                dr = r.dr[at, :] + norm_back(da, standard, scale, g1)
                drp = norm_back(dap, before, before_scale, g1)
                drp = jnp.where(first, 0.0, drp)
                r.gr[6:7, :] += jnp.sum(dr + drp, axis=0, keepdims=True)
                r.small_acc[...] += mm(dr.astype(bf16), r.frames[at, :], TN)
                r.small_acc[...] += mm(drp.astype(bf16), r.halo[at, :], TN)
            else:
                r.da[at, :] = da
                before, before_scale = normalize(r.mem[at, :].astype(f32))
                dap = jnp.where(first, r.dap[at, :].astype(f32), 0.0)
                r.gr[0:1, :] += jnp.sum(dap * before, axis=0, keepdims=True)
                r.gr[1:2, :] += jnp.sum(dap, axis=0, keepdims=True)
        return carry

    lax.fori_loop(0, streams, finish, 0)
    if layer == 0:
        listed = [r.gr[6:7, :], r.gr_last[0:2, :], r.gr[0:4, :], r.gr_one[0:2, :] + r.gr[4:6, :], r.gr_one[2:4, :]]
        listed = [jnp.zeros((features, width), f32)] + listed + [jnp.zeros((128 - features - nvec, width), f32)]
        lane = lax.broadcasted_iota(jnp.int32, (1, 128), 1)
        merged = jnp.where(lane < features, r.small_acc[...], jnp.concatenate(listed, axis=0).T)
        put_blocks(r.grad_b, layout_b, 1, 0, merged)
        done_b.end_d()
        done_a.end_d()
        broad.end_c()
    else:
        head.end_d()
        narrow.end_a()
        broad.end_b()
        for stream in range(streams):
            at = tile(stream, span)
            back.sent(stream, at)
            back.arrived(stream, at)


def lanes_of(entries):
    lane = lax.broadcasted_iota(jnp.int32, (1, 128), 1)
    row = jnp.zeros((1, 128), f32)
    for number, value in entries:
        row = jnp.where(lane == number, value, row)
    return row


def pick(row, number):
    lane = lax.broadcasted_iota(jnp.int32, (1, 128), 1)
    return jnp.sum(jnp.where(lane == number, row, 0.0))


class State:
    def __init__(self, blocks, layers, rows, totals):
        wide, self.narrow, last, head = layouts(blocks)
        self.rows = rows
        self.items = []
        for layer in range(layers):
            broad_total, narrow_total = totals[2 * layer : 2 * layer + 2]
            narrow = last if layer == 0 else self.narrow
            self.items += [
                (1, layer, narrow_total, narrow, 0, 1 + layer),
                (2, layer, broad_total, wide, 2, 1 + layers + layer),
                (3, layer, broad_total, wide, 1, 1 + 2 * layers + layer),
                (4, layer, broad_total, wide, 0, 1 + 3 * layers + layer),
            ]
        self.items.append((5, None, totals[-1], head, 0, 1 + 4 * layers))
        self.vector_start = 2 + 4 * layers
        self.small = (totals[1], last.spot(1, 0))

    def place(self, array, layer, block):
        across = block % 4 if array == 4 else block
        up = block // 4 if array == 4 else 0
        rows, cols = up * self.rows, across * 128
        if not isinstance(block, int):
            rows, cols = pl.multiple_of(rows, self.rows), pl.multiple_of(cols, 128)
        where = (pl.ds(rows, self.rows), pl.ds(cols, 128))
        return where if layer is None else (layer,) + where


def tail_kernel(sizes, layers, r):
    (stream_devices, block_devices, streams, span, heads, features, nvec) = sizes
    place = Place(stream_devices, block_devices)
    index = lax.axis_index(STREAM)
    sems = (r.out_sem, r.in_sem)
    broad = Reduce(place, sems, 0, total=r.total_a)
    narrow = Reduce(
        place, sems, 4, grad=r.grad_b, pair=r.pair_b, mates=r.mates_b, own=r.own_b, line=r.line_b, total=r.total_b
    )
    r.fetch()
    r.total_a[broad.piece(place.block)] = r.part_a[...]
    barrier = pltpu.get_barrier_semaphore()
    for distance in range(1, stream_devices):
        device = {STREAM: (index + distance) % stream_devices}
        pl.semaphore_signal(barrier, inc=1, device_id=device, device_id_type=MESH)
    for distance in range(1, block_devices):
        pl.semaphore_signal(barrier, inc=1, device_id={SEQ: place.peer(distance)}, device_id_type=MESH)
    pl.semaphore_wait(barrier, stream_devices - 1 + block_devices - 1)
    narrow.start_a()
    broad.start_d()
    rows = r.total_a.shape[1]
    state = State(block_devices, layers, rows, [r.total_a, r.total_b, r.total_a_one, r.total_b_one, r.total_head])
    arrays = [[getattr(r, f"{kind}_{number}") for number in range(7)] for kind in KINDS]
    weights, firsts, seconds = arrays
    square = jnp.zeros((rows, 128), f32)
    for ref in (r.total_a, r.total_a_one, r.total_b_one, r.total_head):
        size = ref.shape[0] // block_devices
        value = ref[pl.ds(place.block * size, size)].astype(f32)
        square = square + jnp.sum(value * value, axis=0)
    narrow.end_a()
    narrow.start_b()
    for array in arrays:
        r.ready(*array)

    shares = []
    for array, layer, total, layout, part, matrix in state.items:
        base, per, count = layout.parts[part]
        for number in range(per):
            block = place.block * per + number
            valid = jnp.where(block < count, 1.0, 0.0)
            spot = state.place(array, layer, jnp.minimum(block, count - 1))
            shares.append((array, spot, total, place.block * layout.size + base + number, matrix, valid))
    edge = jnp.where(place.block == 0, 1.0, 0.0)

    def matrix_squares(value_of, turned, vector_rows):
        found = {}
        for array, spot, total, block, matrix, valid in shares:
            value = value_of(array, spot, total, block)
            value = value * value * valid
            found[matrix] = value if matrix not in found else found[matrix] + value
        entries = [(matrix, jnp.sum(value)) for matrix, value in found.items()]
        entries.append((0, jnp.sum(turned * turned) * edge))
        row = lanes_of(entries)
        lane = lax.broadcasted_iota(jnp.int32, (nvec, 128), 1)
        down = lax.broadcasted_iota(jnp.int32, (nvec, 128), 0)
        column = jnp.sum(vector_rows * vector_rows, axis=1, keepdims=True) * edge
        return row + jnp.sum(jnp.where(lane == state.vector_start + down, column, 0.0), axis=0, keepdims=True)

    weight_row = matrix_squares(lambda array, spot, total, block: weights[array][spot], weights[0][...], weights[6][...])
    for ref in (r.near_one, r.near_two):
        ref[place.block] = jnp.zeros((8, 128), f32)
    narrow.end_b()
    narrow.start_c()

    def exchange(near, far, first):
        def along(ref, axis, mine, count, start):
            def copy(distance, source):
                return pltpu.make_async_remote_copy(
                    src_ref=ref.at[source],
                    dst_ref=ref.at[source],
                    send_sem=r.all_out.at[start + distance],
                    recv_sem=r.all_in.at[start + distance],
                    device_id={axis: (mine + distance) % count},
                    device_id_type=MESH,
                )

            for distance in range(1, count):
                copy(distance, mine).start()
            for distance in range(1, count):
                copy(distance, (mine + count - distance) % count).wait_recv()
            for distance in range(1, count):
                copy(distance, mine).wait_send()
            return jnp.sum(ref[...], axis=0)

        far[index] = along(near, SEQ, place.block, block_devices, first)
        return along(far, STREAM, index, stream_devices, first + block_devices)

    lane = lax.broadcasted_iota(jnp.int32, (8, 128), 1)
    down = lax.broadcasted_iota(jnp.int32, (8, 128), 0)
    plain = jnp.where(lane == 1, r.loss[...], 0.0) * jnp.where(down == 0, 1.0, 0.0)
    for layer, ref in enumerate((r.gs_zero, r.gs_one)):
        plain = plain + jnp.where(lane == 16 + layer * heads + down, ref[...], 0.0)
    narrow.end_c()
    narrow.start_d()
    size = r.total_b.shape[0] // block_devices
    value = r.total_b[pl.ds(place.block * size, size)].astype(f32)
    square = square + jnp.sum(value * value, axis=0)
    r.near_one[place.block, 0:1, :] = jnp.sum(plain, axis=0, keepdims=True) + lanes_of([(0, jnp.sum(square))])
    sums = exchange(r.near_one, r.far_one, 0)[0:1, :]
    lane = lax.broadcasted_iota(jnp.int32, (1, 128), 1)
    slope_lanes = jnp.logical_and(lane >= 16, lane < 16 + layers * heads)
    clip = jnp.sqrt(
        jnp.full((1, 128), pick(sums, 0)) + jnp.sum(jnp.where(slope_lanes, sums * sums, 0.0), axis=1, keepdims=True)
    )
    factor = jnp.minimum(1.0, clip_limit / clip)
    scale = factor[:, 0:1]

    def direction(weight, grad, first, second):
        return adam_direction(weight, grad, first, second, decay_rate)[2]

    small = r.total_b[place.block * size + state.small[1]].astype(f32)
    turned = direction(weights[0][...], small[:, :features] * scale, firsts[0][...], seconds[0][...])
    vector_rows = direction(
        weights[6][...], small.T[features : features + nvec] * scale, firsts[6][...], seconds[6][...]
    )
    r.near_two[place.block, 0:1, :] = matrix_squares(
        lambda array, spot, total, block: direction(
            weights[array][spot], total[block].astype(f32) * factor, firsts[array][spot], seconds[array][spot]
        ),
        turned,
        vector_rows,
    )
    r.near_two[place.block, 1:2, :] = weight_row
    r.sums[...] = exchange(r.near_two, r.far_two, stream_devices + block_devices)
    r.sums[2:3, :] = sums
    r.sums[3:4, :] = clip
    r.sums[4:5, :] = factor
    broad.end_d()
    narrow.end_d()


def update_kernel(sizes, layers, r):
    (stream_devices, block_devices, streams, span, heads, features, nvec) = sizes
    keep = pltpu.make_async_copy(r.low, r.layer_inputs, r.keep_sem.at[0])
    r.fetch()
    weights, firsts, seconds = ([getattr(r, f"{kind}_{number}") for number in range(7)] for kind in KINDS)
    fresh, new_firsts, new_seconds = ([getattr(r, f"new_{kind}_{number}") for number in range(7)] for kind in KINDS)
    r.ready(r.total_a, r.total_b, r.total_a_one, r.total_b_one, r.total_head)
    rows = r.total_a.shape[1]
    state = State(block_devices, layers, rows, [r.total_a, r.total_b, r.total_a_one, r.total_b_one, r.total_head])
    factor = r.sums[4:5, :]
    scale = factor[:, 0:1]
    norms = jnp.sqrt(r.sums[0:2, :])
    ratios = norms[1:2] / norms[0:1]
    small = r.total_b[state.small[1]].astype(f32)
    lane = lax.broadcasted_iota(jnp.int32, (nvec, 128), 1)
    down = lax.broadcasted_iota(jnp.int32, (nvec, 128), 0)
    vector_ratio = jnp.sum(jnp.where(lane == state.vector_start + down, ratios, 0.0), axis=1, keepdims=True)

    def finish(array):
        r.flush(fresh[array], new_firsts[array], new_seconds[array])

    for array, grad, ratio in (
        (0, small[:, :features], jnp.full((1, 1), pick(ratios, 0))),
        (6, small.T[features : features + nvec], vector_ratio),
    ):
        r.ready(weights[array], firsts[array], seconds[array])
        weight = weights[array][...]
        first, second, direction = adam_direction(
            weight, grad * scale, firsts[array][...], seconds[array][...], decay_rate
        )
        new_firsts[array][...] = first
        new_seconds[array][...] = second
        fresh[array][...] = weight - lamb_rate * ratio * direction
        finish(array)
    for number in range(1, 6):
        r.ready(weights[number], firsts[number], seconds[number])
        for array, layer, total, layout, part, matrix in state.items:
            if array != number:
                continue
            ratio = jnp.full((1, 128), lamb_rate * pick(ratios, matrix))
            for block in range(layout.parts[part][2]):
                spot = state.place(array, layer, block)
                weight = weights[array][spot]
                first, second, direction = adam_direction(
                    weight,
                    total[layout.spot(part, block)].astype(f32) * factor,
                    firsts[array][spot],
                    seconds[array][spot],
                    decay_rate,
                )
                new_firsts[array][spot] = first
                new_seconds[array][spot] = second
                fresh[array][spot] = weight - ratio * direction
        finish(number)
    sums = r.sums[2:3, :]
    grad = jnp.concatenate([sums[:, 16 + layer * heads : 16 + (layer + 1) * heads] for layer in range(layers)], axis=0)
    slopes = r.slopes[...]
    first, second, direction = adam_direction(slopes, grad * scale, r.first_slopes[...], r.second_slopes[...], 0.0)
    r.new_first_slopes[...] = first
    r.new_second_slopes[...] = second
    r.fresh_slopes[...] = slopes - slope_rate * direction
    count = state.vector_start + nvec
    r.norms[0:1, 0:count] = norms[1:2, :count]
    r.norms[1:2, 0:count] = norms[0:1, :count]
    r.norms[0:1, count : count + 1] = jnp.full((1, 1), jnp.sqrt(jnp.sum(slopes * slopes)))
    r.norms[1:2, count : count + 1] = jnp.full((1, 1), jnp.sqrt(jnp.sum(direction * direction)))
    r.loss[...] = sums[:, 1:2]
    r.clip[...] = r.sums[3:4, 0:1]
    r.ready(r.low)
    keep.start()
    r.flushed()
    keep.wait()


def whole(space=pltpu.VMEM):
    return pl.BlockSpec(memory_space=space)


def call_named(
    kernel,
    ins,
    outs,
    scratch=None,
    sems=None,
    any_ins=None,
    lazy=None,
    flush=None,
    any_outs=None,
    smem=None,
    layer=None,
    layered=(),
    flops=0,
    collective=None,
):
    any_ins, lazy, flush = any_ins or {}, lazy or {}, flush or {}
    any_outs, smem = any_outs or {}, smem or {}
    scratch, sems = dict(scratch or {}), dict(sems or {})
    dma = pltpu.SemaphoreType.DMA
    for key, array in lazy.items():
        scratch[key] = (array.shape[1:] if key in layered else array.shape, array.dtype)
    scratch.update(flush)
    if lazy:
        sems.update(load_sem=dma((len(lazy),)))
    if flush:
        sems.update(store_sem=dma((len(flush),)))
    far = [FAR + key for key in lazy]
    names = list(ins) + list(any_ins) + far + list(smem)
    names += list(outs) + list(any_outs) + [FAR + key for key in flush] + list(scratch) + list(sems)
    out_shapes = list(outs.values()) + list(any_outs.values()) + list(flush.values())
    made = pl.pallas_call(
        lambda *refs: kernel(Refs(names, refs, lazy, flush, layer, layered)),
        name=kernel.func.__name__ if layer is None else f"{kernel.func.__name__}_{layer}",
        out_shape=[jax.ShapeDtypeStruct(*out) for out in out_shapes],
        in_specs=[whole()] * len(ins)
        + [whole(pl.ANY)] * (len(any_ins) + len(lazy))
        + [whole(pltpu.SMEM)] * len(smem),
        out_specs=[whole()] * len(outs) + [whole(pl.ANY)] * (len(any_outs) + len(flush)),
        scratch_shapes=[pltpu.VMEM(*item) for item in scratch.values()] + list(sems.values()),
        compiler_params=pltpu.CompilerParams(
            vmem_limit_bytes=VMEM_LIMIT, collective_id=collective, has_side_effects=collective is not None
        ),
        cost_estimate=pl.CostEstimate(flops=flops, bytes_accessed=20000000, transcendentals=0),
    )(*ins.values(), *any_ins.values(), *lazy.values(), *smem.values())
    return dict(zip(list(outs) + list(any_outs) + list(flush), made))


class Made:
    def __init__(self, *args, **options):
        for name, array in call_named(*args, **options).items():
            setattr(self, name, array)


class Groups:
    def __init__(self, layout, shapes):
        self.layout = layout
        for name, shape in shapes.items():
            setattr(self, name, shape)


def adam_direction(weight, grad, first, second, decay):
    new_first = beta_one * first + (1.0 - beta_one) * grad
    new_second = beta_two * second + (1.0 - beta_two) * grad * grad
    first_hat = new_first / (1.0 - beta_one**STEP)
    second_hat = new_second / (1.0 - beta_two**STEP)
    return (new_first, new_second, first_hat / (jnp.sqrt(second_hat) + adam_eps) + decay * weight)


def shards(
    frames,
    targets,
    frame_count,
    memory,
    memory_len,
    input_weight,
    project_weight,
    output_weight,
    up_weight,
    down_weight,
    head_weight,
    vectors,
    slopes,
    first_input,
    first_project,
    first_output,
    first_up,
    first_down,
    first_head,
    first_vectors,
    first_slopes,
    second_input,
    second_project,
    second_output,
    second_up,
    second_down,
    second_head,
    second_vectors,
    second_slopes,
):
    streams, span, features = frames.shape
    layers, heads = slopes.shape
    nvec = vectors.shape[0]
    width = project_weight.shape[2] // 3
    hidden = up_weight.shape[2]
    codes = head_weight.shape[1]
    count = streams * span
    devices, blocks = lax.axis_size(STREAM), lax.axis_size(SEQ)
    chips = devices // 2
    sizes = (devices, blocks, streams, span, heads, features, nvec)
    memory_flat = memory.reshape((layers, count, width))
    rows_each = width // devices
    full = ((count, width), f32)
    low = ((count, width), bf16)
    joined = ((2 * count, width), bf16)
    wide = ((count, hidden), bf16)
    lse = ((streams * heads, span), f32)
    cost = 2 * count * (5 * width * width + width * width + 2 * width * hidden) + 4 * count * 2 * span * width
    dma = pltpu.SemaphoreType.DMA

    def gathered(rows_all, cols):
        return ((chips, 2, rows_all // devices, cols), bf16)

    def grads_of(number):
        return dict(
            grad=((chips, 2, number, rows_each, 128), bf16),
            pair=((chips, number, rows_each, 128), bf16),
            mates=((chips, number, rows_each, 128), bf16),
            own=((number, rows_each, 128), bf16),
            line=((blocks, number // blocks, rows_each, 128), bf16),
            total=((number, rows_each, 128), bf16),
        )

    group_a, group_b, group_last, group_head = (Groups(layout, grads_of(layout.total)) for layout in layouts(blocks))
    kept = dict(
        a=low, ap=low, q=low, k=joined, v=joined, o=low, lse=lse, r1=full, a2=low, u=wide, gp=wide, res=full, low=low
    )
    weight_shapes = dict(
        wp=gathered(width, 3 * width), wo=gathered(width, width), wu=gathered(width, hidden), wd=gathered(hidden, width)
    )
    layer_weights = {f"{key}_{layer}": item for layer in range(layers) for key, item in weight_shapes.items()}
    gather_count = 2 + len(layer_weights)
    score = ((2 * span, span // 2), f32)
    chance = ((2 * span, span // 2), bf16)
    scalars = dict(memory_len=memory_len, slopes=slopes)
    made = Made(
        functools.partial(forward_kernel, sizes),
        dict(
            frames=frames.transpose((0, 2, 1)),
            targets=targets.reshape((count // 128, 128)).astype(f32),
            input_turned=input_weight.T,
            vectors=vectors,
        ),
        dict(
            rows=((16, width), f32),
            dr=full,
            gr_last=((8, width), f32),
            loss=((8, 128), f32),
            grad_head=group_head.grad,
            halo=((count, 128), bf16),
            frames_wide=((count, 128), bf16),
        ),
        dict(
            kept,
            **layer_weights,
            res_two=full,
            pr=full,
            nxt=low,
            behind=low,
            small=gathered(width, 128),
            wh=gathered(width, codes),
            small_rows=((128 - features, rows_each), f32),
            frames_tall=((128, span), bf16),
            kf=((streams, 2, 2 * span, 128), bf16),
            acc=((width, codes), f32),
            score_one=score,
            score_two=score,
            chance_one=chance,
            chance_two=chance,
        ),
        dict(
            out_sem=dma((gather_count, chips)),
            in_sem=dma((gather_count, chips)),
            frame_sem=dma((2, 1)),
            next_out=dma((streams,)),
            next_in=dma((streams,)),
            save_sem=dma((layers, len(kept), streams)),
            weight_sem=dma((layers, 4)),
            pr_sem=dma((streams,)),
        ),
        any_outs=dict(
            far_pr=full,
            **{FAR + key: ((layers,) + item[0], item[1]) for key, item in kept.items()},
            **{FAR + key: item for key, item in layer_weights.items()},
        ),
        lazy=dict(
            pw=project_weight, ow=output_weight, uw=up_weight, dw=down_weight, hw=head_weight, mem=memory_flat
        ),
        smem=dict(scalars, frame_count=frame_count),
        flops=2 * cost,
        collective=0,
    )

    def loaded(layer):
        held = [getattr(made, f"{FAR}{key}_{layer}") for key in weight_shapes]
        return dict(
            wd=held[3],
            a2=made.far_a2,
            wu=held[2],
            r1=made.far_r1,
            wo=held[1],
            o=made.far_o,
            lse=made.far_lse,
            q=made.far_q,
            k=made.far_k,
            v=made.far_v,
            wp=held[0],
            a=made.far_a,
            ap=made.far_ap,
        )

    layered = tuple(kept) + tuple(dict(mem=0))
    slots = max(chips, blocks)
    work = dict(
        do=low,
        dq=low,
        dk=joined,
        dv=joined,
        turned=((width, count), bf16),
        kf=((streams, 2, 2 * span, 128), bf16),
        pair_a=group_a.pair,
        mates_a=group_a.mates,
        grad_a=group_a.grad,
        u_two=((2, count, 512), bf16),
        gp_two=((2, count, 512), bf16),
    )
    work_sems = dict(out_sem=dma((12, slots)), in_sem=dma((12, slots)), u_sem=dma((2, 2)), first_sem=dma((5,)))
    streamed = dict(u=made.far_u, gp=made.far_gp)
    one = Made(
        functools.partial(backward_kernel, 1, sizes),
        dict(rows=made.rows, grad_head=made.grad_head),
        dict(
            gr=((8, width), f32),
            gs=((8, 128), f32),
            dr=full,
            da=full,
            back=low,
            own_a=group_a.own,
            pair_b=group_b.pair,
            total_head=group_head.total,
        ),
        dict(
            work,
            dap=low,
            grad_b=group_b.grad,
            pair_head=group_head.pair,
            mates_head=group_head.mates,
            own_head=group_head.own,
            line_head=group_head.line,
        ),
        dict(work_sems, back_out=dma((streams,)), back_in=dma((streams,))),
        any_ins=dict(streamed, dr_in=made.dr),
        lazy=dict(loaded(1), mem=memory_flat),
        layered=layered,
        layer=1,
        smem=scalars,
        flops=2 * cost,
        collective=2,
    )
    zero = Made(
        functools.partial(backward_kernel, 0, sizes),
        dict(
            rows=made.rows,
            frames=made.frames_wide,
            halo=made.halo,
            back=one.back,
            gr_last=made.gr_last,
            gr_one=one.gr,
            own_a_one=one.own_a,
            pair_b_one=one.pair_b,
        ),
        dict(
            gs=((8, 128), f32),
            part_a=((group_a.layout.size, rows_each, 128), bf16),
            grad_b=group_last.grad,
            total_a_one=group_a.total,
            total_b_one=group_b.total,
        ),
        dict(
            work,
            gr=((8, width), f32),
            dr=full,
            da=full,
            small_acc=((width, 128), f32),
            wide_one=full,
            wide_two=full,
            own_a=group_a.own,
            line_a=group_a.line,
            line_a_one=group_a.line,
            mates_b_one=group_b.mates,
            own_b_one=group_b.own,
            line_b_one=group_b.line,
        ),
        work_sems,
        any_ins=dict(streamed, dr1_in=one.dr, da_in=one.da, r=made.far_res, pr=made.far_pr),
        lazy=loaded(0),
        layered=layered,
        layer=0,
        smem=scalars,
        flops=2 * cost,
        collective=3,
    )
    arrays = (
        (input_weight.T, project_weight, output_weight, up_weight, down_weight, head_weight, vectors),
        (first_input.T, first_project, first_output, first_up, first_down, first_head, first_vectors),
        (second_input.T, second_project, second_output, second_up, second_down, second_head, second_vectors),
    )
    order = (0, 6, 1, 2, 3, 4, 5)
    state = {f"{kind}_{number}": array[number] for number in order for kind, array in zip(KINDS, arrays)}
    tile_shape = ((8, 128), f32)
    tail = Made(
        functools.partial(tail_kernel, sizes, layers),
        dict(
            part_a=zero.part_a,
            grad_b=zero.grad_b,
            total_a_one=zero.total_a_one,
            total_b_one=zero.total_b_one,
            total_head=one.total_head,
            gs_zero=zero.gs,
            gs_one=one.gs,
            loss=made.loss,
        ),
        dict(total_a=group_a.total, total_b=group_last.total, sums=tile_shape),
        dict(
            pair_b=group_last.pair,
            mates_b=group_last.mates,
            own_b=group_last.own,
            line_b=group_last.line,
            near_one=((blocks, 8, 128), f32),
            near_two=((blocks, 8, 128), f32),
            far_one=((devices, 8, 128), f32),
            far_two=((devices, 8, 128), f32),
        ),
        dict(
            out_sem=dma((8, slots)),
            in_sem=dma((8, slots)),
            all_out=dma((2 * (devices + blocks),)),
            all_in=dma((2 * (devices + blocks),)),
        ),
        lazy=state,
        collective=4,
    )
    moved = {f"new_{kind}_{number}": (array[number].shape, f32) for number in order for kind, array in zip(KINDS, arrays)}
    fresh = Made(
        functools.partial(update_kernel, sizes, layers),
        dict(slopes=slopes, first_slopes=first_slopes, second_slopes=second_slopes, sums=tail.sums),
        dict(
            fresh_slopes=(slopes.shape, f32),
            new_first_slopes=(slopes.shape, f32),
            new_second_slopes=(slopes.shape, f32),
            norms=((2, 3 + 4 * layers + nvec), f32),
            loss=((1, 1), f32),
            clip=((1, 1), f32),
        ),
        sems=dict(keep_sem=dma((1,))),
        any_outs=dict(layer_inputs=((layers, count, width), bf16)),
        lazy=dict(
            total_a=tail.total_a,
            total_b=tail.total_b,
            total_a_one=zero.total_a_one,
            total_b_one=zero.total_b_one,
            total_head=one.total_head,
            **state,
            low=made.far_low,
        ),
        flush=moved,
    )

    def results(kind, last):
        found = [getattr(fresh, f"new_{kind}_{number}") for number in range(7)]
        return [found[0].T] + found[1:] + [last]

    return (
        fresh.loss.reshape(()),
        fresh.layer_inputs.reshape((layers, streams, span, width)),
        fresh.clip.reshape(()),
        fresh.norms.T,
        *results(KINDS[0], fresh.fresh_slopes),
        *results(KINDS[1], fresh.new_first_slopes),
        *results(KINDS[2], fresh.new_second_slopes),
    )


def solution(mesh):
    rows3 = P(None, STREAM, None)
    state = (P(None, STREAM), rows3, rows3, rows3, rows3, P(STREAM, None), P(None, STREAM), P())
    in_specs = (
        P(STREAM, SEQ, None),
        P(STREAM, SEQ),
        P(STREAM),
        P(None, STREAM, None, None),
        P(STREAM),
    ) + state * 3
    out_specs = (P(), P(None, STREAM, SEQ, None), P(), P()) + state * 3
    return jax.shard_map(shards, mesh=mesh, in_specs=in_specs, out_specs=out_specs, check_vma=False)
```

```python
import functools

import jax
import jax.numpy as jnp
from jax import lax
from jax.experimental import pallas as pl
from jax.experimental.pallas import tpu as pltpu
from jax.sharding import PartitionSpec as P

STEP = 10


ln_eps = 1e-05
clip_limit = 0.002
beta_one = 0.9
beta_two = 0.999
lamb_rate = 0.3
slope_rate = 0.001
decay_rate = 0.01
adam_eps = 1e-11
masked_score = -1e30

STREAM, SEQ, FAR = "stream", "seq", "far_"
KINDS = ("weight", "first", "second")
WIDE = ("a", "c")
REDUCED = ("grad", "pair", "mates", "own", "line", "part", "total")
NN = (((1,), (0,)), ((), ()))
NT = (((1,), (1,)), ((), ()))
TN = (((0,), (0,)), ((), ()))
VMEM_LIMIT = 63 * 1024 * 1024
f32 = jnp.float32
bf16 = jnp.bfloat16


def mm(left, right, dims=NN):
    return lax.dot_general(left, right, dims, preferred_element_type=f32)


MESH = pl.DeviceIdType.MESH


class Place:
    def __init__(self, streams, blocks):
        self.chips = streams // 2
        self.blocks = blocks
        index = lax.axis_index(STREAM)
        self.chip = index // 2
        self.core = index % 2
        self.block = lax.axis_index(SEQ)
        self.sibling = {STREAM: 2 * self.chip + 1 - self.core}
        self.across = self.chip // 2 * 2 + 1 - self.chip % 2
        self.along = (self.chip + 2) % 4
        self.opposite = 3 - self.chip

    def chip_device(self, chip):
        return {STREAM: 2 * chip + self.core}

    def other(self, distance):
        return (self.chip + distance) % self.chips

    def mate(self, distance):
        return {STREAM: 2 * self.other(distance) + self.core}

    def peer(self, distance):
        return (self.block + distance) % self.blocks

    def greet(self, line=False, column=False):
        barrier = pltpu.get_barrier_semaphore()

        def hello(device):
            pl.semaphore_signal(barrier, inc=1, device_id=device, device_id_type=MESH)

        hello(self.sibling)
        for distance in range(1, self.chips):
            hello(self.mate(distance))
        if line:

            @pl.when(self.block > 0)
            def _():
                hello({SEQ: self.block - 1})

            pl.semaphore_wait(barrier, self.chips + jnp.where(self.block < self.blocks - 1, 1, 0))
        elif column:
            for distance in range(1, self.blocks):
                hello({SEQ: self.peer(distance)})
            pl.semaphore_wait(barrier, self.chips + self.blocks - 1)
        else:
            pl.semaphore_wait(barrier, self.chips)


class Gather:
    def __init__(self, place, ref, sems, row, direct=False):
        self.place, self.ref, self.sems, self.row = place, ref, sems, row
        self.square = place.chips == 4 and not direct

    def copy(self, slot, view, device):
        return pltpu.make_async_remote_copy(
            src_ref=view,
            dst_ref=view,
            send_sem=self.sems[0].at[self.row, slot],
            recv_sem=self.sems[1].at[self.row, slot],
            device_id=device,
            device_id_type=MESH,
        )

    def shard(self, chip, half=None):
        view = self.ref.at[chip, self.place.core]
        if half is None:
            return view
        size = self.ref.shape[2] // 2
        return view.at[pl.ds(half * size, size)]

    def far(self, distance, chip):
        return self.copy(distance, self.shard(chip), self.place.mate(distance))

    def beside(self, slot, chip, half, target):
        return self.copy(slot, self.shard(chip, half), self.place.chip_device(target))

    def near(self, core):
        return self.copy(0, self.ref.at[:, core], self.place.sibling)

    def push(self):
        place = self.place
        if self.square:
            self.beside(1, place.chip, None, place.across).start()
            self.beside(2, place.chip, None, place.along).start()
        else:
            for distance in range(1, place.chips):
                self.far(distance, place.chip).start()

    def pass_on(self):
        place = self.place
        if self.square:
            self.beside(1, place.across, None, place.across).wait_recv()
            self.beside(2, place.along, None, place.along).wait_recv()
            self.beside(3, place.across, 0, place.along).start()
            self.beside(4, place.along, 1, place.across).start()

    def relay(self):
        place = self.place
        if self.square:
            self.beside(3, place.opposite, 0, place.along).wait_recv()
            self.beside(4, place.opposite, 1, place.across).wait_recv()
        else:
            for distance in range(1, place.chips):
                self.far(distance, place.other(place.chips - distance)).wait_recv()
        self.near(place.core).start()

    def finish(self):
        place = self.place
        self.near(1 - place.core).wait_recv()
        self.near(place.core).wait_send()
        if self.square:
            self.beside(1, place.chip, None, place.across).wait_send()
            self.beside(2, place.chip, None, place.along).wait_send()
            self.beside(3, place.across, 0, place.along).wait_send()
            self.beside(4, place.along, 1, place.across).wait_send()
        else:
            for distance in range(1, place.chips):
                self.far(distance, place.chip).wait_send()


class Reduce:
    def __init__(self, place, sems, row, grad=None, pair=None, mates=None, own=None, line=None, total=None, part=None):
        self.part = part
        self.place, self.sems, self.row = place, sems, row
        self.grad, self.pair, self.mates = grad, pair, mates
        self.own, self.line, self.total = own, line, total

    def copy(self, phase, slot, src, dst, device):
        return pltpu.make_async_remote_copy(
            src_ref=src,
            dst_ref=dst,
            send_sem=self.sems[0].at[self.row + phase, slot],
            recv_sem=self.sems[1].at[self.row + phase, slot],
            device_id=device,
            device_id_type=MESH,
        )

    def copy_a(self):
        place = self.place
        return self.copy(0, 0, self.grad.at[:, 1 - place.core], self.pair, place.sibling)

    def copy_b(self, distance, source=None):
        place = self.place
        slot = place.chip if source is None else source
        return self.copy(
            1, distance, self.pair.at[place.other(distance)], self.mates.at[slot], place.mate(distance)
        )

    def piece(self, block):
        size = (self.total if self.own is None else self.own).shape[0] // self.place.blocks
        return pl.ds(block * size, size)

    def copy_c(self, distance, source=None):
        place = self.place
        slot = place.block if source is None else source
        there = place.peer(distance)
        return self.copy(2, distance, self.own.at[self.piece(there)], self.line.at[slot], {SEQ: there})

    def copy_d(self, distance, source=None):
        place = self.place
        slot = self.piece(place.block if source is None else source)
        return self.copy(3, distance, self.total.at[slot], self.total.at[slot], {SEQ: place.peer(distance)})

    def start_a(self):
        self.copy_a().start()

    def end_a(self):
        place = self.place
        self.copy_a().wait_recv()

        def add(chip, carry):
            self.pair[chip] = (self.pair[chip].astype(f32) + self.grad[chip, place.core].astype(f32)).astype(bf16)
            return carry

        lax.fori_loop(0, place.chips, add, 0)
        self.copy_a().wait_send()

    def start_b(self):
        for distance in range(1, self.place.chips):
            self.copy_b(distance).start()

    def end_b(self):
        place = self.place
        total = self.pair[place.chip].astype(f32)
        for distance in range(1, place.chips):
            source = place.other(place.chips - distance)
            self.copy_b(distance, source).wait_recv()
            total = total + self.mates[source].astype(f32)
        self.own[...] = total.astype(bf16)
        for distance in range(1, place.chips):
            self.copy_b(distance).wait_send()

    def start_c(self):
        for distance in range(1, self.place.blocks):
            self.copy_c(distance).start()

    def end_c(self):
        place = self.place
        mine = self.piece(place.block)
        total = self.own[mine].astype(f32)
        for distance in range(1, place.blocks):
            source = place.peer(place.blocks - distance)
            self.copy_c(distance, source).wait_recv()
            total = total + self.line[source].astype(f32)
        if self.part is None:
            self.total[mine] = total.astype(bf16)
        else:
            self.part[...] = total.astype(bf16)
        for distance in range(1, place.blocks):
            self.copy_c(distance).wait_send()

    def start_d(self):
        for distance in range(1, self.place.blocks):
            self.copy_d(distance).start()

    def end_d(self):
        place = self.place
        for distance in range(1, place.blocks):
            self.copy_d(distance, place.peer(place.blocks - distance)).wait_recv()
        for distance in range(1, place.blocks):
            self.copy_d(distance).wait_send()


def put_blocks(grad, layout, array, first, value):
    chips, cores, unused_blocks, rows, lanes = grad.shape
    for spot in range(value.shape[1] // lanes):
        part = value[:, spot * lanes : (spot + 1) * lanes].astype(bf16)
        grad[:, :, layout.spot(array, first + spot)] = part.reshape((chips, cores, rows, lanes))


def put_down(grad, layout, array, value, part, parts):
    chips, cores, unused_blocks, rows, lanes = grad.shape
    few = chips // parts
    high = value.shape[0] // (few * cores * rows)
    wide = value.shape[1] // lanes
    value = value.astype(bf16).reshape((few, cores, high, rows, value.shape[1]))
    for up in range(high):
        for spot in range(wide):
            grad[pl.ds(part * few, few), :, layout.spot(array, up * wide + spot)] = value[
                :, :, up, :, spot * lanes : (spot + 1) * lanes
            ]


class Refs:
    def __init__(self, names, refs, lazy, flush, layer, layered):
        for name, ref in zip(names, refs, strict=True):
            setattr(self, name, ref)
        self.loads, self.stores = {}, {}
        for number, name in enumerate(lazy):
            far = getattr(self, FAR + name)
            if name in layered:
                far = far.at[layer]
            near = getattr(self, name)
            self.loads[id(near)] = pltpu.make_async_copy(far, near, self.load_sem.at[number])
        for number, name in enumerate(flush):
            near = getattr(self, name)
            self.stores[id(near)] = pltpu.make_async_copy(near, getattr(self, FAR + name), self.store_sem.at[number])

    def fetch(self, *refs):
        for load in [self.loads[id(ref)] for ref in refs] if refs else self.loads.values():
            load.start()

    def ready(self, *refs):
        for ref in refs:
            self.loads[id(ref)].wait()

    def flush(self, *refs):
        for ref in refs:
            self.stores[id(ref)].start()

    def flushed(self):
        for store in self.stores.values():
            store.wait()


class Layout:
    def __init__(self, devices, counts):
        self.parts, self.size = [], 0
        for count in counts:
            per = -(-count // devices)
            self.parts.append((self.size, per, count))
            self.size += per
        self.total = self.size * devices

    def spot(self, array, block):
        base, per, unused_count = self.parts[array]
        return block // per * self.size + base + block % per

    def unused(self):
        taken = {self.spot(array, block) for array, part in enumerate(self.parts) for block in range(part[2])}
        return [block for block in range(self.total) if block not in taken]


def layouts(blocks, halves):
    wides = [(16 // halves, 16 // halves) for half in range(halves - 1)] + [(16 // halves, 16 // halves, 4)]
    counts = (*wides, (12,), (1,), (8,))
    made = [Layout(blocks, item) for item in counts]
    return made[:halves], made[halves], made[halves + 1], made[halves + 2]


def kept_spot(block, halves):
    return block if halves == 1 else block % 2 * 8 + block // 2


def up_part(ref, half, part, halves):
    if halves == 1:
        return flat(ref, tile(part, 512))
    columns = [flat(ref, tile(2 * (4 * part + spot) + half, 128)) for spot in range(4)]
    return jnp.concatenate(columns, axis=1)


def down_part(ref, half, part, parts, halves):
    chips, rows = ref.shape[0] // parts, ref.shape[2] // halves
    value = ref[pl.ds(part * chips, chips), :, half * rows : (half + 1) * rows]
    return value.reshape((-1, value.shape[-1]))


class Ahead:
    def __init__(self, place, step, src, dst, sems):
        self.place, self.step, self.src, self.dst, self.sems = place, step, src, dst, sems
        self.sends = place.block < place.blocks - 1 if step > 0 else place.block > 0
        self.receives = place.block > 0 if step > 0 else place.block < place.blocks - 1

    def copy(self, slot, rows):
        return pltpu.make_async_remote_copy(
            src_ref=self.src.at[rows],
            dst_ref=self.dst.at[rows],
            send_sem=self.sems[0].at[slot],
            recv_sem=self.sems[1].at[slot],
            device_id={SEQ: self.place.block + self.step},
            device_id_type=MESH,
        )

    def start(self, slot, rows):
        @pl.when(self.sends)
        def _():
            self.copy(slot, rows).start()

    def arrived(self, slot, rows):
        @pl.when(self.receives)
        def _():
            self.copy(slot, rows).wait_recv()

    def sent(self, slot, rows):
        @pl.when(self.sends)
        def _():
            self.copy(slot, rows).wait_send()


def flat(ref, cols=slice(None)):
    value = ref[:, :, :, cols]
    return value.reshape((-1, value.shape[-1]))


def flat_rows(ref, part, parts):
    chips = ref.shape[0] // parts
    value = ref[pl.ds(part * chips, chips)]
    return value.reshape((-1, value.shape[-1]))


def normalize(values):
    centred = values - jnp.mean(values, axis=-1, keepdims=True)
    scale = lax.rsqrt(jnp.mean(centred * centred, axis=-1, keepdims=True) + ln_eps)
    return (centred * scale, scale)


def norm_back(grad_out, standard, scale, gain):
    scaled = grad_out * gain
    return scale * (
        scaled
        - jnp.mean(scaled, axis=-1, keepdims=True)
        - standard * jnp.mean(scaled * standard, axis=-1, keepdims=True)
    )


def gelu_pair(x):
    cumulative = 0.5 * (1.0 + lax.erf(x * 0.7071067811865476))
    bell = jnp.exp(-0.5 * x * x)
    return (x * cumulative, cumulative + x * (bell * 0.3989422804014327))


def tile(index, size):
    return pl.ds(pl.multiple_of(index * size, size), size)


def half_masks():
    lane = lax.broadcasted_iota(jnp.int32, (1, 128), 1)
    left = jnp.where(lane < 64, 1.0, 0.0).astype(bf16)
    right = jnp.where(lane < 64, 0.0, 1.0).astype(bf16)
    return (left, right)


def build_marks(kf_ref, lens_ref, first):
    streams, unused_halves, keys, lanes = kf_ref.shape
    key = lax.broadcasted_iota(jnp.int32, (keys, lanes), 0)
    lane = lax.broadcasted_iota(jnp.int32, (keys, lanes), 1)
    coarse = (key // 256 * 256).astype(f32)
    fine = (key % 256).astype(f32)
    for stream in range(streams):
        veiled = jnp.where(jnp.logical_and(first, key < keys // 2 - lens_ref[stream]), 1.0, 0.0)
        for half in range(2):
            spot = lane - 64 * (1 - half)
            value = jnp.where(spot == 6, veiled, jnp.where(spot == 7, 1.0, 0.0))
            value = jnp.where(jnp.logical_and(spot >= 3, spot < 6), fine, value)
            value = jnp.where(jnp.logical_and(spot >= 0, spot < 3), coarse, value)
            kf_ref[stream, half] = value.astype(bf16)


def query_marks(slope, half):
    spot = lax.broadcasted_iota(jnp.int32, (1, 128), 1) - 64 * (1 - half)
    whole_slope = jnp.full((1, 128), slope)
    one = whole_slope.astype(bf16).astype(f32)
    two = (whole_slope - one).astype(bf16).astype(f32)
    three = whole_slope - one - two
    value = jnp.where(spot == 6, masked_score, 0.0)
    for number, part in enumerate((one, two, three)):
        value = jnp.where(jnp.logical_or(spot == number, spot == number + 3), part, value)
    return value.astype(bf16)


def attend(span, heads, q_ref, k_ref, v_ref, kf_ref, slope_of, o_ref, lse_ref, score_refs, chance_refs, stream, early):
    pairs = heads // 2
    step = span // 2
    masks = half_masks()
    key_at = lax.broadcasted_iota(jnp.int32, (step, step), 0)
    query_at = lax.broadcasted_iota(jnp.int32, (step, step), 1)
    down = lax.broadcasted_iota(jnp.int32, (128, 1), 0)
    row_masks = (jnp.where(down < 64, 1.0, 0.0).astype(bf16), jnp.where(down < 64, 0.0, 1.0).astype(bf16))

    def group(first_pair, count):
        work = []
        for pair in [first_pair + i for i in range(count)]:
            cols = tile(pair, 128)
            k_pair = k_ref[tile(stream, 2 * span), cols]
            v_turned = v_ref[tile(stream, 2 * span), cols].T
            for part in range(2):
                for half in range(2):
                    work.append((pair, cols, k_pair, v_turned, part, half))
        peaks, mixed_rows = {}, {}

        def scores(item):
            pair, cols, k_pair, unused_v, part, half = work[item]
            seen = span + part * step
            q_pair = q_ref[pl.ds(pl.multiple_of(stream * span + part * step, step), step), cols]
            q_aug = q_pair * masks[half] + query_marks(slope_of(2 * pair + half), half)
            k_aug = k_pair[: seen + step] * masks[half] + kf_ref[stream, half, : seen + step]
            score = mm(k_aug, q_aug, NT)
            near = jnp.where(key_at <= query_at, score[seen:], masked_score)
            peaks[item] = jnp.maximum(
                jnp.max(score[:seen], axis=0, keepdims=True), jnp.max(near, axis=0, keepdims=True)
            )
            out = score_refs[item % 2]
            out[:seen, :] = score[:seen]
            out[seen : seen + step, :] = near

        def soften(item):
            seen = span + (work[item][4] + 1) * step
            chance_refs[item % 2][:seen, :] = jnp.exp(score_refs[item % 2][:seen, :] - peaks[item]).astype(bf16)

        def mix(item):
            pair, cols, unused_k, v_turned, part, half = work[item]
            seen = span + (part + 1) * step
            v_aug = v_turned[:, :seen] * row_masks[half] + row_masks[1 - half]
            mixed = mm(v_aug, chance_refs[item % 2][:seen, :])
            own = mixed[half * 64 : half * 64 + 64]
            total = mixed[64 - half * 64 : 128 - half * 64]
            mixed_rows[half] = own / total
            lse_ref[pl.ds(stream * heads + 2 * pair + half, 1), part * step : (part + 1) * step] = peaks[
                item
            ] + jnp.log(total[:1])
            if half == 1:
                rows = pl.ds(pl.multiple_of(stream * span + part * step, step), step)
                o_ref[rows, cols] = jnp.concatenate([mixed_rows[0], mixed_rows[1]], axis=0).T.astype(bf16)

        scores(0)
        for item in range(len(work)):
            if item + 1 < len(work):
                scores(item + 1)
            soften(item)
            if item > 0:
                mix(item - 1)
        mix(len(work) - 1)

    def inner(index, carry):
        group(2 * index, 2)
        early(index)
        return carry

    lax.fori_loop(0, pairs // 2, inner, 0)


def forward_kernel(sizes, r):
    (stream_devices, block_devices, streams, span, heads, features, nvec, halves) = sizes
    place = Place(stream_devices, block_devices)
    chip, core = place.chip, place.core
    first = place.block == 0
    layers = r.mem.shape[0]
    width = r.a.shape[1]
    count = streams * span
    step = span // 2
    sems = (r.out_sem, r.in_sem)
    weight_names = ("wp", "wo", "wu", "wd")
    weights = [[getattr(r, f"{name}_{layer}") for name in weight_names] for layer in range(layers)]
    gather_small, gather_head = Gather(place, r.small, sems, 0, direct=True), Gather(place, r.wh, sems, 1)
    gathers = [
        [
            Gather(place, ref, sems, 2 + 4 * layer + number, direct=layer + number == 0)
            for number, ref in enumerate(weights[layer])
        ]
        for layer in range(layers)
    ]
    early_names, look_names, feed_names = ("ap", "q", "k", "v", "low"), ("o", "lse"), ("r1", "a2", "u", "gp")
    saved_names = early_names + look_names + feed_names + ("a", "res")

    def save(layer, name, stream, source=None):
        source = getattr(r, name) if source is None else source
        size = source.shape[0] // streams
        at = tile(stream, size)
        far = getattr(r, FAR + name)
        return pltpu.make_async_copy(
            source.at[at], far.at[layer, at], r.save_sem.at[layer, saved_names.index(name), stream]
        )

    def save_weight(layer, number):
        return pltpu.make_async_copy(
            weights[layer][number],
            getattr(r, f"{FAR}{weight_names[number]}_{layer}"),
            r.weight_sem.at[layer, number],
        )

    r.fetch()
    frames_ahead = Ahead(place, 1, r.frames_wide, r.halo, (r.frame_sem.at[0], r.frame_sem.at[1]))
    next_ahead = Ahead(place, 1, r.nxt, r.behind, (r.next_out, r.next_in))
    every = pl.ds(0, count)

    @pl.when(first)
    def _():
        r.halo[...] = jnp.zeros_like(r.halo)
        r.behind[...] = jnp.zeros_like(r.behind)

    r.small_rows[...] = jnp.zeros_like(r.small_rows)
    r.small_rows[0:nvec, :] = r.vectors[...]
    own_rows = jnp.concatenate([r.input_turned[...], r.small_rows[...].T], axis=1)
    r.small[chip, core] = own_rows.astype(bf16)
    r.frames_tall[...] = jnp.zeros_like(r.frames_tall)
    r.frames_tall[features : features + 16, :] = jnp.where(
        lax.broadcasted_iota(jnp.int32, (16, span), 0) == 0, 1.0, 0.0
    ).astype(bf16)
    for stream in range(streams):
        r.frames_tall[0:features, :] = r.frames[stream]
        r.frames_wide[stream * span : (stream + 1) * span, :] = r.frames_tall[...].T
    r.ready(r.pw)
    r.wp_0[chip, core] = r.pw[0].astype(bf16)
    place.greet(line=True)
    gather_small.push()
    gathers[0][0].push()
    frames_ahead.start(0, every)
    r.ready(r.ow, r.uw, r.dw, r.hw)
    r.wo_0[chip, core] = r.ow[0].astype(bf16)
    r.wu_0[chip, core] = r.uw[0].astype(bf16)
    r.wd_0[chip, core] = r.dw[0].astype(bf16)
    r.wp_1[chip, core] = r.pw[1].astype(bf16)
    r.wo_1[chip, core] = r.ow[1].astype(bf16)
    r.wu_1[chip, core] = r.uw[1].astype(bf16)
    r.wd_1[chip, core] = r.dw[1].astype(bf16)
    r.wh[chip, core] = r.hw[...].astype(bf16)
    build_marks(r.kf, r.memory_len, first)
    r.rows[...] = jnp.zeros_like(r.rows)
    r.ready(r.mem)
    gathers[0][1].push()
    gathers[0][2].push()
    gather_small.relay()
    gathers[0][0].relay()
    gathers[0][3].push()
    gather_small.finish()
    r.rows[:nvec, :] = flat(r.small).astype(f32).T[features : features + nvec]
    gathers[0][0].finish()
    frames_ahead.arrived(0, every)
    residuals = (r.res, r.res_two)

    for layer in range(layers):
        residual, outcome = residuals[layer % 2], residuals[(layer + 1) % 2]
        row = 3 + 4 * layer
        g1, b1, g2, b2 = (r.rows[row + i : row + i + 1, :] for i in range(4))
        wp, wo, wu, wd = weights[layer]
        own_a = r.a if layer == 0 else r.nxt

        def wait_old(names, stream):
            if layer > 0:
                for name in names:
                    save(layer - 1, name, stream).wait()

        wq, wk, wv = (slice(i * width, (i + 1) * width) for i in range(3))

        def project_own(stream):
            wait_old(("q", "k", "v", "low"), stream)
            for part in range(2):
                at = pl.ds(pl.multiple_of(stream * span + part * step, step), step)
                here = pl.ds(pl.multiple_of(stream * 2 * span + span + part * step, step), step)
                if layer == 0:
                    value = mm(r.frames_wide[at, :], flat(r.small), NT)
                    residual[at, :] = value
                    own_a[at, :] = (normalize(value)[0] * g1 + b1).astype(bf16)
                else:
                    value = residual[at, :]
                r.low[at, :] = value.astype(bf16)
                a = own_a[at, :]
                r.q[at, :] = (mm(a, flat(wp, wq)) * 0.125).astype(bf16)
                r.k[here, :] = mm(a, flat(wp, wk)).astype(bf16)
                r.v[here, :] = mm(a, flat(wp, wv)).astype(bf16)
            for name in ("q", "low"):
                save(layer, name, stream).start()
            save(layer, saved_names[-1], stream, residual).start()
            save(layer, saved_names[-2], stream, own_a).start()

        def project_behind(stream):
            wait_old(("ap",), stream)
            for part in range(2):
                at = pl.ds(pl.multiple_of(stream * span + part * step, step), step)
                behind = pl.ds(pl.multiple_of(stream * 2 * span + part * step, step), step)
                if layer == 0:
                    before = mm(r.halo[at, :], flat(r.small), NT)
                    before = jnp.where(first, r.mem[layer, at, :].astype(f32), before)
                    r.pr[at, :] = before
                    ap = (normalize(before)[0] * g1 + b1).astype(bf16)
                else:
                    ap = (normalize(r.mem[layer, at, :].astype(f32))[0] * g1 + b1).astype(bf16)
                    ap = jnp.where(first, ap.astype(f32), r.behind[at, :].astype(f32)).astype(bf16)
                r.ap[at, :] = ap
                r.k[behind, :] = mm(ap, flat(wp, wk)).astype(bf16)
                r.v[behind, :] = mm(ap, flat(wp, wv)).astype(bf16)
            for name in ("ap", "k", "v"):
                save(layer, name, stream).start()
            if layer == 0:
                at = tile(stream, span)
                pltpu.make_async_copy(r.pr.at[at], r.far_pr.at[at], r.pr_sem.at[stream]).start()

        def look(stream):
            wait_old(look_names, stream)

            def early(index):
                def at(when_stream, when_index):
                    return pl.when(jnp.logical_and(stream == when_stream, index == when_index))

                @at(0, 0)
                def _():
                    if layer == 0:
                        gathers[0][3].pass_on()
                    else:
                        gathers[1][2].pass_on()

                @at(0, 1)
                def _():
                    if layer == 0:
                        gathers[0][1].relay()
                        gathers[0][2].relay()
                        gathers[1][0].push()
                        gathers[1][1].push()
                    else:
                        gathers[1][3].pass_on()

                @at(1, 0)
                def _():
                    if layer == 0:
                        gathers[0][3].relay()
                    else:
                        gather_head.pass_on()
                        gathers[1][2].relay()
                        gathers[1][3].relay()

                @at(1, 1)
                def _():
                    if layer == 0:
                        gathers[1][0].pass_on()
                        gathers[1][1].pass_on()
                    else:
                        gather_head.relay()

            attend(
                span,
                heads,
                r.q,
                r.k,
                r.v,
                r.kf,
                lambda head: r.slopes[layer, head],
                r.o,
                r.lse,
                (r.score_one, r.score_two),
                (r.chance_one, r.chance_two),
                stream,
                early,
            )
            for name in look_names:
                save(layer, name, stream).start()

        def feed(stream, carry):
            if layer > 0:
                save(layer - 1, saved_names[-1], stream, outcome).wait()
            wait_old(feed_names, stream)
            at = tile(stream, span)
            after = residual[at, :] + mm(r.o[at, :], flat(wo))
            r.r1[at, :] = after
            a2 = (normalize(after)[0] * g2 + b2).astype(bf16)
            r.a2[at, :] = a2
            for name in feed_names[:2]:
                save(layer, name, stream).start()
            total = after
            parts = wu.shape[3] // 512
            later = mm(a2, flat(wu, slice(0, 512)))
            for part in range(parts):
                cols = slice(part * 512, (part + 1) * 512)
                value = later
                if part + 1 < parts:
                    later = mm(a2, flat(wu, slice((part + 1) * 512, (part + 2) * 512)))
                active, slope = gelu_pair(value)
                active = active.astype(bf16)
                slope = slope.astype(bf16)
                for spot in range(4):
                    there = kept_spot(part * 4 + spot, halves)
                    there = slice(there * 128, (there + 1) * 128)
                    r.u[at, there] = active[:, spot * 128 : (spot + 1) * 128]
                    r.gp[at, there] = slope[:, spot * 128 : (spot + 1) * 128]
                total = total + mm(active, flat_rows(wd, part, parts))
            outcome[at, :] = total
            for name in feed_names[2:]:
                save(layer, name, stream).start()
            if layer == 0:
                g, b = r.rows[row + 4 : row + 5, :], r.rows[row + 5 : row + 6, :]
                r.nxt[at, :] = (normalize(total)[0] * g + b).astype(bf16)
                next_ahead.start(stream, at)

                @pl.when(stream == 0)
                def _():
                    gathers[1][0].relay()
                    gathers[1][1].relay()

            return carry

        if layer == 0:

            def all_project(stream, carry):
                project_own(stream)
                project_behind(stream)

                @pl.when(stream == 0)
                def _():
                    gathers[0][1].pass_on()
                    gathers[0][2].pass_on()

                return carry

            def all_look(stream, carry):
                look(stream)
                return carry

            lax.fori_loop(0, streams, all_project, 0)
            lax.fori_loop(0, streams, all_look, 0)
            for gather in gathers[1][2:] + [gather_head]:
                gather.push()
            for gather in gathers[0][1:]:
                gather.finish()
        else:
            gathers[1][0].finish()
            gathers[1][1].finish()

            def all_own(stream, carry):
                project_own(stream)
                return carry

            def both(stream, carry):
                next_ahead.arrived(stream, tile(stream, span))
                project_behind(stream)
                look(stream)
                return carry

            lax.fori_loop(0, streams, all_own, 0)
            lax.fori_loop(0, streams, both, 0)
            gathers[1][2].finish()
            gathers[1][3].finish()
        for number in range(4):
            save_weight(layer, number).start()
        lax.fori_loop(0, streams, feed, 0)
    gather_head.finish()
    head_stage(place, streams, span, stream_devices, residuals[layers % 2], r)
    last = pltpu.make_async_copy(residuals[layers % 2], r.dr, r.dr_sem.at[0])
    last.start()
    for layer in range(layers):
        for number in range(4):
            save_weight(layer, number).wait()
    for stream in range(streams):
        at = tile(stream, span)
        for name in early_names + look_names + feed_names:
            save(layers - 1, name, stream).wait()
        for layer in range(layers):
            save(layer, saved_names[-2], stream, r.a if layer == 0 else r.nxt).wait()
        save(layers - 1, saved_names[-1], stream, residuals[(layers - 1) % 2]).wait()
        pltpu.make_async_copy(r.pr.at[at], r.far_pr.at[at], r.pr_sem.at[stream]).wait()
        next_ahead.sent(stream, at)
    frames_ahead.sent(0, every)
    last.wait()


def head_stage(place, streams, span, stream_devices, residual, r):
    gain, bias = r.rows[1:2, :], r.rows[2:3, :]
    step = span // 2
    r.acc[...] = jnp.zeros_like(r.acc)
    r.gr_last[...] = jnp.zeros_like(r.gr_last)
    r.loss[...] = jnp.zeros_like(r.loss)
    target_columns = r.targets[...].T
    lane = lax.broadcasted_iota(jnp.int32, target_columns.shape, 1)

    def column(index):
        return jnp.sum(jnp.where(lane == index, target_columns, 0.0), axis=1, keepdims=True)

    def one(index, carry):
        at = tile(index, step)
        stream, part = index // 2, index % 2
        standard, scale = normalize(residual[at, :])
        f = (standard * gain + bias).astype(bf16)
        z = mm(f, flat(r.wh))
        per = step // 128
        target = jnp.concatenate([column(index * per + i) for i in range(per)], axis=0)
        frames = jnp.full((step, 1), r.frame_count[stream])
        position = lax.broadcasted_iota(jnp.int32, (step, 1), 0) + (place.block * span + part * step)
        share = jnp.where(position < frames, 1.0 / (frames.astype(f32) * (streams * stream_devices)), 0.0)
        peak = jnp.max(z, axis=-1, keepdims=True)
        raised = jnp.exp(z - peak)
        total = jnp.sum(raised, axis=-1, keepdims=True)
        code = lax.broadcasted_iota(jnp.int32, z.shape, 1)
        hit = code == target.astype(jnp.int32)
        picked = jnp.sum(jnp.where(hit, z, 0.0), axis=-1, keepdims=True)
        r.loss[...] += jnp.sum(share * (peak + jnp.log(total) - picked))
        soft = raised * (1.0 / total)
        dz = (share * jnp.where(hit, soft - 1.0, soft)).astype(bf16)
        r.acc[...] += mm(f, dz, TN)
        df = mm(dz, flat(r.wh), NT)
        r.gr_last[0:1, :] += jnp.sum(df * standard, axis=0, keepdims=True)
        r.gr_last[1:2, :] += jnp.sum(df, axis=0, keepdims=True)
        residual[at, :] = norm_back(df, standard, scale, gain)
        return carry

    lax.fori_loop(0, streams * 2, one, 0)
    put_blocks(r.grad_head, layouts(place.blocks, 1)[3], 0, 0, r.acc[...])


def attend_back(streams, span, heads, refs, early, between):
    (q_ref, k_ref, v_ref, o_ref, lse_ref, kf_ref, slope_of, do_ref, dq_ref, dk_ref, dv_ref, gs_ref, p_ref, ds_ref) = refs
    pairs = heads // 2
    step = span // 2
    masks = half_masks()
    key_at = lax.broadcasted_iota(jnp.int32, (step, step), 0)
    query_at = lax.broadcasted_iota(jnp.int32, (step, step), 1)
    head_row = lax.broadcasted_iota(jnp.int32, (8, 128), 0)
    place = lax.broadcasted_iota(jnp.int32, (1, step), 1)
    gs_ref[...] = jnp.zeros_like(gs_ref)

    def one(stream, pair):
        cols = tile(pair, 128)
        k_pair = k_ref[tile(stream, 2 * span), cols]
        v_pair = v_ref[tile(stream, 2 * span), cols]
        k_augs = [k_pair * masks[half] + kf_ref[stream, half] for half in range(2)]
        queries, outs = [], []
        for part in range(2):
            seen = span + part * step
            rows = pl.ds(pl.multiple_of(stream * span + part * step, step), step)
            q_pair, do_pair = q_ref[rows, cols], do_ref[rows, cols]
            both = (do_pair.astype(f32) * o_ref[rows, cols].astype(f32)).T
            for half in range(2):
                head = 2 * pair + half
                q_own, do_own = q_pair * masks[half], do_pair * masks[half]
                queries.append(q_own)
                outs.append(do_own)
                delta = jnp.sum(both[half * 64 : half * 64 + 64], axis=0, keepdims=True)
                log_total = lse_ref[pl.ds(stream * heads + head, 1), part * step : (part + 1) * step]
                scores = mm(k_augs[half][: seen + step], q_own + query_marks(slope_of(head), half), NT)
                dp = mm(v_pair[: seen + step], do_own, NT)
                at = slice(half * step, (half + 1) * step)
                for low, high in ((0, seen), (seen, seen + step)):
                    score = scores[low:high]
                    if low:
                        score = jnp.where(key_at <= query_at, score, masked_score)
                    chance = jnp.exp(score - log_total)
                    p_ref[part, low:high, at] = chance.astype(bf16)
                    ds_ref[part, low:high, at] = (chance * (dp[low:high] - delta)).astype(bf16)
        common = span + step
        q_parts = [jnp.concatenate(queries[2 * part : 2 * part + 2], axis=0) for part in range(2)]
        do_parts = [jnp.concatenate(outs[2 * part : 2 * part + 2], axis=0) for part in range(2)]
        base = stream * 2 * span
        for source, out_ref, parts in ((p_ref, dv_ref, do_parts), (ds_ref, dk_ref, q_parts)):
            out_ref[pl.ds(pl.multiple_of(base, step), common), cols] = (
                mm(source[0, :common, :], parts[0]) + mm(source[1, :common, :], parts[1])
            ).astype(bf16)
            out_ref[pl.ds(pl.multiple_of(base + common, step), step), cols] = mm(
                source[1, common:, :], parts[1]
            ).astype(bf16)
        k_turned = [k_aug.T for k_aug in k_augs]
        for part in range(2):
            seen = span + (part + 1) * step
            done = []
            for half in range(2):
                head = 2 * pair + half
                turned = mm(k_turned[half][:, :seen], ds_ref[part, :seen, half * step : (half + 1) * step])
                done.append(turned[half * 64 : half * 64 + 64] * 0.125)
                base_row = 64 - half * 64
                lean = (
                    turned[base_row : base_row + 1]
                    + turned[base_row + 3 : base_row + 4]
                    - (place + (part * step + span)).astype(f32) * turned[base_row + 7 : base_row + 8]
                )
                gs_ref[...] += jnp.where(head_row == head, jnp.sum(lean), 0.0)
            rows = pl.ds(pl.multiple_of(stream * span + part * step, step), step)
            dq_ref[rows, cols] = jnp.concatenate(done, axis=0).T.astype(bf16)

    def over(stream, carry):
        def inner(pair, carry):
            one(stream, pair)
            early(stream * pairs + pair)
            return carry

        carry = lax.fori_loop(0, pairs, inner, carry)
        between(stream)
        return carry

    lax.fori_loop(0, streams, over, 0)


def backward_kernel(layer, sizes, r):
    (stream_devices, block_devices, streams, span, heads, features, nvec, halves) = sizes
    place = Place(stream_devices, block_devices)
    width = r.a.shape[1]
    count = streams * span
    first = place.block == 0
    row = 3 + 4 * layer
    g1, g2 = r.rows[row : row + 1, :], r.rows[row + 2 : row + 3, :]
    step = 256
    tiles = count // step
    sems = (r.out_sem, r.in_sem)
    wide_layouts, layout_b, layout_small, unused_head = layouts(place.blocks, halves)

    def wide_reduce(half, row, *names):
        return Reduce(place, sems, row, **{name: getattr(r, f"{name}_{WIDE[half]}") for name in names})

    broads = [wide_reduce(half, 4 * half, *REDUCED[:4]) for half in range(halves)]
    row_b = 4 * halves
    if layer == 0:
        for half, broad in enumerate(broads):
            broad.line = getattr(r, f"{REDUCED[4]}_{WIDE[half]}")
            if half < halves - 1:
                broad.total = getattr(r, f"{REDUCED[6]}_{WIDE[half]}")
            else:
                broad.part = getattr(r, f"{REDUCED[5]}_{WIDE[half]}")
        dones = [
            Reduce(
                place,
                sems,
                row_b + 4 + 4 * half,
                **{name: getattr(r, f"{name}_one_{WIDE[half]}") for name in REDUCED[3:7:1] if name != REDUCED[5]},
            )
            for half in range(halves)
        ]
        narrow = Reduce(
            place, sems, 4 + 8 * halves, grad=r.grad_b, pair=r.pair_b, mates=r.mates_b, own=r.own_b
        )
        done_b = Reduce(
            place, sems, row_b, pair=r.pair_b_one, mates=r.mates_b_one, own=r.own_b_one, line=r.line_b_one, total=r.total_b_one
        )
    else:
        narrow = Reduce(place, sems, row_b, grad=r.grad_b, pair=r.pair_b)
        head = Reduce(
            place, sems, row_b + 4, grad=r.grad_head, pair=r.pair_head, mates=r.mates_head, own=r.own_head, line=r.line_head, total=r.total_head
        )
        back = Ahead(place, -1, r.dap, r.back, (r.back_out, r.back_in))

        @pl.when(place.block == place.blocks - 1)
        def _():
            r.back[...] = jnp.zeros_like(r.back)

    for grad, layout in [(broad.grad, layout) for broad, layout in zip(broads, wide_layouts)] + [(r.grad_b, layout_b)]:
        for block in layout.unused():
            grad[:, :, block] = jnp.zeros(grad.shape[:2] + grad.shape[3:], bf16)
    r.gr[...] = jnp.zeros_like(r.gr)
    hidden_parts = r.wu.shape[3] // 512

    def stream_in(part, slot):
        cols = tile(part, 512)
        return (
            pltpu.make_async_copy(r.u.at[layer, :, cols], r.u_two.at[slot], r.u_sem.at[0, slot]),
            pltpu.make_async_copy(r.gp.at[layer, :, cols], r.gp_two.at[slot], r.u_sem.at[1, slot]),
        )

    first_loads = []
    if layer == 0:
        first_loads = [
            pltpu.make_async_copy(r.dr1_in, r.dr, r.first_sem.at[0]),
            pltpu.make_async_copy(r.r.at[1], r.da, r.first_sem.at[1]),
            pltpu.make_async_copy(r.da_in, r.wide_one, r.first_sem.at[2]),
        ]
        late_loads = [
            pltpu.make_async_copy(r.r.at[0], r.wide_one, r.first_sem.at[3]),
            pltpu.make_async_copy(r.pr, r.r1, r.first_sem.at[4]),
        ]
    else:
        first_loads = [pltpu.make_async_copy(r.dr_in, r.dr, r.first_sem.at[0])]
    for load in first_loads:
        load.start()
    for load in stream_in(0, 0):
        load.start()
    r.fetch(r.wd, r.a2, r.wu)

    def fetch_rest():
        r.fetch(r.r1, r.wo, r.o, r.lse, r.q, r.k, r.v, r.wp, r.a, r.ap)
        if layer == 1:
            r.fetch(r.mem)

    place.greet(column=True)
    if layer == 0:
        for done in dones:
            done.start_c()
        done_b.start_b()

        g = r.rows[row + 4 : row + 5, :]

        def join(index, carry):
            at = tile(index, step)
            standard, scale = normalize(r.da[at, :])
            da = r.wide_one[at, :] + r.back[at, :].astype(f32)
            r.gr[4:5, :] += jnp.sum(da * standard, axis=0, keepdims=True)
            r.gr[5:6, :] += jnp.sum(da, axis=0, keepdims=True)
            r.dr[at, :] = r.dr[at, :] + norm_back(da, standard, scale, g)
            return carry

        build_marks(r.kf, r.memory_len, first)
        for load in first_loads:
            load.wait()
        fetch_rest()
        lax.fori_loop(0, tiles, join, 0)
        late_loads[0].start()
    else:
        head.start_a()
        build_marks(r.kf, r.memory_len, first)
        first_loads[0].wait()
        fetch_rest()

    r.da[...] = jnp.zeros_like(r.da)
    r.ready(r.wd, r.a2, r.wu)
    r.turned[...] = r.a2[...].T
    parts = hidden_parts
    each = parts // halves

    def feed(half, spot, carry):
        part = half * each + spot
        slot = part % 2

        @pl.when(part + 1 < parts)
        def _():
            for load in stream_in(part + 1, 1 - slot):
                load.start()

        for load in stream_in(part, slot):
            load.wait()
        dy = r.dr[...].astype(bf16)
        dh = (mm(dy, down_part(r.wd, half, spot, each, halves), NT) * r.gp_two[slot].astype(f32)).astype(bf16)
        put_down(broads[half].grad, wide_layouts[half], 0, mm(r.u_two[slot], dy, TN), spot, each)
        put_blocks(broads[half].grad, wide_layouts[half], 1, 4 * spot, mm(r.turned[...], dh))
        r.da[...] += mm(dh, up_part(r.wu, half, spot, halves), NT)
        if half == 0 and layer == 1:

            @pl.when(spot == 0)
            def _():
                head.end_a()
                head.start_b()

        if half == 1:

            @pl.when(spot == 0)
            def _():
                broads[0].end_a()
                broads[0].start_b()

        return carry

    for half in range(halves):
        lax.fori_loop(0, each, functools.partial(feed, half), 0)
        if half < halves - 1:
            broads[half].start_a()
    r.ready(r.r1, r.wo, r.o, r.lse)

    def middle(index, carry):
        at = tile(index, step)
        standard, scale = normalize(r.r1[at, :])
        da = r.da[at, :]
        r.gr[2:3, :] += jnp.sum(da * standard, axis=0, keepdims=True)
        r.gr[3:4, :] += jnp.sum(da, axis=0, keepdims=True)
        dr = r.dr[at, :] + norm_back(da, standard, scale, g2)
        r.dr[at, :] = dr
        r.do[at, :] = mm(dr.astype(bf16), flat(r.wo), NT).astype(bf16)
        return carry

    lax.fori_loop(0, tiles, middle, 0)
    if layer == 0:
        late_loads[1].start()
    put_blocks(broads[-1].grad, wide_layouts[-1], 2, 0, mm(r.o[...], r.dr[...].astype(bf16), TN))
    broads[-1].start_a()
    if layer == 0:
        for done in dones:
            done.end_c()
        done_b.end_b()
        done_b.start_c()
        for done in dones:
            done.start_d()
    else:
        head.end_b()
        head.start_c()
    wk, wv = (slice(i * width, (i + 1) * width) for i in (1, 2))

    def behind_gradient(at, behind):
        return mm(r.dk[behind, :], flat(r.wp, wk), NT) + mm(r.dv[behind, :], flat(r.wp, wv), NT)

    def early(index):
        @pl.when(index == 1)
        def _():
            broads[-1].end_a()
            broads[-1].start_b()
            if layer == 1:
                head.end_c()
                head.start_d()

    def between(stream):
        if layer == 0:

            @pl.when(stream == 0)
            def _():
                done_b.end_c()
                done_b.start_d()

            if halves > 1:

                @pl.when(stream == 1)
                def _():
                    broads[0].end_b()
                    broads[0].start_c()

        else:
            for part in range(span // step):
                at = pl.ds(pl.multiple_of(stream * span + part * step, step), step)
                behind = pl.ds(pl.multiple_of(stream * 2 * span + part * step, step), step)
                r.dap[at, :] = behind_gradient(at, behind).astype(bf16)
            back.start(stream, tile(stream, span))


    r.ready(r.q, r.k, r.v, r.wp)
    attend_back(
        streams,
        span,
        heads,
        (r.q, r.k, r.v, r.o, r.lse, r.kf, lambda head: r.slopes[layer, head], r.do, r.dq, r.dk, r.dv, r.gs, r.u_two, r.gp_two),
        early,
        between,
    )

    r.ready(r.a, r.ap)
    r.turned[...] = r.a[...].T
    put_blocks(r.grad_b, layout_b, 0, 0, mm(r.turned[...], r.dq[...]))
    for spot, ref in ((1, r.dk), (2, r.dv)):
        total = jnp.zeros((width, width), f32)
        for stream in range(streams):
            behind = slice(stream * 2 * span, stream * 2 * span + span)
            here = slice(stream * 2 * span + span, (stream + 1) * 2 * span)
            own = slice(stream * span, (stream + 1) * span)
            total = total + mm(r.turned[:, own], ref[here, :])
            total = total + mm(r.ap[own, :], ref[behind, :], TN)
        put_blocks(r.grad_b, layout_b, 0, 4 * spot, total)

    if layer == 0:
        r.small_acc[...] = jnp.zeros_like(r.small_acc)
        for load in late_loads:
            load.wait()
        narrow.start_a()
        broads[-1].end_b()
        broads[-1].start_c()
        for broad in broads[:-1]:
            broad.end_c()
            broad.start_d()
    else:
        narrow.start_a()
        r.ready(r.mem)

    def finish(stream, carry):
        for part in range(span // step):
            at = pl.ds(pl.multiple_of(stream * span + part * step, step), step)
            behind = pl.ds(pl.multiple_of(stream * 2 * span + part * step, step), step)
            here = pl.ds(pl.multiple_of(stream * 2 * span + span + part * step, step), step)
            da = (
                mm(r.dq[at, :], flat(r.wp, slice(0, width)), NT)
                + mm(r.dk[here, :], flat(r.wp, wk), NT)
                + mm(r.dv[here, :], flat(r.wp, wv), NT)
            )
            if layer == 0:
                dap = behind_gradient(at, behind)
                standard, scale = normalize(r.wide_one[at, :])
                before, before_scale = normalize(r.r1[at, :])
                r.gr[0:1, :] += jnp.sum(da * standard + dap * before, axis=0, keepdims=True)
                r.gr[1:2, :] += jnp.sum(da + dap, axis=0, keepdims=True)
                dr = r.dr[at, :] + norm_back(da, standard, scale, g1)
                drp = norm_back(dap, before, before_scale, g1)
                drp = jnp.where(first, 0.0, drp)
                r.gr[6:7, :] += jnp.sum(dr + drp, axis=0, keepdims=True)
                r.small_acc[...] += mm(dr.astype(bf16), r.frames[at, :], TN)
                r.small_acc[...] += mm(drp.astype(bf16), r.halo[at, :], TN)
                if part == 0:

                    @pl.when(stream == 1)
                    def _():
                        narrow.end_a()
                        narrow.start_b()

            else:
                r.da[at, :] = da
                before, before_scale = normalize(r.mem[at, :].astype(f32))
                dap = jnp.where(first, r.dap[at, :].astype(f32), 0.0)
                r.gr[0:1, :] += jnp.sum(dap * before, axis=0, keepdims=True)
                r.gr[1:2, :] += jnp.sum(dap, axis=0, keepdims=True)
        return carry

    lax.fori_loop(0, streams, finish, 0)
    if layer == 0:
        listed = [r.gr[6:7, :], r.gr_last[0:2, :], r.gr[0:4, :], r.gr_one[0:2, :] + r.gr[4:6, :], r.gr_one[2:4, :]]
        listed = [jnp.zeros((features, width), f32)] + listed + [jnp.zeros((128 - features - nvec, width), f32)]
        lane = lax.broadcasted_iota(jnp.int32, (1, 128), 1)
        merged = jnp.where(lane < features, r.small_acc[...], jnp.concatenate(listed, axis=0).T)
        for block in layout_small.unused():
            r.grad_small[:, :, block] = jnp.zeros(r.grad_small.shape[:2] + r.grad_small.shape[3:], bf16)
        put_blocks(r.grad_small, layout_small, 0, 0, merged)
        done_b.end_d()
        for done in dones:
            done.end_d()
        for broad in broads[:-1]:
            broad.end_d()
        broads[-1].end_c()
        narrow.end_b()
    else:
        head.end_d()
        narrow.end_a()
        for broad in broads:
            broad.end_b()
        for stream in range(streams):
            at = tile(stream, span)
            back.sent(stream, at)
            back.arrived(stream, at)


def lanes_of(entries):
    lane = lax.broadcasted_iota(jnp.int32, (1, 128), 1)
    row = jnp.zeros((1, 128), f32)
    for number, value in entries:
        row = jnp.where(lane == number, value, row)
    return row


def pick(row, number):
    lane = lax.broadcasted_iota(jnp.int32, (1, 128), 1)
    return jnp.sum(jnp.where(lane == number, row, 0.0))


class State:
    def __init__(self, blocks, layers, rows, halves, wides, narrows, head):
        wide_layouts, plain, last, head_layout = layouts(blocks, halves)
        self.small = last.spot(0, 0)
        self.rows, self.halves = rows, halves
        self.items = []
        for layer in range(layers):
            self.items.append((1, layer, narrows[layer], plain, 0, 1 + layer, 0))
            self.items.append((2, layer, wides[layer][-1], wide_layouts[-1], 2, 1 + layers + layer, 0))
            for half in range(halves):
                total, layout = wides[layer][half], wide_layouts[half]
                self.items.append((3, layer, total, layout, 1, 1 + 2 * layers + layer, half))
                self.items.append((4, layer, total, layout, 0, 1 + 3 * layers + layer, half))
        self.items.append((5, None, head, head_layout, 0, 1 + 4 * layers, 0))
        self.vector_start = 2 + 4 * layers

    def place(self, array, layer, block, half):
        across, up = block, 0
        if array == 3 and self.halves == 2:
            across = 2 * block + half
        if array == 4:
            across, up = block % 4, block // 4 + half * (4 // self.halves)
        rows, cols = up * self.rows, across * 128
        if not isinstance(block, int):
            rows, cols = pl.multiple_of(rows, self.rows), pl.multiple_of(cols, 128)
        where = (pl.ds(rows, self.rows), pl.ds(cols, 128))
        return where if layer is None else (layer,) + where


def state_of(block_devices, layers, halves, r):
    zero = [getattr(r, f"{REDUCED[6]}_{WIDE[half]}") for half in range(halves)]
    one = [getattr(r, f"{REDUCED[6]}_one_{WIDE[half]}") for half in range(halves)]
    return State(
        block_devices, layers, r.total_b.shape[1], halves, (zero, one), (r.total_b, r.total_b_one), r.total_head
    )


def tail_kernel(sizes, layers, r):
    (stream_devices, block_devices, streams, span, heads, features, nvec, halves) = sizes
    place = Place(stream_devices, block_devices)
    index = lax.axis_index(STREAM)
    sems = (r.out_sem, r.in_sem)
    wide_name = WIDE[halves - 1]
    broad = Reduce(place, sems, 0, total=getattr(r, f"{REDUCED[6]}_{wide_name}"))
    narrow = Reduce(place, sems, 4 * halves, own=r.own_b, line=r.line_b, total=r.total_b)
    small = Reduce(
        place,
        sems,
        4 * halves + 4,
        grad=r.grad_small,
        pair=r.pair_small,
        mates=r.mates_small,
        own=r.own_small,
        line=r.line_small,
        total=r.total_small,
    )
    r.fetch()
    broad.total[broad.piece(place.block)] = getattr(r, f"{REDUCED[5]}_{wide_name}")[...]
    barrier = pltpu.get_barrier_semaphore()
    everyone = stream_devices * block_devices
    mine = place.block * stream_devices + index

    def device_of(number):
        return {SEQ: number // stream_devices, STREAM: number % stream_devices}

    def greet(distance, carry):
        device = device_of((mine + distance) % everyone)
        pl.semaphore_signal(barrier, inc=1, device_id=device, device_id_type=MESH)
        return carry

    lax.fori_loop(1, everyone, greet, 0)
    pl.semaphore_wait(barrier, everyone - 1)
    small.start_a()
    narrow.start_c()
    rows = r.total_b.shape[1]
    state = state_of(block_devices, layers, halves, r)
    arrays = [[getattr(r, f"{kind}_{number}") for number in range(7)] for kind in KINDS]
    weights, firsts, seconds = arrays
    square = jnp.zeros((rows, 128), f32)
    finished = [getattr(r, f"{REDUCED[6]}_{WIDE[half]}") for half in range(halves)] + [r.total_b_one, r.total_head]
    finished += [getattr(r, f"{REDUCED[6]}_one_{WIDE[half]}") for half in range(halves)]
    for ref in finished:
        size = ref.shape[0] // block_devices
        value = ref[pl.ds(place.block * size, size)].astype(f32)
        square = square + jnp.sum(value * value, axis=0)
    small.end_a()
    small.start_b()
    for array in arrays:
        r.ready(*array)

    shares = []
    for array, layer, total, layout, part, matrix, half in state.items:
        base, per, count = layout.parts[part]
        for number in range(per):
            block = place.block * per + number
            valid = jnp.where(block < count, 1.0, 0.0)
            spot = state.place(array, layer, jnp.minimum(block, count - 1), half)
            shares.append((array, spot, total, place.block * layout.size + base + number, matrix, valid))
    edge = jnp.where(place.block == 0, 1.0, 0.0)

    def matrix_squares(value_of, turned, vector_rows, base):
        found = {}
        for array, spot, total, block, matrix, valid in shares:
            value = value_of(array, spot, total, block)
            value = value * value * valid
            found[matrix] = value if matrix not in found else found[matrix] + value
        entries = [(base + matrix, jnp.sum(value)) for matrix, value in found.items()]
        entries.append((base, jnp.sum(turned * turned) * edge))
        row = lanes_of(entries)
        lane = lax.broadcasted_iota(jnp.int32, (nvec, 128), 1)
        down = lax.broadcasted_iota(jnp.int32, (nvec, 128), 0)
        column = jnp.sum(vector_rows * vector_rows, axis=1, keepdims=True) * edge
        return row + jnp.sum(jnp.where(lane == base + state.vector_start + down, column, 0.0), axis=0, keepdims=True)

    weight_row = matrix_squares(
        lambda array, spot, total, block: weights[array][spot], weights[0][...], weights[6][...], 64
    )
    narrow.end_c()
    size = r.total_b.shape[0] // block_devices
    value = r.total_b[pl.ds(place.block * size, size)].astype(f32)
    square = square + jnp.sum(value * value, axis=0)
    small.end_b()
    small.start_c()

    def exchange(ref, first, meanwhile=None):
        def copy(distance, source):
            return pltpu.make_async_remote_copy(
                src_ref=ref.at[source],
                dst_ref=ref.at[source],
                send_sem=r.all_out.at[first + distance],
                recv_sem=r.all_in.at[first + distance],
                device_id=device_of((mine + distance) % everyone),
                device_id_type=MESH,
            )

        def send(distance, carry):
            copy(distance, mine).start()
            return carry

        def receive(distance, carry):
            copy(distance, (mine + everyone - distance) % everyone).wait_recv()
            return carry

        def sent(distance, carry):
            copy(distance, mine).wait_send()
            return carry

        lax.fori_loop(1, everyone, send, 0)
        if meanwhile is not None:
            meanwhile()
        lax.fori_loop(1, everyone, receive, 0)
        lax.fori_loop(1, everyone, sent, 0)
        return jnp.sum(ref[...], axis=0)

    lane = lax.broadcasted_iota(jnp.int32, (8, 128), 1)
    down = lax.broadcasted_iota(jnp.int32, (8, 128), 0)
    plain = jnp.where(lane == 1, r.loss[...], 0.0) * jnp.where(down == 0, 1.0, 0.0)
    for layer, ref in enumerate((r.gs_zero, r.gs_one)):
        plain = plain + jnp.where(lane == 16 + layer * heads + down, ref[...], 0.0)
    plain = jnp.sum(plain, axis=0, keepdims=True) + weight_row
    small.end_c()
    size = r.total_small.shape[0] // block_devices
    value = r.total_small[pl.ds(place.block * size, size)].astype(f32)
    square = square + jnp.sum(value * value, axis=0)
    r.rows_one[mine] = plain + lanes_of([(0, jnp.sum(square))])

    def hand_round():
        broad.start_d()
        narrow.start_d()
        small.start_d()

    sums = exchange(r.rows_one, 0, hand_round)
    lane = lax.broadcasted_iota(jnp.int32, (1, 128), 1)
    slope_lanes = jnp.logical_and(lane >= 16, lane < 16 + layers * heads)
    clip = jnp.sqrt(
        jnp.full((1, 128), pick(sums, 0)) + jnp.sum(jnp.where(slope_lanes, sums * sums, 0.0), axis=1, keepdims=True)
    )
    factor = jnp.minimum(1.0, clip_limit / clip)
    scale = factor[:, 0:1]

    def direction(weight, grad, first, second):
        return adam_direction(weight, grad, first, second, decay_rate)[2]

    both = r.total_small[place.block * size + state.small].astype(f32)
    turned = direction(weights[0][...], both[:, :features] * scale, firsts[0][...], seconds[0][...])
    vector_rows = direction(
        weights[6][...], both.T[features : features + nvec] * scale, firsts[6][...], seconds[6][...]
    )
    r.rows_two[mine] = matrix_squares(
        lambda array, spot, total, block: direction(
            weights[array][spot], total[block].astype(f32) * factor, firsts[array][spot], seconds[array][spot]
        ),
        turned,
        vector_rows,
        0,
    )
    r.sums[0:1, :] = exchange(r.rows_two, everyone)
    r.sums[1:2, :] = jnp.concatenate([sums[:, 64:], sums[:, :64]], axis=1)
    r.sums[2:3, :] = sums
    r.sums[3:4, :] = clip
    r.sums[4:5, :] = factor
    broad.end_d()
    narrow.end_d()
    small.end_d()


def update_kernel(sizes, layers, r):
    (stream_devices, block_devices, streams, span, heads, features, nvec, halves) = sizes
    keep = pltpu.make_async_copy(r.low, r.layer_inputs, r.keep_sem.at[0])
    weights, firsts, seconds = ([getattr(r, f"{kind}_{number}") for number in range(7)] for kind in KINDS)
    fresh, new_firsts, new_seconds = ([getattr(r, f"new_{kind}_{number}") for number in range(7)] for kind in KINDS)
    state = state_of(block_devices, layers, halves, r)
    totals = {id(item[2]): item[2] for item in state.items}
    r.fetch(r.total_small, *totals.values())
    for number in (0, 6, 1, 2):
        r.fetch(weights[number], firsts[number], seconds[number])
    r.ready(r.total_small, *totals.values())
    factor = r.sums[4:5, :]
    scale = factor[:, 0:1]
    norms = jnp.sqrt(r.sums[0:2, :])
    ratios = norms[1:2] / norms[0:1]
    small = r.total_small[state.small].astype(f32)
    lane = lax.broadcasted_iota(jnp.int32, (nvec, 128), 1)
    down = lax.broadcasted_iota(jnp.int32, (nvec, 128), 0)
    vector_ratio = jnp.sum(jnp.where(lane == state.vector_start + down, ratios, 0.0), axis=1, keepdims=True)

    def finish(array):
        r.flush(fresh[array], new_firsts[array], new_seconds[array])

    for array, grad, ratio in (
        (0, small[:, :features], jnp.full((1, 1), pick(ratios, 0))),
        (6, small.T[features : features + nvec], vector_ratio),
    ):
        r.ready(weights[array], firsts[array], seconds[array])
        weight = weights[array][...]
        first, second, direction = adam_direction(
            weight, grad * scale, firsts[array][...], seconds[array][...], decay_rate
        )
        new_firsts[array][...] = first
        new_seconds[array][...] = second
        fresh[array][...] = weight - lamb_rate * ratio * direction
        finish(array)
    for number in range(1, 6):
        if number + 2 < 6:
            r.fetch(weights[number + 2], firsts[number + 2], seconds[number + 2])
        elif number + 2 == 6:
            r.fetch(r.low)
        r.ready(weights[number], firsts[number], seconds[number])
        for array, layer, total, layout, part, matrix, half in state.items:
            if array != number:
                continue
            ratio = jnp.full((1, 128), lamb_rate * pick(ratios, matrix))
            for block in range(layout.parts[part][2]):
                spot = state.place(array, layer, block, half)
                weight = weights[array][spot]
                first, second, direction = adam_direction(
                    weight,
                    total[layout.spot(part, block)].astype(f32) * factor,
                    firsts[array][spot],
                    seconds[array][spot],
                    decay_rate,
                )
                new_firsts[array][spot] = first
                new_seconds[array][spot] = second
                fresh[array][spot] = weight - ratio * direction
        finish(number)
    r.ready(r.low)
    keep.start()
    sums = r.sums[2:3, :]
    grad = jnp.concatenate([sums[:, 16 + layer * heads : 16 + (layer + 1) * heads] for layer in range(layers)], axis=0)
    slopes = r.slopes[...]
    first, second, direction = adam_direction(slopes, grad * scale, r.first_slopes[...], r.second_slopes[...], 0.0)
    r.new_first_slopes[...] = first
    r.new_second_slopes[...] = second
    r.fresh_slopes[...] = slopes - slope_rate * direction
    count = state.vector_start + nvec
    r.norms[0:1, 0:count] = norms[1:2, :count]
    r.norms[1:2, 0:count] = norms[0:1, :count]
    r.norms[0:1, count : count + 1] = jnp.full((1, 1), jnp.sqrt(jnp.sum(slopes * slopes)))
    r.norms[1:2, count : count + 1] = jnp.full((1, 1), jnp.sqrt(jnp.sum(direction * direction)))
    r.loss[...] = sums[:, 1:2]
    r.clip[...] = r.sums[3:4, 0:1]
    r.flushed()
    keep.wait()


def whole(space=pltpu.VMEM):
    return pl.BlockSpec(memory_space=space)


def call_named(
    kernel,
    ins,
    outs,
    scratch=None,
    sems=None,
    any_ins=None,
    lazy=None,
    flush=None,
    any_outs=None,
    smem=None,
    layer=None,
    layered=(),
    flops=0,
    collective=None,
):
    any_ins, lazy, flush = any_ins or {}, lazy or {}, flush or {}
    any_outs, smem = any_outs or {}, smem or {}
    scratch, sems = dict(scratch or {}), dict(sems or {})
    dma = pltpu.SemaphoreType.DMA
    for key, array in lazy.items():
        scratch[key] = (array.shape[1:] if key in layered else array.shape, array.dtype)
    scratch.update(flush)
    if lazy:
        sems.update(load_sem=dma((len(lazy),)))
    if flush:
        sems.update(store_sem=dma((len(flush),)))
    far = [FAR + key for key in lazy]
    names = list(ins) + list(any_ins) + far + list(smem)
    names += list(outs) + list(any_outs) + [FAR + key for key in flush] + list(scratch) + list(sems)
    out_shapes = list(outs.values()) + list(any_outs.values()) + list(flush.values())
    made = pl.pallas_call(
        lambda *refs: kernel(Refs(names, refs, lazy, flush, layer, layered)),
        name=kernel.func.__name__ if layer is None else f"{kernel.func.__name__}_{layer}",
        out_shape=[jax.ShapeDtypeStruct(*out) for out in out_shapes],
        in_specs=[whole()] * len(ins)
        + [whole(pl.ANY)] * (len(any_ins) + len(lazy))
        + [whole(pltpu.SMEM)] * len(smem),
        out_specs=[whole()] * len(outs) + [whole(pl.ANY)] * (len(any_outs) + len(flush)),
        scratch_shapes=[pltpu.VMEM(*item) for item in scratch.values()] + list(sems.values()),
        compiler_params=pltpu.CompilerParams(
            vmem_limit_bytes=VMEM_LIMIT, collective_id=collective, has_side_effects=collective is not None
        ),
        cost_estimate=pl.CostEstimate(flops=flops, bytes_accessed=20000000, transcendentals=0),
    )(*ins.values(), *any_ins.values(), *lazy.values(), *smem.values())
    return dict(zip(list(outs) + list(any_outs) + list(flush), made))


class Made:
    def __init__(self, *args, **options):
        for name, array in call_named(*args, **options).items():
            setattr(self, name, array)


class Groups:
    def __init__(self, layout, shapes):
        self.layout = layout
        for name, shape in shapes.items():
            setattr(self, name, shape)


def adam_direction(weight, grad, first, second, decay):
    new_first = beta_one * first + (1.0 - beta_one) * grad
    new_second = beta_two * second + (1.0 - beta_two) * grad * grad
    second_hat = new_second * (1.0 / (1.0 - beta_two**STEP))
    below = second_hat * lax.rsqrt(second_hat) + adam_eps
    return (new_first, new_second, (new_first * (1.0 / (1.0 - beta_one**STEP))) / below + decay * weight)


def shards(
    frames,
    targets,
    frame_count,
    memory,
    memory_len,
    input_weight,
    project_weight,
    output_weight,
    up_weight,
    down_weight,
    head_weight,
    vectors,
    slopes,
    first_input,
    first_project,
    first_output,
    first_up,
    first_down,
    first_head,
    first_vectors,
    first_slopes,
    second_input,
    second_project,
    second_output,
    second_up,
    second_down,
    second_head,
    second_vectors,
    second_slopes,
):
    streams, span, features = frames.shape
    layers, heads = slopes.shape
    nvec = vectors.shape[0]
    width = project_weight.shape[2] // 3
    hidden = up_weight.shape[2]
    codes = head_weight.shape[1]
    count = streams * span
    devices, blocks = lax.axis_size(STREAM), lax.axis_size(SEQ)
    halves = 2 if hidden // devices == 256 else 1
    chips = devices // 2
    sizes = (devices, blocks, streams, span, heads, features, nvec, halves)
    memory_flat = memory.reshape((layers, count, width))
    rows_each = width // devices
    full = ((count, width), f32)
    low = ((count, width), bf16)
    joined = ((2 * count, width), bf16)
    wide = ((count, hidden), bf16)
    lse = ((streams * heads, span), f32)
    cost = 2 * count * (5 * width * width + width * width + 2 * width * hidden) + 4 * count * 2 * span * width
    dma = pltpu.SemaphoreType.DMA

    def gathered(rows_all, cols):
        return ((chips, 2, rows_all // devices, cols), bf16)

    def grads_of(number):
        return dict(
            grad=((chips, 2, number, rows_each, 128), bf16),
            pair=((chips, number, rows_each, 128), bf16),
            mates=((chips, number, rows_each, 128), bf16),
            own=((number, rows_each, 128), bf16),
            line=((blocks, number // blocks, rows_each, 128), bf16),
            part=((number // blocks, rows_each, 128), bf16),
            total=((number, rows_each, 128), bf16),
        )

    wide_layouts, *other_layouts = layouts(blocks, halves)
    group_b, group_small, group_head = (Groups(layout, grads_of(layout.total)) for layout in other_layouts)
    groups_wide = [Groups(layout, grads_of(layout.total)) for layout in wide_layouts]

    def wide_named(name, form=""):
        return {f"{name}{form}_{WIDE[half]}": getattr(group, name) for half, group in enumerate(groups_wide)}

    def of(source, name, form="", start=0, end=halves):
        names = [f"{name}{form}_{WIDE[half]}" for half in range(start, end)]
        return {key: getattr(source, key) for key in names}

    def last_named(name):
        return {f"{name}_{WIDE[halves - 1]}": getattr(groups_wide[-1], name)}

    def early_named(name):
        return {f"{name}_{WIDE[half]}": getattr(group, name) for half, group in enumerate(groups_wide[:-1])}

    grad_name, pair_name, mates_name, own_name, line_name, part_name, total_name = REDUCED
    kept = dict(
        a=low, ap=low, q=low, k=joined, v=joined, o=low, lse=lse, r1=full, a2=low, u=wide, gp=wide, res=full, low=low
    )
    weight_shapes = dict(
        wp=gathered(width, 3 * width), wo=gathered(width, width), wu=gathered(width, hidden), wd=gathered(hidden, width)
    )
    layer_weights = {f"{key}_{layer}": item for layer in range(layers) for key, item in weight_shapes.items()}
    gather_count = 2 + len(layer_weights)
    score = ((2 * span, span // 2), f32)
    chance = ((2 * span, span // 2), bf16)
    scalars = dict(memory_len=memory_len, slopes=slopes)
    made = Made(
        functools.partial(forward_kernel, sizes),
        dict(
            frames=frames.transpose((0, 2, 1)),
            targets=targets.reshape((count // 128, 128)).astype(f32),
            input_turned=input_weight.T,
            vectors=vectors,
        ),
        dict(
            rows=((16, width), f32),
            gr_last=((8, width), f32),
            loss=((8, 128), f32),
            grad_head=group_head.grad,
            halo=((count, 128), bf16),
            frames_wide=((count, 128), bf16),
        ),
        dict(
            kept,
            **layer_weights,
            res_two=full,
            pr=full,
            nxt=low,
            behind=low,
            small=gathered(width, 128),
            wh=gathered(width, codes),
            small_rows=((128 - features, rows_each), f32),
            frames_tall=((128, span), bf16),
            kf=((streams, 2, 2 * span, 128), bf16),
            acc=((width, codes), f32),
            score_one=score,
            score_two=score,
            chance_one=chance,
            chance_two=chance,
        ),
        dict(
            out_sem=dma((gather_count, max(chips, 5))),
            in_sem=dma((gather_count, max(chips, 5))),
            frame_sem=dma((2, 1)),
            next_out=dma((streams,)),
            next_in=dma((streams,)),
            save_sem=dma((layers, len(kept), streams)),
            weight_sem=dma((layers, 4)),
            pr_sem=dma((streams,)),
            dr_sem=dma((1,)),
        ),
        any_outs=dict(
            far_pr=full,
            dr=full,
            **{FAR + key: ((layers,) + item[0], item[1]) for key, item in kept.items()},
            **{FAR + key: item for key, item in layer_weights.items()},
        ),
        lazy=dict(
            pw=project_weight, ow=output_weight, uw=up_weight, dw=down_weight, hw=head_weight, mem=memory_flat
        ),
        smem=dict(scalars, frame_count=frame_count),
        flops=2 * cost,
        collective=0,
    )

    def loaded(layer):
        held = [getattr(made, f"{FAR}{key}_{layer}") for key in weight_shapes]
        return dict(
            wd=held[3],
            a2=made.far_a2,
            wu=held[2],
            r1=made.far_r1,
            wo=held[1],
            o=made.far_o,
            lse=made.far_lse,
            q=made.far_q,
            k=made.far_k,
            v=made.far_v,
            wp=held[0],
            a=made.far_a,
            ap=made.far_ap,
        )

    layered = tuple(kept) + tuple(dict(mem=0))
    slots = max(chips, blocks)
    work = dict(
        do=low,
        dq=low,
        dk=joined,
        dv=joined,
        turned=((width, count), bf16),
        kf=((streams, 2, 2 * span, 128), bf16),
        **wide_named(pair_name),
        **wide_named(mates_name),
        **wide_named(grad_name),
        u_two=((2, count, 512), bf16),
        gp_two=((2, count, 512), bf16),
    )
    work_sems = dict(out_sem=dma((8 + 8 * halves, slots)), in_sem=dma((8 + 8 * halves, slots)), u_sem=dma((2, 2)), first_sem=dma((5,)))
    streamed = dict(u=made.far_u, gp=made.far_gp)
    one = Made(
        functools.partial(backward_kernel, 1, sizes),
        dict(rows=made.rows, grad_head=made.grad_head),
        dict(
            gr=((8, width), f32),
            gs=((8, 128), f32),
            dr=full,
            da=full,
            back=low,
            **wide_named(own_name),
            pair_b=group_b.pair,
            total_head=group_head.total,
        ),
        dict(
            work,
            dap=low,
            grad_b=group_b.grad,
            pair_head=group_head.pair,
            mates_head=group_head.mates,
            own_head=group_head.own,
            line_head=group_head.line,
        ),
        dict(work_sems, back_out=dma((streams,)), back_in=dma((streams,))),
        any_ins=dict(streamed, dr_in=made.dr),
        lazy=dict(loaded(1), mem=memory_flat),
        layered=layered,
        layer=1,
        smem=scalars,
        flops=2 * cost,
        collective=2,
    )
    zero = Made(
        functools.partial(backward_kernel, 0, sizes),
        dict(
            rows=made.rows,
            frames=made.frames_wide,
            halo=made.halo,
            back=one.back,
            gr_last=made.gr_last,
            gr_one=one.gr,
            **{f"{own_name}_one_{WIDE[half]}": getattr(one, f"{own_name}_{WIDE[half]}") for half in range(halves)},
            pair_b_one=one.pair_b,
        ),
        dict(
            gs=((8, 128), f32),
            **last_named(part_name),
            **early_named(total_name),
            own_b=group_b.own,
            grad_small=group_small.grad,
            **wide_named(total_name, form="_one"),
            total_b_one=group_b.total,
        ),
        dict(
            work,
            gr=((8, width), f32),
            dr=full,
            da=full,
            small_acc=((width, 128), f32),
            wide_one=full,
            **wide_named(own_name),
            **wide_named(line_name),
            **wide_named(line_name, form="_one"),
            grad_b=group_b.grad,
            pair_b=group_b.pair,
            mates_b=group_b.mates,
            mates_b_one=group_b.mates,
            own_b_one=group_b.own,
            line_b_one=group_b.line,
        ),
        work_sems,
        any_ins=dict(streamed, dr1_in=one.dr, da_in=one.da, r=made.far_res, pr=made.far_pr),
        lazy=loaded(0),
        layered=layered,
        layer=0,
        smem=scalars,
        flops=2 * cost,
        collective=3,
    )
    arrays = (
        (input_weight.T, project_weight, output_weight, up_weight, down_weight, head_weight, vectors),
        (first_input.T, first_project, first_output, first_up, first_down, first_head, first_vectors),
        (second_input.T, second_project, second_output, second_up, second_down, second_head, second_vectors),
    )
    order = (0, 6, 1, 2, 3, 4, 5)
    state = {f"{kind}_{number}": array[number] for number in order for kind, array in zip(KINDS, arrays)}
    tile_shape = ((8, 128), f32)
    tail = Made(
        functools.partial(tail_kernel, sizes, layers),
        dict(
            **of(zero, part_name, start=halves - 1),
            **of(zero, total_name, end=halves - 1),
            own_b=zero.own_b,
            grad_small=zero.grad_small,
            **of(zero, total_name, form="_one"),
            total_b_one=zero.total_b_one,
            total_head=one.total_head,
            gs_zero=zero.gs,
            gs_one=one.gs,
            loss=made.loss,
        ),
        dict(last_named(total_name), total_b=group_b.total, total_small=group_small.total, sums=tile_shape),
        dict(
            line_b=group_b.line,
            pair_small=group_small.pair,
            mates_small=group_small.mates,
            own_small=group_small.own,
            line_small=group_small.line,
            rows_one=((devices * blocks, 1, 128), f32),
            rows_two=((devices * blocks, 1, 128), f32),
        ),
        dict(
            out_sem=dma((8 + 4 * halves, slots)),
            in_sem=dma((8 + 4 * halves, slots)),
            all_out=dma((2 * devices * blocks,)),
            all_in=dma((2 * devices * blocks,)),
        ),
        lazy=state,
        collective=4,
    )
    moved = {f"new_{kind}_{number}": (array[number].shape, f32) for number in order for kind, array in zip(KINDS, arrays)}
    fresh = Made(
        functools.partial(update_kernel, sizes, layers),
        dict(slopes=slopes, first_slopes=first_slopes, second_slopes=second_slopes, sums=tail.sums),
        dict(
            fresh_slopes=(slopes.shape, f32),
            new_first_slopes=(slopes.shape, f32),
            new_second_slopes=(slopes.shape, f32),
            norms=((2, 3 + 4 * layers + nvec), f32),
            loss=((1, 1), f32),
            clip=((1, 1), f32),
        ),
        sems=dict(keep_sem=dma((1,))),
        any_outs=dict(layer_inputs=((layers, count, width), bf16)),
        lazy=dict(
            **of(tail, total_name, start=halves - 1),
            **of(zero, total_name, end=halves - 1),
            total_b=tail.total_b,
            total_small=tail.total_small,
            **of(zero, total_name, form="_one"),
            total_b_one=zero.total_b_one,
            total_head=one.total_head,
            **state,
            low=made.far_low,
        ),
        flush=moved,
    )

    def results(kind, last):
        found = [getattr(fresh, f"new_{kind}_{number}") for number in range(7)]
        return [found[0].T] + found[1:] + [last]

    return (
        fresh.loss.reshape(()),
        fresh.layer_inputs.reshape((layers, streams, span, width)),
        fresh.clip.reshape(()),
        fresh.norms.T,
        *results(KINDS[0], fresh.fresh_slopes),
        *results(KINDS[1], fresh.new_first_slopes),
        *results(KINDS[2], fresh.new_second_slopes),
    )


def solution(mesh):
    rows3 = P(None, STREAM, None)
    state = (P(None, STREAM), rows3, rows3, rows3, rows3, P(STREAM, None), P(None, STREAM), P())
    in_specs = (
        P(STREAM, SEQ, None),
        P(STREAM, SEQ),
        P(STREAM),
        P(None, STREAM, None, None),
        P(STREAM),
    ) + state * 3
    out_specs = (P(), P(None, STREAM, SEQ, None), P(), P()) + state * 3
    return jax.shard_map(shards, mesh=mesh, in_specs=in_specs, out_specs=out_specs, check_vma=False)
```

```python
import functools

import jax
import jax.numpy as jnp
from jax import lax
from jax.experimental import pallas as pl
from jax.experimental.pallas import tpu as pltpu
from jax.sharding import PartitionSpec as P

STEP = 10


ln_eps = 1e-05
clip_limit = 0.002
beta_one = 0.9
beta_two = 0.999
lamb_rate = 0.3
slope_rate = 0.001
decay_rate = 0.01
adam_eps = 1e-11
masked_score = -1e30

STREAM, SEQ, FAR = "stream", "seq", "far_"
KINDS = ("weight", "first", "second")
WIDE = ("a", "c")
REDUCED = ("grad", "pair", "mates", "own", "line", "part", "total")
NN = (((1,), (0,)), ((), ()))
NT = (((1,), (1,)), ((), ()))
TN = (((0,), (0,)), ((), ()))
VMEM_LIMIT = 63 * 1024 * 1024
f32 = jnp.float32
bf16 = jnp.bfloat16


def mm(left, right, dims=NN):
    return lax.dot_general(left, right, dims, preferred_element_type=f32)


MESH = pl.DeviceIdType.MESH


class Place:
    def __init__(self, streams, blocks):
        self.chips = streams // 2
        self.blocks = blocks
        index = lax.axis_index(STREAM)
        self.chip = index // 2
        self.core = index % 2
        self.block = lax.axis_index(SEQ)
        self.sibling = {STREAM: 2 * self.chip + 1 - self.core}
        self.across = self.chip // 2 * 2 + 1 - self.chip % 2
        self.along = (self.chip + 2) % 4
        self.opposite = 3 - self.chip

        self.pair_block = self.block // 2 * 2 + 1 - self.block % 2
        self.far_block = (self.block + 2) % 4

    def chip_device(self, chip):
        return {STREAM: 2 * chip + self.core}

    def other(self, distance):
        return (self.chip + distance) % self.chips

    def mate(self, distance):
        return {STREAM: 2 * self.other(distance) + self.core}

    def peer(self, distance):
        return (self.block + distance) % self.blocks

    def greet(self, line=False, column=False):
        barrier = pltpu.get_barrier_semaphore()

        def hello(device):
            pl.semaphore_signal(barrier, inc=1, device_id=device, device_id_type=MESH)

        hello(self.sibling)
        for distance in range(1, self.chips):
            hello(self.mate(distance))
        if line:

            @pl.when(self.block > 0)
            def _():
                hello({SEQ: self.block - 1})

            pl.semaphore_wait(barrier, self.chips + jnp.where(self.block < self.blocks - 1, 1, 0))
        elif column:
            for distance in range(1, self.blocks):
                hello({SEQ: self.peer(distance)})
            pl.semaphore_wait(barrier, self.chips + self.blocks - 1)
        else:
            pl.semaphore_wait(barrier, self.chips)


class Gather:
    def __init__(self, place, ref, sems, row, direct=False):
        self.place, self.ref, self.sems, self.row = place, ref, sems, row
        self.square = place.chips == 4 and not direct

    def copy(self, slot, view, device):
        return pltpu.make_async_remote_copy(
            src_ref=view,
            dst_ref=view,
            send_sem=self.sems[0].at[self.row, slot],
            recv_sem=self.sems[1].at[self.row, slot],
            device_id=device,
            device_id_type=MESH,
        )

    def shard(self, chip, half=None):
        view = self.ref.at[chip, self.place.core]
        if half is None:
            return view
        size = self.ref.shape[2] // 2
        return view.at[pl.ds(half * size, size)]

    def far(self, distance, chip):
        return self.copy(distance, self.shard(chip), self.place.mate(distance))

    def beside(self, slot, chip, half, target):
        return self.copy(slot, self.shard(chip, half), self.place.chip_device(target))

    def near(self, core):
        return self.copy(0, self.ref.at[:, core], self.place.sibling)

    def push(self):
        place = self.place
        if self.square:
            self.beside(1, place.chip, None, place.across).start()
            self.beside(2, place.chip, None, place.along).start()
        else:
            for distance in range(1, place.chips):
                self.far(distance, place.chip).start()

    def pass_on(self):
        place = self.place
        if self.square:
            self.beside(1, place.across, None, place.across).wait_recv()
            self.beside(2, place.along, None, place.along).wait_recv()
            self.beside(3, place.across, 0, place.along).start()
            self.beside(4, place.along, 1, place.across).start()

    def relay(self):
        place = self.place
        if self.square:
            self.beside(3, place.opposite, 0, place.along).wait_recv()
            self.beside(4, place.opposite, 1, place.across).wait_recv()
        else:
            for distance in range(1, place.chips):
                self.far(distance, place.other(place.chips - distance)).wait_recv()
        self.near(place.core).start()

    def finish(self):
        place = self.place
        self.near(1 - place.core).wait_recv()
        self.near(place.core).wait_send()
        if self.square:
            self.beside(1, place.chip, None, place.across).wait_send()
            self.beside(2, place.chip, None, place.along).wait_send()
            self.beside(3, place.across, 0, place.along).wait_send()
            self.beside(4, place.along, 1, place.across).wait_send()
        else:
            for distance in range(1, place.chips):
                self.far(distance, place.chip).wait_send()


class Reduce:
    def __init__(self, place, sems, row, grad=None, pair=None, mates=None, own=None, line=None, total=None, part=None):
        self.part = part
        self.place, self.sems, self.row = place, sems, row
        self.grad, self.pair, self.mates = grad, pair, mates
        self.own, self.line, self.total = own, line, total

    def copy(self, phase, slot, src, dst, device):
        return pltpu.make_async_remote_copy(
            src_ref=src,
            dst_ref=dst,
            send_sem=self.sems[0].at[self.row + phase, slot],
            recv_sem=self.sems[1].at[self.row + phase, slot],
            device_id=device,
            device_id_type=MESH,
        )

    def copy_a(self):
        place = self.place
        return self.copy(0, 0, self.grad.at[:, 1 - place.core], self.pair, place.sibling)

    def copy_b(self, distance, source=None):
        place = self.place
        slot = place.chip if source is None else source
        return self.copy(
            1, distance, self.pair.at[place.other(distance)], self.mates.at[slot], place.mate(distance)
        )

    def piece(self, block):
        size = (self.total if self.own is None else self.own).shape[0] // self.place.blocks
        return pl.ds(block * size, size)

    def copy_c(self, distance, source=None):
        place = self.place
        slot = place.block if source is None else source
        there = place.peer(distance)
        return self.copy(2, distance, self.own.at[self.piece(there)], self.line.at[slot], {SEQ: there})

    def copy_d(self, slot, source, target):
        view = self.total.at[self.piece(source)]
        return self.copy(3, slot, view, view, {SEQ: target})

    def steps_d(self):
        place = self.place
        mine = place.block
        if place.blocks == 4:
            return [(mine, place.far_block), (mine, place.pair_block), (place.far_block, place.pair_block)]
        return [(mine, place.peer(distance)) for distance in range(1, place.blocks)]

    def arrivals_d(self):
        place = self.place
        if place.blocks == 4:
            return [place.far_block, place.pair_block, 3 - place.block]
        return [place.peer(place.blocks - distance) for distance in range(1, place.blocks)]

    def start_a(self):
        self.copy_a().start()

    def end_a(self):
        place = self.place
        self.copy_a().wait_recv()

        def add(chip, carry):
            self.pair[chip] = (self.pair[chip].astype(f32) + self.grad[chip, place.core].astype(f32)).astype(bf16)
            return carry

        lax.fori_loop(0, place.chips, add, 0)
        self.copy_a().wait_send()

    def start_b(self):
        for distance in range(1, self.place.chips):
            self.copy_b(distance).start()

    def end_b(self):
        place = self.place
        total = self.pair[place.chip].astype(f32)
        for distance in range(1, place.chips):
            source = place.other(place.chips - distance)
            self.copy_b(distance, source).wait_recv()
            total = total + self.mates[source].astype(f32)
        self.own[...] = total.astype(bf16)
        for distance in range(1, place.chips):
            self.copy_b(distance).wait_send()

    def start_c(self):
        for distance in range(1, self.place.blocks):
            self.copy_c(distance).start()

    def end_c(self):
        place = self.place
        mine = self.piece(place.block)
        total = self.own[mine].astype(f32)
        for distance in range(1, place.blocks):
            source = place.peer(place.blocks - distance)
            self.copy_c(distance, source).wait_recv()
            total = total + self.line[source].astype(f32)
        if self.part is None:
            self.total[mine] = total.astype(bf16)
        else:
            self.part[...] = total.astype(bf16)
        for distance in range(1, place.blocks):
            self.copy_c(distance).wait_send()

    def start_d(self):
        steps = self.steps_d()
        for slot, (source, target) in enumerate(steps[:2] if self.place.blocks == 4 else steps):
            self.copy_d(slot, source, target).start()

    def pass_d(self):
        if self.place.blocks == 4:
            source, target = self.steps_d()[2]
            self.copy_d(0, self.arrivals_d()[0], target).wait_recv()
            self.copy_d(2, source, target).start()

    def end_d(self):
        direct = self.place.blocks != 4
        for slot, source in enumerate(self.arrivals_d()):
            if direct or slot > 0:
                self.copy_d(slot, source, self.place.peer(1)).wait_recv()
        for slot, (source, target) in enumerate(self.steps_d()):
            self.copy_d(slot, source, target).wait_send()


def put_blocks(grad, layout, array, first, value):
    chips, cores, unused_blocks, rows, lanes = grad.shape
    for spot in range(value.shape[1] // lanes):
        part = value[:, spot * lanes : (spot + 1) * lanes].astype(bf16)
        grad[:, :, layout.spot(array, first + spot)] = part.reshape((chips, cores, rows, lanes))


def put_down(grad, layout, array, value, part, parts):
    chips, cores, unused_blocks, rows, lanes = grad.shape
    few = chips // parts
    high = value.shape[0] // (few * cores * rows)
    wide = value.shape[1] // lanes
    value = value.astype(bf16).reshape((few, cores, high, rows, value.shape[1]))
    for up in range(high):
        for spot in range(wide):
            grad[pl.ds(part * few, few), :, layout.spot(array, up * wide + spot)] = value[
                :, :, up, :, spot * lanes : (spot + 1) * lanes
            ]


class Refs:
    def __init__(self, names, refs, lazy, flush, layer, layered):
        for name, ref in zip(names, refs, strict=True):
            setattr(self, name, ref)
        self.loads, self.stores = {}, {}
        for number, name in enumerate(lazy):
            far = getattr(self, FAR + name)
            if name in layered:
                far = far.at[layer]
            near = getattr(self, name)
            self.loads[id(near)] = pltpu.make_async_copy(far, near, self.load_sem.at[number])
        for number, name in enumerate(flush):
            near = getattr(self, name)
            self.stores[id(near)] = pltpu.make_async_copy(near, getattr(self, FAR + name), self.store_sem.at[number])

    def fetch(self, *refs):
        for load in [self.loads[id(ref)] for ref in refs] if refs else self.loads.values():
            load.start()

    def ready(self, *refs):
        for ref in refs:
            self.loads[id(ref)].wait()

    def flush(self, *refs):
        for ref in refs:
            self.stores[id(ref)].start()

    def flushed(self):
        for store in self.stores.values():
            store.wait()


class Layout:
    def __init__(self, devices, counts):
        self.parts, self.size = [], 0
        for count in counts:
            per = -(-count // devices)
            self.parts.append((self.size, per, count))
            self.size += per
        self.total = self.size * devices

    def spot(self, array, block):
        base, per, unused_count = self.parts[array]
        return block // per * self.size + base + block % per

    def unused(self):
        taken = {self.spot(array, block) for array, part in enumerate(self.parts) for block in range(part[2])}
        return [block for block in range(self.total) if block not in taken]


def layouts(blocks, halves):
    wides = [(16 // halves, 16 // halves) for half in range(halves - 1)] + [(16 // halves, 16 // halves, 4)]
    counts = (*wides, (12,), (1,), (8,))
    made = [Layout(blocks, item) for item in counts]
    return made[:halves], made[halves], made[halves + 1], made[halves + 2]


def kept_spot(block, halves):
    return block if halves == 1 else block % 2 * 8 + block // 2


def up_part(ref, half, part, halves):
    if halves == 1:
        return flat(ref, tile(part, 512))
    columns = [flat(ref, tile(2 * (4 * part + spot) + half, 128)) for spot in range(4)]
    return jnp.concatenate(columns, axis=1)


def down_part(ref, half, part, parts, halves):
    chips, rows = ref.shape[0] // parts, ref.shape[2] // halves
    value = ref[pl.ds(part * chips, chips), :, half * rows : (half + 1) * rows]
    return value.reshape((-1, value.shape[-1]))


class Ahead:
    def __init__(self, place, step, src, dst, sems):
        self.place, self.step, self.src, self.dst, self.sems = place, step, src, dst, sems
        self.sends = place.block < place.blocks - 1 if step > 0 else place.block > 0
        self.receives = place.block > 0 if step > 0 else place.block < place.blocks - 1

    def copy(self, slot, rows):
        return pltpu.make_async_remote_copy(
            src_ref=self.src.at[rows],
            dst_ref=self.dst.at[rows],
            send_sem=self.sems[0].at[slot],
            recv_sem=self.sems[1].at[slot],
            device_id={SEQ: self.place.block + self.step},
            device_id_type=MESH,
        )

    def start(self, slot, rows):
        @pl.when(self.sends)
        def _():
            self.copy(slot, rows).start()

    def arrived(self, slot, rows):
        @pl.when(self.receives)
        def _():
            self.copy(slot, rows).wait_recv()

    def sent(self, slot, rows):
        @pl.when(self.sends)
        def _():
            self.copy(slot, rows).wait_send()


def flat(ref, cols=slice(None)):
    value = ref[:, :, :, cols]
    return value.reshape((-1, value.shape[-1]))


def flat_rows(ref, part, parts):
    chips = ref.shape[0] // parts
    value = ref[pl.ds(part * chips, chips)]
    return value.reshape((-1, value.shape[-1]))


def normalize(values):
    centred = values - jnp.mean(values, axis=-1, keepdims=True)
    scale = lax.rsqrt(jnp.mean(centred * centred, axis=-1, keepdims=True) + ln_eps)
    return (centred * scale, scale)


def norm_back(grad_out, standard, scale, gain):
    scaled = grad_out * gain
    return scale * (
        scaled
        - jnp.mean(scaled, axis=-1, keepdims=True)
        - standard * jnp.mean(scaled * standard, axis=-1, keepdims=True)
    )


def gelu_pair(x):
    cumulative = 0.5 * (1.0 + lax.erf(x * 0.7071067811865476))
    bell = jnp.exp(-0.5 * x * x)
    return (x * cumulative, cumulative + x * (bell * 0.3989422804014327))


def tile(index, size):
    return pl.ds(pl.multiple_of(index * size, size), size)


def half_masks():
    lane = lax.broadcasted_iota(jnp.int32, (1, 128), 1)
    left = jnp.where(lane < 64, 1.0, 0.0).astype(bf16)
    right = jnp.where(lane < 64, 0.0, 1.0).astype(bf16)
    return (left, right)


def build_marks(kf_ref, lens_ref, first):
    streams, unused_halves, keys, lanes = kf_ref.shape
    key = lax.broadcasted_iota(jnp.int32, (keys, lanes), 0)
    lane = lax.broadcasted_iota(jnp.int32, (keys, lanes), 1)
    coarse = (key // 256 * 256).astype(f32)
    fine = (key % 256).astype(f32)
    for stream in range(streams):
        veiled = jnp.where(jnp.logical_and(first, key < keys // 2 - lens_ref[stream]), 1.0, 0.0)
        for half in range(2):
            spot = lane - 64 * (1 - half)
            value = jnp.where(spot == 6, veiled, jnp.where(spot == 7, 1.0, 0.0))
            value = jnp.where(jnp.logical_and(spot >= 3, spot < 6), fine, value)
            value = jnp.where(jnp.logical_and(spot >= 0, spot < 3), coarse, value)
            kf_ref[stream, half] = value.astype(bf16)


def query_marks(slope, half):
    spot = lax.broadcasted_iota(jnp.int32, (1, 128), 1) - 64 * (1 - half)
    whole_slope = jnp.full((1, 128), slope)
    one = whole_slope.astype(bf16).astype(f32)
    two = (whole_slope - one).astype(bf16).astype(f32)
    three = whole_slope - one - two
    value = jnp.where(spot == 6, masked_score, 0.0)
    for number, part in enumerate((one, two, three)):
        value = jnp.where(jnp.logical_or(spot == number, spot == number + 3), part, value)
    return value.astype(bf16)


def attend(span, heads, q_ref, k_ref, v_ref, kf_ref, slope_of, o_ref, lse_ref, score_refs, chance_refs, stream, early):
    pairs = heads // 2
    step = span // 2
    masks = half_masks()
    key_at = lax.broadcasted_iota(jnp.int32, (step, step), 0)
    query_at = lax.broadcasted_iota(jnp.int32, (step, step), 1)
    down = lax.broadcasted_iota(jnp.int32, (128, 1), 0)
    row_masks = (jnp.where(down < 64, 1.0, 0.0).astype(bf16), jnp.where(down < 64, 0.0, 1.0).astype(bf16))

    def group(first_pair, count):
        work = []
        for pair in [first_pair + i for i in range(count)]:
            cols = tile(pair, 128)
            k_pair = k_ref[tile(stream, 2 * span), cols]
            v_turned = v_ref[tile(stream, 2 * span), cols].T
            for part in range(2):
                for half in range(2):
                    work.append((pair, cols, k_pair, v_turned, part, half))
        peaks, mixed_rows = {}, {}

        def scores(item):
            pair, cols, k_pair, unused_v, part, half = work[item]
            seen = span + part * step
            q_pair = q_ref[pl.ds(pl.multiple_of(stream * span + part * step, step), step), cols]
            q_aug = q_pair * masks[half] + query_marks(slope_of(2 * pair + half), half)
            k_aug = k_pair[: seen + step] * masks[half] + kf_ref[stream, half, : seen + step]
            score = mm(k_aug, q_aug, NT)
            near = jnp.where(key_at <= query_at, score[seen:], masked_score)
            peaks[item] = jnp.maximum(
                jnp.max(score[:seen], axis=0, keepdims=True), jnp.max(near, axis=0, keepdims=True)
            )
            out = score_refs[item % 2]
            out[:seen, :] = score[:seen]
            out[seen : seen + step, :] = near

        def soften(item):
            seen = span + (work[item][4] + 1) * step
            chance_refs[item % 2][:seen, :] = jnp.exp(score_refs[item % 2][:seen, :] - peaks[item]).astype(bf16)

        def mix(item):
            pair, cols, unused_k, v_turned, part, half = work[item]
            seen = span + (part + 1) * step
            v_aug = v_turned[:, :seen] * row_masks[half] + row_masks[1 - half]
            mixed = mm(v_aug, chance_refs[item % 2][:seen, :])
            own = mixed[half * 64 : half * 64 + 64]
            total = mixed[64 - half * 64 : 128 - half * 64]
            mixed_rows[half] = own / total
            lse_ref[pl.ds(stream * heads + 2 * pair + half, 1), part * step : (part + 1) * step] = peaks[
                item
            ] + jnp.log(total[:1])
            if half == 1:
                rows = pl.ds(pl.multiple_of(stream * span + part * step, step), step)
                o_ref[rows, cols] = jnp.concatenate([mixed_rows[0], mixed_rows[1]], axis=0).T.astype(bf16)

        scores(0)
        for item in range(len(work)):
            if item + 1 < len(work):
                scores(item + 1)
            soften(item)
            if item > 0:
                mix(item - 1)
        mix(len(work) - 1)

    def inner(index, carry):
        group(2 * index, 2)
        early(index)
        return carry

    lax.fori_loop(0, pairs // 2, inner, 0)


def forward_kernel(sizes, r):
    (stream_devices, block_devices, streams, span, heads, features, nvec, halves) = sizes
    place = Place(stream_devices, block_devices)
    chip, core = place.chip, place.core
    first = place.block == 0
    layers = r.mem.shape[0]
    width = r.a.shape[1]
    count = streams * span
    step = span // 2
    sems = (r.out_sem, r.in_sem)
    weight_names = ("wp", "wo", "wu", "wd")
    weights = [[getattr(r, f"{name}_{layer}") for name in weight_names] for layer in range(layers)]
    gather_small, gather_head = Gather(place, r.small, sems, 0, direct=True), Gather(place, r.wh, sems, 1)
    gathers = [
        [
            Gather(place, ref, sems, 2 + 4 * layer + number)
            for number, ref in enumerate(weights[layer])
        ]
        for layer in range(layers)
    ]
    early_names, look_names, feed_names = ("ap", "q", "k", "v", "low"), ("o", "lse"), ("r1", "a2", "u", "gp")
    saved_names = early_names + look_names + feed_names + ("a", "res")

    def save(layer, name, stream, source=None):
        source = getattr(r, name) if source is None else source
        size = source.shape[0] // streams
        at = tile(stream, size)
        far = getattr(r, FAR + name)
        return pltpu.make_async_copy(
            source.at[at], far.at[layer, at], r.save_sem.at[layer, saved_names.index(name), stream]
        )

    def save_weight(layer, number):
        return pltpu.make_async_copy(
            weights[layer][number],
            getattr(r, f"{FAR}{weight_names[number]}_{layer}"),
            r.weight_sem.at[layer, number],
        )

    r.fetch()
    frames_ahead = Ahead(place, 1, r.frames_wide, r.halo, (r.frame_sem.at[0], r.frame_sem.at[1]))
    next_ahead = Ahead(place, 1, r.nxt, r.behind, (r.next_out, r.next_in))
    every = pl.ds(0, count)

    @pl.when(first)
    def _():
        r.halo[...] = jnp.zeros_like(r.halo)
        r.behind[...] = jnp.zeros_like(r.behind)

    r.small_rows[...] = jnp.zeros_like(r.small_rows)
    r.small_rows[0:nvec, :] = r.vectors[...]
    own_rows = jnp.concatenate([r.input_turned[...], r.small_rows[...].T], axis=1)
    r.small[chip, core] = own_rows.astype(bf16)
    r.frames_tall[...] = jnp.zeros_like(r.frames_tall)
    r.frames_tall[features : features + 16, :] = jnp.where(
        lax.broadcasted_iota(jnp.int32, (16, span), 0) == 0, 1.0, 0.0
    ).astype(bf16)
    for stream in range(streams):
        r.frames_tall[0:features, :] = r.frames[stream]
        r.frames_wide[stream * span : (stream + 1) * span, :] = r.frames_tall[...].T
    r.ready(r.pw)
    r.wp_0[chip, core] = r.pw[0].astype(bf16)
    place.greet(line=True)
    gather_small.push()
    gathers[0][0].push()
    frames_ahead.start(0, every)
    r.ready(r.ow, r.uw, r.dw, r.hw)
    r.wo_0[chip, core] = r.ow[0].astype(bf16)
    r.wu_0[chip, core] = r.uw[0].astype(bf16)
    r.wd_0[chip, core] = r.dw[0].astype(bf16)
    r.wp_1[chip, core] = r.pw[1].astype(bf16)
    r.wo_1[chip, core] = r.ow[1].astype(bf16)
    r.wu_1[chip, core] = r.uw[1].astype(bf16)
    r.wd_1[chip, core] = r.dw[1].astype(bf16)
    r.wh[chip, core] = r.hw[...].astype(bf16)
    build_marks(r.kf, r.memory_len, first)
    r.rows[...] = jnp.zeros_like(r.rows)
    r.ready(r.mem)
    gathers[0][0].pass_on()
    gathers[0][1].push()
    gathers[0][2].push()
    gather_small.relay()
    gathers[0][0].relay()
    gathers[0][3].push()
    gather_small.finish()
    r.rows[:nvec, :] = flat(r.small).astype(f32).T[features : features + nvec]
    gathers[0][0].finish()
    frames_ahead.arrived(0, every)
    residuals = (r.res, r.res_two)

    for layer in range(layers):
        residual, outcome = residuals[layer % 2], residuals[(layer + 1) % 2]
        row = 3 + 4 * layer
        g1, b1, g2, b2 = (r.rows[row + i : row + i + 1, :] for i in range(4))
        wp, wo, wu, wd = weights[layer]
        own_a = r.a if layer == 0 else r.nxt

        def wait_old(names, stream):
            if layer > 0:
                for name in names:
                    save(layer - 1, name, stream).wait()

        wq, wk, wv = (slice(i * width, (i + 1) * width) for i in range(3))

        def project_own(stream):
            wait_old(("q", "k", "v", "low"), stream)
            for part in range(2):
                at = pl.ds(pl.multiple_of(stream * span + part * step, step), step)
                here = pl.ds(pl.multiple_of(stream * 2 * span + span + part * step, step), step)
                if layer == 0:
                    value = mm(r.frames_wide[at, :], flat(r.small), NT)
                    residual[at, :] = value
                    own_a[at, :] = (normalize(value)[0] * g1 + b1).astype(bf16)
                else:
                    value = residual[at, :]
                r.low[at, :] = value.astype(bf16)
                a = own_a[at, :]
                r.q[at, :] = (mm(a, flat(wp, wq)) * 0.125).astype(bf16)
                r.k[here, :] = mm(a, flat(wp, wk)).astype(bf16)
                r.v[here, :] = mm(a, flat(wp, wv)).astype(bf16)
            for name in ("q", "low"):
                save(layer, name, stream).start()
            save(layer, saved_names[-1], stream, residual).start()
            save(layer, saved_names[-2], stream, own_a).start()

        def project_behind(stream):
            wait_old(("ap",), stream)
            for part in range(2):
                at = pl.ds(pl.multiple_of(stream * span + part * step, step), step)
                behind = pl.ds(pl.multiple_of(stream * 2 * span + part * step, step), step)
                if layer == 0:
                    before = mm(r.halo[at, :], flat(r.small), NT)
                    before = jnp.where(first, r.mem[layer, at, :].astype(f32), before)
                    r.pr[at, :] = before
                    ap = (normalize(before)[0] * g1 + b1).astype(bf16)
                else:
                    ap = (normalize(r.mem[layer, at, :].astype(f32))[0] * g1 + b1).astype(bf16)
                    ap = jnp.where(first, ap.astype(f32), r.behind[at, :].astype(f32)).astype(bf16)
                r.ap[at, :] = ap
                r.k[behind, :] = mm(ap, flat(wp, wk)).astype(bf16)
                r.v[behind, :] = mm(ap, flat(wp, wv)).astype(bf16)
            for name in ("ap", "k", "v"):
                save(layer, name, stream).start()
            if layer == 0:
                at = tile(stream, span)
                pltpu.make_async_copy(r.pr.at[at], r.far_pr.at[at], r.pr_sem.at[stream]).start()

        def look(stream):
            wait_old(look_names, stream)

            def early(index):
                def at(when_stream, when_index):
                    return pl.when(jnp.logical_and(stream == when_stream, index == when_index))

                @at(0, 0)
                def _():
                    if layer == 0:
                        gathers[0][3].pass_on()
                    else:
                        gathers[1][2].pass_on()

                @at(0, 1)
                def _():
                    if layer == 0:
                        gathers[0][1].relay()
                        gathers[0][2].relay()
                        gathers[1][0].push()
                        gathers[1][1].push()
                    else:
                        gathers[1][3].pass_on()

                @at(1, 0)
                def _():
                    if layer == 0:
                        gathers[0][3].relay()
                    else:
                        gather_head.pass_on()
                        gathers[1][2].relay()
                        gathers[1][3].relay()

                @at(1, 1)
                def _():
                    if layer == 0:
                        gathers[1][0].pass_on()
                        gathers[1][1].pass_on()
                    else:
                        gather_head.relay()

            attend(
                span,
                heads,
                r.q,
                r.k,
                r.v,
                r.kf,
                lambda head: r.slopes[layer, head],
                r.o,
                r.lse,
                (r.score_one, r.score_two),
                (r.chance_one, r.chance_two),
                stream,
                early,
            )
            for name in look_names:
                save(layer, name, stream).start()

        def feed(stream, carry):
            if layer > 0:
                save(layer - 1, saved_names[-1], stream, outcome).wait()
            wait_old(feed_names, stream)
            at = tile(stream, span)
            after = residual[at, :] + mm(r.o[at, :], flat(wo))
            r.r1[at, :] = after
            a2 = (normalize(after)[0] * g2 + b2).astype(bf16)
            r.a2[at, :] = a2
            for name in feed_names[:2]:
                save(layer, name, stream).start()
            total = after
            parts = wu.shape[3] // 512
            later = mm(a2, flat(wu, slice(0, 512)))
            for part in range(parts):
                cols = slice(part * 512, (part + 1) * 512)
                value = later
                if part + 1 < parts:
                    later = mm(a2, flat(wu, slice((part + 1) * 512, (part + 2) * 512)))
                active, slope = gelu_pair(value)
                active = active.astype(bf16)
                slope = slope.astype(bf16)
                for spot in range(4):
                    there = kept_spot(part * 4 + spot, halves)
                    there = slice(there * 128, (there + 1) * 128)
                    r.u[at, there] = active[:, spot * 128 : (spot + 1) * 128]
                    r.gp[at, there] = slope[:, spot * 128 : (spot + 1) * 128]
                total = total + mm(active, flat_rows(wd, part, parts))
            outcome[at, :] = total
            for name in feed_names[2:]:
                save(layer, name, stream).start()
            if layer == 0:
                g, b = r.rows[row + 4 : row + 5, :], r.rows[row + 5 : row + 6, :]
                r.nxt[at, :] = (normalize(total)[0] * g + b).astype(bf16)
                next_ahead.start(stream, at)

                @pl.when(stream == 0)
                def _():
                    gathers[1][0].relay()
                    gathers[1][1].relay()

            return carry

        if layer == 0:

            def all_project(stream, carry):
                project_own(stream)
                project_behind(stream)

                @pl.when(stream == 0)
                def _():
                    gathers[0][1].pass_on()
                    gathers[0][2].pass_on()

                return carry

            def all_look(stream, carry):
                look(stream)
                return carry

            lax.fori_loop(0, streams, all_project, 0)
            lax.fori_loop(0, streams, all_look, 0)
            for gather in gathers[1][2:] + [gather_head]:
                gather.push()
            for gather in gathers[0][1:]:
                gather.finish()
        else:
            gathers[1][0].finish()
            gathers[1][1].finish()

            def all_own(stream, carry):
                project_own(stream)
                return carry

            def both(stream, carry):
                next_ahead.arrived(stream, tile(stream, span))
                project_behind(stream)
                look(stream)
                return carry

            lax.fori_loop(0, streams, all_own, 0)
            lax.fori_loop(0, streams, both, 0)
            gathers[1][2].finish()
            gathers[1][3].finish()
        for number in range(4):
            save_weight(layer, number).start()
        lax.fori_loop(0, streams, feed, 0)
    gather_head.finish()
    head_stage(place, streams, span, stream_devices, residuals[layers % 2], r)
    last = pltpu.make_async_copy(residuals[layers % 2], r.dr, r.dr_sem.at[0])
    last.start()
    for layer in range(layers):
        for number in range(4):
            save_weight(layer, number).wait()
    for stream in range(streams):
        at = tile(stream, span)
        for name in early_names + look_names + feed_names:
            save(layers - 1, name, stream).wait()
        for layer in range(layers):
            save(layer, saved_names[-2], stream, r.a if layer == 0 else r.nxt).wait()
        save(layers - 1, saved_names[-1], stream, residuals[(layers - 1) % 2]).wait()
        pltpu.make_async_copy(r.pr.at[at], r.far_pr.at[at], r.pr_sem.at[stream]).wait()
        next_ahead.sent(stream, at)
    frames_ahead.sent(0, every)
    last.wait()


def head_stage(place, streams, span, stream_devices, residual, r):
    gain, bias = r.rows[1:2, :], r.rows[2:3, :]
    step = span // 2
    r.acc[...] = jnp.zeros_like(r.acc)
    r.gr_last[...] = jnp.zeros_like(r.gr_last)
    r.loss[...] = jnp.zeros_like(r.loss)
    target_columns = r.targets[...].astype(f32).T
    lane = lax.broadcasted_iota(jnp.int32, target_columns.shape, 1)

    def column(index):
        return jnp.sum(jnp.where(lane == index, target_columns, 0.0), axis=1, keepdims=True)

    def one(index, carry):
        at = tile(index, step)
        stream, part = index // 2, index % 2
        standard, scale = normalize(residual[at, :])
        f = (standard * gain + bias).astype(bf16)
        z = mm(f, flat(r.wh))
        per = step // 128
        target = jnp.concatenate([column(index * per + i) for i in range(per)], axis=0)
        frames = jnp.full((step, 1), r.frame_count[stream])
        position = lax.broadcasted_iota(jnp.int32, (step, 1), 0) + (place.block * span + part * step)
        share = jnp.where(position < frames, 1.0 / (frames.astype(f32) * (streams * stream_devices)), 0.0)
        peak = jnp.max(z, axis=-1, keepdims=True)
        raised = jnp.exp(z - peak)
        total = jnp.sum(raised, axis=-1, keepdims=True)
        code = lax.broadcasted_iota(jnp.int32, z.shape, 1)
        hit = code == target.astype(jnp.int32)
        picked = jnp.sum(jnp.where(hit, z, 0.0), axis=-1, keepdims=True)
        r.loss[...] += jnp.sum(share * (peak + jnp.log(total) - picked))
        soft = raised * (1.0 / total)
        dz = (share * jnp.where(hit, soft - 1.0, soft)).astype(bf16)
        r.acc[...] += mm(f, dz, TN)
        df = mm(dz, flat(r.wh), NT)
        r.gr_last[0:1, :] += jnp.sum(df * standard, axis=0, keepdims=True)
        r.gr_last[1:2, :] += jnp.sum(df, axis=0, keepdims=True)
        residual[at, :] = norm_back(df, standard, scale, gain)
        return carry

    lax.fori_loop(0, streams * 2, one, 0)
    put_blocks(r.grad_head, layouts(place.blocks, 1)[3], 0, 0, r.acc[...])


def attend_back(streams, span, heads, refs, early, between):
    (q_ref, k_ref, v_ref, o_ref, lse_ref, kf_ref, slope_of, do_ref, dq_ref, dk_ref, dv_ref, gs_ref, p_ref, ds_ref) = refs
    pairs = heads // 2
    step = span // 2
    masks = half_masks()
    key_at = lax.broadcasted_iota(jnp.int32, (step, step), 0)
    query_at = lax.broadcasted_iota(jnp.int32, (step, step), 1)
    head_row = lax.broadcasted_iota(jnp.int32, (8, 128), 0)
    place = lax.broadcasted_iota(jnp.int32, (1, step), 1)
    gs_ref[...] = jnp.zeros_like(gs_ref)

    def one(stream, pair):
        cols = tile(pair, 128)
        k_pair = k_ref[tile(stream, 2 * span), cols]
        v_pair = v_ref[tile(stream, 2 * span), cols]
        k_augs = [k_pair * masks[half] + kf_ref[stream, half] for half in range(2)]
        queries, outs = [], []
        for part in range(2):
            seen = span + part * step
            rows = pl.ds(pl.multiple_of(stream * span + part * step, step), step)
            q_pair, do_pair = q_ref[rows, cols], do_ref[rows, cols]
            both = (do_pair.astype(f32) * o_ref[rows, cols].astype(f32)).T
            for half in range(2):
                head = 2 * pair + half
                q_own, do_own = q_pair * masks[half], do_pair * masks[half]
                queries.append(q_own)
                outs.append(do_own)
                delta = jnp.sum(both[half * 64 : half * 64 + 64], axis=0, keepdims=True)
                log_total = lse_ref[pl.ds(stream * heads + head, 1), part * step : (part + 1) * step]
                scores = mm(k_augs[half][: seen + step], q_own + query_marks(slope_of(head), half), NT)
                dp = mm(v_pair[: seen + step], do_own, NT)
                at = slice(half * step, (half + 1) * step)
                for low, high in ((0, seen), (seen, seen + step)):
                    score = scores[low:high]
                    if low:
                        score = jnp.where(key_at <= query_at, score, masked_score)
                    chance = jnp.exp(score - log_total)
                    p_ref[part, low:high, at] = chance.astype(bf16)
                    ds_ref[part, low:high, at] = (chance * (dp[low:high] - delta)).astype(bf16)
        common = span + step
        q_parts = [jnp.concatenate(queries[2 * part : 2 * part + 2], axis=0) for part in range(2)]
        do_parts = [jnp.concatenate(outs[2 * part : 2 * part + 2], axis=0) for part in range(2)]
        base = stream * 2 * span
        for source, out_ref, parts in ((p_ref, dv_ref, do_parts), (ds_ref, dk_ref, q_parts)):
            out_ref[pl.ds(pl.multiple_of(base, step), common), cols] = (
                mm(source[0, :common, :], parts[0]) + mm(source[1, :common, :], parts[1])
            ).astype(bf16)
            out_ref[pl.ds(pl.multiple_of(base + common, step), step), cols] = mm(
                source[1, common:, :], parts[1]
            ).astype(bf16)
        k_turned = [k_aug.T for k_aug in k_augs]
        for part in range(2):
            seen = span + (part + 1) * step
            done = []
            for half in range(2):
                head = 2 * pair + half
                turned = mm(k_turned[half][:, :seen], ds_ref[part, :seen, half * step : (half + 1) * step])
                done.append(turned[half * 64 : half * 64 + 64] * 0.125)
                base_row = 64 - half * 64
                lean = (
                    turned[base_row : base_row + 1]
                    + turned[base_row + 3 : base_row + 4]
                    - (place + (part * step + span)).astype(f32) * turned[base_row + 7 : base_row + 8]
                )
                gs_ref[...] += jnp.where(head_row == head, jnp.sum(lean), 0.0)
            rows = pl.ds(pl.multiple_of(stream * span + part * step, step), step)
            dq_ref[rows, cols] = jnp.concatenate(done, axis=0).T.astype(bf16)

    def over(stream, carry):
        def inner(pair, carry):
            one(stream, pair)
            early(stream * pairs + pair)
            return carry

        carry = lax.fori_loop(0, pairs, inner, carry)
        between(stream)
        return carry

    lax.fori_loop(0, streams, over, 0)


def backward_kernel(layer, sizes, r):
    (stream_devices, block_devices, streams, span, heads, features, nvec, halves) = sizes
    place = Place(stream_devices, block_devices)
    width = r.a.shape[1]
    count = streams * span
    first = place.block == 0
    row = 3 + 4 * layer
    g1, g2 = r.rows[row : row + 1, :], r.rows[row + 2 : row + 3, :]
    step = 256
    tiles = count // step
    sems = (r.out_sem, r.in_sem)
    wide_layouts, layout_b, layout_small, unused_head = layouts(place.blocks, halves)

    def wide_reduce(half, row, *names):
        return Reduce(place, sems, row, **{name: getattr(r, f"{name}_{WIDE[half]}") for name in names})

    broads = [wide_reduce(half, 4 * half, *REDUCED[:4]) for half in range(halves)]
    row_b = 4 * halves
    if layer == 0:
        for half, broad in enumerate(broads):
            broad.line = getattr(r, f"{REDUCED[4]}_{WIDE[half]}")
            if half < halves - 1:
                broad.total = getattr(r, f"{REDUCED[6]}_{WIDE[half]}")
            else:
                broad.part = getattr(r, f"{REDUCED[5]}_{WIDE[half]}")
        dones = [
            Reduce(
                place,
                sems,
                row_b + 4 + 4 * half,
                **{name: getattr(r, f"{name}_one_{WIDE[half]}") for name in REDUCED[3:7:1] if name != REDUCED[5]},
            )
            for half in range(halves)
        ]
        narrow = Reduce(
            place, sems, 4 + 8 * halves, grad=r.grad_b, pair=r.pair_b, mates=r.mates_b, own=r.own_b
        )
        done_b = Reduce(
            place, sems, row_b, pair=r.pair_b_one, mates=r.mates_b_one, own=r.own_b_one, line=r.line_b_one, total=r.total_b_one
        )
    else:
        narrow = Reduce(place, sems, row_b, grad=r.grad_b, pair=r.pair_b)
        head = Reduce(
            place, sems, row_b + 4, grad=r.grad_head, pair=r.pair_head, mates=r.mates_head, own=r.own_head, line=r.line_head, total=r.total_head
        )
        back = Ahead(place, -1, r.dap, r.back, (r.back_out, r.back_in))

        @pl.when(place.block == place.blocks - 1)
        def _():
            r.back[...] = jnp.zeros_like(r.back)

    for grad, layout in [(broad.grad, layout) for broad, layout in zip(broads, wide_layouts)] + [(r.grad_b, layout_b)]:
        for block in layout.unused():
            grad[:, :, block] = jnp.zeros(grad.shape[:2] + grad.shape[3:], bf16)
    r.gr[...] = jnp.zeros_like(r.gr)
    hidden_parts = r.wu.shape[3] // 512

    def stream_in(part, slot):
        cols = tile(part, 512)
        return (
            pltpu.make_async_copy(r.u.at[layer, :, cols], r.u_two.at[slot], r.u_sem.at[0, slot]),
            pltpu.make_async_copy(r.gp.at[layer, :, cols], r.gp_two.at[slot], r.u_sem.at[1, slot]),
        )

    first_loads = []
    if layer == 0:
        first_loads = [
            pltpu.make_async_copy(r.dr1_in, r.dr, r.first_sem.at[0]),
            pltpu.make_async_copy(r.r.at[1], r.da, r.first_sem.at[1]),
            pltpu.make_async_copy(r.da_in, r.wide_one, r.first_sem.at[2]),
        ]
        late_loads = [
            pltpu.make_async_copy(r.r.at[0], r.wide_one, r.first_sem.at[3]),
            pltpu.make_async_copy(r.pr, r.r1, r.first_sem.at[4]),
        ]
    else:
        first_loads = [pltpu.make_async_copy(r.dr_in, r.dr, r.first_sem.at[0])]
    for load in first_loads:
        load.start()
    for load in stream_in(0, 0):
        load.start()
    r.fetch(r.wd, r.a2, r.wu)

    def fetch_rest():
        r.fetch(r.r1, r.wo, r.o, r.lse, r.q, r.k, r.v, r.wp, r.a, r.ap)
        if layer == 1:
            r.fetch(r.mem)

    place.greet(column=True)
    if layer == 0:
        for done in dones:
            done.start_c()
        done_b.start_b()

        g = r.rows[row + 4 : row + 5, :]

        def join(index, carry):
            at = tile(index, step)
            standard, scale = normalize(r.da[at, :])
            da = r.wide_one[at, :] + r.back[at, :].astype(f32)
            r.gr[4:5, :] += jnp.sum(da * standard, axis=0, keepdims=True)
            r.gr[5:6, :] += jnp.sum(da, axis=0, keepdims=True)
            r.dr[at, :] = r.dr[at, :] + norm_back(da, standard, scale, g)
            return carry

        build_marks(r.kf, r.memory_len, first)
        for load in first_loads:
            load.wait()
        fetch_rest()
        lax.fori_loop(0, tiles, join, 0)
        late_loads[0].start()
    else:
        head.start_a()
        build_marks(r.kf, r.memory_len, first)
        first_loads[0].wait()
        fetch_rest()

    r.da[...] = jnp.zeros_like(r.da)
    r.ready(r.wd, r.a2, r.wu)
    r.turned[...] = r.a2[...].T
    parts = hidden_parts
    each = parts // halves

    def feed(half, spot, carry):
        part = half * each + spot
        slot = part % 2

        @pl.when(part + 1 < parts)
        def _():
            for load in stream_in(part + 1, 1 - slot):
                load.start()

        for load in stream_in(part, slot):
            load.wait()
        dy = r.dr[...].astype(bf16)
        dh = (mm(dy, down_part(r.wd, half, spot, each, halves), NT) * r.gp_two[slot].astype(f32)).astype(bf16)
        put_down(broads[half].grad, wide_layouts[half], 0, mm(r.u_two[slot], dy, TN), spot, each)
        put_blocks(broads[half].grad, wide_layouts[half], 1, 4 * spot, mm(r.turned[...], dh))
        r.da[...] += mm(dh, up_part(r.wu, half, spot, halves), NT)
        if half == 0 and layer == 1:

            @pl.when(spot == 0)
            def _():
                head.end_a()
                head.start_b()

        if half == 1:

            @pl.when(spot == 0)
            def _():
                broads[0].end_a()
                broads[0].start_b()

        return carry

    for half in range(halves):
        lax.fori_loop(0, each, functools.partial(feed, half), 0)
        if half < halves - 1:
            broads[half].start_a()
    r.ready(r.r1, r.wo, r.o, r.lse)

    def middle(index, carry):
        at = tile(index, step)
        standard, scale = normalize(r.r1[at, :])
        da = r.da[at, :]
        r.gr[2:3, :] += jnp.sum(da * standard, axis=0, keepdims=True)
        r.gr[3:4, :] += jnp.sum(da, axis=0, keepdims=True)
        dr = r.dr[at, :] + norm_back(da, standard, scale, g2)
        r.dr[at, :] = dr
        r.do[at, :] = mm(dr.astype(bf16), flat(r.wo), NT).astype(bf16)
        return carry

    lax.fori_loop(0, tiles, middle, 0)
    if layer == 0:
        late_loads[1].start()
    put_blocks(broads[-1].grad, wide_layouts[-1], 2, 0, mm(r.o[...], r.dr[...].astype(bf16), TN))
    broads[-1].start_a()
    if layer == 0:
        for done in dones:
            done.end_c()
        done_b.end_b()
        done_b.start_c()
        for done in dones:
            done.start_d()
    else:
        head.end_b()
        head.start_c()
    wk, wv = (slice(i * width, (i + 1) * width) for i in (1, 2))

    def behind_gradient(at, behind):
        return mm(r.dk[behind, :], flat(r.wp, wk), NT) + mm(r.dv[behind, :], flat(r.wp, wv), NT)

    def early(index):
        @pl.when(index == 1)
        def _():
            broads[-1].end_a()
            broads[-1].start_b()
            if layer == 1:
                head.end_c()
                head.start_d()

        @pl.when(index == 4)
        def _():
            if layer == 1:
                head.pass_d()
            else:
                for done in dones:
                    done.pass_d()

    def between(stream):
        if layer == 0:

            @pl.when(stream == 0)
            def _():
                done_b.end_c()
                done_b.start_d()

            @pl.when(stream == 1)
            def _():
                done_b.pass_d()
                for broad in broads[:-1]:
                    broad.end_b()
                    broad.start_c()

        else:
            for part in range(span // step):
                at = pl.ds(pl.multiple_of(stream * span + part * step, step), step)
                behind = pl.ds(pl.multiple_of(stream * 2 * span + part * step, step), step)
                r.dap[at, :] = behind_gradient(at, behind).astype(bf16)
            back.start(stream, tile(stream, span))


    r.ready(r.q, r.k, r.v, r.wp)
    attend_back(
        streams,
        span,
        heads,
        (r.q, r.k, r.v, r.o, r.lse, r.kf, lambda head: r.slopes[layer, head], r.do, r.dq, r.dk, r.dv, r.gs, r.u_two, r.gp_two),
        early,
        between,
    )

    r.ready(r.a, r.ap)
    r.turned[...] = r.a[...].T
    put_blocks(r.grad_b, layout_b, 0, 0, mm(r.turned[...], r.dq[...]))
    for spot, ref in ((1, r.dk), (2, r.dv)):
        total = jnp.zeros((width, width), f32)
        for stream in range(streams):
            behind = slice(stream * 2 * span, stream * 2 * span + span)
            here = slice(stream * 2 * span + span, (stream + 1) * 2 * span)
            own = slice(stream * span, (stream + 1) * span)
            total = total + mm(r.turned[:, own], ref[here, :])
            total = total + mm(r.ap[own, :], ref[behind, :], TN)
        put_blocks(r.grad_b, layout_b, 0, 4 * spot, total)

    if layer == 0:
        r.small_acc[...] = jnp.zeros_like(r.small_acc)
        for load in late_loads:
            load.wait()
        narrow.start_a()
        broads[-1].end_b()
        broads[-1].start_c()
        for broad in broads[:-1]:
            broad.end_c()
            broad.start_d()
    else:
        narrow.start_a()
        r.ready(r.mem)

    def finish(stream, carry):
        for part in range(span // step):
            at = pl.ds(pl.multiple_of(stream * span + part * step, step), step)
            behind = pl.ds(pl.multiple_of(stream * 2 * span + part * step, step), step)
            here = pl.ds(pl.multiple_of(stream * 2 * span + span + part * step, step), step)
            da = (
                mm(r.dq[at, :], flat(r.wp, slice(0, width)), NT)
                + mm(r.dk[here, :], flat(r.wp, wk), NT)
                + mm(r.dv[here, :], flat(r.wp, wv), NT)
            )
            if layer == 0:
                dap = behind_gradient(at, behind)
                standard, scale = normalize(r.wide_one[at, :])
                before, before_scale = normalize(r.r1[at, :])
                r.gr[0:1, :] += jnp.sum(da * standard + dap * before, axis=0, keepdims=True)
                r.gr[1:2, :] += jnp.sum(da + dap, axis=0, keepdims=True)
                dr = r.dr[at, :] + norm_back(da, standard, scale, g1)
                drp = norm_back(dap, before, before_scale, g1)
                drp = jnp.where(first, 0.0, drp)
                r.gr[6:7, :] += jnp.sum(dr + drp, axis=0, keepdims=True)
                r.small_acc[...] += mm(dr.astype(bf16), r.frames[at, :], TN)
                r.small_acc[...] += mm(drp.astype(bf16), r.halo[at, :], TN)
                if part == 0:

                    @pl.when(stream == 1)
                    def _():
                        narrow.end_a()
                        narrow.start_b()
                        for broad in broads[:-1]:
                            broad.pass_d()

            else:
                r.da[at, :] = da
                before, before_scale = normalize(r.mem[at, :].astype(f32))
                dap = jnp.where(first, r.dap[at, :].astype(f32), 0.0)
                r.gr[0:1, :] += jnp.sum(dap * before, axis=0, keepdims=True)
                r.gr[1:2, :] += jnp.sum(dap, axis=0, keepdims=True)
        return carry

    lax.fori_loop(0, streams, finish, 0)
    if layer == 0:
        listed = [r.gr[6:7, :], r.gr_last[0:2, :], r.gr[0:4, :], r.gr_one[0:2, :] + r.gr[4:6, :], r.gr_one[2:4, :]]
        listed = [jnp.zeros((features, width), f32)] + listed + [jnp.zeros((128 - features - nvec, width), f32)]
        lane = lax.broadcasted_iota(jnp.int32, (1, 128), 1)
        merged = jnp.where(lane < features, r.small_acc[...], jnp.concatenate(listed, axis=0).T)
        for block in layout_small.unused():
            r.grad_small[:, :, block] = jnp.zeros(r.grad_small.shape[:2] + r.grad_small.shape[3:], bf16)
        put_blocks(r.grad_small, layout_small, 0, 0, merged)
        done_b.end_d()
        for done in dones:
            done.end_d()
        for broad in broads[:-1]:
            broad.end_d()
        broads[-1].end_c()
        narrow.end_b()
    else:
        head.end_d()
        narrow.end_a()
        for broad in broads:
            broad.end_b()
        for stream in range(streams):
            at = tile(stream, span)
            back.sent(stream, at)
            back.arrived(stream, at)


def lanes_of(entries):
    lane = lax.broadcasted_iota(jnp.int32, (1, 128), 1)
    row = jnp.zeros((1, 128), f32)
    for number, value in entries:
        row = jnp.where(lane == number, value, row)
    return row


def pick(row, number):
    lane = lax.broadcasted_iota(jnp.int32, (1, 128), 1)
    return jnp.sum(jnp.where(lane == number, row, 0.0))


class State:
    def __init__(self, blocks, layers, rows, halves, wides, narrows, head):
        wide_layouts, plain, last, head_layout = layouts(blocks, halves)
        self.small = last.spot(0, 0)
        self.rows, self.halves = rows, halves
        self.items = []
        for layer in range(layers):
            self.items.append((1, layer, narrows[layer], plain, 0, 1 + layer, 0))
            self.items.append((2, layer, wides[layer][-1], wide_layouts[-1], 2, 1 + layers + layer, 0))
            for half in range(halves):
                total, layout = wides[layer][half], wide_layouts[half]
                self.items.append((3, layer, total, layout, 1, 1 + 2 * layers + layer, half))
                self.items.append((4, layer, total, layout, 0, 1 + 3 * layers + layer, half))
        self.items.append((5, None, head, head_layout, 0, 1 + 4 * layers, 0))
        self.vector_start = 2 + 4 * layers

    def place(self, array, layer, block, half):
        across, up = block, 0
        if array == 3 and self.halves == 2:
            across = 2 * block + half
        if array == 4:
            across, up = block % 4, block // 4 + half * (4 // self.halves)
        rows, cols = up * self.rows, across * 128
        if not isinstance(block, int):
            rows, cols = pl.multiple_of(rows, self.rows), pl.multiple_of(cols, 128)
        where = (pl.ds(rows, self.rows), pl.ds(cols, 128))
        return where if layer is None else (layer,) + where


def state_of(block_devices, layers, halves, r):
    zero = [getattr(r, f"{REDUCED[6]}_{WIDE[half]}") for half in range(halves)]
    one = [getattr(r, f"{REDUCED[6]}_one_{WIDE[half]}") for half in range(halves)]
    return State(
        block_devices, layers, r.total_b.shape[1], halves, (zero, one), (r.total_b, r.total_b_one), r.total_head
    )


def tail_kernel(sizes, layers, r):
    (stream_devices, block_devices, streams, span, heads, features, nvec, halves) = sizes
    place = Place(stream_devices, block_devices)
    index = lax.axis_index(STREAM)
    sems = (r.out_sem, r.in_sem)
    wide_name = WIDE[halves - 1]
    broad = Reduce(place, sems, 0, total=getattr(r, f"{REDUCED[6]}_{wide_name}"))
    narrow = Reduce(place, sems, 4 * halves, own=r.own_b, line=r.line_b, total=r.total_b)
    small = Reduce(
        place,
        sems,
        4 * halves + 4,
        grad=r.grad_small,
        pair=r.pair_small,
        mates=r.mates_small,
        own=r.own_small,
        line=r.line_small,
        total=r.total_small,
    )
    r.fetch()
    broad.total[broad.piece(place.block)] = getattr(r, f"{REDUCED[5]}_{wide_name}")[...]
    barrier = pltpu.get_barrier_semaphore()
    everyone = stream_devices * block_devices
    mine = place.block * stream_devices + index

    def device_of(number):
        return {SEQ: lax.div(number, stream_devices), STREAM: lax.rem(number, stream_devices)}

    def greet(distance, carry):
        device = device_of(lax.rem(mine + distance, everyone))
        pl.semaphore_signal(barrier, inc=1, device_id=device, device_id_type=MESH)
        return carry

    lax.fori_loop(1, everyone, greet, 0)
    pl.semaphore_wait(barrier, everyone - 1)
    small.start_a()
    narrow.start_c()
    rows = r.total_b.shape[1]
    state = state_of(block_devices, layers, halves, r)
    arrays = [[getattr(r, f"{kind}_{number}") for number in range(7)] for kind in KINDS]
    weights, firsts, seconds = arrays
    square = jnp.zeros((rows, 128), f32)
    finished = [getattr(r, f"{REDUCED[6]}_{WIDE[half]}") for half in range(halves)] + [r.total_b_one, r.total_head]
    finished += [getattr(r, f"{REDUCED[6]}_one_{WIDE[half]}") for half in range(halves)]
    for ref in finished:
        size = ref.shape[0] // block_devices
        value = ref[pl.ds(place.block * size, size)].astype(f32)
        square = square + jnp.sum(value * value, axis=0)
    small.end_a()
    small.start_b()
    for array in arrays:
        r.ready(*array)

    shares = []
    for array, layer, total, layout, part, matrix, half in state.items:
        base, per, count = layout.parts[part]
        for number in range(per):
            block = place.block * per + number
            valid = jnp.where(block < count, 1.0, 0.0)
            spot = state.place(array, layer, jnp.minimum(block, count - 1), half)
            shares.append((array, spot, total, place.block * layout.size + base + number, matrix, valid))
    edge = jnp.where(place.block == 0, 1.0, 0.0)

    def matrix_squares(value_of, turned, vector_rows, base):
        found = {}
        for array, spot, total, block, matrix, valid in shares:
            value = value_of(array, spot, total, block)
            value = value * value * valid
            found[matrix] = value if matrix not in found else found[matrix] + value
        entries = [(base + matrix, jnp.sum(value)) for matrix, value in found.items()]
        entries.append((base, jnp.sum(turned * turned) * edge))
        row = lanes_of(entries)
        lane = lax.broadcasted_iota(jnp.int32, (nvec, 128), 1)
        down = lax.broadcasted_iota(jnp.int32, (nvec, 128), 0)
        column = jnp.sum(vector_rows * vector_rows, axis=1, keepdims=True) * edge
        return row + jnp.sum(jnp.where(lane == base + state.vector_start + down, column, 0.0), axis=0, keepdims=True)

    weight_row = matrix_squares(
        lambda array, spot, total, block: weights[array][spot], weights[0][...], weights[6][...], 64
    )
    narrow.end_c()
    size = r.total_b.shape[0] // block_devices
    value = r.total_b[pl.ds(place.block * size, size)].astype(f32)
    square = square + jnp.sum(value * value, axis=0)
    small.end_b()
    small.start_c()

    def exchange(ref, slot, meanwhile=None):
        def copy(view, device):
            return pltpu.make_async_remote_copy(
                src_ref=view,
                dst_ref=view,
                send_sem=r.all_out.at[slot],
                recv_sem=r.all_in.at[slot],
                device_id=device,
                device_id_type=MESH,
            )

        def send(distance, carry):
            copy(ref.at[mine], device_of(lax.rem(mine + distance, everyone))).start()
            return carry

        lax.fori_loop(1, everyone, send, 0)
        if meanwhile is not None:
            meanwhile()
        others = copy(ref.at[pl.ds(0, everyone - 1)], place.sibling)
        others.wait_recv()
        others.wait_send()
        return jnp.sum(ref[...], axis=0)

    lane = lax.broadcasted_iota(jnp.int32, (8, 128), 1)
    down = lax.broadcasted_iota(jnp.int32, (8, 128), 0)
    plain = jnp.where(lane == 1, r.loss[...], 0.0) * jnp.where(down == 0, 1.0, 0.0)
    for layer, ref in enumerate((r.gs_zero, r.gs_one)):
        plain = plain + jnp.where(lane == 16 + layer * heads + down, ref[...], 0.0)
    plain = jnp.sum(plain, axis=0, keepdims=True) + weight_row
    small.end_c()
    size = r.total_small.shape[0] // block_devices
    value = r.total_small[pl.ds(place.block * size, size)].astype(f32)
    square = square + jnp.sum(value * value, axis=0)
    r.rows_one[mine] = plain + lanes_of([(0, jnp.sum(square))])

    def hand_round():
        broad.start_d()
        narrow.start_d()
        small.start_d()

    sums = exchange(r.rows_one, 0, hand_round)
    for group in (broad, narrow, small):
        group.pass_d()
    lane = lax.broadcasted_iota(jnp.int32, (1, 128), 1)
    slope_lanes = jnp.logical_and(lane >= 16, lane < 16 + layers * heads)
    clip = jnp.sqrt(
        jnp.full((1, 128), pick(sums, 0)) + jnp.sum(jnp.where(slope_lanes, sums * sums, 0.0), axis=1, keepdims=True)
    )
    factor = jnp.minimum(1.0, clip_limit / clip)
    scale = factor[:, 0:1]

    def direction(weight, grad, first, second):
        return adam_direction(weight, grad, first, second, decay_rate)[2]

    both = r.total_small[place.block * size + state.small].astype(f32)
    turned = direction(weights[0][...], both[:, :features] * scale, firsts[0][...], seconds[0][...])
    vector_rows = direction(
        weights[6][...], both.T[features : features + nvec] * scale, firsts[6][...], seconds[6][...]
    )
    r.rows_two[mine] = matrix_squares(
        lambda array, spot, total, block: direction(
            weights[array][spot], total[block].astype(f32) * factor, firsts[array][spot], seconds[array][spot]
        ),
        turned,
        vector_rows,
        0,
    )
    r.sums[0:1, :] = exchange(r.rows_two, 1)
    r.sums[1:2, :] = jnp.concatenate([sums[:, 64:], sums[:, :64]], axis=1)
    r.sums[2:3, :] = sums
    r.sums[3:4, :] = clip
    r.sums[4:5, :] = factor
    broad.end_d()
    narrow.end_d()
    small.end_d()


def update_kernel(sizes, layers, r):
    (stream_devices, block_devices, streams, span, heads, features, nvec, halves) = sizes
    keep = pltpu.make_async_copy(r.low, r.layer_inputs, r.keep_sem.at[0])
    weights, firsts, seconds = ([getattr(r, f"{kind}_{number}") for number in range(7)] for kind in KINDS)
    fresh, new_firsts, new_seconds = ([getattr(r, f"new_{kind}_{number}") for number in range(7)] for kind in KINDS)
    state = state_of(block_devices, layers, halves, r)
    totals = {id(item[2]): item[2] for item in state.items}
    r.fetch(r.total_small, *totals.values())
    for number in (0, 6, 1, 2):
        r.fetch(weights[number], firsts[number], seconds[number])
    r.ready(r.total_small, *totals.values())
    factor = r.sums[4:5, :]
    scale = factor[:, 0:1]
    norms = jnp.sqrt(r.sums[0:2, :])
    ratios = norms[1:2] / norms[0:1]
    small = r.total_small[state.small].astype(f32)
    lane = lax.broadcasted_iota(jnp.int32, (nvec, 128), 1)
    down = lax.broadcasted_iota(jnp.int32, (nvec, 128), 0)
    vector_ratio = jnp.sum(jnp.where(lane == state.vector_start + down, ratios, 0.0), axis=1, keepdims=True)

    def finish(array):
        r.flush(fresh[array], new_firsts[array], new_seconds[array])

    for array, grad, ratio in (
        (0, small[:, :features], jnp.full((1, 1), pick(ratios, 0))),
        (6, small.T[features : features + nvec], vector_ratio),
    ):
        r.ready(weights[array], firsts[array], seconds[array])
        weight = weights[array][...]
        first, second, direction = adam_direction(
            weight, grad * scale, firsts[array][...], seconds[array][...], decay_rate
        )
        new_firsts[array][...] = first
        new_seconds[array][...] = second
        fresh[array][...] = weight - lamb_rate * ratio * direction
        finish(array)
    for number in range(1, 6):
        if number + 2 < 6:
            r.fetch(weights[number + 2], firsts[number + 2], seconds[number + 2])
        elif number + 2 == 6:
            r.fetch(r.low)
        r.ready(weights[number], firsts[number], seconds[number])
        for array, layer, total, layout, part, matrix, half in state.items:
            if array != number:
                continue
            ratio = jnp.full((1, 128), lamb_rate * pick(ratios, matrix))
            for block in range(layout.parts[part][2]):
                spot = state.place(array, layer, block, half)
                weight = weights[array][spot]
                first, second, direction = adam_direction(
                    weight,
                    total[layout.spot(part, block)].astype(f32) * factor,
                    firsts[array][spot],
                    seconds[array][spot],
                    decay_rate,
                )
                new_firsts[array][spot] = first
                new_seconds[array][spot] = second
                fresh[array][spot] = weight - ratio * direction
        finish(number)
    r.ready(r.low)
    keep.start()
    sums = r.sums[2:3, :]
    grad = jnp.concatenate([sums[:, 16 + layer * heads : 16 + (layer + 1) * heads] for layer in range(layers)], axis=0)
    slopes = r.slopes[...]
    first, second, direction = adam_direction(slopes, grad * scale, r.first_slopes[...], r.second_slopes[...], 0.0)
    r.new_first_slopes[...] = first
    r.new_second_slopes[...] = second
    r.fresh_slopes[...] = slopes - slope_rate * direction
    count = state.vector_start + nvec
    r.norms[0:1, 0:count] = norms[1:2, :count]
    r.norms[1:2, 0:count] = norms[0:1, :count]
    r.norms[0:1, count : count + 1] = jnp.full((1, 1), jnp.sqrt(jnp.sum(slopes * slopes)))
    r.norms[1:2, count : count + 1] = jnp.full((1, 1), jnp.sqrt(jnp.sum(direction * direction)))
    r.loss[...] = sums[:, 1:2]
    r.clip[...] = r.sums[3:4, 0:1]
    r.flushed()
    keep.wait()


def whole(space=pltpu.VMEM):
    return pl.BlockSpec(memory_space=space)


def call_named(
    kernel,
    ins,
    outs,
    scratch=None,
    sems=None,
    any_ins=None,
    lazy=None,
    flush=None,
    any_outs=None,
    smem=None,
    layer=None,
    layered=(),
    flops=0,
    collective=None,
):
    any_ins, lazy, flush = any_ins or {}, lazy or {}, flush or {}
    any_outs, smem = any_outs or {}, smem or {}
    scratch, sems = dict(scratch or {}), dict(sems or {})
    dma = pltpu.SemaphoreType.DMA
    for key, array in lazy.items():
        scratch[key] = (array.shape[1:] if key in layered else array.shape, array.dtype)
    scratch.update(flush)
    if lazy:
        sems.update(load_sem=dma((len(lazy),)))
    if flush:
        sems.update(store_sem=dma((len(flush),)))
    far = [FAR + key for key in lazy]
    names = list(ins) + list(any_ins) + far + list(smem)
    names += list(outs) + list(any_outs) + [FAR + key for key in flush] + list(scratch) + list(sems)
    out_shapes = list(outs.values()) + list(any_outs.values()) + list(flush.values())
    made = pl.pallas_call(
        lambda *refs: kernel(Refs(names, refs, lazy, flush, layer, layered)),
        name=kernel.func.__name__ if layer is None else f"{kernel.func.__name__}_{layer}",
        out_shape=[jax.ShapeDtypeStruct(*out) for out in out_shapes],
        in_specs=[whole()] * len(ins)
        + [whole(pl.ANY)] * (len(any_ins) + len(lazy))
        + [whole(pltpu.SMEM)] * len(smem),
        out_specs=[whole()] * len(outs) + [whole(pl.ANY)] * (len(any_outs) + len(flush)),
        scratch_shapes=[pltpu.VMEM(*item) for item in scratch.values()] + list(sems.values()),
        compiler_params=pltpu.CompilerParams(
            vmem_limit_bytes=VMEM_LIMIT, collective_id=collective, has_side_effects=collective is not None
        ),
        cost_estimate=pl.CostEstimate(flops=flops, bytes_accessed=20000000, transcendentals=0),
    )(*ins.values(), *any_ins.values(), *lazy.values(), *smem.values())
    return dict(zip(list(outs) + list(any_outs) + list(flush), made))


class Made:
    def __init__(self, *args, **options):
        for name, array in call_named(*args, **options).items():
            setattr(self, name, array)


class Groups:
    def __init__(self, layout, shapes):
        self.layout = layout
        for name, shape in shapes.items():
            setattr(self, name, shape)


def adam_direction(weight, grad, first, second, decay):
    new_first = beta_one * first + (1.0 - beta_one) * grad
    new_second = beta_two * second + (1.0 - beta_two) * grad * grad
    second_hat = new_second * (1.0 / (1.0 - beta_two**STEP))
    below = second_hat * lax.rsqrt(second_hat) + adam_eps
    return (new_first, new_second, (new_first * (1.0 / (1.0 - beta_one**STEP))) / below + decay * weight)


def shards(
    frames,
    targets,
    frame_count,
    memory,
    memory_len,
    input_weight,
    project_weight,
    output_weight,
    up_weight,
    down_weight,
    head_weight,
    vectors,
    slopes,
    first_input,
    first_project,
    first_output,
    first_up,
    first_down,
    first_head,
    first_vectors,
    first_slopes,
    second_input,
    second_project,
    second_output,
    second_up,
    second_down,
    second_head,
    second_vectors,
    second_slopes,
):
    streams, span, features = frames.shape
    layers, heads = slopes.shape
    nvec = vectors.shape[0]
    width = project_weight.shape[2] // 3
    hidden = up_weight.shape[2]
    codes = head_weight.shape[1]
    count = streams * span
    devices, blocks = lax.axis_size(STREAM), lax.axis_size(SEQ)
    halves = 2 if hidden // devices == 256 else 1
    chips = devices // 2
    sizes = (devices, blocks, streams, span, heads, features, nvec, halves)
    memory_flat = memory.reshape((layers, count, width))
    rows_each = width // devices
    full = ((count, width), f32)
    low = ((count, width), bf16)
    joined = ((2 * count, width), bf16)
    wide = ((count, hidden), bf16)
    lse = ((streams * heads, span), f32)
    cost = 2 * count * (5 * width * width + width * width + 2 * width * hidden) + 4 * count * 2 * span * width
    dma = pltpu.SemaphoreType.DMA

    def gathered(rows_all, cols):
        return ((chips, 2, rows_all // devices, cols), bf16)

    def grads_of(number):
        return dict(
            grad=((chips, 2, number, rows_each, 128), bf16),
            pair=((chips, number, rows_each, 128), bf16),
            mates=((chips, number, rows_each, 128), bf16),
            own=((number, rows_each, 128), bf16),
            line=((blocks, number // blocks, rows_each, 128), bf16),
            part=((number // blocks, rows_each, 128), bf16),
            total=((number, rows_each, 128), bf16),
        )

    wide_layouts, *other_layouts = layouts(blocks, halves)
    group_b, group_small, group_head = (Groups(layout, grads_of(layout.total)) for layout in other_layouts)
    groups_wide = [Groups(layout, grads_of(layout.total)) for layout in wide_layouts]

    def wide_named(name, form=""):
        return {f"{name}{form}_{WIDE[half]}": getattr(group, name) for half, group in enumerate(groups_wide)}

    def of(source, name, form="", start=0, end=halves):
        names = [f"{name}{form}_{WIDE[half]}" for half in range(start, end)]
        return {key: getattr(source, key) for key in names}

    def last_named(name):
        return {f"{name}_{WIDE[halves - 1]}": getattr(groups_wide[-1], name)}

    def early_named(name):
        return {f"{name}_{WIDE[half]}": getattr(group, name) for half, group in enumerate(groups_wide[:-1])}

    grad_name, pair_name, mates_name, own_name, line_name, part_name, total_name = REDUCED
    kept = dict(
        a=low, ap=low, q=low, k=joined, v=joined, o=low, lse=lse, r1=full, a2=low, u=wide, gp=wide, res=full, low=low
    )
    weight_shapes = dict(
        wp=gathered(width, 3 * width), wo=gathered(width, width), wu=gathered(width, hidden), wd=gathered(hidden, width)
    )
    layer_weights = {f"{key}_{layer}": item for layer in range(layers) for key, item in weight_shapes.items()}
    gather_count = 2 + len(layer_weights)
    score = ((2 * span, span // 2), f32)
    chance = ((2 * span, span // 2), bf16)
    scalars = dict(memory_len=memory_len, slopes=slopes)
    made = Made(
        functools.partial(forward_kernel, sizes),
        dict(
            frames=frames.transpose((0, 2, 1)),
            targets=targets.reshape((count // 128, 128)),
            input_turned=input_weight.T,
            vectors=vectors,
        ),
        dict(
            rows=((16, width), f32),
            gr_last=((8, width), f32),
            loss=((8, 128), f32),
            grad_head=group_head.grad,
            halo=((count, 128), bf16),
            frames_wide=((count, 128), bf16),
        ),
        dict(
            kept,
            **layer_weights,
            res_two=full,
            pr=full,
            nxt=low,
            behind=low,
            small=gathered(width, 128),
            wh=gathered(width, codes),
            small_rows=((128 - features, rows_each), f32),
            frames_tall=((128, span), bf16),
            kf=((streams, 2, 2 * span, 128), bf16),
            acc=((width, codes), f32),
            score_one=score,
            score_two=score,
            chance_one=chance,
            chance_two=chance,
        ),
        dict(
            out_sem=dma((gather_count, max(chips, 5))),
            in_sem=dma((gather_count, max(chips, 5))),
            frame_sem=dma((2, 1)),
            next_out=dma((streams,)),
            next_in=dma((streams,)),
            save_sem=dma((layers, len(kept), streams)),
            weight_sem=dma((layers, 4)),
            pr_sem=dma((streams,)),
            dr_sem=dma((1,)),
        ),
        any_outs=dict(
            far_pr=full,
            dr=full,
            **{FAR + key: ((layers,) + item[0], item[1]) for key, item in kept.items()},
            **{FAR + key: item for key, item in layer_weights.items()},
        ),
        lazy=dict(
            pw=project_weight, ow=output_weight, uw=up_weight, dw=down_weight, hw=head_weight, mem=memory_flat
        ),
        smem=dict(scalars, frame_count=frame_count),
        flops=2 * cost,
        collective=0,
    )

    def loaded(layer):
        held = [getattr(made, f"{FAR}{key}_{layer}") for key in weight_shapes]
        return dict(
            wd=held[3],
            a2=made.far_a2,
            wu=held[2],
            r1=made.far_r1,
            wo=held[1],
            o=made.far_o,
            lse=made.far_lse,
            q=made.far_q,
            k=made.far_k,
            v=made.far_v,
            wp=held[0],
            a=made.far_a,
            ap=made.far_ap,
        )

    layered = tuple(kept) + tuple(dict(mem=0))
    slots = max(chips, blocks)
    work = dict(
        do=low,
        dq=low,
        dk=joined,
        dv=joined,
        turned=((width, count), bf16),
        kf=((streams, 2, 2 * span, 128), bf16),
        **wide_named(pair_name),
        **wide_named(mates_name),
        **wide_named(grad_name),
        u_two=((2, count, 512), bf16),
        gp_two=((2, count, 512), bf16),
    )
    work_sems = dict(out_sem=dma((8 + 8 * halves, slots)), in_sem=dma((8 + 8 * halves, slots)), u_sem=dma((2, 2)), first_sem=dma((5,)))
    streamed = dict(u=made.far_u, gp=made.far_gp)
    one = Made(
        functools.partial(backward_kernel, 1, sizes),
        dict(rows=made.rows, grad_head=made.grad_head),
        dict(
            gr=((8, width), f32),
            gs=((8, 128), f32),
            dr=full,
            da=full,
            back=low,
            **wide_named(own_name),
            pair_b=group_b.pair,
            total_head=group_head.total,
        ),
        dict(
            work,
            dap=low,
            grad_b=group_b.grad,
            pair_head=group_head.pair,
            mates_head=group_head.mates,
            own_head=group_head.own,
            line_head=group_head.line,
        ),
        dict(work_sems, back_out=dma((streams,)), back_in=dma((streams,))),
        any_ins=dict(streamed, dr_in=made.dr),
        lazy=dict(loaded(1), mem=memory_flat),
        layered=layered,
        layer=1,
        smem=scalars,
        flops=2 * cost,
        collective=2,
    )
    zero = Made(
        functools.partial(backward_kernel, 0, sizes),
        dict(
            rows=made.rows,
            frames=made.frames_wide,
            halo=made.halo,
            back=one.back,
            gr_last=made.gr_last,
            gr_one=one.gr,
            **{f"{own_name}_one_{WIDE[half]}": getattr(one, f"{own_name}_{WIDE[half]}") for half in range(halves)},
            pair_b_one=one.pair_b,
        ),
        dict(
            gs=((8, 128), f32),
            **last_named(part_name),
            **early_named(total_name),
            own_b=group_b.own,
            grad_small=group_small.grad,
            **wide_named(total_name, form="_one"),
            total_b_one=group_b.total,
        ),
        dict(
            work,
            gr=((8, width), f32),
            dr=full,
            da=full,
            small_acc=((width, 128), f32),
            wide_one=full,
            **wide_named(own_name),
            **wide_named(line_name),
            **wide_named(line_name, form="_one"),
            grad_b=group_b.grad,
            pair_b=group_b.pair,
            mates_b=group_b.mates,
            mates_b_one=group_b.mates,
            own_b_one=group_b.own,
            line_b_one=group_b.line,
        ),
        work_sems,
        any_ins=dict(streamed, dr1_in=one.dr, da_in=one.da, r=made.far_res, pr=made.far_pr),
        lazy=loaded(0),
        layered=layered,
        layer=0,
        smem=scalars,
        flops=2 * cost,
        collective=3,
    )
    arrays = (
        (input_weight.T, project_weight, output_weight, up_weight, down_weight, head_weight, vectors),
        (first_input.T, first_project, first_output, first_up, first_down, first_head, first_vectors),
        (second_input.T, second_project, second_output, second_up, second_down, second_head, second_vectors),
    )
    order = (0, 6, 1, 2, 3, 4, 5)
    state = {f"{kind}_{number}": array[number] for number in order for kind, array in zip(KINDS, arrays)}
    tile_shape = ((8, 128), f32)
    tail = Made(
        functools.partial(tail_kernel, sizes, layers),
        dict(
            **of(zero, part_name, start=halves - 1),
            **of(zero, total_name, end=halves - 1),
            own_b=zero.own_b,
            grad_small=zero.grad_small,
            **of(zero, total_name, form="_one"),
            total_b_one=zero.total_b_one,
            total_head=one.total_head,
            gs_zero=zero.gs,
            gs_one=one.gs,
            loss=made.loss,
        ),
        dict(last_named(total_name), total_b=group_b.total, total_small=group_small.total, sums=tile_shape),
        dict(
            line_b=group_b.line,
            pair_small=group_small.pair,
            mates_small=group_small.mates,
            own_small=group_small.own,
            line_small=group_small.line,
            rows_one=((devices * blocks, 1, 128), f32),
            rows_two=((devices * blocks, 1, 128), f32),
        ),
        dict(
            out_sem=dma((8 + 4 * halves, slots)),
            in_sem=dma((8 + 4 * halves, slots)),
            all_out=dma((2,)),
            all_in=dma((2,)),
        ),
        lazy=state,
        collective=4,
    )
    moved = {f"new_{kind}_{number}": (array[number].shape, f32) for number in order for kind, array in zip(KINDS, arrays)}
    fresh = Made(
        functools.partial(update_kernel, sizes, layers),
        dict(slopes=slopes, first_slopes=first_slopes, second_slopes=second_slopes, sums=tail.sums),
        dict(
            fresh_slopes=(slopes.shape, f32),
            new_first_slopes=(slopes.shape, f32),
            new_second_slopes=(slopes.shape, f32),
            norms=((2, 3 + 4 * layers + nvec), f32),
            loss=((1, 1), f32),
            clip=((1, 1), f32),
        ),
        sems=dict(keep_sem=dma((1,))),
        any_outs=dict(layer_inputs=((layers, count, width), bf16)),
        lazy=dict(
            **of(tail, total_name, start=halves - 1),
            **of(zero, total_name, end=halves - 1),
            total_b=tail.total_b,
            total_small=tail.total_small,
            **of(zero, total_name, form="_one"),
            total_b_one=zero.total_b_one,
            total_head=one.total_head,
            **state,
            low=made.far_low,
        ),
        flush=moved,
    )

    def results(kind, last):
        found = [getattr(fresh, f"new_{kind}_{number}") for number in range(7)]
        return [found[0].T] + found[1:] + [last]

    return (
        fresh.loss.reshape(()),
        fresh.layer_inputs.reshape((layers, streams, span, width)),
        fresh.clip.reshape(()),
        fresh.norms.T,
        *results(KINDS[0], fresh.fresh_slopes),
        *results(KINDS[1], fresh.new_first_slopes),
        *results(KINDS[2], fresh.new_second_slopes),
    )


def solution(mesh):
    rows3 = P(None, STREAM, None)
    state = (P(None, STREAM), rows3, rows3, rows3, rows3, P(STREAM, None), P(None, STREAM), P())
    in_specs = (
        P(STREAM, SEQ, None),
        P(STREAM, SEQ),
        P(STREAM),
        P(None, STREAM, None, None),
        P(STREAM),
    ) + state * 3
    out_specs = (P(), P(None, STREAM, SEQ, None), P(), P()) + state * 3
    return jax.shard_map(shards, mesh=mesh, in_specs=in_specs, out_specs=out_specs, check_vma=False)
```

```python
import functools

import jax
import jax.numpy as jnp
from jax import lax
from jax.experimental import pallas as pl
from jax.experimental.pallas import tpu as pltpu
from jax.sharding import PartitionSpec as P

STEP = 10


ln_eps = 1e-05
clip_limit = 0.002
beta_one = 0.9
beta_two = 0.999
lamb_rate = 0.3
slope_rate = 0.001
decay_rate = 0.01
adam_eps = 1e-11
masked_score = -1e30

STREAM, SEQ, FAR = "stream", "seq", "far_"
KINDS = ("weight", "first", "second")
WIDE = ("a", "c")
REDUCED = ("grad", "pair", "mates", "own", "line", "part", "total")
NN = (((1,), (0,)), ((), ()))
NT = (((1,), (1,)), ((), ()))
TN = (((0,), (0,)), ((), ()))
VMEM_LIMIT = 63 * 1024 * 1024
f32 = jnp.float32
bf16 = jnp.bfloat16


def mm(left, right, dims=NN):
    return lax.dot_general(left, right, dims, preferred_element_type=f32)


MESH = pl.DeviceIdType.MESH


class Place:
    def __init__(self, streams, blocks):
        self.chips = streams // 2
        self.blocks = blocks
        index = lax.axis_index(STREAM)
        self.chip = index // 2
        self.core = index % 2
        self.block = lax.axis_index(SEQ)
        self.sibling = {STREAM: 2 * self.chip + 1 - self.core}
        self.across = self.chip // 2 * 2 + 1 - self.chip % 2
        self.along = (self.chip + 2) % 4
        self.opposite = 3 - self.chip

        self.pair_block = self.block // 2 * 2 + 1 - self.block % 2
        self.far_block = (self.block + 2) % 4

    def chip_device(self, chip):
        return {STREAM: 2 * chip + self.core}

    def other(self, distance):
        return (self.chip + distance) % self.chips

    def mate(self, distance):
        return {STREAM: 2 * self.other(distance) + self.core}

    def peer(self, distance):
        return (self.block + distance) % self.blocks

    def greet(self, line=False, column=False):
        barrier = pltpu.get_barrier_semaphore()

        def hello(device):
            pl.semaphore_signal(barrier, inc=1, device_id=device, device_id_type=MESH)

        hello(self.sibling)
        for distance in range(1, self.chips):
            hello(self.mate(distance))
        if line:

            @pl.when(self.block > 0)
            def _():
                hello({SEQ: self.block - 1})

            pl.semaphore_wait(barrier, self.chips + jnp.where(self.block < self.blocks - 1, 1, 0))
        elif column:
            for distance in range(1, self.blocks):
                hello({SEQ: self.peer(distance)})
            pl.semaphore_wait(barrier, self.chips + self.blocks - 1)
        else:
            pl.semaphore_wait(barrier, self.chips)


class Gather:
    def __init__(self, place, ref, sems, row, direct=False):
        self.place, self.ref, self.sems, self.row = place, ref, sems, row
        self.square = place.chips == 4 and not direct

    def copy(self, slot, view, device):
        return pltpu.make_async_remote_copy(
            src_ref=view,
            dst_ref=view,
            send_sem=self.sems[0].at[self.row, slot],
            recv_sem=self.sems[1].at[self.row, slot],
            device_id=device,
            device_id_type=MESH,
        )

    def shard(self, chip, half=None):
        view = self.ref.at[chip, self.place.core]
        if half is None:
            return view
        size = self.ref.shape[2] // 2
        return view.at[pl.ds(half * size, size)]

    def far(self, distance, chip):
        return self.copy(distance, self.shard(chip), self.place.mate(distance))

    def beside(self, slot, chip, half, target):
        return self.copy(slot, self.shard(chip, half), self.place.chip_device(target))

    def near(self, core):
        return self.copy(0, self.ref.at[:, core], self.place.sibling)

    def push(self):
        place = self.place
        if self.square:
            self.beside(1, place.chip, None, place.across).start()
            self.beside(2, place.chip, None, place.along).start()
        else:
            for distance in range(1, place.chips):
                self.far(distance, place.chip).start()

    def pass_on(self):
        place = self.place
        if self.square:
            self.beside(1, place.across, None, place.across).wait_recv()
            self.beside(2, place.along, None, place.along).wait_recv()
            self.beside(3, place.across, 0, place.along).start()
            self.beside(4, place.along, 1, place.across).start()

    def relay(self):
        place = self.place
        if self.square:
            self.beside(3, place.opposite, 0, place.along).wait_recv()
            self.beside(4, place.opposite, 1, place.across).wait_recv()
        else:
            for distance in range(1, place.chips):
                self.far(distance, place.other(place.chips - distance)).wait_recv()
        self.near(place.core).start()

    def finish(self):
        place = self.place
        self.near(1 - place.core).wait_recv()
        self.near(place.core).wait_send()
        if self.square:
            self.beside(1, place.chip, None, place.across).wait_send()
            self.beside(2, place.chip, None, place.along).wait_send()
            self.beside(3, place.across, 0, place.along).wait_send()
            self.beside(4, place.along, 1, place.across).wait_send()
        else:
            for distance in range(1, place.chips):
                self.far(distance, place.chip).wait_send()


class Reduce:
    def __init__(self, place, sems, row, grad=None, pair=None, mates=None, own=None, line=None, total=None, part=None):
        self.part = part
        self.place, self.sems, self.row = place, sems, row
        self.grad, self.pair, self.mates = grad, pair, mates
        self.own, self.line, self.total = own, line, total

    def copy(self, phase, slot, src, dst, device):
        return pltpu.make_async_remote_copy(
            src_ref=src,
            dst_ref=dst,
            send_sem=self.sems[0].at[self.row + phase, slot],
            recv_sem=self.sems[1].at[self.row + phase, slot],
            device_id=device,
            device_id_type=MESH,
        )

    def copy_a(self):
        place = self.place
        return self.copy(0, 0, self.grad.at[:, 1 - place.core], self.pair, place.sibling)

    def copy_b(self, distance, source=None):
        place = self.place
        slot = place.chip if source is None else source
        return self.copy(
            1, distance, self.pair.at[place.other(distance)], self.mates.at[slot], place.mate(distance)
        )

    def piece(self, block):
        size = (self.total if self.own is None else self.own).shape[0] // self.place.blocks
        return pl.ds(block * size, size)

    def copy_c(self, distance, source=None):
        place = self.place
        slot = place.block if source is None else source
        there = place.peer(distance)
        return self.copy(2, distance, self.own.at[self.piece(there)], self.line.at[slot], {SEQ: there})

    def copy_d(self, slot, source, target):
        view = self.total.at[self.piece(source)]
        return self.copy(3, slot, view, view, {SEQ: target})

    def steps_d(self):
        place = self.place
        mine = place.block
        if place.blocks == 4:
            return [(mine, place.far_block), (mine, place.pair_block), (place.far_block, place.pair_block)]
        return [(mine, place.peer(distance)) for distance in range(1, place.blocks)]

    def arrivals_d(self):
        place = self.place
        if place.blocks == 4:
            return [place.far_block, place.pair_block, 3 - place.block]
        return [place.peer(place.blocks - distance) for distance in range(1, place.blocks)]

    def start_a(self):
        self.copy_a().start()

    def end_a(self):
        place = self.place
        self.copy_a().wait_recv()

        def add(chip, carry):
            self.pair[chip] = (self.pair[chip].astype(f32) + self.grad[chip, place.core].astype(f32)).astype(bf16)
            return carry

        lax.fori_loop(0, place.chips, add, 0)
        self.copy_a().wait_send()

    def start_b(self):
        for distance in range(1, self.place.chips):
            self.copy_b(distance).start()

    def end_b(self):
        place = self.place
        total = self.pair[place.chip].astype(f32)
        for distance in range(1, place.chips):
            source = place.other(place.chips - distance)
            self.copy_b(distance, source).wait_recv()
            total = total + self.mates[source].astype(f32)
        self.own[...] = total.astype(bf16)
        for distance in range(1, place.chips):
            self.copy_b(distance).wait_send()

    def start_c(self):
        for distance in range(1, self.place.blocks):
            self.copy_c(distance).start()

    def end_c(self):
        place = self.place
        mine = self.piece(place.block)
        total = self.own[mine].astype(f32)
        for distance in range(1, place.blocks):
            source = place.peer(place.blocks - distance)
            self.copy_c(distance, source).wait_recv()
            total = total + self.line[source].astype(f32)
        if self.part is None:
            self.total[mine] = total.astype(bf16)
        else:
            self.part[...] = total.astype(bf16)
        for distance in range(1, place.blocks):
            self.copy_c(distance).wait_send()

    def start_d(self):
        steps = self.steps_d()
        for slot, (source, target) in enumerate(steps[:2] if self.place.blocks == 4 else steps):
            self.copy_d(slot, source, target).start()

    def pass_d(self):
        if self.place.blocks == 4:
            source, target = self.steps_d()[2]
            self.copy_d(0, self.arrivals_d()[0], target).wait_recv()
            self.copy_d(2, source, target).start()

    def end_d(self):
        direct = self.place.blocks != 4
        for slot, source in enumerate(self.arrivals_d()):
            if direct or slot > 0:
                self.copy_d(slot, source, self.place.peer(1)).wait_recv()
        for slot, (source, target) in enumerate(self.steps_d()):
            self.copy_d(slot, source, target).wait_send()


def put_blocks(grad, layout, array, first, value):
    chips, cores, unused_blocks, rows, lanes = grad.shape
    for spot in range(value.shape[1] // lanes):
        part = value[:, spot * lanes : (spot + 1) * lanes].astype(bf16)
        grad[:, :, layout.spot(array, first + spot)] = part.reshape((chips, cores, rows, lanes))


def put_down(grad, layout, array, value, part, parts):
    chips, cores, unused_blocks, rows, lanes = grad.shape
    few = chips // parts
    high = value.shape[0] // (few * cores * rows)
    wide = value.shape[1] // lanes
    value = value.astype(bf16).reshape((few, cores, high, rows, value.shape[1]))
    for up in range(high):
        for spot in range(wide):
            grad[pl.ds(part * few, few), :, layout.spot(array, up * wide + spot)] = value[
                :, :, up, :, spot * lanes : (spot + 1) * lanes
            ]


class Refs:
    def __init__(self, names, refs, lazy, flush, layer, layered):
        for name, ref in zip(names, refs, strict=True):
            setattr(self, name, ref)
        self.loads, self.stores = {}, {}
        for number, name in enumerate(lazy):
            far = getattr(self, FAR + name)
            if name in layered:
                far = far.at[layer]
            near = getattr(self, name)
            self.loads[id(near)] = pltpu.make_async_copy(far, near, self.load_sem.at[number])
        for number, name in enumerate(flush):
            near = getattr(self, name)
            self.stores[id(near)] = pltpu.make_async_copy(near, getattr(self, FAR + name), self.store_sem.at[number])

    def fetch(self, *refs):
        for load in [self.loads[id(ref)] for ref in refs] if refs else self.loads.values():
            load.start()

    def ready(self, *refs):
        for ref in refs:
            self.loads[id(ref)].wait()

    def flush(self, *refs):
        for ref in refs:
            self.stores[id(ref)].start()

    def flushed(self):
        for store in self.stores.values():
            store.wait()


class Layout:
    def __init__(self, devices, counts):
        self.parts, self.size = [], 0
        for count in counts:
            per = -(-count // devices)
            self.parts.append((self.size, per, count))
            self.size += per
        self.total = self.size * devices

    def spot(self, array, block):
        base, per, unused_count = self.parts[array]
        return block // per * self.size + base + block % per

    def unused(self):
        taken = {self.spot(array, block) for array, part in enumerate(self.parts) for block in range(part[2])}
        return [block for block in range(self.total) if block not in taken]


def layouts(blocks, halves):
    wides = [(16 // halves, 16 // halves) for half in range(halves - 1)] + [(16 // halves, 16 // halves, 4)]
    counts = (*wides, (12,), (1,), (8,))
    made = [Layout(blocks, item) for item in counts]
    return made[:halves], made[halves], made[halves + 1], made[halves + 2]


def kept_spot(block, halves):
    return block if halves == 1 else block % 2 * 8 + block // 2


def up_part(ref, half, part, halves):
    if halves == 1:
        return flat(ref, tile(part, 512))
    columns = [flat(ref, tile(2 * (4 * part + spot) + half, 128)) for spot in range(4)]
    return jnp.concatenate(columns, axis=1)


def down_part(ref, half, part, parts, halves):
    chips, rows = ref.shape[0] // parts, ref.shape[2] // halves
    value = ref[pl.ds(part * chips, chips), :, half * rows : (half + 1) * rows]
    return value.reshape((-1, value.shape[-1]))


class Ahead:
    def __init__(self, place, step, src, dst, sems):
        self.place, self.step, self.src, self.dst, self.sems = place, step, src, dst, sems
        self.sends = place.block < place.blocks - 1 if step > 0 else place.block > 0
        self.receives = place.block > 0 if step > 0 else place.block < place.blocks - 1

    def copy(self, slot, rows):
        return pltpu.make_async_remote_copy(
            src_ref=self.src.at[rows],
            dst_ref=self.dst.at[rows],
            send_sem=self.sems[0].at[slot],
            recv_sem=self.sems[1].at[slot],
            device_id={SEQ: self.place.block + self.step},
            device_id_type=MESH,
        )

    def start(self, slot, rows):
        @pl.when(self.sends)
        def _():
            self.copy(slot, rows).start()

    def arrived(self, slot, rows):
        @pl.when(self.receives)
        def _():
            self.copy(slot, rows).wait_recv()

    def sent(self, slot, rows):
        @pl.when(self.sends)
        def _():
            self.copy(slot, rows).wait_send()


def flat(ref, cols=slice(None)):
    value = ref[:, :, :, cols]
    return value.reshape((-1, value.shape[-1]))


def flat_rows(ref, part, parts):
    chips = ref.shape[0] // parts
    value = ref[pl.ds(part * chips, chips)]
    return value.reshape((-1, value.shape[-1]))


def normalize(values):
    centred = values - jnp.mean(values, axis=-1, keepdims=True)
    scale = lax.rsqrt(jnp.mean(centred * centred, axis=-1, keepdims=True) + ln_eps)
    return (centred * scale, scale)


def norm_back(grad_out, standard, scale, gain):
    scaled = grad_out * gain
    return scale * (
        scaled
        - jnp.mean(scaled, axis=-1, keepdims=True)
        - standard * jnp.mean(scaled * standard, axis=-1, keepdims=True)
    )


def gelu_pair(x):
    cumulative = 0.5 * (1.0 + lax.erf(x * 0.7071067811865476))
    bell = jnp.exp(-0.5 * x * x)
    return (x * cumulative, cumulative + x * (bell * 0.3989422804014327))


def tile(index, size):
    return pl.ds(pl.multiple_of(index * size, size), size)


def half_masks():
    lane = lax.broadcasted_iota(jnp.int32, (1, 128), 1)
    left = jnp.where(lane < 64, 1.0, 0.0).astype(bf16)
    right = jnp.where(lane < 64, 0.0, 1.0).astype(bf16)
    return (left, right)


def build_marks(kf_ref, lens_ref, first):
    streams, unused_halves, keys, lanes = kf_ref.shape
    key = lax.broadcasted_iota(jnp.int32, (keys, lanes), 0)
    lane = lax.broadcasted_iota(jnp.int32, (keys, lanes), 1)
    coarse = (key // 256 * 256).astype(f32)
    fine = (key % 256).astype(f32)
    for stream in range(streams):
        veiled = jnp.where(jnp.logical_and(first, key < keys // 2 - lens_ref[stream]), 1.0, 0.0)
        for half in range(2):
            spot = lane - 64 * (1 - half)
            value = jnp.where(spot == 6, veiled, jnp.where(spot == 7, 1.0, 0.0))
            value = jnp.where(jnp.logical_and(spot >= 3, spot < 6), fine, value)
            value = jnp.where(jnp.logical_and(spot >= 0, spot < 3), coarse, value)
            kf_ref[stream, half] = value.astype(bf16)


def query_marks(slope, half):
    spot = lax.broadcasted_iota(jnp.int32, (1, 128), 1) - 64 * (1 - half)
    whole_slope = jnp.full((1, 128), slope)
    one = whole_slope.astype(bf16).astype(f32)
    two = (whole_slope - one).astype(bf16).astype(f32)
    three = whole_slope - one - two
    value = jnp.where(spot == 6, masked_score, 0.0)
    for number, part in enumerate((one, two, three)):
        value = jnp.where(jnp.logical_or(spot == number, spot == number + 3), part, value)
    return value.astype(bf16)


def attend(span, heads, q_ref, k_ref, v_ref, kf_ref, slope_of, o_ref, lse_ref, score_refs, chance_refs, stream, early):
    pairs = heads // 2
    step = span // 2
    masks = half_masks()
    key_at = lax.broadcasted_iota(jnp.int32, (step, step), 0)
    query_at = lax.broadcasted_iota(jnp.int32, (step, step), 1)
    down = lax.broadcasted_iota(jnp.int32, (128, 1), 0)
    row_masks = (jnp.where(down < 64, 1.0, 0.0).astype(bf16), jnp.where(down < 64, 0.0, 1.0).astype(bf16))

    def group(first_pair, count):
        work = []
        for pair in [first_pair + i for i in range(count)]:
            cols = tile(pair, 128)
            k_pair = k_ref[tile(stream, 2 * span), cols]
            v_turned = v_ref[tile(stream, 2 * span), cols].T
            for part in range(2):
                for half in range(2):
                    work.append((pair, cols, k_pair, v_turned, part, half))
        peaks, mixed_rows = {}, {}

        def scores(item):
            pair, cols, k_pair, unused_v, part, half = work[item]
            seen = span + part * step
            q_pair = q_ref[pl.ds(pl.multiple_of(stream * span + part * step, step), step), cols]
            q_aug = q_pair * masks[half] + query_marks(slope_of(2 * pair + half), half)
            k_aug = k_pair[: seen + step] * masks[half] + kf_ref[stream, half, : seen + step]
            score = mm(k_aug, q_aug, NT)
            near = jnp.where(key_at <= query_at, score[seen:], masked_score)
            peaks[item] = jnp.maximum(
                jnp.max(score[:seen], axis=0, keepdims=True), jnp.max(near, axis=0, keepdims=True)
            )
            out = score_refs[item % 2]
            out[:seen, :] = score[:seen]
            out[seen : seen + step, :] = near

        def soften(item):
            seen = span + (work[item][4] + 1) * step
            chance_refs[item % 2][:seen, :] = jnp.exp(score_refs[item % 2][:seen, :] - peaks[item]).astype(bf16)

        def mix(item):
            pair, cols, unused_k, v_turned, part, half = work[item]
            seen = span + (part + 1) * step
            v_aug = v_turned[:, :seen] * row_masks[half] + row_masks[1 - half]
            mixed = mm(v_aug, chance_refs[item % 2][:seen, :])
            own = mixed[half * 64 : half * 64 + 64]
            total = mixed[64 - half * 64 : 128 - half * 64]
            mixed_rows[half] = own / total
            lse_ref[pl.ds(stream * heads + 2 * pair + half, 1), part * step : (part + 1) * step] = peaks[
                item
            ] + jnp.log(total[:1])
            if half == 1:
                rows = pl.ds(pl.multiple_of(stream * span + part * step, step), step)
                o_ref[rows, cols] = jnp.concatenate([mixed_rows[0], mixed_rows[1]], axis=0).T.astype(bf16)

        scores(0)
        for item in range(len(work)):
            if item + 1 < len(work):
                scores(item + 1)
            soften(item)
            if item > 0:
                mix(item - 1)
        mix(len(work) - 1)

    def inner(index, carry):
        group(2 * index, 2)
        early(index)
        return carry

    lax.fori_loop(0, pairs // 2, inner, 0)


def forward_kernel(sizes, r):
    (stream_devices, block_devices, streams, span, heads, features, nvec, halves) = sizes
    place = Place(stream_devices, block_devices)
    chip, core = place.chip, place.core
    first = place.block == 0
    layers = r.mem.shape[0]
    width = r.a.shape[1]
    count = streams * span
    step = span // 2
    sems = (r.out_sem, r.in_sem)
    weight_names = ("wp", "wo", "wu", "wd")
    weights = [[getattr(r, f"{name}_{layer}") for name in weight_names] for layer in range(layers)]
    gather_small, gather_head = Gather(place, r.small, sems, 0, direct=True), Gather(place, r.wh, sems, 1)
    gathers = [
        [
            Gather(place, ref, sems, 2 + 4 * layer + number)
            for number, ref in enumerate(weights[layer])
        ]
        for layer in range(layers)
    ]
    early_names, look_names, feed_names = ("ap", "q", "k", "v", "low"), ("o", "lse"), ("r1", "a2", "u", "gp")
    saved_names = early_names + look_names + feed_names + ("a", "res")

    def save(layer, name, stream, source=None):
        source = getattr(r, name) if source is None else source
        size = source.shape[0] // streams
        at = tile(stream, size)
        far = getattr(r, FAR + name)
        return pltpu.make_async_copy(
            source.at[at], far.at[layer, at], r.save_sem.at[layer, saved_names.index(name), stream]
        )

    def save_weight(layer, number):
        return pltpu.make_async_copy(
            weights[layer][number],
            getattr(r, f"{FAR}{weight_names[number]}_{layer}"),
            r.weight_sem.at[layer, number],
        )

    r.fetch()
    frames_ahead = Ahead(place, 1, r.frames_wide, r.halo, (r.frame_sem.at[0], r.frame_sem.at[1]))
    next_ahead = Ahead(place, 1, r.nxt, r.behind, (r.next_out, r.next_in))
    every = pl.ds(0, count)

    @pl.when(first)
    def _():
        r.halo[...] = jnp.zeros_like(r.halo)
        r.behind[...] = jnp.zeros_like(r.behind)

    r.small_rows[...] = jnp.zeros_like(r.small_rows)
    r.small_rows[0:nvec, :] = r.vectors[...]
    own_rows = jnp.concatenate([r.input_turned[...], r.small_rows[...].T], axis=1)
    r.small[chip, core] = own_rows.astype(bf16)
    r.frames_tall[...] = jnp.zeros_like(r.frames_tall)
    r.frames_tall[features : features + 16, :] = jnp.where(
        lax.broadcasted_iota(jnp.int32, (16, span), 0) == 0, 1.0, 0.0
    ).astype(bf16)
    for stream in range(streams):
        r.frames_tall[0:features, :] = r.frames[stream]
        r.frames_wide[stream * span : (stream + 1) * span, :] = r.frames_tall[...].T
    r.ready(r.pw)
    r.wp_0[chip, core] = r.pw[0].astype(bf16)
    place.greet(line=True)
    gather_small.push()
    gathers[0][0].push()
    frames_ahead.start(0, every)
    r.ready(r.ow, r.uw, r.dw, r.hw)
    r.wo_0[chip, core] = r.ow[0].astype(bf16)
    r.wu_0[chip, core] = r.uw[0].astype(bf16)
    r.wd_0[chip, core] = r.dw[0].astype(bf16)
    r.wp_1[chip, core] = r.pw[1].astype(bf16)
    r.wo_1[chip, core] = r.ow[1].astype(bf16)
    r.wu_1[chip, core] = r.uw[1].astype(bf16)
    r.wd_1[chip, core] = r.dw[1].astype(bf16)
    r.wh[chip, core] = r.hw[...].astype(bf16)
    build_marks(r.kf, r.memory_len, first)
    r.rows[...] = jnp.zeros_like(r.rows)
    r.ready(r.mem)
    gathers[0][0].pass_on()
    gathers[0][1].push()
    gathers[0][2].push()
    gather_small.relay()
    gathers[0][0].relay()
    gathers[0][3].push()
    gather_small.finish()
    r.rows[:nvec, :] = flat(r.small).astype(f32).T[features : features + nvec]
    gathers[0][0].finish()
    frames_ahead.arrived(0, every)
    residuals = (r.res, r.res_two)

    for layer in range(layers):
        residual, outcome = residuals[layer % 2], residuals[(layer + 1) % 2]
        row = 3 + 4 * layer
        g1, b1, g2, b2 = (r.rows[row + i : row + i + 1, :] for i in range(4))
        wp, wo, wu, wd = weights[layer]
        own_a = r.a if layer == 0 else r.nxt

        def wait_old(names, stream):
            if layer > 0:
                for name in names:
                    save(layer - 1, name, stream).wait()

        wq, wk, wv = (slice(i * width, (i + 1) * width) for i in range(3))

        def project_own(stream):
            wait_old(("q", "k", "v", "low"), stream)
            for part in range(2):
                at = pl.ds(pl.multiple_of(stream * span + part * step, step), step)
                here = pl.ds(pl.multiple_of(stream * 2 * span + span + part * step, step), step)
                if layer == 0:
                    value = mm(r.frames_wide[at, :], flat(r.small), NT)
                    residual[at, :] = value
                    own_a[at, :] = (normalize(value)[0] * g1 + b1).astype(bf16)
                else:
                    value = residual[at, :]
                r.low[at, :] = value.astype(bf16)
                a = own_a[at, :]
                r.q[at, :] = (mm(a, flat(wp, wq)) * 0.125).astype(bf16)
                r.k[here, :] = mm(a, flat(wp, wk)).astype(bf16)
                r.v[here, :] = mm(a, flat(wp, wv)).astype(bf16)
            for name in ("q", "low"):
                save(layer, name, stream).start()
            save(layer, saved_names[-1], stream, residual).start()
            save(layer, saved_names[-2], stream, own_a).start()

        def project_behind(stream):
            wait_old(("ap",), stream)
            for part in range(2):
                at = pl.ds(pl.multiple_of(stream * span + part * step, step), step)
                behind = pl.ds(pl.multiple_of(stream * 2 * span + part * step, step), step)
                if layer == 0:
                    before = mm(r.halo[at, :], flat(r.small), NT)
                    before = jnp.where(first, r.mem[layer, at, :].astype(f32), before)
                    r.pr[at, :] = before
                    ap = (normalize(before)[0] * g1 + b1).astype(bf16)
                else:
                    ap = (normalize(r.mem[layer, at, :].astype(f32))[0] * g1 + b1).astype(bf16)
                    ap = jnp.where(first, ap.astype(f32), r.behind[at, :].astype(f32)).astype(bf16)
                r.ap[at, :] = ap
                r.k[behind, :] = mm(ap, flat(wp, wk)).astype(bf16)
                r.v[behind, :] = mm(ap, flat(wp, wv)).astype(bf16)
            for name in ("ap", "k", "v"):
                save(layer, name, stream).start()
            if layer == 0:
                at = tile(stream, span)
                pltpu.make_async_copy(r.pr.at[at], r.far_pr.at[at], r.pr_sem.at[stream]).start()

        def look(stream):
            wait_old(look_names, stream)

            def early(index):
                def at(when_stream, when_index):
                    return pl.when(jnp.logical_and(stream == when_stream, index == when_index))

                @at(0, 0)
                def _():
                    if layer == 0:
                        gathers[0][3].pass_on()
                    else:
                        gathers[1][2].pass_on()

                @at(0, 1)
                def _():
                    if layer == 0:
                        gathers[0][1].relay()
                        gathers[0][2].relay()
                        gathers[1][0].push()
                        gathers[1][1].push()
                    else:
                        gathers[1][3].pass_on()

                @at(1, 0)
                def _():
                    if layer == 0:
                        gathers[0][3].relay()
                    else:
                        gather_head.pass_on()
                        gathers[1][2].relay()
                        gathers[1][3].relay()

                @at(1, 1)
                def _():
                    if layer == 0:
                        gathers[1][0].pass_on()
                        gathers[1][1].pass_on()
                    else:
                        gather_head.relay()

            attend(
                span,
                heads,
                r.q,
                r.k,
                r.v,
                r.kf,
                lambda head: r.slopes[layer, head],
                r.o,
                r.lse,
                (r.score_one, r.score_two),
                (r.chance_one, r.chance_two),
                stream,
                early,
            )
            for name in look_names:
                save(layer, name, stream).start()

        def feed(stream, carry):
            if layer > 0:
                save(layer - 1, saved_names[-1], stream, outcome).wait()
            wait_old(feed_names, stream)
            at = tile(stream, span)
            after = residual[at, :] + mm(r.o[at, :], flat(wo))
            r.r1[at, :] = after
            a2 = (normalize(after)[0] * g2 + b2).astype(bf16)
            r.a2[at, :] = a2
            for name in feed_names[:2]:
                save(layer, name, stream).start()
            total = after
            parts = wu.shape[3] // 512
            later = mm(a2, flat(wu, slice(0, 512)))
            for part in range(parts):
                cols = slice(part * 512, (part + 1) * 512)
                value = later
                if part + 1 < parts:
                    later = mm(a2, flat(wu, slice((part + 1) * 512, (part + 2) * 512)))
                active, slope = gelu_pair(value)
                active = active.astype(bf16)
                slope = slope.astype(bf16)
                for spot in range(4):
                    there = kept_spot(part * 4 + spot, halves)
                    there = slice(there * 128, (there + 1) * 128)
                    r.u[at, there] = active[:, spot * 128 : (spot + 1) * 128]
                    r.gp[at, there] = slope[:, spot * 128 : (spot + 1) * 128]
                total = total + mm(active, flat_rows(wd, part, parts))
            outcome[at, :] = total
            for name in feed_names[2:]:
                save(layer, name, stream).start()
            if layer == 0:
                g, b = r.rows[row + 4 : row + 5, :], r.rows[row + 5 : row + 6, :]
                r.nxt[at, :] = (normalize(total)[0] * g + b).astype(bf16)
                next_ahead.start(stream, at)

                @pl.when(stream == 0)
                def _():
                    gathers[1][0].relay()
                    gathers[1][1].relay()

            return carry

        if layer == 0:

            def all_project(stream, carry):
                project_own(stream)
                project_behind(stream)

                @pl.when(stream == 0)
                def _():
                    gathers[0][1].pass_on()
                    gathers[0][2].pass_on()

                return carry

            def all_look(stream, carry):
                look(stream)
                return carry

            lax.fori_loop(0, streams, all_project, 0)
            lax.fori_loop(0, streams, all_look, 0)
            for gather in gathers[1][2:] + [gather_head]:
                gather.push()
            for gather in gathers[0][1:]:
                gather.finish()
        else:
            gathers[1][0].finish()
            gathers[1][1].finish()

            def all_own(stream, carry):
                project_own(stream)
                return carry

            def both(stream, carry):
                next_ahead.arrived(stream, tile(stream, span))
                project_behind(stream)
                look(stream)
                return carry

            lax.fori_loop(0, streams, all_own, 0)
            lax.fori_loop(0, streams, both, 0)
            gathers[1][2].finish()
            gathers[1][3].finish()
        for number in range(4):
            save_weight(layer, number).start()
        lax.fori_loop(0, streams, feed, 0)
    gather_head.finish()
    head_stage(place, streams, span, stream_devices, residuals[layers % 2], r)
    last = pltpu.make_async_copy(residuals[layers % 2], r.dr, r.dr_sem.at[0])
    last.start()
    for layer in range(layers):
        for number in range(4):
            save_weight(layer, number).wait()
    for stream in range(streams):
        at = tile(stream, span)
        for name in early_names + look_names + feed_names:
            save(layers - 1, name, stream).wait()
        for layer in range(layers):
            save(layer, saved_names[-2], stream, r.a if layer == 0 else r.nxt).wait()
        save(layers - 1, saved_names[-1], stream, residuals[(layers - 1) % 2]).wait()
        pltpu.make_async_copy(r.pr.at[at], r.far_pr.at[at], r.pr_sem.at[stream]).wait()
        next_ahead.sent(stream, at)
    frames_ahead.sent(0, every)
    last.wait()


def head_stage(place, streams, span, stream_devices, residual, r):
    gain, bias = r.rows[1:2, :], r.rows[2:3, :]
    step = span // 2
    r.acc[...] = jnp.zeros_like(r.acc)
    r.gr_last[...] = jnp.zeros_like(r.gr_last)
    r.loss[...] = jnp.zeros_like(r.loss)
    target_columns = r.targets[...].astype(f32).T
    lane = lax.broadcasted_iota(jnp.int32, target_columns.shape, 1)

    def column(index):
        return jnp.sum(jnp.where(lane == index, target_columns, 0.0), axis=1, keepdims=True)

    def one(index, carry):
        at = tile(index, step)
        stream, part = index // 2, index % 2
        standard, scale = normalize(residual[at, :])
        f = (standard * gain + bias).astype(bf16)
        z = mm(f, flat(r.wh))
        per = step // 128
        target = jnp.concatenate([column(index * per + i) for i in range(per)], axis=0)
        frames = jnp.full((step, 1), r.frame_count[stream])
        position = lax.broadcasted_iota(jnp.int32, (step, 1), 0) + (place.block * span + part * step)
        share = jnp.where(position < frames, 1.0 / (frames.astype(f32) * (streams * stream_devices)), 0.0)
        peak = jnp.max(z, axis=-1, keepdims=True)
        raised = jnp.exp(z - peak)
        total = jnp.sum(raised, axis=-1, keepdims=True)
        code = lax.broadcasted_iota(jnp.int32, z.shape, 1)
        hit = code == target.astype(jnp.int32)
        picked = jnp.sum(jnp.where(hit, z, 0.0), axis=-1, keepdims=True)
        r.loss[...] += jnp.sum(share * (peak + jnp.log(total) - picked))
        soft = raised * (1.0 / total)
        dz = (share * jnp.where(hit, soft - 1.0, soft)).astype(bf16)
        r.acc[...] += mm(f, dz, TN)
        df = mm(dz, flat(r.wh), NT)
        r.gr_last[0:1, :] += jnp.sum(df * standard, axis=0, keepdims=True)
        r.gr_last[1:2, :] += jnp.sum(df, axis=0, keepdims=True)
        residual[at, :] = norm_back(df, standard, scale, gain)
        return carry

    lax.fori_loop(0, streams * 2, one, 0)
    put_blocks(r.grad_head, layouts(place.blocks, 1)[3], 0, 0, r.acc[...])


def attend_back(streams, span, heads, refs, early, between):
    (q_ref, k_ref, v_ref, o_ref, lse_ref, kf_ref, slope_of, do_ref, dq_ref, dk_ref, dv_ref, gs_ref, p_ref, ds_ref) = refs
    pairs = heads // 2
    step = span // 2
    masks = half_masks()
    key_at = lax.broadcasted_iota(jnp.int32, (step, step), 0)
    query_at = lax.broadcasted_iota(jnp.int32, (step, step), 1)
    head_row = lax.broadcasted_iota(jnp.int32, (8, 128), 0)
    place = lax.broadcasted_iota(jnp.int32, (1, step), 1)
    gs_ref[...] = jnp.zeros_like(gs_ref)

    def one(stream, pair):
        cols = tile(pair, 128)
        k_pair = k_ref[tile(stream, 2 * span), cols]
        v_pair = v_ref[tile(stream, 2 * span), cols]
        k_augs = [k_pair * masks[half] + kf_ref[stream, half] for half in range(2)]
        queries, outs = [], []
        for part in range(2):
            seen = span + part * step
            rows = pl.ds(pl.multiple_of(stream * span + part * step, step), step)
            q_pair, do_pair = q_ref[rows, cols], do_ref[rows, cols]
            both = (do_pair.astype(f32) * o_ref[rows, cols].astype(f32)).T
            for half in range(2):
                head = 2 * pair + half
                q_own, do_own = q_pair * masks[half], do_pair * masks[half]
                queries.append(q_own)
                outs.append(do_own)
                delta = jnp.sum(both[half * 64 : half * 64 + 64], axis=0, keepdims=True)
                log_total = lse_ref[pl.ds(stream * heads + head, 1), part * step : (part + 1) * step]
                scores = mm(k_augs[half][: seen + step], q_own + query_marks(slope_of(head), half), NT)
                dp = mm(v_pair[: seen + step], do_own, NT)
                at = slice(half * step, (half + 1) * step)
                for low, high in ((0, seen), (seen, seen + step)):
                    score = scores[low:high]
                    if low:
                        score = jnp.where(key_at <= query_at, score, masked_score)
                    chance = jnp.exp(score - log_total)
                    p_ref[part, low:high, at] = chance.astype(bf16)
                    ds_ref[part, low:high, at] = (chance * (dp[low:high] - delta)).astype(bf16)
        common = span + step
        q_parts = [jnp.concatenate(queries[2 * part : 2 * part + 2], axis=0) for part in range(2)]
        do_parts = [jnp.concatenate(outs[2 * part : 2 * part + 2], axis=0) for part in range(2)]
        base = stream * 2 * span
        for source, out_ref, parts in ((p_ref, dv_ref, do_parts), (ds_ref, dk_ref, q_parts)):
            out_ref[pl.ds(pl.multiple_of(base, step), common), cols] = (
                mm(source[0, :common, :], parts[0]) + mm(source[1, :common, :], parts[1])
            ).astype(bf16)
            out_ref[pl.ds(pl.multiple_of(base + common, step), step), cols] = mm(
                source[1, common:, :], parts[1]
            ).astype(bf16)
        k_turned = [k_aug.T for k_aug in k_augs]
        for part in range(2):
            seen = span + (part + 1) * step
            done = []
            for half in range(2):
                head = 2 * pair + half
                turned = mm(k_turned[half][:, :seen], ds_ref[part, :seen, half * step : (half + 1) * step])
                done.append(turned[half * 64 : half * 64 + 64] * 0.125)
                base_row = 64 - half * 64
                lean = (
                    turned[base_row : base_row + 1]
                    + turned[base_row + 3 : base_row + 4]
                    - (place + (part * step + span)).astype(f32) * turned[base_row + 7 : base_row + 8]
                )
                gs_ref[...] += jnp.where(head_row == head, jnp.sum(lean), 0.0)
            rows = pl.ds(pl.multiple_of(stream * span + part * step, step), step)
            dq_ref[rows, cols] = jnp.concatenate(done, axis=0).T.astype(bf16)

    def over(stream, carry):
        def inner(pair, carry):
            one(stream, pair)
            early(stream * pairs + pair)
            return carry

        carry = lax.fori_loop(0, pairs, inner, carry)
        between(stream)
        return carry

    lax.fori_loop(0, streams, over, 0)


def backward_kernel(layer, sizes, r):
    (stream_devices, block_devices, streams, span, heads, features, nvec, halves) = sizes
    place = Place(stream_devices, block_devices)
    width = r.a.shape[1]
    count = streams * span
    first = place.block == 0
    row = 3 + 4 * layer
    g1, g2 = r.rows[row : row + 1, :], r.rows[row + 2 : row + 3, :]
    step = 256
    tiles = count // step
    sems = (r.out_sem, r.in_sem)
    wide_layouts, layout_b, layout_small, unused_head = layouts(place.blocks, halves)

    def wide_reduce(half, row, *names):
        return Reduce(place, sems, row, **{name: getattr(r, f"{name}_{WIDE[half]}") for name in names})

    broads = [wide_reduce(half, 4 * half, *REDUCED[:4]) for half in range(halves)]
    row_b = 4 * halves
    if layer == 0:
        for half, broad in enumerate(broads):
            broad.line = getattr(r, f"{REDUCED[4]}_{WIDE[half]}")
            if half < halves - 1:
                broad.total = getattr(r, f"{REDUCED[6]}_{WIDE[half]}")
            else:
                broad.part = getattr(r, f"{REDUCED[5]}_{WIDE[half]}")
        dones = [
            Reduce(
                place,
                sems,
                row_b + 4 + 4 * half,
                **{name: getattr(r, f"{name}_one_{WIDE[half]}") for name in REDUCED[3:7:1] if name != REDUCED[5]},
            )
            for half in range(halves)
        ]
        narrow = Reduce(
            place, sems, 4 + 8 * halves, grad=r.grad_b, pair=r.pair_b, mates=r.mates_b, own=r.own_b
        )
        done_b = Reduce(
            place, sems, row_b, pair=r.pair_b_one, mates=r.mates_b_one, own=r.own_b_one, line=r.line_b_one, total=r.total_b_one
        )
    else:
        narrow = Reduce(place, sems, row_b, grad=r.grad_b, pair=r.pair_b)
        head = Reduce(
            place, sems, row_b + 4, grad=r.grad_head, pair=r.pair_head, mates=r.mates_head, own=r.own_head, line=r.line_head, total=r.total_head
        )
        back = Ahead(place, -1, r.dap, r.back, (r.back_out, r.back_in))

        @pl.when(place.block == place.blocks - 1)
        def _():
            r.back[...] = jnp.zeros_like(r.back)

    for grad, layout in [(broad.grad, layout) for broad, layout in zip(broads, wide_layouts)] + [(r.grad_b, layout_b)]:
        for block in layout.unused():
            grad[:, :, block] = jnp.zeros(grad.shape[:2] + grad.shape[3:], bf16)
    r.gr[...] = jnp.zeros_like(r.gr)
    hidden_parts = r.wu.shape[3] // 512

    def stream_in(part, slot):
        cols = tile(part, 512)
        return (
            pltpu.make_async_copy(r.u.at[layer, :, cols], r.u_two.at[slot], r.u_sem.at[0, slot]),
            pltpu.make_async_copy(r.gp.at[layer, :, cols], r.gp_two.at[slot], r.u_sem.at[1, slot]),
        )

    first_loads = []
    if layer == 0:
        first_loads = [
            pltpu.make_async_copy(r.dr1_in, r.dr, r.first_sem.at[0]),
            pltpu.make_async_copy(r.r.at[1], r.da, r.first_sem.at[1]),
            pltpu.make_async_copy(r.da_in, r.wide_one, r.first_sem.at[2]),
        ]
        late_loads = [
            pltpu.make_async_copy(r.r.at[0], r.wide_one, r.first_sem.at[3]),
            pltpu.make_async_copy(r.pr, r.r1, r.first_sem.at[4]),
        ]
    else:
        first_loads = [pltpu.make_async_copy(r.dr_in, r.dr, r.first_sem.at[0])]
    for load in first_loads:
        load.start()
    for load in stream_in(0, 0):
        load.start()
    r.fetch(r.wd, r.a2, r.wu)

    def fetch_rest():
        r.fetch(r.r1, r.wo, r.o, r.lse, r.q, r.k, r.v, r.wp, r.a, r.ap)
        if layer == 1:
            r.fetch(r.mem)

    place.greet(column=True)
    if layer == 0:
        for done in dones:
            done.start_c()
        done_b.start_b()

        g = r.rows[row + 4 : row + 5, :]

        def join(index, carry):
            at = tile(index, step)
            standard, scale = normalize(r.da[at, :])
            da = r.wide_one[at, :] + r.back[at, :].astype(f32)
            r.gr[4:5, :] += jnp.sum(da * standard, axis=0, keepdims=True)
            r.gr[5:6, :] += jnp.sum(da, axis=0, keepdims=True)
            r.dr[at, :] = r.dr[at, :] + norm_back(da, standard, scale, g)
            return carry

        build_marks(r.kf, r.memory_len, first)
        for load in first_loads:
            load.wait()
        fetch_rest()
        lax.fori_loop(0, tiles, join, 0)
        late_loads[0].start()
    else:
        head.start_a()
        build_marks(r.kf, r.memory_len, first)
        first_loads[0].wait()
        fetch_rest()

    r.da[...] = jnp.zeros_like(r.da)
    r.ready(r.wd, r.a2, r.wu)
    r.turned[...] = r.a2[...].T
    parts = hidden_parts
    each = parts // halves

    def feed(half, spot, carry):
        part = half * each + spot
        slot = part % 2

        @pl.when(part + 1 < parts)
        def _():
            for load in stream_in(part + 1, 1 - slot):
                load.start()

        for load in stream_in(part, slot):
            load.wait()
        dy = r.dr[...].astype(bf16)
        dh = (mm(dy, down_part(r.wd, half, spot, each, halves), NT) * r.gp_two[slot].astype(f32)).astype(bf16)
        put_down(broads[half].grad, wide_layouts[half], 0, mm(r.u_two[slot], dy, TN), spot, each)
        put_blocks(broads[half].grad, wide_layouts[half], 1, 4 * spot, mm(r.turned[...], dh))
        r.da[...] += mm(dh, up_part(r.wu, half, spot, halves), NT)
        if half == 0 and layer == 1:

            @pl.when(spot == 0)
            def _():
                head.end_a()
                head.start_b()

        if half == 1:

            @pl.when(spot == 0)
            def _():
                broads[0].end_a()
                broads[0].start_b()

        return carry

    for half in range(halves):
        lax.fori_loop(0, each, functools.partial(feed, half), 0)
        if half < halves - 1:
            broads[half].start_a()
    r.ready(r.r1, r.wo, r.o, r.lse)

    def middle(index, carry):
        at = tile(index, step)
        standard, scale = normalize(r.r1[at, :])
        da = r.da[at, :]
        r.gr[2:3, :] += jnp.sum(da * standard, axis=0, keepdims=True)
        r.gr[3:4, :] += jnp.sum(da, axis=0, keepdims=True)
        dr = r.dr[at, :] + norm_back(da, standard, scale, g2)
        r.dr[at, :] = dr
        r.do[at, :] = mm(dr.astype(bf16), flat(r.wo), NT).astype(bf16)
        return carry

    lax.fori_loop(0, tiles, middle, 0)
    if layer == 0:
        late_loads[1].start()
    put_blocks(broads[-1].grad, wide_layouts[-1], 2, 0, mm(r.o[...], r.dr[...].astype(bf16), TN))
    broads[-1].start_a()
    if layer == 0:
        for done in dones:
            done.end_c()
        done_b.end_b()
        done_b.start_c()
        for done in dones:
            done.start_d()
    else:
        head.end_b()
        head.start_c()
    wk, wv = (slice(i * width, (i + 1) * width) for i in (1, 2))

    def behind_gradient(at, behind):
        return mm(r.dk[behind, :], flat(r.wp, wk), NT) + mm(r.dv[behind, :], flat(r.wp, wv), NT)

    def early(index):
        @pl.when(index == 1)
        def _():
            broads[-1].end_a()
            broads[-1].start_b()
            if layer == 1:
                head.end_c()
                head.start_d()

        @pl.when(index == 4)
        def _():
            if layer == 1:
                head.pass_d()
            else:
                for done in dones:
                    done.pass_d()

        @pl.when(index == 5)
        def _():
            if layer == 0:
                for broad in broads[:-1]:
                    broad.end_b()
                    broad.start_c()

    def between(stream):
        if layer == 0:

            @pl.when(stream == 0)
            def _():
                done_b.end_c()
                done_b.start_d()

            @pl.when(stream == 1)
            def _():
                done_b.pass_d()

        else:
            for part in range(span // step):
                at = pl.ds(pl.multiple_of(stream * span + part * step, step), step)
                behind = pl.ds(pl.multiple_of(stream * 2 * span + part * step, step), step)
                r.dap[at, :] = behind_gradient(at, behind).astype(bf16)
            back.start(stream, tile(stream, span))


    r.ready(r.q, r.k, r.v, r.wp)
    attend_back(
        streams,
        span,
        heads,
        (r.q, r.k, r.v, r.o, r.lse, r.kf, lambda head: r.slopes[layer, head], r.do, r.dq, r.dk, r.dv, r.gs, r.u_two, r.gp_two),
        early,
        between,
    )

    r.ready(r.a, r.ap)
    r.turned[...] = r.a[...].T
    put_blocks(r.grad_b, layout_b, 0, 0, mm(r.turned[...], r.dq[...]))
    for spot, ref in ((1, r.dk), (2, r.dv)):
        total = jnp.zeros((width, width), f32)
        for stream in range(streams):
            behind = slice(stream * 2 * span, stream * 2 * span + span)
            here = slice(stream * 2 * span + span, (stream + 1) * 2 * span)
            own = slice(stream * span, (stream + 1) * span)
            total = total + mm(r.turned[:, own], ref[here, :])
            total = total + mm(r.ap[own, :], ref[behind, :], TN)
        put_blocks(r.grad_b, layout_b, 0, 4 * spot, total)

    if layer == 0:
        r.small_acc[...] = jnp.zeros_like(r.small_acc)
        for load in late_loads:
            load.wait()
        narrow.start_a()
        broads[-1].end_b()
        broads[-1].start_c()
        for broad in broads[:-1]:
            broad.end_c()
            broad.start_d()
    else:
        narrow.start_a()
        r.ready(r.mem)

    def finish(stream, carry):
        for part in range(span // step):
            at = pl.ds(pl.multiple_of(stream * span + part * step, step), step)
            behind = pl.ds(pl.multiple_of(stream * 2 * span + part * step, step), step)
            here = pl.ds(pl.multiple_of(stream * 2 * span + span + part * step, step), step)
            da = (
                mm(r.dq[at, :], flat(r.wp, slice(0, width)), NT)
                + mm(r.dk[here, :], flat(r.wp, wk), NT)
                + mm(r.dv[here, :], flat(r.wp, wv), NT)
            )
            if layer == 0:
                dap = behind_gradient(at, behind)
                standard, scale = normalize(r.wide_one[at, :])
                before, before_scale = normalize(r.r1[at, :])
                r.gr[0:1, :] += jnp.sum(da * standard + dap * before, axis=0, keepdims=True)
                r.gr[1:2, :] += jnp.sum(da + dap, axis=0, keepdims=True)
                dr = r.dr[at, :] + norm_back(da, standard, scale, g1)
                drp = norm_back(dap, before, before_scale, g1)
                drp = jnp.where(first, 0.0, drp)
                r.gr[6:7, :] += jnp.sum(dr + drp, axis=0, keepdims=True)
                r.small_acc[...] += mm(dr.astype(bf16), r.frames[at, :], TN)
                r.small_acc[...] += mm(drp.astype(bf16), r.halo[at, :], TN)
                if part == 0:

                    @pl.when(stream == 1)
                    def _():
                        narrow.end_a()
                        narrow.start_b()
                        for broad in broads[:-1]:
                            broad.pass_d()

            else:
                r.da[at, :] = da
                before, before_scale = normalize(r.mem[at, :].astype(f32))
                dap = jnp.where(first, r.dap[at, :].astype(f32), 0.0)
                r.gr[0:1, :] += jnp.sum(dap * before, axis=0, keepdims=True)
                r.gr[1:2, :] += jnp.sum(dap, axis=0, keepdims=True)
        return carry

    lax.fori_loop(0, streams, finish, 0)
    if layer == 0:
        listed = [r.gr[6:7, :], r.gr_last[0:2, :], r.gr[0:4, :], r.gr_one[0:2, :] + r.gr[4:6, :], r.gr_one[2:4, :]]
        listed = [jnp.zeros((features, width), f32)] + listed + [jnp.zeros((128 - features - nvec, width), f32)]
        lane = lax.broadcasted_iota(jnp.int32, (1, 128), 1)
        merged = jnp.where(lane < features, r.small_acc[...], jnp.concatenate(listed, axis=0).T)
        for block in layout_small.unused():
            r.grad_small[:, :, block] = jnp.zeros(r.grad_small.shape[:2] + r.grad_small.shape[3:], bf16)
        put_blocks(r.grad_small, layout_small, 0, 0, merged)
        done_b.end_d()
        for done in dones:
            done.end_d()
        for broad in broads[:-1]:
            broad.end_d()
        broads[-1].end_c()
        narrow.end_b()
    else:
        head.end_d()
        narrow.end_a()
        for broad in broads:
            broad.end_b()
        for stream in range(streams):
            at = tile(stream, span)
            back.sent(stream, at)
            back.arrived(stream, at)


def lanes_of(entries):
    lane = lax.broadcasted_iota(jnp.int32, (1, 128), 1)
    row = jnp.zeros((1, 128), f32)
    for number, value in entries:
        row = jnp.where(lane == number, value, row)
    return row


def pick(row, number):
    lane = lax.broadcasted_iota(jnp.int32, (1, 128), 1)
    return jnp.sum(jnp.where(lane == number, row, 0.0))


class State:
    def __init__(self, blocks, layers, rows, halves, wides, narrows, head):
        wide_layouts, plain, last, head_layout = layouts(blocks, halves)
        self.small = last.spot(0, 0)
        self.rows, self.halves = rows, halves
        self.items = []
        for layer in range(layers):
            self.items.append((1, layer, narrows[layer], plain, 0, 1 + layer, 0))
            self.items.append((2, layer, wides[layer][-1], wide_layouts[-1], 2, 1 + layers + layer, 0))
            for half in range(halves):
                total, layout = wides[layer][half], wide_layouts[half]
                self.items.append((3, layer, total, layout, 1, 1 + 2 * layers + layer, half))
                self.items.append((4, layer, total, layout, 0, 1 + 3 * layers + layer, half))
        self.items.append((5, None, head, head_layout, 0, 1 + 4 * layers, 0))
        self.vector_start = 2 + 4 * layers

    def place(self, array, layer, block, half):
        across, up = block, 0
        if array == 3 and self.halves == 2:
            across = 2 * block + half
        if array == 4:
            across, up = block % 4, block // 4 + half * (4 // self.halves)
        rows, cols = up * self.rows, across * 128
        if not isinstance(block, int):
            rows, cols = pl.multiple_of(rows, self.rows), pl.multiple_of(cols, 128)
        where = (pl.ds(rows, self.rows), pl.ds(cols, 128))
        return where if layer is None else (layer,) + where


def state_of(block_devices, layers, halves, r):
    zero = [getattr(r, f"{REDUCED[6]}_{WIDE[half]}") for half in range(halves)]
    one = [getattr(r, f"{REDUCED[6]}_one_{WIDE[half]}") for half in range(halves)]
    return State(
        block_devices, layers, r.total_b.shape[1], halves, (zero, one), (r.total_b, r.total_b_one), r.total_head
    )


def tail_kernel(sizes, layers, r):
    (stream_devices, block_devices, streams, span, heads, features, nvec, halves) = sizes
    place = Place(stream_devices, block_devices)
    index = lax.axis_index(STREAM)
    sems = (r.out_sem, r.in_sem)
    wide_name = WIDE[halves - 1]
    broad = Reduce(place, sems, 0, total=getattr(r, f"{REDUCED[6]}_{wide_name}"))
    narrow = Reduce(place, sems, 4 * halves, own=r.own_b, line=r.line_b, total=r.total_b)
    small = Reduce(
        place,
        sems,
        4 * halves + 4,
        grad=r.grad_small,
        pair=r.pair_small,
        mates=r.mates_small,
        own=r.own_small,
        line=r.line_small,
        total=r.total_small,
    )
    r.fetch()
    broad.total[broad.piece(place.block)] = getattr(r, f"{REDUCED[5]}_{wide_name}")[...]
    barrier = pltpu.get_barrier_semaphore()
    everyone = stream_devices * block_devices
    mine = place.block * stream_devices + index

    def device_of(number):
        return {SEQ: lax.div(number, stream_devices), STREAM: lax.rem(number, stream_devices)}

    def greet(distance, carry):
        device = device_of(lax.rem(mine + distance, everyone))
        pl.semaphore_signal(barrier, inc=1, device_id=device, device_id_type=MESH)
        return carry

    lax.fori_loop(1, everyone, greet, 0)
    pl.semaphore_wait(barrier, everyone - 1)
    small.start_a()
    narrow.start_c()
    rows = r.total_b.shape[1]
    state = state_of(block_devices, layers, halves, r)
    arrays = [[getattr(r, f"{kind}_{number}") for number in range(7)] for kind in KINDS]
    weights, firsts, seconds = arrays
    square = jnp.zeros((rows, 128), f32)
    finished = [getattr(r, f"{REDUCED[6]}_{WIDE[half]}") for half in range(halves)] + [r.total_b_one, r.total_head]
    finished += [getattr(r, f"{REDUCED[6]}_one_{WIDE[half]}") for half in range(halves)]
    for ref in finished:
        size = ref.shape[0] // block_devices
        value = ref[pl.ds(place.block * size, size)].astype(f32)
        square = square + jnp.sum(value * value, axis=0)
    small.end_a()
    small.start_b()
    for array in arrays:
        r.ready(*array)

    shares = []
    for array, layer, total, layout, part, matrix, half in state.items:
        base, per, count = layout.parts[part]
        for number in range(per):
            block = place.block * per + number
            valid = jnp.where(block < count, 1.0, 0.0)
            spot = state.place(array, layer, jnp.minimum(block, count - 1), half)
            shares.append((array, spot, total, place.block * layout.size + base + number, matrix, valid))
    edge = jnp.where(place.block == 0, 1.0, 0.0)

    def matrix_squares(value_of, turned, vector_rows, base):
        found = {}
        for array, spot, total, block, matrix, valid in shares:
            value = value_of(array, spot, total, block)
            value = value * value * valid
            found[matrix] = value if matrix not in found else found[matrix] + value
        entries = [(base + matrix, jnp.sum(value)) for matrix, value in found.items()]
        entries.append((base, jnp.sum(turned * turned) * edge))
        row = lanes_of(entries)
        lane = lax.broadcasted_iota(jnp.int32, (nvec, 128), 1)
        down = lax.broadcasted_iota(jnp.int32, (nvec, 128), 0)
        column = jnp.sum(vector_rows * vector_rows, axis=1, keepdims=True) * edge
        return row + jnp.sum(jnp.where(lane == base + state.vector_start + down, column, 0.0), axis=0, keepdims=True)

    weight_row = matrix_squares(
        lambda array, spot, total, block: weights[array][spot], weights[0][...], weights[6][...], 64
    )
    narrow.end_c()
    size = r.total_b.shape[0] // block_devices
    value = r.total_b[pl.ds(place.block * size, size)].astype(f32)
    square = square + jnp.sum(value * value, axis=0)
    small.end_b()
    small.start_c()

    def exchange(ref, slot, meanwhile=None):
        def copy(view, device):
            return pltpu.make_async_remote_copy(
                src_ref=view,
                dst_ref=view,
                send_sem=r.all_out.at[slot],
                recv_sem=r.all_in.at[slot],
                device_id=device,
                device_id_type=MESH,
            )

        def send(distance, carry):
            copy(ref.at[mine], device_of(lax.rem(mine + distance, everyone))).start()
            return carry

        lax.fori_loop(1, everyone, send, 0)
        if meanwhile is not None:
            meanwhile()
        others = copy(ref.at[pl.ds(0, everyone - 1)], place.sibling)
        others.wait_recv()
        others.wait_send()
        return jnp.sum(ref[...], axis=0)

    lane = lax.broadcasted_iota(jnp.int32, (8, 128), 1)
    down = lax.broadcasted_iota(jnp.int32, (8, 128), 0)
    plain = jnp.where(lane == 1, r.loss[...], 0.0) * jnp.where(down == 0, 1.0, 0.0)
    for layer, ref in enumerate((r.gs_zero, r.gs_one)):
        plain = plain + jnp.where(lane == 16 + layer * heads + down, ref[...], 0.0)
    plain = jnp.sum(plain, axis=0, keepdims=True) + weight_row
    small.end_c()
    size = r.total_small.shape[0] // block_devices
    value = r.total_small[pl.ds(place.block * size, size)].astype(f32)
    square = square + jnp.sum(value * value, axis=0)
    r.rows_one[mine] = plain + lanes_of([(0, jnp.sum(square))])

    def hand_round():
        broad.start_d()
        narrow.start_d()
        small.start_d()

    sums = exchange(r.rows_one, 0, hand_round)
    for group in (broad, narrow, small):
        group.pass_d()
    lane = lax.broadcasted_iota(jnp.int32, (1, 128), 1)
    slope_lanes = jnp.logical_and(lane >= 16, lane < 16 + layers * heads)
    clip = jnp.sqrt(
        jnp.full((1, 128), pick(sums, 0)) + jnp.sum(jnp.where(slope_lanes, sums * sums, 0.0), axis=1, keepdims=True)
    )
    factor = jnp.minimum(1.0, clip_limit / clip)
    scale = factor[:, 0:1]

    def direction(weight, grad, first, second):
        return adam_direction(weight, grad, first, second, decay_rate)[2]

    both = r.total_small[place.block * size + state.small].astype(f32)
    turned = direction(weights[0][...], both[:, :features] * scale, firsts[0][...], seconds[0][...])
    vector_rows = direction(
        weights[6][...], both.T[features : features + nvec] * scale, firsts[6][...], seconds[6][...]
    )
    r.rows_two[mine] = matrix_squares(
        lambda array, spot, total, block: direction(
            weights[array][spot], total[block].astype(f32) * factor, firsts[array][spot], seconds[array][spot]
        ),
        turned,
        vector_rows,
        0,
    )
    r.sums[0:1, :] = exchange(r.rows_two, 1)
    r.sums[1:2, :] = jnp.concatenate([sums[:, 64:], sums[:, :64]], axis=1)
    r.sums[2:3, :] = sums
    r.sums[3:4, :] = clip
    r.sums[4:5, :] = factor
    broad.end_d()
    narrow.end_d()
    small.end_d()


def update_kernel(sizes, layers, r):
    (stream_devices, block_devices, streams, span, heads, features, nvec, halves) = sizes
    keep = pltpu.make_async_copy(r.low, r.layer_inputs, r.keep_sem.at[0])
    weights, firsts, seconds = ([getattr(r, f"{kind}_{number}") for number in range(7)] for kind in KINDS)
    fresh, new_firsts, new_seconds = ([getattr(r, f"new_{kind}_{number}") for number in range(7)] for kind in KINDS)
    state = state_of(block_devices, layers, halves, r)
    totals = {id(item[2]): item[2] for item in state.items}
    r.fetch(r.total_small, *totals.values())
    for number in (0, 6, 1, 2):
        r.fetch(weights[number], firsts[number], seconds[number])
    r.ready(r.total_small, *totals.values())
    factor = r.sums[4:5, :]
    scale = factor[:, 0:1]
    norms = jnp.sqrt(r.sums[0:2, :])
    ratios = norms[1:2] / norms[0:1]
    small = r.total_small[state.small].astype(f32)
    lane = lax.broadcasted_iota(jnp.int32, (nvec, 128), 1)
    down = lax.broadcasted_iota(jnp.int32, (nvec, 128), 0)
    vector_ratio = jnp.sum(jnp.where(lane == state.vector_start + down, ratios, 0.0), axis=1, keepdims=True)

    def finish(array):
        r.flush(fresh[array], new_firsts[array], new_seconds[array])

    for array, grad, ratio in (
        (0, small[:, :features], jnp.full((1, 1), pick(ratios, 0))),
        (6, small.T[features : features + nvec], vector_ratio),
    ):
        r.ready(weights[array], firsts[array], seconds[array])
        weight = weights[array][...]
        first, second, direction = adam_direction(
            weight, grad * scale, firsts[array][...], seconds[array][...], decay_rate
        )
        new_firsts[array][...] = first
        new_seconds[array][...] = second
        fresh[array][...] = weight - lamb_rate * ratio * direction
        finish(array)
    for number in range(1, 6):
        if number + 2 < 6:
            r.fetch(weights[number + 2], firsts[number + 2], seconds[number + 2])
        elif number + 2 == 6:
            r.fetch(r.low)
        r.ready(weights[number], firsts[number], seconds[number])
        for array, layer, total, layout, part, matrix, half in state.items:
            if array != number:
                continue
            ratio = jnp.full((1, 128), lamb_rate * pick(ratios, matrix))
            for block in range(layout.parts[part][2]):
                spot = state.place(array, layer, block, half)
                weight = weights[array][spot]
                first, second, direction = adam_direction(
                    weight,
                    total[layout.spot(part, block)].astype(f32) * factor,
                    firsts[array][spot],
                    seconds[array][spot],
                    decay_rate,
                )
                new_firsts[array][spot] = first
                new_seconds[array][spot] = second
                fresh[array][spot] = weight - ratio * direction
        finish(number)
    r.ready(r.low)
    keep.start()
    sums = r.sums[2:3, :]
    grad = jnp.concatenate([sums[:, 16 + layer * heads : 16 + (layer + 1) * heads] for layer in range(layers)], axis=0)
    slopes = r.slopes[...]
    first, second, direction = adam_direction(slopes, grad * scale, r.first_slopes[...], r.second_slopes[...], 0.0)
    r.new_first_slopes[...] = first
    r.new_second_slopes[...] = second
    r.fresh_slopes[...] = slopes - slope_rate * direction
    count = state.vector_start + nvec
    r.norms[0:1, 0:count] = norms[1:2, :count]
    r.norms[1:2, 0:count] = norms[0:1, :count]
    r.norms[0:1, count : count + 1] = jnp.full((1, 1), jnp.sqrt(jnp.sum(slopes * slopes)))
    r.norms[1:2, count : count + 1] = jnp.full((1, 1), jnp.sqrt(jnp.sum(direction * direction)))
    r.loss[...] = sums[:, 1:2]
    r.clip[...] = r.sums[3:4, 0:1]
    r.flushed()
    keep.wait()


def whole(space=pltpu.VMEM):
    return pl.BlockSpec(memory_space=space)


def call_named(
    kernel,
    ins,
    outs,
    scratch=None,
    sems=None,
    any_ins=None,
    lazy=None,
    flush=None,
    any_outs=None,
    smem=None,
    layer=None,
    layered=(),
    flops=0,
    collective=None,
):
    any_ins, lazy, flush = any_ins or {}, lazy or {}, flush or {}
    any_outs, smem = any_outs or {}, smem or {}
    scratch, sems = dict(scratch or {}), dict(sems or {})
    dma = pltpu.SemaphoreType.DMA
    for key, array in lazy.items():
        scratch[key] = (array.shape[1:] if key in layered else array.shape, array.dtype)
    scratch.update(flush)
    if lazy:
        sems.update(load_sem=dma((len(lazy),)))
    if flush:
        sems.update(store_sem=dma((len(flush),)))
    far = [FAR + key for key in lazy]
    names = list(ins) + list(any_ins) + far + list(smem)
    names += list(outs) + list(any_outs) + [FAR + key for key in flush] + list(scratch) + list(sems)
    out_shapes = list(outs.values()) + list(any_outs.values()) + list(flush.values())
    made = pl.pallas_call(
        lambda *refs: kernel(Refs(names, refs, lazy, flush, layer, layered)),
        name=kernel.func.__name__ if layer is None else f"{kernel.func.__name__}_{layer}",
        out_shape=[jax.ShapeDtypeStruct(*out) for out in out_shapes],
        in_specs=[whole()] * len(ins)
        + [whole(pl.ANY)] * (len(any_ins) + len(lazy))
        + [whole(pltpu.SMEM)] * len(smem),
        out_specs=[whole()] * len(outs) + [whole(pl.ANY)] * (len(any_outs) + len(flush)),
        scratch_shapes=[pltpu.VMEM(*item) for item in scratch.values()] + list(sems.values()),
        compiler_params=pltpu.CompilerParams(
            vmem_limit_bytes=VMEM_LIMIT, collective_id=collective, has_side_effects=collective is not None
        ),
        cost_estimate=pl.CostEstimate(flops=flops, bytes_accessed=20000000, transcendentals=0),
    )(*ins.values(), *any_ins.values(), *lazy.values(), *smem.values())
    return dict(zip(list(outs) + list(any_outs) + list(flush), made))


class Made:
    def __init__(self, *args, **options):
        for name, array in call_named(*args, **options).items():
            setattr(self, name, array)


class Groups:
    def __init__(self, layout, shapes):
        self.layout = layout
        for name, shape in shapes.items():
            setattr(self, name, shape)


def adam_direction(weight, grad, first, second, decay):
    new_first = beta_one * first + (1.0 - beta_one) * grad
    new_second = beta_two * second + (1.0 - beta_two) * grad * grad
    second_hat = new_second * (1.0 / (1.0 - beta_two**STEP))
    below = second_hat * lax.rsqrt(second_hat) + adam_eps
    return (new_first, new_second, (new_first * (1.0 / (1.0 - beta_one**STEP))) / below + decay * weight)


def shards(
    frames,
    targets,
    frame_count,
    memory,
    memory_len,
    input_weight,
    project_weight,
    output_weight,
    up_weight,
    down_weight,
    head_weight,
    vectors,
    slopes,
    first_input,
    first_project,
    first_output,
    first_up,
    first_down,
    first_head,
    first_vectors,
    first_slopes,
    second_input,
    second_project,
    second_output,
    second_up,
    second_down,
    second_head,
    second_vectors,
    second_slopes,
):
    streams, span, features = frames.shape
    layers, heads = slopes.shape
    nvec = vectors.shape[0]
    width = project_weight.shape[2] // 3
    hidden = up_weight.shape[2]
    codes = head_weight.shape[1]
    count = streams * span
    devices, blocks = lax.axis_size(STREAM), lax.axis_size(SEQ)
    halves = 2 if hidden // devices == 256 else 1
    chips = devices // 2
    sizes = (devices, blocks, streams, span, heads, features, nvec, halves)
    memory_flat = memory.reshape((layers, count, width))
    rows_each = width // devices
    full = ((count, width), f32)
    low = ((count, width), bf16)
    joined = ((2 * count, width), bf16)
    wide = ((count, hidden), bf16)
    lse = ((streams * heads, span), f32)
    cost = 2 * count * (5 * width * width + width * width + 2 * width * hidden) + 4 * count * 2 * span * width
    dma = pltpu.SemaphoreType.DMA

    def gathered(rows_all, cols):
        return ((chips, 2, rows_all // devices, cols), bf16)

    def grads_of(number):
        return dict(
            grad=((chips, 2, number, rows_each, 128), bf16),
            pair=((chips, number, rows_each, 128), bf16),
            mates=((chips, number, rows_each, 128), bf16),
            own=((number, rows_each, 128), bf16),
            line=((blocks, number // blocks, rows_each, 128), bf16),
            part=((number // blocks, rows_each, 128), bf16),
            total=((number, rows_each, 128), bf16),
        )

    wide_layouts, *other_layouts = layouts(blocks, halves)
    group_b, group_small, group_head = (Groups(layout, grads_of(layout.total)) for layout in other_layouts)
    groups_wide = [Groups(layout, grads_of(layout.total)) for layout in wide_layouts]

    def wide_named(name, form=""):
        return {f"{name}{form}_{WIDE[half]}": getattr(group, name) for half, group in enumerate(groups_wide)}

    def of(source, name, form="", start=0, end=halves):
        names = [f"{name}{form}_{WIDE[half]}" for half in range(start, end)]
        return {key: getattr(source, key) for key in names}

    def last_named(name):
        return {f"{name}_{WIDE[halves - 1]}": getattr(groups_wide[-1], name)}

    def early_named(name):
        return {f"{name}_{WIDE[half]}": getattr(group, name) for half, group in enumerate(groups_wide[:-1])}

    grad_name, pair_name, mates_name, own_name, line_name, part_name, total_name = REDUCED
    kept = dict(
        a=low, ap=low, q=low, k=joined, v=joined, o=low, lse=lse, r1=full, a2=low, u=wide, gp=wide, res=full, low=low
    )
    weight_shapes = dict(
        wp=gathered(width, 3 * width), wo=gathered(width, width), wu=gathered(width, hidden), wd=gathered(hidden, width)
    )
    layer_weights = {f"{key}_{layer}": item for layer in range(layers) for key, item in weight_shapes.items()}
    gather_count = 2 + len(layer_weights)
    score = ((2 * span, span // 2), f32)
    chance = ((2 * span, span // 2), bf16)
    scalars = dict(memory_len=memory_len, slopes=slopes)
    made = Made(
        functools.partial(forward_kernel, sizes),
        dict(
            frames=frames.transpose((0, 2, 1)),
            targets=targets.reshape((count // 128, 128)),
            input_turned=input_weight.T,
            vectors=vectors,
        ),
        dict(
            rows=((16, width), f32),
            gr_last=((8, width), f32),
            loss=((8, 128), f32),
            grad_head=group_head.grad,
            halo=((count, 128), bf16),
            frames_wide=((count, 128), bf16),
        ),
        dict(
            kept,
            **layer_weights,
            res_two=full,
            pr=full,
            nxt=low,
            behind=low,
            small=gathered(width, 128),
            wh=gathered(width, codes),
            small_rows=((128 - features, rows_each), f32),
            frames_tall=((128, span), bf16),
            kf=((streams, 2, 2 * span, 128), bf16),
            acc=((width, codes), f32),
            score_one=score,
            score_two=score,
            chance_one=chance,
            chance_two=chance,
        ),
        dict(
            out_sem=dma((gather_count, max(chips, 5))),
            in_sem=dma((gather_count, max(chips, 5))),
            frame_sem=dma((2, 1)),
            next_out=dma((streams,)),
            next_in=dma((streams,)),
            save_sem=dma((layers, len(kept), streams)),
            weight_sem=dma((layers, 4)),
            pr_sem=dma((streams,)),
            dr_sem=dma((1,)),
        ),
        any_outs=dict(
            far_pr=full,
            dr=full,
            **{FAR + key: ((layers,) + item[0], item[1]) for key, item in kept.items()},
            **{FAR + key: item for key, item in layer_weights.items()},
        ),
        lazy=dict(
            pw=project_weight, ow=output_weight, uw=up_weight, dw=down_weight, hw=head_weight, mem=memory_flat
        ),
        smem=dict(scalars, frame_count=frame_count),
        flops=2 * cost,
        collective=0,
    )

    def loaded(layer):
        held = [getattr(made, f"{FAR}{key}_{layer}") for key in weight_shapes]
        return dict(
            wd=held[3],
            a2=made.far_a2,
            wu=held[2],
            r1=made.far_r1,
            wo=held[1],
            o=made.far_o,
            lse=made.far_lse,
            q=made.far_q,
            k=made.far_k,
            v=made.far_v,
            wp=held[0],
            a=made.far_a,
            ap=made.far_ap,
        )

    layered = tuple(kept) + tuple(dict(mem=0))
    slots = max(chips, blocks)
    work = dict(
        do=low,
        dq=low,
        dk=joined,
        dv=joined,
        turned=((width, count), bf16),
        kf=((streams, 2, 2 * span, 128), bf16),
        **wide_named(pair_name),
        **wide_named(mates_name),
        **wide_named(grad_name),
        u_two=((2, count, 512), bf16),
        gp_two=((2, count, 512), bf16),
    )
    work_sems = dict(out_sem=dma((8 + 8 * halves, slots)), in_sem=dma((8 + 8 * halves, slots)), u_sem=dma((2, 2)), first_sem=dma((5,)))
    streamed = dict(u=made.far_u, gp=made.far_gp)
    one = Made(
        functools.partial(backward_kernel, 1, sizes),
        dict(rows=made.rows, grad_head=made.grad_head),
        dict(
            gr=((8, width), f32),
            gs=((8, 128), f32),
            dr=full,
            da=full,
            back=low,
            **wide_named(own_name),
            pair_b=group_b.pair,
            total_head=group_head.total,
        ),
        dict(
            work,
            dap=low,
            grad_b=group_b.grad,
            pair_head=group_head.pair,
            mates_head=group_head.mates,
            own_head=group_head.own,
            line_head=group_head.line,
        ),
        dict(work_sems, back_out=dma((streams,)), back_in=dma((streams,))),
        any_ins=dict(streamed, dr_in=made.dr),
        lazy=dict(loaded(1), mem=memory_flat),
        layered=layered,
        layer=1,
        smem=scalars,
        flops=2 * cost,
        collective=2,
    )
    zero = Made(
        functools.partial(backward_kernel, 0, sizes),
        dict(
            rows=made.rows,
            frames=made.frames_wide,
            halo=made.halo,
            back=one.back,
            gr_last=made.gr_last,
            gr_one=one.gr,
            **{f"{own_name}_one_{WIDE[half]}": getattr(one, f"{own_name}_{WIDE[half]}") for half in range(halves)},
            pair_b_one=one.pair_b,
        ),
        dict(
            gs=((8, 128), f32),
            **last_named(part_name),
            **early_named(total_name),
            own_b=group_b.own,
            grad_small=group_small.grad,
            **wide_named(total_name, form="_one"),
            total_b_one=group_b.total,
        ),
        dict(
            work,
            gr=((8, width), f32),
            dr=full,
            da=full,
            small_acc=((width, 128), f32),
            wide_one=full,
            **wide_named(own_name),
            **wide_named(line_name),
            **wide_named(line_name, form="_one"),
            grad_b=group_b.grad,
            pair_b=group_b.pair,
            mates_b=group_b.mates,
            mates_b_one=group_b.mates,
            own_b_one=group_b.own,
            line_b_one=group_b.line,
        ),
        work_sems,
        any_ins=dict(streamed, dr1_in=one.dr, da_in=one.da, r=made.far_res, pr=made.far_pr),
        lazy=loaded(0),
        layered=layered,
        layer=0,
        smem=scalars,
        flops=2 * cost,
        collective=3,
    )
    arrays = (
        (input_weight.T, project_weight, output_weight, up_weight, down_weight, head_weight, vectors),
        (first_input.T, first_project, first_output, first_up, first_down, first_head, first_vectors),
        (second_input.T, second_project, second_output, second_up, second_down, second_head, second_vectors),
    )
    order = (0, 6, 1, 2, 3, 4, 5)
    state = {f"{kind}_{number}": array[number] for number in order for kind, array in zip(KINDS, arrays)}
    tile_shape = ((8, 128), f32)
    tail = Made(
        functools.partial(tail_kernel, sizes, layers),
        dict(
            **of(zero, part_name, start=halves - 1),
            **of(zero, total_name, end=halves - 1),
            own_b=zero.own_b,
            grad_small=zero.grad_small,
            **of(zero, total_name, form="_one"),
            total_b_one=zero.total_b_one,
            total_head=one.total_head,
            gs_zero=zero.gs,
            gs_one=one.gs,
            loss=made.loss,
        ),
        dict(last_named(total_name), total_b=group_b.total, total_small=group_small.total, sums=tile_shape),
        dict(
            line_b=group_b.line,
            pair_small=group_small.pair,
            mates_small=group_small.mates,
            own_small=group_small.own,
            line_small=group_small.line,
            rows_one=((devices * blocks, 1, 128), f32),
            rows_two=((devices * blocks, 1, 128), f32),
        ),
        dict(
            out_sem=dma((8 + 4 * halves, slots)),
            in_sem=dma((8 + 4 * halves, slots)),
            all_out=dma((2,)),
            all_in=dma((2,)),
        ),
        lazy=state,
        collective=4,
    )
    moved = {f"new_{kind}_{number}": (array[number].shape, f32) for number in order for kind, array in zip(KINDS, arrays)}
    fresh = Made(
        functools.partial(update_kernel, sizes, layers),
        dict(slopes=slopes, first_slopes=first_slopes, second_slopes=second_slopes, sums=tail.sums),
        dict(
            fresh_slopes=(slopes.shape, f32),
            new_first_slopes=(slopes.shape, f32),
            new_second_slopes=(slopes.shape, f32),
            norms=((2, 3 + 4 * layers + nvec), f32),
            loss=((1, 1), f32),
            clip=((1, 1), f32),
        ),
        sems=dict(keep_sem=dma((1,))),
        any_outs=dict(layer_inputs=((layers, count, width), bf16)),
        lazy=dict(
            **of(tail, total_name, start=halves - 1),
            **of(zero, total_name, end=halves - 1),
            total_b=tail.total_b,
            total_small=tail.total_small,
            **of(zero, total_name, form="_one"),
            total_b_one=zero.total_b_one,
            total_head=one.total_head,
            **state,
            low=made.far_low,
        ),
        flush=moved,
    )

    def results(kind, last):
        found = [getattr(fresh, f"new_{kind}_{number}") for number in range(7)]
        return [found[0].T] + found[1:] + [last]

    return (
        fresh.loss.reshape(()),
        fresh.layer_inputs.reshape((layers, streams, span, width)),
        fresh.clip.reshape(()),
        fresh.norms.T,
        *results(KINDS[0], fresh.fresh_slopes),
        *results(KINDS[1], fresh.new_first_slopes),
        *results(KINDS[2], fresh.new_second_slopes),
    )


def solution(mesh):
    rows3 = P(None, STREAM, None)
    state = (P(None, STREAM), rows3, rows3, rows3, rows3, P(STREAM, None), P(None, STREAM), P())
    in_specs = (
        P(STREAM, SEQ, None),
        P(STREAM, SEQ),
        P(STREAM),
        P(None, STREAM, None, None),
        P(STREAM),
    ) + state * 3
    out_specs = (P(), P(None, STREAM, SEQ, None), P(), P()) + state * 3
    return jax.shard_map(shards, mesh=mesh, in_specs=in_specs, out_specs=out_specs, check_vma=False)
```
